32 devices in a mesh: groups: 2 (over y), dp: 4 (over z), owner: 4 (over x, core).
Axes of the slice: x: 2, y: 2, z: 4, core: 2. Of those that a mesh axis runs over, the one named last changes fastest.
Arguments:
- activations: bfloat16 [4096, 4096], P(('groups', 'dp'), 'owner'), parts along dimension 0, may hold values from -64 to 64
- gradients: bfloat16 [4096, 14336], P(('groups', 'dp'), 'owner'), parts along dimension 0, may hold values from -64 to 64
- basis_act: bfloat16 [32, 128, 128], P('owner', 'dp'), may hold values from -0.5 to 0.5
- basis_grad: bfloat16 [112, 128, 128], P('owner', 'dp'), may hold values from -0.5 to 0.5
Outputs:
- act_covariance: float32 [64, 128, 128], P(('groups', 'owner'), 'dp'), parts along dimension 0
- grad_covariance: float32 [224, 128, 128], P(('groups', 'owner'), 'dp'), parts along dimension 0
- act_eigen: float32 [8192], P(('groups', 'owner')), parts along dimension 0
- grad_eigen: float32 [28672], P(('groups', 'owner')), parts along dimension 0
- token_scores: float32 [4096], P(('groups', 'dp')), parts along dimension 0
The draws below stay inside these ranges and needn't reach their ends.
There are 2 independent parts, one for each index of `groups`. The reference program is written for one: setup_inputs(seed, part) draws one part's arguments, and reference() takes and returns one part's arrays. A program takes and returns all parts, laid end to end along the dimension named above; an argument that names none is the same for every part. Nothing has to cross between parts.
All inputs are finite; a program needn't handle non-finite values.
Results may differ from the reference program's by a relative error of at most 0.0003.
Values may be sent and summed in bfloat16 or wider, within the bound.
No kernel may reach another device: no remote copies, remote signals or barrier semaphores. Data moves between devices by JAX's collectives and lax.ppermute only.
A program may use at most 64 MiB of HBM per device.

```python
import math
import jax
import jax.numpy as jnp
from jax import lax

D = 4096
FF = 14336
BLK = 128
TOKENS = 2048


def shape_field(base, key_rows, key_cols, spread):
    total_rows = base.shape[0]
    width = base.shape[1]
    positions = jnp.arange(total_rows, dtype=jnp.float32)[:, None]
    row_scale = jnp.sqrt((1.0 + 2.2 * positions / total_rows) / 3.2)
    row_scale = row_scale * jnp.exp(jax.random.uniform(key_rows, (total_rows, 1), jnp.float32, -0.9, 0.9))
    columns = jnp.arange(width, dtype=jnp.float32)[None, :]
    col_scale = jnp.sqrt((1.0 + 4.0 * columns / width) / 5.0)
    col_scale = col_scale * jnp.exp(jax.random.uniform(key_cols, (1, width), jnp.float32, -math.log(spread), math.log(spread)))
    return base * row_scale * col_scale


def shared_part(loads, directions):
    return 0.7071 * (loads[:, 0:1] * directions[0:1, :] + loads[:, 1:2] * directions[1:2, :])


def draw_activations(key, part):
    key = jax.random.fold_in(key, 11)
    keys = jax.random.split(key, 5)
    directions = jax.random.uniform(keys[4], (2, D), jnp.float32, -1.0, 1.0)
    noise = jax.random.truncated_normal(keys[0], -3.0, 3.0, (TOKENS, D), jnp.float32)
    loads = jax.random.truncated_normal(keys[3], -3.0, 3.0, (TOKENS, 2), jnp.float32)
    spread = 3.2
    base = 0.7 * noise + shared_part(loads, directions)
    return shape_field(base, keys[1], keys[2], spread).astype(jnp.bfloat16)


def draw_gradients(key, part):
    key = jax.random.fold_in(key, 12)
    keys = jax.random.split(key, 5)
    directions = jax.random.uniform(keys[4], (2, FF), jnp.float32, -1.0, 1.0)
    noise = jax.random.truncated_normal(keys[0], -3.0, 3.0, (TOKENS, FF), jnp.float32)
    loads = jax.random.truncated_normal(keys[3], -3.0, 3.0, (TOKENS, 2), jnp.float32)
    spread = 3.2
    base = 0.7 * noise + shared_part(loads, directions)
    return shape_field(base, keys[1], keys[2], spread).astype(jnp.bfloat16)


def block_levels(rng, dims, pieces, least, largest):
    def one(axis_at, blocks):
        draws = jax.random.uniform(jax.random.fold_in(jax.random.fold_in(rng, 6), axis_at), (blocks,), jnp.float32, least / len(pieces), largest / len(pieces))
        return jnp.repeat(jnp.exp(draws), dims[axis_at] // blocks).reshape((-1,) + (1,) * (len(dims) - axis_at - 1))

    gain = one(*pieces[0])
    for cut in pieces[1:]:
        gain = gain * one(*cut)
    return gain


def centred(key, extent, scale, most, pieces=(), held_as=jnp.bfloat16):
    loudness = block_levels(key, extent, pieces, -0.22, 0.18) if pieces else 1.0
    array = jax.random.normal(key, extent, jnp.float32) * scale * loudness
    return jnp.minimum(jnp.maximum(array, -most), most).astype(held_as)


def setup_inputs(seed: int = 0, part: int = 0) -> dict:
    streams_of = jax.random.split(jax.random.key(seed), 5)
    own_keys = jax.random.split(jax.random.fold_in(streams_of[4], part), 5)
    activations = draw_activations(jax.random.fold_in(jax.random.fold_in(streams_of[4], part), 71), part)
    gradients = draw_gradients(jax.random.fold_in(jax.random.fold_in(streams_of[4], part), 71), part)
    basis_act = centred(streams_of[2], (D // BLK, BLK, BLK), BLK ** -0.5, 0.5, ((0, 4), (1, 4)))
    basis_grad = centred(streams_of[3], (FF // BLK, BLK, BLK), BLK ** -0.5, 0.5, ((0, 4), (1, 4)))
    return {"activations": activations, "gradients": gradients, "basis_act": basis_act, "basis_grad": basis_grad}


highest = lax.Precision.HIGHEST
damp_root = 0.31622776601683794


def project_rows(values, basis_blocks):
    blocks = values.astype(jnp.float32).reshape(values.shape[0], -1, BLK)
    projected = jnp.einsum("tni,nij->tnj", blocks, basis_blocks.astype(jnp.float32), precision=highest)
    return projected.reshape(values.shape[0], -1)


def rayleigh(covariance, basis_blocks):
    basis_wide = basis_blocks.astype(jnp.float32)
    rotated = jnp.einsum("nrk,nkj->nrj", covariance, basis_wide, precision=highest)
    return jnp.sum(rotated * basis_wide, axis=1).reshape(-1)


def reference(activations, gradients, basis_act, basis_grad):
    block_rows = min(2048, TOKENS)
    block_count = TOKENS // block_rows

    def gram_step(carry, position):
        first_row = position * block_rows
        act_rows = lax.dynamic_slice_in_dim(activations, first_row, block_rows, 0).astype(jnp.float32).reshape(block_rows, -1, BLK)
        grad_rows = lax.dynamic_slice_in_dim(gradients, first_row, block_rows, 0).astype(jnp.float32).reshape(block_rows, -1, BLK)
        act_sum = carry[0] + jnp.einsum("tni,tnj->nij", act_rows, act_rows, precision=highest)
        grad_sum = carry[1] + jnp.einsum("tni,tnj->nij", grad_rows, grad_rows, precision=highest)
        return (act_sum, grad_sum), None

    initial = (jnp.zeros((D // BLK, BLK, BLK), jnp.float32), jnp.zeros((FF // BLK, BLK, BLK), jnp.float32))
    sums, unused = lax.scan(gram_step, initial, jnp.arange(block_count, dtype=jnp.int32))
    act_covariance = sums[0] * (1.0 / TOKENS)
    grad_covariance = sums[1] * (1.0 / TOKENS)
    act_eigen = rayleigh(act_covariance, basis_act)
    grad_eigen = rayleigh(grad_covariance, basis_grad)
    damp_act = damp_root * jnp.mean(act_eigen)
    damp_grad = damp_root * jnp.mean(grad_eigen)

    def score_block(position):
        first_row = position * block_rows
        proj_act = project_rows(lax.dynamic_slice_in_dim(activations, first_row, block_rows, 0), basis_act)
        proj_grad = project_rows(lax.dynamic_slice_in_dim(gradients, first_row, block_rows, 0), basis_grad)
        act_weight = jnp.sum(proj_act * proj_act / (act_eigen[None, :] + damp_act), axis=1)
        grad_weight = jnp.sum(proj_grad * proj_grad / (grad_eigen[None, :] + damp_grad), axis=1)
        return act_weight * grad_weight

    scores = lax.map(score_block, jnp.arange(block_count, dtype=jnp.int32)).reshape(-1)
    token_scores = scores * (1.0 / (D * FF))
    return act_covariance, grad_covariance, act_eigen, grad_eigen, token_scores
```

```python
import functools

import jax
import jax.numpy as jnp
from jax import lax
from jax.experimental import pallas as pl
from jax.experimental.pallas import tpu as pltpu
from jax.sharding import PartitionSpec as P

D = 4096
FF = 14336
BLK = 128
STEPS = 4
VMEM_LIMIT = 48 * 1024 * 1024

damp_root = 0.31622776601683794
contract_rows = (((0,), (0,)), ((), ()))
contract_lanes = (((1,), (1,)), ((), ()))


def params():
    return pltpu.CompilerParams(vmem_limit_bytes=VMEM_LIMIT)


def gram_kernel(pieces, scale, me_ref, act_ref, grad_ref, *refs):
    out_refs, whole = refs[:pieces], refs[pieces]
    rows = BLK // pieces
    me = me_ref[0]
    act_here = act_ref.shape[1] // BLK
    grad_here = grad_ref.shape[1] // BLK
    for block in range(act_here + grad_here):
        if block < act_here:
            values = act_ref[:, block * BLK : (block + 1) * BLK]
        else:
            at = block - act_here
            values = grad_ref[:, at * BLK : (at + 1) * BLK]
        gram = lax.dot_general(
            values, values, contract_rows, preferred_element_type=jnp.float32
        )
        whole[block] = gram * scale
        for shift in range(pieces):
            first = pl.multiple_of(lax.rem(me + shift, pieces) * rows, rows)
            out_refs[shift][0, block] = whole[block, pl.ds(first, rows), :]


def partial_gram(me, activations, gradients, pieces, scale):
    tokens, act_width = activations.shape
    grad_width = gradients.shape[1]
    act_step, grad_step = act_width // STEPS, grad_width // STEPS
    blocks = (act_step + grad_step) // BLK
    rows = BLK // pieces
    return pl.pallas_call(
        functools.partial(gram_kernel, pieces, scale),
        grid_spec=pltpu.PrefetchScalarGridSpec(
            num_scalar_prefetch=1,
            grid=(STEPS,),
            in_specs=[
                pl.BlockSpec((tokens, act_step), lambda i, me: (0, i)),
                pl.BlockSpec((tokens, grad_step), lambda i, me: (0, i)),
            ],
            out_specs=[
                pl.BlockSpec((1, blocks, rows, BLK), lambda i, me: (i, 0, 0, 0))
            ]
            * pieces,
            scratch_shapes=[pltpu.VMEM((blocks, BLK, BLK), jnp.float32)],
        ),
        out_shape=[jax.ShapeDtypeStruct((STEPS, blocks, rows, BLK), jnp.float32)] * pieces,
        compiler_params=params(),
        name="partial_gram",
    )(me, activations, gradients)


def sum_kernel(*refs):
    parts, (act_ref, grad_ref) = refs[:-2], refs[-2:]
    act_here = act_ref.shape[0]
    total = parts[0][0]
    for part in parts[1:]:
        total = total + part[0]
    act_ref[...] = total[:act_here]
    grad_ref[...] = total[act_here:]


def sum_pieces(parts, act_blocks, grad_blocks):
    _, blocks, rows, _ = parts[0].shape
    return pl.pallas_call(
        sum_kernel,
        grid=(STEPS,),
        in_specs=[pl.BlockSpec((1, blocks, rows, BLK), lambda i: (i, 0, 0, 0))] * len(parts),
        out_specs=[
            pl.BlockSpec((act_blocks // STEPS, rows, BLK), lambda i: (i, 0, 0)),
            pl.BlockSpec((grad_blocks // STEPS, rows, BLK), lambda i: (i, 0, 0)),
        ],
        out_shape=[
            jax.ShapeDtypeStruct((act_blocks, rows, BLK), jnp.float32),
            jax.ShapeDtypeStruct((grad_blocks, rows, BLK), jnp.float32),
        ],
        compiler_params=params(),
        name="sum_pieces",
    )(*parts)


def project(me, values, shard_refs, block, basis):
    pieces = len(shard_refs)
    rows = BLK // pieces
    for shift in range(pieces):
        first = pl.multiple_of(lax.rem(me - shift + pieces, pieces) * rows, rows)
        basis[pl.ds(first, rows), :] = shard_refs[shift][block]
    return lax.dot_general(
        values, basis[...], (((1,), (0,)), ((), ())), preferred_element_type=jnp.float32
    )


def eigen_kernel(pieces, scale, me_ref, act_ref, grad_ref, *refs):
    act_shards, grad_shards = refs[:pieces], refs[pieces : 2 * pieces]
    eigen_ref, basis = refs[2 * pieces :]
    me = me_ref[0]
    act_here = act_ref.shape[1] // BLK
    grad_here = grad_ref.shape[1] // BLK
    for block in range(act_here + grad_here):
        if block < act_here:
            source, shards, at = act_ref, act_shards, block
        else:
            source, shards, at = grad_ref, grad_shards, block - act_here
        values = source[:, at * BLK : (at + 1) * BLK]
        projected = project(me, values, shards, at, basis.at[block])
        eigen_ref[0, block : block + 1, :] = (
            jnp.sum(projected * projected, axis=0, keepdims=True) * scale
        )


def shard_specs(shards, step_blocks):
    rows = shards[0].shape[1]
    return [pl.BlockSpec((step_blocks, rows, BLK), lambda i, me: (i, 0, 0))] * len(shards)


def partial_eigen(me, activations, gradients, act_shards, grad_shards, scale):
    tokens, act_width = activations.shape
    grad_width = gradients.shape[1]
    act_step, grad_step = act_width // STEPS, grad_width // STEPS
    blocks = (act_step + grad_step) // BLK
    pieces = len(act_shards)
    return pl.pallas_call(
        functools.partial(eigen_kernel, pieces, scale),
        grid_spec=pltpu.PrefetchScalarGridSpec(
            num_scalar_prefetch=1,
            grid=(STEPS,),
            in_specs=[
                pl.BlockSpec((tokens, act_step), lambda i, me: (0, i)),
                pl.BlockSpec((tokens, grad_step), lambda i, me: (0, i)),
                *shard_specs(act_shards, act_step // BLK),
                *shard_specs(grad_shards, grad_step // BLK),
            ],
            out_specs=pl.BlockSpec((1, blocks, BLK), lambda i, me: (i, 0, 0)),
            scratch_shapes=[pltpu.VMEM((blocks, BLK, BLK), jnp.bfloat16)],
        ),
        out_shape=jax.ShapeDtypeStruct((STEPS, blocks, BLK), jnp.float32),
        compiler_params=params(),
        name="partial_eigen",
    )(me, activations, gradients, *act_shards, *grad_shards)


def weight_kernel(pieces, me_ref, act_ref, grad_ref, eigen_ref, damp_ref, *refs):
    act_shards, grad_shards = refs[:pieces], refs[pieces : 2 * pieces]
    weight_ref, basis, act_sum, grad_sum = refs[2 * pieces :]
    me = me_ref[0]
    step = pl.program_id(0)
    act_here = act_ref.shape[1] // BLK
    grad_here = grad_ref.shape[1] // BLK

    @pl.when(step == 0)
    def _():
        act_sum[...] = jnp.zeros_like(act_sum)
        grad_sum[...] = jnp.zeros_like(grad_sum)

    for block in range(act_here + grad_here):
        if block < act_here:
            source, shards, at, total, damp = act_ref, act_shards, block, act_sum, damp_ref[0]
        else:
            source, shards, at = grad_ref, grad_shards, block - act_here
            total, damp = grad_sum, damp_ref[1]
        values = source[:, at * BLK : (at + 1) * BLK]
        projected = project(me, values, shards, at, basis.at[block])
        inverse = 1.0 / (eigen_ref[0, block : block + 1, :] + damp)
        total[...] += projected * projected * inverse

    @pl.when(step == STEPS - 1)
    def _():
        ones = jnp.ones((8, BLK), jnp.float32)
        for index, total in enumerate((act_sum, grad_sum)):
            sums = lax.dot_general(
                ones,
                total[...],
                contract_lanes,
                precision=lax.Precision.HIGHEST,
                preferred_element_type=jnp.float32,
            )
            weight_ref[index : index + 1, :] = sums[0:1]


def partial_weights(me, activations, gradients, eigen, damp, act_shards, grad_shards):
    tokens, act_width = activations.shape
    grad_width = gradients.shape[1]
    act_step, grad_step = act_width // STEPS, grad_width // STEPS
    blocks = (act_step + grad_step) // BLK
    pieces = len(act_shards)
    return pl.pallas_call(
        functools.partial(weight_kernel, pieces),
        grid_spec=pltpu.PrefetchScalarGridSpec(
            num_scalar_prefetch=1,
            grid=(STEPS,),
            in_specs=[
                pl.BlockSpec((tokens, act_step), lambda i, me: (0, i)),
                pl.BlockSpec((tokens, grad_step), lambda i, me: (0, i)),
                pl.BlockSpec((1, blocks, BLK), lambda i, me: (i, 0, 0)),
                pl.BlockSpec(memory_space=pltpu.SMEM),
                *shard_specs(act_shards, act_step // BLK),
                *shard_specs(grad_shards, grad_step // BLK),
            ],
            out_specs=pl.BlockSpec((2, tokens), lambda i, me: (0, 0)),
            scratch_shapes=[
                pltpu.VMEM((blocks, BLK, BLK), jnp.bfloat16),
                pltpu.VMEM((tokens, BLK), jnp.float32),
                pltpu.VMEM((tokens, BLK), jnp.float32),
            ],
        ),
        out_shape=jax.ShapeDtypeStruct((2, tokens), jnp.float32),
        compiler_params=params(),
        name="partial_weights",
    )(me, activations, gradients, eigen, damp, *act_shards, *grad_shards)


def rotate(value, axis, shift):
    count = lax.axis_size(axis)
    return lax.ppermute(value, axis, [(i, (i + shift) % count) for i in range(count)])


def sum_over(value, axis, direct):
    if not direct:
        return lax.psum(value, axis)
    total = value
    for shift in range(1, lax.axis_size(axis)):
        total = total + rotate(value, axis, shift)
    return total


def local(activations, gradients, basis_act, basis_grad):
    tokens = activations.shape[0]
    act_blocks, grad_blocks = basis_act.shape[0], basis_grad.shape[0]
    act_per_step = act_blocks // STEPS
    dp = lax.axis_size("dp")
    scale = 1.0 / (tokens * dp)
    direct = BLK // dp >= 32
    pieces = dp if direct else 1
    me = jnp.full((1,), lax.axis_index("dp") if direct else 0, jnp.int32)

    if direct:
        act_shards = [basis_act] + [rotate(basis_act, "dp", s) for s in range(1, dp)]
        grad_shards = [basis_grad] + [rotate(basis_grad, "dp", s) for s in range(1, dp)]
    else:
        act_shards = [lax.all_gather(basis_act, "dp", axis=1, tiled=True)]
        grad_shards = [lax.all_gather(basis_grad, "dp", axis=1, tiled=True)]

    grams = partial_gram(me, activations, gradients, pieces, scale)
    if direct:
        parts = [grams[0]] + [rotate(grams[s], "dp", s) for s in range(1, dp)]
    else:
        parts = [lax.psum_scatter(grams[0], "dp", scatter_dimension=2, tiled=True)]
    act_covariance, grad_covariance = sum_pieces(parts, act_blocks, grad_blocks)

    eigen = partial_eigen(me, activations, gradients, act_shards, grad_shards, scale)
    eigen = sum_over(eigen, "dp", direct)
    act_eigen, grad_eigen = eigen[:, :act_per_step], eigen[:, act_per_step:]
    sums = jnp.stack([jnp.sum(act_eigen), jnp.sum(grad_eigen)])
    sums = sum_over(sums, "owner", direct)
    damp = sums * jnp.array([damp_root / D, damp_root / FF], jnp.float32)
    weights = partial_weights(
        me, activations, gradients, eigen, damp, act_shards, grad_shards
    )
    weights = sum_over(weights, "owner", direct)
    token_scores = weights[0] * weights[1] * (1.0 / (D * FF))
    return (
        act_covariance,
        grad_covariance,
        act_eigen.reshape(-1),
        grad_eigen.reshape(-1),
        token_scores,
    )


def solution(mesh):
    return jax.shard_map(
        local,
        mesh=mesh,
        in_specs=(
            P(("groups", "dp"), "owner"),
            P(("groups", "dp"), "owner"),
            P("owner", "dp", None),
            P("owner", "dp", None),
        ),
        out_specs=(
            P(("groups", "owner"), "dp", None),
            P(("groups", "owner"), "dp", None),
            P(("groups", "owner")),
            P(("groups", "owner")),
            P(("groups", "dp")),
        ),
        check_vma=False,
    )
```

```python
import functools

import jax
import jax.numpy as jnp
from jax import lax
from jax.experimental import pallas as pl
from jax.experimental.pallas import tpu as pltpu
from jax.sharding import PartitionSpec as P

D = 4096
FF = 14336
BLK = 128
GROUP = 4
VMEM_LIMIT = 40 * 1024 * 1024
CODE_TOP = 2.0**7.875
SMALLEST = 1e-36

damp_root = 0.31622776601683794
contract_rows = (((0,), (0,)), ((), ()))
contract_inner = (((1,), (0,)), ((), ()))
contract_lanes = (((1,), (1,)), ((), ()))


def call(kernel, out_shape, name, flops, bytes_accessed, in_specs, scratch_shapes=()):
    return pl.pallas_call(
        kernel,
        out_shape=out_shape,
        in_specs=in_specs,
        out_specs=jax.tree.map(lambda _: pl.BlockSpec(memory_space=pltpu.VMEM), out_shape),
        scratch_shapes=scratch_shapes,
        compiler_params=pltpu.CompilerParams(vmem_limit_bytes=VMEM_LIMIT),
        cost_estimate=pl.CostEstimate(
            flops=flops, bytes_accessed=bytes_accessed, transcendentals=0
        ),
        name=name,
    )


def vmem(count):
    return [pl.BlockSpec(memory_space=pltpu.VMEM)] * count


def smem(count):
    return [pl.BlockSpec(memory_space=pltpu.SMEM)] * count


def f32(*shape):
    return jax.ShapeDtypeStruct(shape, jnp.float32)


def bf16(*shape):
    return jax.ShapeDtypeStruct(shape, jnp.bfloat16)


def over_blocks(act_ref, grad_ref, visit):
    first = 0
    for ref in (act_ref, grad_ref):
        blocks = ref.shape[1] // BLK

        @pl.loop(0, blocks // GROUP)
        def _(step, ref=ref, first=first):
            for offset in range(GROUP):
                block = step * GROUP + offset
                columns = pl.ds(pl.multiple_of(block * BLK, BLK), BLK)
                visit(ref, columns, first + block)

        first += blocks


def encode(values):
    power = values * values
    power = power * power
    power = power * power
    power = power * power
    return jnp.where(values < 0.0, -power, power).astype(jnp.bfloat16)


def decode(coded):
    coded = coded.astype(jnp.float32)
    root = jnp.abs(coded)
    for _ in range(4):
        root = lax.rsqrt(root)
    return jnp.where(coded > 0.0, root, jnp.where(coded < 0.0, -root, 0.0))


def gram_kernel(pieces, scale, me_ref, act_ref, grad_ref, own_ref, *refs):
    sent_refs, top_ref, whole = refs[: pieces - 1], refs[pieces - 1], refs[pieces]
    rows = BLK // pieces
    me = me_ref[0]

    def visit(ref, columns, block):
        values = ref[:, columns]
        gram = scale * lax.dot_general(
            values, values, contract_rows, preferred_element_type=jnp.float32
        )
        if pieces == 1:
            own_ref[block] = gram
            return
        slot = lax.rem(block, GROUP)
        whole[slot] = gram
        top = jnp.maximum(jnp.max(jnp.abs(gram), axis=0, keepdims=True), SMALLEST)
        top_ref[pl.ds(block, 1), :] = top * (1.0 / CODE_TOP)
        gain = CODE_TOP / top
        own_ref[block] = whole[slot, pl.ds(pl.multiple_of(me * rows, rows), rows), :]
        for shift in range(1, pieces):
            first = pl.multiple_of(lax.rem(me + shift, pieces) * rows, rows)
            sent_refs[shift - 1][block] = encode(whole[slot, pl.ds(first, rows), :] * gain)

    over_blocks(act_ref, grad_ref, visit)


def sum_kernel(blocks, me_ref, sums_ref, own_ref, *refs):
    sent_refs, (act_ref, grad_ref) = refs[:-2], refs[-2:]
    pieces = len(sent_refs) + 1
    me = me_ref[0]
    act_blocks = act_ref.shape[0]

    def total(block):
        value = own_ref[block]
        for shift in range(1, pieces):
            sender = lax.rem(me - shift + pieces, pieces)
            top = sums_ref[sender, pl.ds(blocks + block, 1), :]
            value = value + decode(sent_refs[shift - 1][block]) * top
        return value

    @pl.loop(0, act_blocks)
    def _(block):
        act_ref[block] = total(block)

    @pl.loop(0, blocks - act_blocks)
    def _(block):
        grad_ref[block] = total(act_blocks + block)


def eigen_kernel(pieces, scale, me_ref, side_ref, act_ref, grad_ref, top_ref, *refs):
    *shard_refs, basis_ref, sums_ref = refs
    act_blocks = act_ref.shape[1] // BLK
    blocks = act_blocks + grad_ref.shape[1] // BLK
    rows = BLK // pieces
    me, side = me_ref[0], side_ref[0]
    act_basis_ref, grad_basis_ref = shard_refs[:2]
    own = pl.ds(pl.multiple_of(me * rows, rows), rows)
    basis_ref[:act_blocks, own, :] = act_basis_ref[...]
    basis_ref[act_blocks:, own, :] = grad_basis_ref[...]
    received = shard_refs[2:]
    if received:
        halves = 2 if len(received) > pieces - 1 else 1
        act_half, grad_half = act_blocks // halves, (blocks - act_blocks) // halves
        for index, ref in enumerate(received):
            shift, other = index % (pieces - 1) + 1, index // (pieces - 1)
            half = (side + other) % halves if halves > 1 else 0
            place = pl.ds(pl.multiple_of(lax.rem(me - shift + pieces, pieces) * rows, rows), rows)
            basis_ref[pl.ds(half * act_half, act_half), place, :] = ref[:act_half]
            basis_ref[pl.ds(act_blocks + half * grad_half, grad_half), place, :] = ref[act_half:]

    def visit(ref, columns, block):
        projected = lax.dot_general(
            ref[:, columns], basis_ref[block], contract_inner, preferred_element_type=jnp.float32
        )
        sums_ref[pl.ds(block, 1), :] = scale * jnp.sum(
            projected * projected, axis=0, keepdims=True
        )

    over_blocks(act_ref, grad_ref, visit)
    sums_ref[blocks:, :] = top_ref[...]


def combine_kernel(sums_ref, act_eigen_ref, grad_eigen_ref, total_ref):
    act_blocks, grad_blocks = act_eigen_ref.shape[0], grad_eigen_ref.shape[0]
    blocks = act_blocks + grad_blocks
    eigen = jnp.sum(sums_ref[:, :blocks, :], axis=0)
    act_eigen_ref[...] = eigen[:act_blocks]
    grad_eigen_ref[...] = eigen[act_blocks:]
    total_ref[0:1, :] = jnp.sum(eigen[:act_blocks], axis=0, keepdims=True)
    total_ref[1:2, :] = jnp.sum(eigen[act_blocks:], axis=0, keepdims=True)


def weight_kernel(
    act_ref, grad_ref, basis_ref, act_eigen_ref, grad_eigen_ref, total_ref, weight_ref,
    inverse, act_sum, grad_sum,
):
    act_blocks = act_ref.shape[1] // BLK
    totals = jnp.sum(total_ref[...], axis=0)
    totals = jnp.sum(totals, axis=1, keepdims=True)
    inverse[:act_blocks] = 1.0 / (act_eigen_ref[...] + totals[0:1] * (damp_root / D))
    inverse[act_blocks:] = 1.0 / (grad_eigen_ref[...] + totals[1:2] * (damp_root / FF))
    act_sum[...] = jnp.zeros_like(act_sum)
    grad_sum[...] = jnp.zeros_like(grad_sum)

    def visit(ref, columns, block):
        total = act_sum if ref is act_ref else grad_sum
        projected = lax.dot_general(
            ref[:, columns], basis_ref[block], contract_inner, preferred_element_type=jnp.float32
        )
        total[...] += projected * projected * inverse[pl.ds(block, 1), :]

    over_blocks(act_ref, grad_ref, visit)
    ones = jnp.ones((8, BLK), jnp.float32)
    for index, total in enumerate((act_sum, grad_sum)):
        sums = lax.dot_general(
            ones,
            total[...],
            contract_lanes,
            precision=lax.Precision.HIGHEST,
            preferred_element_type=jnp.float32,
        )
        weight_ref[index : index + 1, :] = sums[0:1]


def score_kernel(weight_ref, score_ref):
    weights = jnp.sum(weight_ref[...], axis=0)
    score_ref[...] = weights[0:1] * weights[1:2] * (1.0 / (D * FF))


def half_kernel(side_ref, act_ref, grad_ref, half_ref):
    side = side_ref[0]
    act_half, grad_half = act_ref.shape[0] // 2, grad_ref.shape[0] // 2
    half_ref[:act_half] = act_ref[pl.ds(side * act_half, act_half)]
    half_ref[act_half:] = grad_ref[pl.ds(side * grad_half, grad_half)]


def rotate(value, axis, shift):
    count = lax.axis_size(axis)
    return lax.ppermute(value, axis, [(i, (i + shift) % count) for i in range(count)])


def gather_or_sum(value, axis, direct):
    if direct:
        return lax.all_gather(value, axis)
    return lax.psum(value, axis)[None]


def local(activations, gradients, basis_act, basis_grad):
    tokens = activations.shape[0]
    act_blocks, grad_blocks = basis_act.shape[0], basis_grad.shape[0]
    blocks = act_blocks + grad_blocks
    dp, groups = lax.axis_size("dp"), lax.axis_size("groups")
    scale = 1.0 / (tokens * dp)
    direct = dp > 1 and BLK // dp >= 32
    pieces = dp if direct else 1
    rows = BLK // pieces
    me = jnp.full((1,), lax.axis_index("dp") if direct else 0, jnp.int32)
    side = jnp.full((1,), lax.axis_index("groups"), jnp.int32)
    macs = tokens * blocks * BLK * BLK
    input_bytes = 2 * tokens * blocks * BLK

    if direct and groups == 2:
        half = call(
            half_kernel, bf16(blocks // 2, rows, BLK), "basis_half", 0, blocks * rows * BLK,
            smem(1) + vmem(2),
        )(side, basis_act, basis_grad)
        own_half = [rotate(half, "dp", shift) for shift in range(1, pieces)]
        other_half = [rotate(part, "groups", 1) for part in own_half]
        shards = [basis_act, basis_grad, *own_half, *other_half]
        first_received = own_half
    elif direct:
        both = jnp.concatenate([basis_act, basis_grad])
        received = [rotate(both, "dp", shift) for shift in range(1, pieces)]
        shards = [basis_act, basis_grad, *received]
        first_received = received
    else:
        shards = [
            lax.all_gather(basis_act, "dp", axis=1, tiled=True),
            lax.all_gather(basis_grad, "dp", axis=1, tiled=True),
        ]

    own, *sent, top = call(
        functools.partial(gram_kernel, pieces, scale),
        [
            f32(blocks, rows, BLK),
            *[bf16(blocks, rows, BLK)] * (pieces - 1),
            f32(blocks, BLK),
        ],
        "partial_gram", 4 * macs, input_bytes,
        smem(1) + vmem(2),
        [pltpu.VMEM((GROUP, BLK, BLK), jnp.float32)],
    )(me, activations, gradients)
    if direct:
        *sent, _ = lax.optimization_barrier((*sent, first_received))
        received = [rotate(part, "dp", shift + 1) for shift, part in enumerate(sent)]
    else:
        own = lax.psum_scatter(own, "dp", scatter_dimension=1, tiled=True)
        received = []

    basis, sums = call(
        functools.partial(eigen_kernel, pieces, scale),
        [bf16(blocks, BLK, BLK), f32(2 * blocks, BLK)],
        "partial_eigen", 2 * macs, input_bytes,
        smem(2) + vmem(3 + len(shards)),
    )(me, side, activations, gradients, top, *shards)
    sums = gather_or_sum(sums, "dp", direct)
    act_eigen, grad_eigen, totals = call(
        combine_kernel,
        [f32(act_blocks, BLK), f32(grad_blocks, BLK), f32(2, BLK)],
        "combine_eigen", 0, 4 * sums.size, vmem(1),
    )(sums)
    totals = gather_or_sum(totals, "owner", direct)
    weights = call(
        weight_kernel, f32(2, tokens), "partial_weights", 2 * macs, input_bytes, vmem(6),
        [
            pltpu.VMEM((blocks, BLK), jnp.float32),
            pltpu.VMEM((tokens, BLK), jnp.float32),
            pltpu.VMEM((tokens, BLK), jnp.float32),
        ],
    )(activations, gradients, basis, act_eigen, grad_eigen, totals)
    weights = gather_or_sum(weights, "owner", direct)
    token_scores = call(
        score_kernel, f32(1, tokens), "token_scores", 0, 4 * weights.size, vmem(1)
    )(weights)
    act_covariance, grad_covariance = call(
        functools.partial(sum_kernel, blocks),
        [f32(act_blocks, *own.shape[1:]), f32(grad_blocks, *own.shape[1:])],
        "sum_covariance", 0, 4 * own.size * pieces, smem(1) + vmem(2 + len(received)),
    )(me, sums, own, *received)
    return (
        act_covariance,
        grad_covariance,
        act_eigen.reshape(-1),
        grad_eigen.reshape(-1),
        token_scores.reshape(-1),
    )


def solution(mesh):
    return jax.shard_map(
        local,
        mesh=mesh,
        in_specs=(
            P(("groups", "dp"), "owner"),
            P(("groups", "dp"), "owner"),
            P("owner", "dp", None),
            P("owner", "dp", None),
        ),
        out_specs=(
            P(("groups", "owner"), "dp", None),
            P(("groups", "owner"), "dp", None),
            P(("groups", "owner")),
            P(("groups", "owner")),
            P(("groups", "dp")),
        ),
        check_vma=False,
    )
```

```python
import functools

import jax
import jax.numpy as jnp
from jax import lax
from jax.experimental import pallas as pl
from jax.experimental.pallas import tpu as pltpu
from jax.sharding import PartitionSpec as P

D = 4096
FF = 14336
BLK = 128
PAIR = 2 * BLK
GROUP = 4
VMEM_LIMIT = 40 * 1024 * 1024
CODE_TOP = 2.0**7.875
SMALLEST = 1e-36

damp_root = 0.31622776601683794
contract_rows = (((0,), (0,)), ((), ()))
contract_inner = (((1,), (0,)), ((), ()))
contract_lanes = (((1,), (1,)), ((), ()))

IN_VMEM = pl.BlockSpec(memory_space=pltpu.VMEM)
IN_SMEM = pl.BlockSpec(memory_space=pltpu.SMEM)
IN_HBM = pl.BlockSpec(memory_space=pltpu.HBM)


def call(
    kernel, out_shape, name, flops, bytes_accessed, in_specs, scratch_shapes=(), limit=VMEM_LIMIT
):
    return pl.pallas_call(
        kernel,
        out_shape=out_shape,
        in_specs=in_specs,
        out_specs=jax.tree.map(lambda _: IN_VMEM, out_shape),
        scratch_shapes=scratch_shapes,
        compiler_params=pltpu.CompilerParams(vmem_limit_bytes=limit),
        cost_estimate=pl.CostEstimate(
            flops=flops, bytes_accessed=bytes_accessed, transcendentals=0
        ),
        name=name,
    )


def f32(*shape):
    return jax.ShapeDtypeStruct(shape, jnp.float32)


def bf16(*shape):
    return jax.ShapeDtypeStruct(shape, jnp.bfloat16)


def encode(values):
    power = values * values
    power = power * power
    power = power * power
    power = power * power
    return jnp.where(values < 0.0, -power, power).astype(jnp.bfloat16)


def decode(coded):
    coded = coded.astype(jnp.float32)
    root = jnp.abs(coded)
    for _ in range(4):
        root = lax.rsqrt(root)
    return jnp.where(coded > 0.0, root, jnp.where(coded < 0.0, -root, 0.0))


def half_kernel(side_ref, act_ref, grad_ref, half_ref, sems):
    side = side_ref[0]
    act_half, grad_half = act_ref.shape[0] // 2, grad_ref.shape[0] // 2
    copies = [
        pltpu.make_async_copy(
            act_ref.at[pl.ds(side * act_half, act_half)],
            half_ref.at[pl.ds(0, act_half)],
            sems.at[0],
        ),
        pltpu.make_async_copy(
            grad_ref.at[pl.ds(side * grad_half, grad_half)],
            half_ref.at[pl.ds(act_half, grad_half)],
            sems.at[1],
        ),
    ]
    for copy in copies:
        copy.start()
    for copy in copies:
        copy.wait()


def gram_kernel(pieces, scale, me_ref, act_ref, grad_ref, own_ref, *refs):
    sent_refs, (whole, tops) = refs[:-2], refs[-2:]
    rows = BLK // pieces
    me = me_ref[0]
    first = 0
    tops[...] = jnp.zeros_like(tops)
    for ref in (act_ref, grad_ref):

        @pl.loop(0, ref.shape[1] // BLK // GROUP)
        def _(step, ref=ref, first=first):
            for offset in range(GROUP):
                block = first + step * GROUP + offset
                at = pl.multiple_of((step * GROUP + offset) * BLK, BLK)
                values = ref[:, pl.ds(at, BLK)]
                gram = scale * lax.dot_general(
                    values, values, contract_rows, preferred_element_type=jnp.float32
                )
                if pieces == 1:
                    own_ref[block] = gram
                    continue
                whole[offset] = gram
                top = jnp.maximum(jnp.max(jnp.abs(gram), axis=0, keepdims=True), SMALLEST)
                top = (top * (1.0 + 2.0**-8)).astype(jnp.bfloat16).astype(jnp.float32)
                tops[pl.ds(block, 1), :] = top
                gain = CODE_TOP / top
                own_ref[block] = whole[offset, pl.ds(pl.multiple_of(me * rows, rows), rows), :]
                for shift in range(1, pieces):
                    row = pl.multiple_of(lax.rem(me + shift, pieces) * rows, rows)
                    place = pl.multiple_of(block * rows, rows)
                    sent_refs[shift - 1][pl.ds(place, rows), :] = encode(
                        whole[offset, pl.ds(row, rows), :] * gain
                    )

        first += ref.shape[1] // BLK
    for sent_ref in sent_refs:
        sent_ref[first * rows :, :] = tops[...].astype(jnp.bfloat16)


def add_kernel(own_ref, sent_ref, *refs):
    out_refs, tops = refs[:-1], refs[-1]
    blocks, rows, _ = own_ref.shape
    tops[...] = sent_ref[blocks * rows :, :].astype(jnp.float32) * (1.0 / CODE_TOP)
    first = 0
    for out_ref in out_refs:

        @pl.loop(0, out_ref.shape[0] // GROUP)
        def _(step, out_ref=out_ref, first=first):
            for offset in range(GROUP):
                at = step * GROUP + offset
                block = first + at
                place = pl.multiple_of(block * rows, rows)
                values = decode(sent_ref[pl.ds(place, rows), :])
                out_ref[at] = own_ref[block] + values * tops[pl.ds(block, 1), :]

        first += out_ref.shape[0]


def pairs_of(part, side, halves, act_ref, grad_ref):
    half = lax.rem(side + part, halves)
    for ref in (act_ref, grad_ref):
        count = ref.shape[1] // PAIR // halves
        for pair in range(count):
            yield ref, pl.multiple_of((half * count + pair) * PAIR, PAIR)


def eigen_kernel(
    part, halves, pieces, scale, me_ref, side_ref, act_ref, grad_ref, act_own, grad_own, *refs
):
    *received, basis_ref, sums_ref = refs
    me, side = me_ref[0], side_ref[0]
    rows = BLK // pieces
    done = 0
    if part:
        *received, done_ref = received
        done = done_ref.shape[0]
        sums_ref[:done] = done_ref[...]
    half = lax.rem(side + part, halves)
    act_half, grad_half = act_own.shape[0] // halves, grad_own.shape[0] // halves
    basis_ref[...] = jnp.zeros_like(basis_ref)

    def put(shard_of, piece):
        for block in range(act_half + grad_half):
            corner = block % 2
            row = pl.multiple_of(corner * BLK + piece * rows, rows)
            columns = slice(corner * BLK, (corner + 1) * BLK)
            basis_ref[block // 2, pl.ds(row, rows), columns] = shard_of(block)

    def own_shard(block):
        if block < act_half:
            return act_own[half * act_half + block]
        return grad_own[half * grad_half + block - act_half]

    put(own_shard, me)
    for index, ref in enumerate(received):
        put(lambda block, ref=ref: ref[block], lax.rem(me - index - 1 + pieces, pieces))

    for pair, (ref, column) in enumerate(pairs_of(part, side, halves, act_ref, grad_ref)):
        projected = lax.dot_general(
            ref[:, pl.ds(column, PAIR)],
            basis_ref[pair],
            contract_inner,
            preferred_element_type=jnp.float32,
        )
        sums = scale * jnp.sum(projected * projected, axis=0, keepdims=True)
        row = done + 2 * pair
        sums_ref[row : row + 1, :] = sums[:, :BLK]
        sums_ref[row + 1 : row + 2, :] = sums[:, BLK:]


def combine_kernel(halves, side_ref, sums_ref, act_eigen_ref, grad_eigen_ref, eigen_ref, total_ref):
    side = side_ref[0]
    act_half, grad_half = act_eigen_ref.shape[0] // halves, grad_eigen_ref.shape[0] // halves
    eigen = jnp.sum(sums_ref[...], axis=0)
    eigen_ref[...] = eigen
    act_total = jnp.zeros((1, BLK), jnp.float32)
    grad_total = jnp.zeros((1, BLK), jnp.float32)
    for part in range(halves):
        half = lax.rem(side + part, halves)
        first = part * (act_half + grad_half)
        act = eigen[first : first + act_half]
        grad = eigen[first + act_half : first + act_half + grad_half]
        act_total += jnp.sum(act, axis=0, keepdims=True)
        grad_total += jnp.sum(grad, axis=0, keepdims=True)
        act_eigen_ref[pl.ds(half * act_half, act_half), :] = act
        grad_eigen_ref[pl.ds(half * grad_half, grad_half), :] = grad
    for copy in range(total_ref.shape[0]):
        total_ref[copy, 0:1, :] = act_total
        total_ref[copy, 1:2, :] = grad_total


def weight_kernel(halves, side_ref, act_ref, grad_ref, eigen_ref, total_ref, *refs):
    *basis_refs, weight_ref, inverse, act_sum, grad_sum = refs
    side = side_ref[0]
    totals = jnp.sum(total_ref[...], axis=0)
    totals = jnp.sum(totals, axis=1, keepdims=True)
    act_half = act_ref.shape[1] // BLK // halves
    grad_half = grad_ref.shape[1] // BLK // halves
    for part in range(halves):
        first = part * (act_half + grad_half)
        act = slice(first, first + act_half)
        grad = slice(first + act_half, first + act_half + grad_half)
        inverse[act] = 1.0 / (eigen_ref[act] + totals[0:1] * (damp_root / D))
        inverse[grad] = 1.0 / (eigen_ref[grad] + totals[1:2] * (damp_root / FF))
    act_sum[...] = jnp.zeros_like(act_sum)
    grad_sum[...] = jnp.zeros_like(grad_sum)
    for part in range(halves):
        first = part * (act_half + grad_half)
        for pair, (ref, column) in enumerate(pairs_of(part, side, halves, act_ref, grad_ref)):
            total = act_sum if ref is act_ref else grad_sum
            projected = lax.dot_general(
                ref[:, pl.ds(column, PAIR)],
                basis_refs[part][pair],
                contract_inner,
                preferred_element_type=jnp.float32,
            )
            row = first + 2 * pair
            left, right = projected[:, :BLK], projected[:, BLK:]
            total[...] += (
                left * left * inverse[row : row + 1, :]
                + right * right * inverse[row + 1 : row + 2, :]
            )
    ones = jnp.ones((8, BLK), jnp.float32)
    for index, total in enumerate((act_sum, grad_sum)):
        sums = lax.dot_general(
            ones,
            total[...],
            contract_lanes,
            precision=lax.Precision.HIGHEST,
            preferred_element_type=jnp.float32,
        )
        weight_ref[index : index + 1, :] = sums[0:1]


def score_kernel(weight_ref, score_ref):
    weights = jnp.sum(weight_ref[...], axis=0)
    score_ref[...] = weights[0:1] * weights[1:2] * (1.0 / (D * FF))


def rotate(value, axis, shift):
    count = lax.axis_size(axis)
    return lax.ppermute(value, axis, [(i, (i + shift) % count) for i in range(count)])


def gather_or_sum(value, axis, direct):
    if direct:
        return lax.all_gather(value, axis)
    return lax.psum(value, axis)[None]


def after(values, done):
    return list(lax.optimization_barrier((tuple(values), done))[0])


def local(activations, gradients, basis_act, basis_grad):
    tokens = activations.shape[0]
    act_blocks, grad_blocks = basis_act.shape[0], basis_grad.shape[0]
    blocks = act_blocks + grad_blocks
    dp, owners = lax.axis_size("dp"), lax.axis_size("owner")
    scale = 1.0 / (tokens * dp)
    direct = dp > 1 and BLK // dp >= 32
    pieces = dp if direct else 1
    halves = 2 if direct and lax.axis_size("groups") == 2 else 1
    rows = BLK // pieces
    me = jnp.full((1,), lax.axis_index("dp") if direct else 0, jnp.int32)
    side = jnp.full((1,), lax.axis_index("groups"), jnp.int32)
    macs = tokens * blocks * BLK * BLK
    input_bytes = 2 * tokens * blocks * BLK
    shifts = range(1, pieces)

    if halves == 2:
        shard = call(
            half_kernel, bf16(blocks // 2, rows, BLK), "basis_half", 0, blocks * rows * BLK,
            [IN_SMEM, IN_HBM, IN_HBM], [pltpu.SemaphoreType.DMA((2,))], 62 * 1024 * 1024,
        )(side, basis_act, basis_grad)
    elif direct:
        shard = jnp.concatenate([basis_act, basis_grad])
    if direct:
        ways = sorted(shifts, key=lambda shift: -min(shift, pieces - shift))
        received = {shift: rotate(shard, "dp", shift) for shift in ways}
        received = [received[shift] for shift in shifts]
    else:
        basis_act = lax.all_gather(basis_act, "dp", axis=1, tiled=True)
        basis_grad = lax.all_gather(basis_grad, "dp", axis=1, tiled=True)
        received = []

    message = blocks * rows + 16 * pl.cdiv(blocks, 16)
    own, *sent = call(
        functools.partial(gram_kernel, pieces, scale),
        [f32(blocks, rows, BLK), *[bf16(message, BLK)] * (pieces - 1)],
        "partial_gram", 4 * macs, input_bytes,
        [IN_SMEM, IN_VMEM, IN_VMEM],
        [
            pltpu.VMEM((GROUP, BLK, BLK), jnp.float32),
            pltpu.VMEM((16 * pl.cdiv(blocks, 16), BLK), jnp.float32),
        ],
    )(me, activations, gradients)
    arrived = []
    if direct:
        arrived.append(rotate(sent[0], "dp", 1))
    else:
        own = lax.psum_scatter(own, "dp", scatter_dimension=1, tiled=True)

    parts = [received]
    if halves == 2:
        parts.append([rotate(after([part], own)[0], "groups", 1) for part in received])
    bases, sums = [], []
    for part, shards in enumerate(parts):
        basis, *sums = call(
            functools.partial(eigen_kernel, part, halves, pieces, scale),
            [bf16(blocks // halves // 2, PAIR, PAIR), f32(blocks // halves * (part + 1), BLK)],
            "partial_eigen", 2 * macs // halves, input_bytes // halves,
            [IN_SMEM, IN_SMEM] + [IN_VMEM] * (4 + len(shards) + len(sums)),
        )(me, side, activations, gradients, basis_act, basis_grad, *shards, *sums)
        bases.append(basis)
    sums = after(sums, arrived)
    sums = gather_or_sum(sums[0], "dp", direct)
    if direct:
        sent[1:] = after(sent[1:], sums)
        for shift in shifts[1:]:
            arrived.append(rotate(sent[shift - 1], "dp", shift))

    copies = owners if direct else 1
    act_eigen, grad_eigen, eigen, totals = call(
        functools.partial(combine_kernel, halves),
        [
            f32(act_blocks, BLK),
            f32(grad_blocks, BLK),
            f32(blocks, BLK),
            f32(copies, 2, BLK),
        ],
        "combine_eigen", 0, 4 * sums.size, [IN_SMEM, IN_VMEM],
    )(side, sums)
    if direct:
        totals = lax.all_to_all(totals, "owner", 0, 0, tiled=True)
    else:
        totals = lax.psum(totals, "owner")
    weights = call(
        functools.partial(weight_kernel, halves),
        f32(2, tokens), "partial_weights", 2 * macs, input_bytes,
        [IN_SMEM] + [IN_VMEM] * (4 + halves),
        [
            pltpu.VMEM((blocks, BLK), jnp.float32),
            pltpu.VMEM((tokens, BLK), jnp.float32),
            pltpu.VMEM((tokens, BLK), jnp.float32),
        ],
    )(side, activations, gradients, eigen, totals, *bases)
    weights = gather_or_sum(weights, "owner", direct)
    token_scores = call(
        score_kernel, f32(1, tokens), "token_scores", 0, 4 * weights.size, [IN_VMEM]
    )(weights)

    covariance = own
    for index, chunk in enumerate(arrived):
        last = index == len(arrived) - 1
        shape = own.shape[1:]
        covariance = call(
            add_kernel,
            [f32(act_blocks, *shape), f32(grad_blocks, *shape)] if last else [f32(*own.shape)],
            "add_chunk", 0, 10 * own.size, [IN_VMEM, IN_VMEM],
            [pltpu.VMEM((message - blocks * rows, BLK), jnp.float32)],
        )(covariance, chunk)
        covariance = covariance if last else covariance[0]
    if not arrived:
        covariance = covariance[:act_blocks], covariance[act_blocks:]
    return (
        *covariance,
        act_eigen.reshape(-1),
        grad_eigen.reshape(-1),
        token_scores.reshape(-1),
    )


def solution(mesh):
    return jax.shard_map(
        local,
        mesh=mesh,
        in_specs=(
            P(("groups", "dp"), "owner"),
            P(("groups", "dp"), "owner"),
            P("owner", "dp", None),
            P("owner", "dp", None),
        ),
        out_specs=(
            P(("groups", "owner"), "dp", None),
            P(("groups", "owner"), "dp", None),
            P(("groups", "owner")),
            P(("groups", "owner")),
            P(("groups", "dp")),
        ),
        check_vma=False,
    )
```

```python
import functools

import jax
import jax.numpy as jnp
from jax import lax
from jax.experimental import pallas as pl
from jax.experimental.pallas import tpu as pltpu
from jax.sharding import PartitionSpec as P

D = 4096
FF = 14336
BLK = 128
PAIR = 2 * BLK
GROUP = 4
TILE = 64
VMEM_LIMIT = 24 * 1024 * 1024
CODE_TOP = 2.0**7.875
SMALLEST = 1e-36

damp_root = 0.31622776601683794
contract_rows = (((0,), (0,)), ((), ()))
contract_inner = (((1,), (0,)), ((), ()))
contract_lanes = (((1,), (1,)), ((), ()))

IN_VMEM = pl.BlockSpec(memory_space=pltpu.VMEM)
IN_SMEM = pl.BlockSpec(memory_space=pltpu.SMEM)
IN_HBM = pl.BlockSpec(memory_space=pltpu.HBM)


def call(
    kernel, out_shape, name, flops, bytes_accessed, in_specs, scratch_shapes=(),
    out_spec=IN_VMEM, limit=VMEM_LIMIT,
):
    return pl.pallas_call(
        kernel,
        out_shape=out_shape,
        in_specs=in_specs,
        out_specs=jax.tree.map(lambda _: out_spec, out_shape),
        scratch_shapes=scratch_shapes,
        compiler_params=pltpu.CompilerParams(vmem_limit_bytes=limit),
        cost_estimate=pl.CostEstimate(
            flops=flops, bytes_accessed=bytes_accessed, transcendentals=0
        ),
        name=name,
    )


def f32(*shape):
    return jax.ShapeDtypeStruct(shape, jnp.float32)


def bf16(*shape):
    return jax.ShapeDtypeStruct(shape, jnp.bfloat16)


def encode(values):
    power = values * values
    power = power * power
    power = power * power
    power = power * power
    return jnp.where(values < 0.0, -power, power).astype(jnp.bfloat16)


def decode(coded):
    coded = coded.astype(jnp.float32)
    root = jnp.abs(coded)
    for _ in range(4):
        root = lax.rsqrt(root)
    return jnp.where(coded > 0.0, root, jnp.where(coded < 0.0, -root, 0.0))


def half_kernel(side_ref, act_ref, grad_ref, half_ref, sems):
    side = side_ref[0]
    act_half, grad_half = act_ref.shape[0] // 2, grad_ref.shape[0] // 2
    copies = [
        pltpu.make_async_copy(
            act_ref.at[pl.ds(side * act_half, act_half)],
            half_ref.at[pl.ds(0, act_half)],
            sems.at[0],
        ),
        pltpu.make_async_copy(
            grad_ref.at[pl.ds(side * grad_half, grad_half)],
            half_ref.at[pl.ds(act_half, grad_half)],
            sems.at[1],
        ),
    ]
    for copy in copies:
        copy.start()
    for copy in copies:
        copy.wait()


def gram_kernel(pieces, scale, me_ref, act_ref, grad_ref, own_ref, *refs):
    sent_refs, (whole, tops) = refs[:-2], refs[-2:]
    rows = BLK // pieces
    me = me_ref[0]
    first = 0
    tops[...] = jnp.zeros_like(tops)
    for ref in (act_ref, grad_ref):

        @pl.loop(0, ref.shape[1] // BLK // GROUP)
        def _(step, ref=ref, first=first):
            for offset in range(GROUP):
                block = first + step * GROUP + offset
                at = pl.multiple_of((step * GROUP + offset) * BLK, BLK)
                values = ref[:, pl.ds(at, BLK)]
                gram = scale * lax.dot_general(
                    values, values, contract_rows, preferred_element_type=jnp.float32
                )
                if pieces == 1:
                    own_ref[block] = gram
                    continue
                whole[offset] = gram
                top = jnp.maximum(jnp.max(jnp.abs(gram), axis=0, keepdims=True), SMALLEST)
                top = (top * (1.0 + 2.0**-8)).astype(jnp.bfloat16).astype(jnp.float32)
                tops[pl.ds(block, 1), :] = top
                gain = CODE_TOP / top
                own_ref[block] = whole[offset, pl.ds(pl.multiple_of(me * rows, rows), rows), :]
                for shift in range(1, pieces):
                    row = pl.multiple_of((me ^ shift) * rows, rows)
                    place = pl.multiple_of(block * rows, rows)
                    sent_refs[shift - 1][pl.ds(place, rows), :] = encode(
                        whole[offset, pl.ds(row, rows), :] * gain
                    )

        first += ref.shape[1] // BLK
    for sent_ref in sent_refs:
        sent_ref[first * rows :, :] = tops[...].astype(jnp.bfloat16)


def add_group(own_ref, sent_ref, tops, first):
    rows = own_ref.shape[1]
    for block in [first + offset for offset in range(GROUP)]:
        values = decode(sent_ref[pl.ds(pl.multiple_of(block * rows, rows), rows), :])
        yield block, own_ref[block] + values * tops[pl.ds(block, 1), :]


def add_kernel(own_ref, sent_ref, sum_ref, tops):
    blocks, rows, _ = own_ref.shape
    tops[...] = sent_ref[blocks * rows :, :].astype(jnp.float32) * (1.0 / CODE_TOP)

    @pl.loop(0, blocks // GROUP)
    def _(step):
        for block, total in add_group(own_ref, sent_ref, tops, step * GROUP):
            sum_ref[block] = total


def last_add_kernel(own_ref, sent_ref, act_ref, grad_ref, tops, sums, sems):
    blocks, rows, _ = own_ref.shape
    tops[...] = sent_ref[blocks * rows :, :].astype(jnp.float32) * (1.0 / CODE_TOP)
    act_steps, grad_steps = act_ref.shape[0] // GROUP, grad_ref.shape[0] // GROUP

    def write(ref, step, first):
        return pltpu.make_async_copy(
            sums.at[pl.ds((first + step) * GROUP, GROUP)],
            ref.at[pl.ds(step * GROUP, GROUP)],
            sems.at[first + step],
        )

    for ref, first, steps in ((act_ref, 0, act_steps), (grad_ref, act_steps, grad_steps)):

        @pl.loop(0, steps)
        def _(step, ref=ref, first=first):
            for block, total in add_group(own_ref, sent_ref, tops, (first + step) * GROUP):
                sums[block] = total
            write(ref, step, first).start()

    for ref, first, steps in ((act_ref, 0, act_steps), (grad_ref, act_steps, grad_steps)):

        @pl.loop(0, steps)
        def _(step, ref=ref, first=first):
            write(ref, step, first).wait()


def pairs_of(part, side, halves, act_ref, grad_ref):
    half = lax.rem(side + part, halves)
    for ref in (act_ref, grad_ref):
        count = ref.shape[1] // PAIR // halves
        for pair in range(count):
            yield ref, pl.multiple_of((half * count + pair) * PAIR, PAIR)


def eigen_kernel(
    part, halves, pieces, scale, me_ref, side_ref, act_ref, grad_ref, act_own, grad_own, *refs
):
    *received, power_ref, sums_ref, basis_ref = refs
    me, side = me_ref[0], side_ref[0]
    rows = BLK // pieces
    done = 0
    if part:
        *received, done_ref = received
        done = done_ref.shape[0]
        sums_ref[:done] = done_ref[...]
    half = lax.rem(side + part, halves)
    act_half, grad_half = act_own.shape[0] // halves, grad_own.shape[0] // halves
    basis_ref[...] = jnp.zeros_like(basis_ref)

    def put(shard_of, piece):
        for block in range(act_half + grad_half):
            corner = block % 2
            row = pl.multiple_of(corner * BLK + piece * rows, rows)
            columns = slice(corner * BLK, (corner + 1) * BLK)
            basis_ref[block // 2, pl.ds(row, rows), columns] = shard_of(block)

    def own_shard(block):
        if block < act_half:
            return act_own[half * act_half + block]
        return grad_own[half * grad_half + block - act_half]

    put(own_shard, me)
    for index, ref in enumerate(received):
        put(lambda block, ref=ref: ref[block], me ^ (index + 1))

    for pair, (ref, column) in enumerate(pairs_of(part, side, halves, act_ref, grad_ref)):
        projected = lax.dot_general(
            ref[:, pl.ds(column, PAIR)],
            basis_ref[pair],
            contract_inner,
            preferred_element_type=jnp.float32,
        )
        power = projected * projected
        power_ref[pair] = power
        sums = scale * jnp.sum(power, axis=0, keepdims=True)
        row = done + 2 * pair
        sums_ref[row : row + 1, :] = sums[:, :BLK]
        sums_ref[row + 1 : row + 2, :] = sums[:, BLK:]


def combine_kernel(halves, side_ref, *refs):
    *sums_refs, act_eigen_ref, grad_eigen_ref, eigen_ref, total_ref = refs
    side = side_ref[0]
    act_half, grad_half = act_eigen_ref.shape[0] // halves, grad_eigen_ref.shape[0] // halves
    eigen = sums_refs[0][...]
    for sums_ref in sums_refs[1:]:
        eigen = eigen + sums_ref[...]
    eigen_ref[...] = eigen
    act_total = jnp.zeros((1, BLK), jnp.float32)
    grad_total = jnp.zeros((1, BLK), jnp.float32)
    for part in range(halves):
        half = lax.rem(side + part, halves)
        first = part * (act_half + grad_half)
        act = eigen[first : first + act_half]
        grad = eigen[first + act_half : first + act_half + grad_half]
        act_total += jnp.sum(act, axis=0, keepdims=True)
        grad_total += jnp.sum(grad, axis=0, keepdims=True)
        act_eigen_ref[pl.ds(half * act_half, act_half), :] = act
        grad_eigen_ref[pl.ds(half * grad_half, grad_half), :] = grad
    total_ref[0:1, :] = act_total
    total_ref[1:2, :] = grad_total


def weight_kernel(halves, act_half, eigen_ref, *refs):
    *refs, weight_ref, inverse, act_sum, grad_sum = refs
    power_refs, total_refs = refs[:halves], refs[halves:]
    totals = total_refs[0][...]
    for total_ref in total_refs[1:]:
        totals = totals + total_ref[...]
    totals = jnp.sum(totals, axis=1, keepdims=True)
    blocks_half = eigen_ref.shape[0] // halves
    for part in range(halves):
        first = part * blocks_half
        act = slice(first, first + act_half)
        grad = slice(first + act_half, first + blocks_half)
        inverse[act] = 1.0 / (eigen_ref[act] + totals[0:1] * (damp_root / D))
        inverse[grad] = 1.0 / (eigen_ref[grad] + totals[1:2] * (damp_root / FF))
    tokens = act_sum.shape[0]

    @pl.loop(0, tokens // TILE)
    def _(tile):
        here = pl.ds(pl.multiple_of(tile * TILE, TILE), TILE)
        sums = [jnp.zeros((TILE, BLK), jnp.float32), jnp.zeros((TILE, BLK), jnp.float32)]
        for part, power_ref in enumerate(power_refs):
            for pair in range(power_ref.shape[0]):
                which = 0 if 2 * pair < act_half else 1
                for side in range(2):
                    row = part * blocks_half + 2 * pair + side
                    power = power_ref[pair, here, side * BLK : (side + 1) * BLK]
                    sums[which] += power * inverse[row : row + 1, :]
        act_sum[here, :], grad_sum[here, :] = sums

    ones = jnp.ones((8, BLK), jnp.float32)
    for index, total in enumerate((act_sum, grad_sum)):
        sums = lax.dot_general(
            ones,
            total[...],
            contract_lanes,
            precision=lax.Precision.HIGHEST,
            preferred_element_type=jnp.float32,
        )
        weight_ref[index : index + 1, :] = sums[0:1]


def score_kernel(*refs):
    *weight_refs, score_ref = refs
    weights = weight_refs[0][...]
    for weight_ref in weight_refs[1:]:
        weights = weights + weight_ref[...]
    score_ref[...] = weights[0:1] * weights[1:2] * (1.0 / (D * FF))


def swap(value, axis, mask):
    count = lax.axis_size(axis)
    return lax.ppermute(value, axis, [(i, i ^ mask) for i in range(count)])


def share(value, axis, direct):
    if not direct:
        return [lax.psum(value, axis)]
    return [value] + [swap(value, axis, mask) for mask in range(1, lax.axis_size(axis))]


def after(values, done):
    return list(lax.optimization_barrier((tuple(values), done))[0])


def local(activations, gradients, basis_act, basis_grad):
    tokens = activations.shape[0]
    act_blocks, grad_blocks = basis_act.shape[0], basis_grad.shape[0]
    blocks = act_blocks + grad_blocks
    dp, owners = lax.axis_size("dp"), lax.axis_size("owner")
    scale = 1.0 / (tokens * dp)
    direct = dp in (2, 4) and owners in (1, 2, 4)
    pieces = dp if direct else 1
    halves = 2 if direct and lax.axis_size("groups") == 2 else 1
    rows = BLK // pieces
    me = jnp.full((1,), lax.axis_index("dp") if direct else 0, jnp.int32)
    side = jnp.full((1,), lax.axis_index("groups"), jnp.int32)
    macs = tokens * blocks * BLK * BLK
    input_bytes = 2 * tokens * blocks * BLK
    masks = range(1, pieces)

    if halves == 2:
        shard = call(
            half_kernel, bf16(blocks // 2, rows, BLK), "basis_half", 0, blocks * rows * BLK,
            [IN_SMEM, IN_HBM, IN_HBM], [pltpu.SemaphoreType.DMA((2,))],
            limit=62 * 1024 * 1024,
        )(side, basis_act, basis_grad)
    elif direct:
        shard = jnp.concatenate([basis_act, basis_grad])
    if direct:
        received = [swap(shard, "dp", mask) for mask in masks]
    else:
        basis_act = lax.all_gather(basis_act, "dp", axis=1, tiled=True)
        basis_grad = lax.all_gather(basis_grad, "dp", axis=1, tiled=True)
        received = []

    scale_rows = 16 * pl.cdiv(blocks, 16)
    message = blocks * rows + scale_rows
    own, *sent = call(
        functools.partial(gram_kernel, pieces, scale),
        [f32(blocks, rows, BLK), *[bf16(message, BLK)] * (pieces - 1)],
        "partial_gram", 4 * macs, input_bytes,
        [IN_SMEM, IN_VMEM, IN_VMEM],
        [pltpu.VMEM((GROUP, BLK, BLK), jnp.float32), pltpu.VMEM((scale_rows, BLK), jnp.float32)],
    )(me, activations, gradients)
    late = 2 if pieces > 2 else None
    arrived = [swap(sent[mask - 1], "dp", mask) for mask in masks if mask != late]
    if not direct:
        own = lax.psum_scatter(own, "dp", scatter_dimension=1, tiled=True)

    parts = [received]
    if halves == 2:
        parts.append([swap(after([part], own)[0], "groups", 1) for part in received])
    powers, sums = [], []
    for part, shards in enumerate(parts):
        power, *sums = call(
            functools.partial(eigen_kernel, part, halves, pieces, scale),
            [f32(blocks // halves // 2, tokens, PAIR), f32(blocks // halves * (part + 1), BLK)],
            "partial_eigen", 2 * macs // halves, input_bytes // halves,
            [IN_SMEM, IN_SMEM] + [IN_VMEM] * (4 + len(shards) + len(sums)),
            [pltpu.VMEM((blocks // halves // 2, PAIR, PAIR), jnp.bfloat16)],
        )(me, side, activations, gradients, basis_act, basis_grad, *shards, *sums)
        powers.append(power)
    sums = share(after(sums, arrived)[0], "dp", direct)
    if late:
        arrived.append(swap(after([sent[late - 1]], sums)[0], "dp", late))
    act_eigen, grad_eigen, eigen, totals = call(
        functools.partial(combine_kernel, halves),
        [f32(act_blocks, BLK), f32(grad_blocks, BLK), f32(blocks, BLK), f32(2, BLK)],
        "combine_eigen", 0, 4 * blocks * BLK * pieces, [IN_SMEM] + [IN_VMEM] * len(sums),
    )(side, *sums)
    totals = share(totals, "owner", direct)
    weights = call(
        functools.partial(weight_kernel, halves, act_blocks // halves),
        f32(2, tokens), "partial_weights", 0, 4 * tokens * blocks * BLK,
        [IN_VMEM] * (1 + halves + len(totals)),
        [
            pltpu.VMEM((blocks, BLK), jnp.float32),
            pltpu.VMEM((tokens, BLK), jnp.float32),
            pltpu.VMEM((tokens, BLK), jnp.float32),
        ],
    )(eigen, *powers, *totals)
    weights = share(weights, "owner", direct)
    token_scores = call(
        score_kernel, f32(1, tokens), "token_scores", 0, 8 * tokens * len(weights),
        [IN_VMEM] * len(weights),
    )(*weights)

    for chunk in arrived[:-1]:
        own = call(
            add_kernel, f32(*own.shape), "add_chunk", 0, 10 * own.size, [IN_VMEM, IN_VMEM],
            [pltpu.VMEM((scale_rows, BLK), jnp.float32)],
        )(own, chunk)
    if arrived:
        covariance = call(
            last_add_kernel, [f32(act_blocks, rows, BLK), f32(grad_blocks, rows, BLK)],
            "add_last_chunk", 0, 10 * own.size, [IN_VMEM, IN_VMEM],
            [
                pltpu.VMEM((scale_rows, BLK), jnp.float32),
                pltpu.VMEM(own.shape, jnp.float32),
                pltpu.SemaphoreType.DMA((blocks // GROUP,)),
            ],
            out_spec=pl.BlockSpec(memory_space=pl.ANY),
        )(own, arrived[-1])
    else:
        covariance = own[:act_blocks], own[act_blocks:]
    return (
        *covariance,
        act_eigen.reshape(-1),
        grad_eigen.reshape(-1),
        token_scores.reshape(-1),
    )


def solution(mesh):
    return jax.shard_map(
        local,
        mesh=mesh,
        in_specs=(
            P(("groups", "dp"), "owner"),
            P(("groups", "dp"), "owner"),
            P("owner", "dp", None),
            P("owner", "dp", None),
        ),
        out_specs=(
            P(("groups", "owner"), "dp", None),
            P(("groups", "owner"), "dp", None),
            P(("groups", "owner")),
            P(("groups", "owner")),
            P(("groups", "dp")),
        ),
        check_vma=False,
    )
```

```python
import functools

import jax
import jax.numpy as jnp
from jax import lax
from jax.experimental import pallas as pl
from jax.experimental.pallas import tpu as pltpu
from jax.sharding import PartitionSpec as P

D = 4096
FF = 14336
BLK = 128
PAIR = 2 * BLK
GROUP = 4
TILE = 64
VMEM_LIMIT = 24 * 1024 * 1024
CODE_TOP = 2.0**7.875
SMALLEST = 1e-36

damp_root = 0.31622776601683794
contract_rows = (((0,), (0,)), ((), ()))
contract_inner = (((1,), (0,)), ((), ()))
contract_lanes = (((1,), (1,)), ((), ()))

IN_VMEM = pl.BlockSpec(memory_space=pltpu.VMEM)
IN_SMEM = pl.BlockSpec(memory_space=pltpu.SMEM)
IN_HBM = pl.BlockSpec(memory_space=pltpu.HBM)


def scale_rows(first, end):
    return 16 * pl.cdiv(end - first, 16)


def call(
    kernel, out_shape, name, flops, bytes_accessed, in_specs, scratch_shapes=(),
    out_spec=IN_VMEM,
):
    return pl.pallas_call(
        kernel,
        out_shape=out_shape,
        in_specs=in_specs,
        out_specs=jax.tree.map(lambda _: out_spec, out_shape),
        scratch_shapes=scratch_shapes,
        compiler_params=pltpu.CompilerParams(vmem_limit_bytes=VMEM_LIMIT),
        cost_estimate=pl.CostEstimate(
            flops=flops, bytes_accessed=bytes_accessed, transcendentals=0
        ),
        name=name,
    )


def in_hbm(value):
    return pltpu.with_memory_space_constraint(value, pltpu.HBM)


def f32(*shape):
    return jax.ShapeDtypeStruct(shape, jnp.float32)


def bf16(*shape):
    return jax.ShapeDtypeStruct(shape, jnp.bfloat16)


def encode(values):
    power = values * values
    power = power * power
    power = power * power
    power = power * power
    return jnp.where(values < 0.0, -power, power).astype(jnp.bfloat16)


def decode(coded):
    coded = coded.astype(jnp.float32)
    root = jnp.abs(coded)
    for _ in range(4):
        root = lax.rsqrt(root)
    return jnp.where(coded > 0.0, root, jnp.where(coded < 0.0, -root, 0.0))


def half_kernel(side_ref, act_ref, grad_ref, half_ref, sems):
    side = side_ref[0]
    act_half, grad_half = act_ref.shape[0] // 2, grad_ref.shape[0] // 2
    copies = [
        pltpu.make_async_copy(
            act_ref.at[pl.ds(side * act_half, act_half)],
            half_ref.at[pl.ds(0, act_half)],
            sems.at[0],
        ),
        pltpu.make_async_copy(
            grad_ref.at[pl.ds(side * grad_half, grad_half)],
            half_ref.at[pl.ds(act_half, grad_half)],
            sems.at[1],
        ),
    ]
    for copy in copies:
        copy.start()
    for copy in copies:
        copy.wait()


def gram_kernel(pieces, messages, scale, me_ref, act_hbm, grad_hbm, act_ref, grad_ref, own_ref, *refs):
    sent_refs, (whole, tops, sems) = refs[:-3], refs[-3:]
    rows = BLK // pieces
    me = me_ref[0]
    steps = []
    for source, target in ((act_hbm, act_ref), (grad_hbm, grad_ref)):
        for first in range(0, source.shape[1], GROUP * BLK):
            columns = slice(first, first + GROUP * BLK)
            copy = pltpu.make_async_copy(
                source.at[:, columns], target.at[:, columns], sems.at[len(steps)]
            )
            copy.start()
            steps.append((target, columns, copy))
    tops[...] = jnp.zeros_like(tops)
    for step, (ref, columns, copy) in enumerate(steps):
        copy.wait()
        for offset in range(GROUP):
            block = step * GROUP + offset
            at = columns.start + offset * BLK
            values = ref[:, at : at + BLK]
            gram = scale * lax.dot_general(
                values, values, contract_rows, preferred_element_type=jnp.float32
            )
            if pieces == 1:
                own_ref[block] = gram
                continue
            whole[offset] = gram
            top = jnp.maximum(jnp.max(jnp.abs(gram), axis=0, keepdims=True), SMALLEST)
            top = (top * (1.0 + 2.0**-8)).astype(jnp.bfloat16).astype(jnp.float32)
            tops[block : block + 1, :] = top
            gain = CODE_TOP / top
            own_ref[block] = whole[offset, pl.ds(pl.multiple_of(me * rows, rows), rows), :]
            for sent_ref, (mask, first, end) in zip(sent_refs, messages):
                if first <= block < end:
                    row = pl.multiple_of((me ^ mask) * rows, rows)
                    place = slice((block - first) * rows, (block - first + 1) * rows)
                    sent_ref[place, :] = encode(whole[offset, pl.ds(row, rows), :] * gain)
    for sent_ref, (_, first, end) in zip(sent_refs, messages):
        sent_ref[(end - first) * rows :, :] = tops[
            first : first + scale_rows(first, end), :
        ].astype(jnp.bfloat16)


def add_group(messages, rows, own_ref, sent_refs, tops_refs, step):
    for block in range(step * GROUP, (step + 1) * GROUP):
        total = own_ref[block]
        for (_, first, end), sent_ref, tops in zip(messages, sent_refs, tops_refs):
            if first <= block < end:
                at = block - first
                values = decode(sent_ref[at * rows : (at + 1) * rows, :])
                total = total + values * tops[at : at + 1, :]
        yield block, total


def load_tops(messages, rows, sent_refs, tops_refs):
    for (_, first, end), sent_ref, tops in zip(messages, sent_refs, tops_refs):
        tops[...] = sent_ref[(end - first) * rows :, :].astype(jnp.float32) * (1.0 / CODE_TOP)


def add_kernel(messages, own_ref, *refs):
    sent_refs, sum_ref, tops_refs = refs[: len(messages)], refs[len(messages)], refs[len(messages) + 1 :]
    blocks, rows, _ = own_ref.shape
    load_tops(messages, rows, sent_refs, tops_refs)
    for step in range(blocks // GROUP):
        for block, total in add_group(messages, rows, own_ref, sent_refs, tops_refs, step):
            sum_ref[block] = total


def last_add_kernel(messages, own_ref, *refs):
    sent_refs, refs = refs[: len(messages)], refs[len(messages) :]
    act_ref, grad_ref, *tops_refs, sums, sems = refs
    blocks, rows, _ = own_ref.shape
    load_tops(messages, rows, sent_refs, tops_refs)
    copies = []
    for step in range(blocks // GROUP):
        for block, total in add_group(messages, rows, own_ref, sent_refs, tops_refs, step):
            sums[block] = total
        first = step * GROUP
        ref, at = act_ref, first
        if first >= act_ref.shape[0]:
            ref, at = grad_ref, first - act_ref.shape[0]
        copies.append(
            pltpu.make_async_copy(
                sums.at[pl.ds(first, GROUP)], ref.at[pl.ds(at, GROUP)], sems.at[step]
            )
        )
        copies[-1].start()
    for copy in copies:
        copy.wait()


def pairs_of(part, side, halves, act_ref, grad_ref):
    half = lax.rem(side + part, halves)
    for ref in (act_ref, grad_ref):
        count = ref.shape[1] // PAIR // halves
        for pair in range(count):
            yield ref, pl.multiple_of((half * count + pair) * PAIR, PAIR)


def eigen_kernel(
    part, halves, pieces, scale, me_ref, side_ref, act_ref, grad_ref, act_own, grad_own, *refs
):
    *received, power_ref, sums_ref, basis_ref = refs
    me, side = me_ref[0], side_ref[0]
    rows = BLK // pieces
    done = 0
    if part:
        *received, done_ref = received
        done = done_ref.shape[0]
        sums_ref[:done] = done_ref[...]
    half = lax.rem(side + part, halves)
    act_half, grad_half = act_own.shape[0] // halves, grad_own.shape[0] // halves
    basis_ref[...] = jnp.zeros_like(basis_ref)

    def put(shard_of, piece):
        for block in range(act_half + grad_half):
            corner = block % 2
            row = pl.multiple_of(corner * BLK + piece * rows, rows)
            columns = slice(corner * BLK, (corner + 1) * BLK)
            basis_ref[block // 2, pl.ds(row, rows), columns] = shard_of(block)

    def own_shard(block):
        if block < act_half:
            return act_own[half * act_half + block]
        return grad_own[half * grad_half + block - act_half]

    put(own_shard, me)
    for index, ref in enumerate(received):
        put(lambda block, ref=ref: ref[block], me ^ (index + 1))

    for pair, (ref, column) in enumerate(pairs_of(part, side, halves, act_ref, grad_ref)):
        projected = lax.dot_general(
            ref[:, pl.ds(column, PAIR)],
            basis_ref[pair],
            contract_inner,
            preferred_element_type=jnp.float32,
        )
        power = projected * projected
        power_ref[pair] = power
        sums = scale * jnp.sum(power, axis=0, keepdims=True)
        row = done + 2 * pair
        sums_ref[row : row + 1, :] = sums[:, :BLK]
        sums_ref[row + 1 : row + 2, :] = sums[:, BLK:]


def combine_kernel(halves, side_ref, *refs):
    *sums_refs, act_eigen_ref, grad_eigen_ref, eigen_ref, total_ref = refs
    side = side_ref[0]
    act_half, grad_half = act_eigen_ref.shape[0] // halves, grad_eigen_ref.shape[0] // halves
    eigen = sums_refs[0][...]
    for sums_ref in sums_refs[1:]:
        eigen = eigen + sums_ref[...]
    eigen_ref[...] = eigen
    act_total = jnp.zeros((1, BLK), jnp.float32)
    grad_total = jnp.zeros((1, BLK), jnp.float32)
    for part in range(halves):
        half = lax.rem(side + part, halves)
        first = part * (act_half + grad_half)
        act = eigen[first : first + act_half]
        grad = eigen[first + act_half : first + act_half + grad_half]
        act_total += jnp.sum(act, axis=0, keepdims=True)
        grad_total += jnp.sum(grad, axis=0, keepdims=True)
        act_eigen_ref[pl.ds(half * act_half, act_half), :] = act
        grad_eigen_ref[pl.ds(half * grad_half, grad_half), :] = grad
    total_ref[0:1, :] = act_total
    total_ref[1:2, :] = grad_total


def weight_kernel(halves, act_half, eigen_ref, *refs):
    *refs, weight_ref, inverse, act_sum, grad_sum = refs
    power_refs, total_refs = refs[:halves], refs[halves:]
    totals = total_refs[0][...]
    for total_ref in total_refs[1:]:
        totals = totals + total_ref[...]
    totals = jnp.sum(totals, axis=1, keepdims=True)
    blocks_half = eigen_ref.shape[0] // halves
    for part in range(halves):
        first = part * blocks_half
        act = slice(first, first + act_half)
        grad = slice(first + act_half, first + blocks_half)
        inverse[act] = 1.0 / (eigen_ref[act] + totals[0:1] * (damp_root / D))
        inverse[grad] = 1.0 / (eigen_ref[grad] + totals[1:2] * (damp_root / FF))
    tokens = act_sum.shape[0]

    @pl.loop(0, tokens // TILE)
    def _(tile):
        here = pl.ds(pl.multiple_of(tile * TILE, TILE), TILE)
        sums = [jnp.zeros((TILE, BLK), jnp.float32), jnp.zeros((TILE, BLK), jnp.float32)]
        for part, power_ref in enumerate(power_refs):
            for pair in range(power_ref.shape[0]):
                which = 0 if 2 * pair < act_half else 1
                for side in range(2):
                    row = part * blocks_half + 2 * pair + side
                    power = power_ref[pair, here, side * BLK : (side + 1) * BLK]
                    sums[which] += power * inverse[row : row + 1, :]
        act_sum[here, :], grad_sum[here, :] = sums

    ones = jnp.ones((8, BLK), jnp.float32)
    for index, total in enumerate((act_sum, grad_sum)):
        sums = lax.dot_general(
            ones,
            total[...],
            contract_lanes,
            precision=lax.Precision.HIGHEST,
            preferred_element_type=jnp.float32,
        )
        weight_ref[index : index + 1, :] = sums[0:1]


def score_kernel(*refs):
    *weight_refs, score_ref = refs
    weights = weight_refs[0][...]
    for weight_ref in weight_refs[1:]:
        weights = weights + weight_ref[...]
    score_ref[...] = weights[0:1] * weights[1:2] * (1.0 / (D * FF))


def swap(value, axis, mask):
    count = lax.axis_size(axis)
    return lax.ppermute(value, axis, [(i, i ^ mask) for i in range(count)])


def share(value, axis, direct):
    if not direct:
        return [lax.psum(value, axis)]
    return [value] + [swap(value, axis, mask) for mask in range(1, lax.axis_size(axis))]


def after(values, done):
    return list(lax.optimization_barrier((tuple(values), done))[0])


def local(activations, gradients, basis_act, basis_grad):
    tokens = activations.shape[0]
    act_blocks, grad_blocks = basis_act.shape[0], basis_grad.shape[0]
    blocks = act_blocks + grad_blocks
    dp, owners = lax.axis_size("dp"), lax.axis_size("owner")
    scale = 1.0 / (tokens * dp)
    direct = dp in (2, 4) and owners in (1, 2, 4)
    pieces = dp if direct else 1
    halves = 2 if direct and lax.axis_size("groups") == 2 else 1
    rows = BLK // pieces
    me = jnp.full((1,), lax.axis_index("dp") if direct else 0, jnp.int32)
    side = jnp.full((1,), lax.axis_index("groups"), jnp.int32)
    macs = tokens * blocks * BLK * BLK
    input_bytes = 2 * tokens * blocks * BLK
    masks = range(1, pieces)

    if halves == 2:
        shard = call(
            half_kernel, bf16(blocks // 2, rows, BLK), "basis_half", 0, blocks * rows * BLK,
            [IN_SMEM, IN_HBM, IN_HBM], [pltpu.SemaphoreType.DMA((2,))],
        )(side, in_hbm(basis_act), in_hbm(basis_grad))
    elif direct:
        shard = jnp.concatenate([basis_act, basis_grad])
    if direct:
        received = [swap(shard, "dp", mask) for mask in masks]
    else:
        basis_act = lax.all_gather(basis_act, "dp", axis=1, tiled=True)
        basis_grad = lax.all_gather(basis_grad, "dp", axis=1, tiled=True)
        received = []

    early, beside, late = [], [], []
    if pieces == 4:
        early = [(1, 0, blocks)]
        beside = [(3, 0, blocks)]
        late = [(2, 0, blocks)]
    elif pieces == 2:
        late = [(1, 0, blocks)]
    messages = early + beside + late
    act_here, grad_here, own, *sent = call(
        functools.partial(gram_kernel, pieces, messages, scale),
        [
            bf16(*activations.shape),
            bf16(*gradients.shape),
            f32(blocks, rows, BLK),
            *[bf16((end - first) * rows + scale_rows(first, end), BLK) for _, first, end in messages],
        ],
        "partial_gram", 4 * macs, input_bytes,
        [IN_SMEM, IN_HBM, IN_HBM],
        [
            pltpu.VMEM((GROUP, BLK, BLK), jnp.float32),
            pltpu.VMEM((scale_rows(0, blocks), BLK), jnp.float32),
            pltpu.SemaphoreType.DMA((blocks // GROUP,)),
        ],
    )(me, in_hbm(activations), in_hbm(gradients))
    sent = dict(zip(messages, sent))
    if not direct:
        own = lax.psum_scatter(own, "dp", scatter_dimension=1, tiled=True)

    def send(messages, done=None):
        chunks = [sent[message] for message in messages]
        if done is not None:
            chunks = after(chunks, done)
        return [swap(chunk, "dp", message[0]) for chunk, message in zip(chunks, messages)]

    early_chunks, beside_chunks = send(early), send(beside)

    parts = [received]
    if halves == 2:
        swapped, last = {}, ()
        for mask in sorted(masks, key=lambda mask: (mask != 1, -mask)):
            last = swap(after([received[mask - 1]], last)[0], "groups", 1)
            swapped[mask] = last
            last = (last, own)
        parts.append([swapped[mask] for mask in masks])
    powers, sums = [], []
    for part, shards in enumerate(parts):
        power, *sums = call(
            functools.partial(eigen_kernel, part, halves, pieces, scale),
            [f32(blocks // halves // 2, tokens, PAIR), f32(blocks // halves * (part + 1), BLK)],
            "partial_eigen", 2 * macs // halves, input_bytes // halves,
            [IN_SMEM, IN_SMEM] + [IN_VMEM] * (4 + len(shards) + len(sums)),
            [pltpu.VMEM((blocks // halves // 2, PAIR, PAIR), jnp.bfloat16)],
        )(me, side, act_here, grad_here, basis_act, basis_grad, *shards, *sums)
        powers.append(power)
    sums = share(after(sums, early_chunks)[0], "dp", direct)
    sums = after(sums, beside_chunks)
    act_eigen, grad_eigen, eigen, totals = call(
        functools.partial(combine_kernel, halves),
        [f32(act_blocks, BLK), f32(grad_blocks, BLK), f32(blocks, BLK), f32(2, BLK)],
        "combine_eigen", 0, 4 * blocks * BLK * pieces, [IN_SMEM] + [IN_VMEM] * len(sums),
    )(side, *sums)
    late_chunks = send(late, totals)
    totals = share(totals, "owner", direct)
    weights = call(
        functools.partial(weight_kernel, halves, act_blocks // halves),
        f32(2, tokens), "partial_weights", 0, 4 * tokens * blocks * BLK,
        [IN_VMEM] * (1 + halves + len(totals)),
        [
            pltpu.VMEM((blocks, BLK), jnp.float32),
            pltpu.VMEM((tokens, BLK), jnp.float32),
            pltpu.VMEM((tokens, BLK), jnp.float32),
        ],
    )(eigen, *powers, *totals)
    weights = share(weights, "owner", direct)
    token_scores = call(
        score_kernel, f32(1, tokens), "token_scores", 0, 8 * tokens * len(weights),
        [IN_VMEM] * len(weights),
    )(*weights)

    def tops_of(messages):
        return [pltpu.VMEM((scale_rows(first, end), BLK), jnp.float32) for _, first, end in messages]

    if early:
        own = call(
            functools.partial(add_kernel, early + beside), f32(*own.shape),
            "add_chunks", 0, 12 * own.size, [IN_VMEM] * (1 + len(early + beside)),
            tops_of(early + beside),
        )(own, *early_chunks, *beside_chunks)
    if late:
        covariance = call(
            functools.partial(last_add_kernel, late),
            [f32(act_blocks, rows, BLK), f32(grad_blocks, rows, BLK)],
            "add_last_chunk", 0, 10 * own.size, [IN_VMEM] * (1 + len(late)),
            [
                *tops_of(late),
                pltpu.VMEM(own.shape, jnp.float32),
                pltpu.SemaphoreType.DMA((blocks // GROUP,)),
            ],
            out_spec=pl.BlockSpec(memory_space=pl.ANY),
        )(own, *late_chunks)
    else:
        covariance = own[:act_blocks], own[act_blocks:]
    return (
        *covariance,
        act_eigen.reshape(-1),
        grad_eigen.reshape(-1),
        token_scores.reshape(-1),
    )


def solution(mesh):
    return jax.shard_map(
        local,
        mesh=mesh,
        in_specs=(
            P(("groups", "dp"), "owner"),
            P(("groups", "dp"), "owner"),
            P("owner", "dp", None),
            P("owner", "dp", None),
        ),
        out_specs=(
            P(("groups", "owner"), "dp", None),
            P(("groups", "owner"), "dp", None),
            P(("groups", "owner")),
            P(("groups", "owner")),
            P(("groups", "dp")),
        ),
        check_vma=False,
    )
```

```python
import functools

import jax
import jax.numpy as jnp
from jax import lax
from jax.experimental import pallas as pl
from jax.experimental.pallas import tpu as pltpu
from jax.sharding import PartitionSpec as P

D = 4096
FF = 14336
BLK = 128
PAIR = 2 * BLK
GROUP = 4
TILE = 64
VMEM_LIMIT = 24 * 1024 * 1024
CODE_TOP = 2.0**7.875
SMALLEST = 1e-36

damp_root = 0.31622776601683794
contract_rows = (((0,), (0,)), ((), ()))
contract_inner = (((1,), (0,)), ((), ()))
contract_lanes = (((1,), (1,)), ((), ()))

IN_VMEM = pl.BlockSpec(memory_space=pltpu.VMEM)
IN_SMEM = pl.BlockSpec(memory_space=pltpu.SMEM)
IN_HBM = pl.BlockSpec(memory_space=pltpu.HBM)


def scale_rows(first, end):
    return 16 * pl.cdiv(end - first, 16)


def call(
    kernel, out_shape, name, flops, bytes_accessed, in_specs, scratch_shapes=(),
    out_spec=IN_VMEM,
):
    return pl.pallas_call(
        kernel,
        out_shape=out_shape,
        in_specs=in_specs,
        out_specs=jax.tree.map(lambda _: out_spec, out_shape),
        scratch_shapes=scratch_shapes,
        compiler_params=pltpu.CompilerParams(vmem_limit_bytes=VMEM_LIMIT),
        cost_estimate=pl.CostEstimate(
            flops=flops, bytes_accessed=bytes_accessed, transcendentals=0
        ),
        name=name,
    )


def in_hbm(value):
    return pltpu.with_memory_space_constraint(value, pltpu.HBM)


def f32(*shape):
    return jax.ShapeDtypeStruct(shape, jnp.float32)


def bf16(*shape):
    return jax.ShapeDtypeStruct(shape, jnp.bfloat16)


def encode(values):
    power = values * values
    power = power * power
    power = power * power
    power = power * power
    return jnp.where(values < 0.0, -power, power).astype(jnp.bfloat16)


def decode(coded):
    coded = coded.astype(jnp.float32)
    root = jnp.abs(coded)
    for _ in range(4):
        root = lax.rsqrt(root)
    return jnp.where(coded > 0.0, root, jnp.where(coded < 0.0, -root, 0.0))


def pack_kernel(side_ref, act_ref, grad_ref, *refs):
    *out_refs, sems = refs
    side = side_ref[0]
    blocks = out_refs[0].shape[0]
    copies = []
    for out_ref in reversed(out_refs):
        halves = blocks // out_ref.shape[0]
        at = 0
        for ref in (act_ref, grad_ref):
            count = ref.shape[0] // halves
            copies.append(
                pltpu.make_async_copy(
                    ref.at[pl.ds(side * count if halves > 1 else 0, count)],
                    out_ref.at[pl.ds(at, count)],
                    sems.at[len(copies)],
                )
            )
            at += count
    for copy in copies:
        copy.start()
    for copy in copies:
        copy.wait()


def gram_kernel(pieces, messages, scale, me_ref, act_hbm, grad_hbm, act_ref, grad_ref, own_ref, *refs):
    sent_refs, (whole, tops, sems) = refs[:-3], refs[-3:]
    rows = BLK // pieces
    me = me_ref[0]
    steps = []
    for source, target in ((act_hbm, act_ref), (grad_hbm, grad_ref)):
        for first in range(0, source.shape[1], GROUP * BLK):
            columns = slice(first, first + GROUP * BLK)
            copy = pltpu.make_async_copy(
                source.at[:, columns], target.at[:, columns], sems.at[len(steps)]
            )
            copy.start()
            steps.append((target, columns, copy))
    tops[...] = jnp.zeros_like(tops)
    for step, (ref, columns, copy) in enumerate(steps):
        copy.wait()
        for offset in range(GROUP):
            block = step * GROUP + offset
            at = columns.start + offset * BLK
            values = ref[:, at : at + BLK]
            gram = scale * lax.dot_general(
                values, values, contract_rows, preferred_element_type=jnp.float32
            )
            if pieces == 1:
                own_ref[block] = gram
                continue
            whole[offset] = gram
            top = jnp.maximum(jnp.max(jnp.abs(gram), axis=0, keepdims=True), SMALLEST)
            top = (top * (1.0 + 2.0**-8)).astype(jnp.bfloat16).astype(jnp.float32)
            tops[block : block + 1, :] = top
            gain = CODE_TOP / top
            own_ref[block] = whole[offset, pl.ds(pl.multiple_of(me * rows, rows), rows), :]
            for sent_ref, (mask, first, end) in zip(sent_refs, messages):
                if first <= block < end:
                    row = pl.multiple_of((me ^ mask) * rows, rows)
                    place = slice((block - first) * rows, (block - first + 1) * rows)
                    sent_ref[place, :] = encode(whole[offset, pl.ds(row, rows), :] * gain)
    for sent_ref, (_, first, end) in zip(sent_refs, messages):
        sent_ref[(end - first) * rows :, :] = tops[
            first : first + scale_rows(first, end), :
        ].astype(jnp.bfloat16)


def add_group(messages, rows, own_ref, sent_refs, tops_refs, step):
    for block in range(step * GROUP, (step + 1) * GROUP):
        total = own_ref[block]
        for (_, first, end), sent_ref, tops in zip(messages, sent_refs, tops_refs):
            if first <= block < end:
                at = block - first
                values = decode(sent_ref[at * rows : (at + 1) * rows, :])
                total = total + values * tops[at : at + 1, :]
        yield block, total


def load_tops(messages, rows, sent_refs, tops_refs):
    for (_, first, end), sent_ref, tops in zip(messages, sent_refs, tops_refs):
        tops[...] = sent_ref[(end - first) * rows :, :].astype(jnp.float32) * (1.0 / CODE_TOP)


def add_kernel(messages, own_ref, *refs):
    sent_refs, sum_ref, tops_refs = refs[: len(messages)], refs[len(messages)], refs[len(messages) + 1 :]
    blocks, rows, _ = own_ref.shape
    load_tops(messages, rows, sent_refs, tops_refs)
    for step in range(blocks // GROUP):
        for block, total in add_group(messages, rows, own_ref, sent_refs, tops_refs, step):
            sum_ref[block] = total


def last_add_kernel(messages, own_ref, *refs):
    sent_refs, refs = refs[: len(messages)], refs[len(messages) :]
    act_ref, grad_ref, *tops_refs, sums, sems = refs
    blocks, rows, _ = own_ref.shape
    load_tops(messages, rows, sent_refs, tops_refs)
    copies = []
    for step in range(blocks // GROUP):
        for block, total in add_group(messages, rows, own_ref, sent_refs, tops_refs, step):
            sums[block] = total
        first = step * GROUP
        ref, at = act_ref, first
        if first >= act_ref.shape[0]:
            ref, at = grad_ref, first - act_ref.shape[0]
        copies.append(
            pltpu.make_async_copy(
                sums.at[pl.ds(first, GROUP)], ref.at[pl.ds(at, GROUP)], sems.at[step]
            )
        )
        copies[-1].start()
    for copy in copies:
        copy.wait()


def pairs_of(part, side, halves, act_ref, grad_ref):
    half = lax.rem(side + part, halves)
    for ref in (act_ref, grad_ref):
        count = ref.shape[1] // PAIR // halves
        for pair in range(count):
            yield ref, pl.multiple_of((half * count + pair) * PAIR, PAIR)


def eigen_kernel(part, halves, masks, pieces, scale, me_ref, side_ref, act_ref, grad_ref, *refs):
    *shard_refs, power_ref, sums_ref, basis_ref = refs
    me, side = me_ref[0], side_ref[0]
    rows = BLK // pieces
    done = 0
    if part:
        *shard_refs, done_ref = shard_refs
        done = done_ref.shape[0]
        sums_ref[:done] = done_ref[...]
    half = lax.rem(side + part, halves)
    act_half = act_ref.shape[1] // BLK // halves
    grad_half = grad_ref.shape[1] // BLK // halves
    basis_ref[...] = jnp.zeros_like(basis_ref)
    for mask, ref in zip(masks, shard_refs):
        whole = halves > 1 and ref.shape[0] == halves * (act_half + grad_half)
        for block in range(act_half + grad_half):
            at = block
            if whole and block < act_half:
                at = half * act_half + block
            elif whole:
                at = (halves - 1) * act_half + half * grad_half + block
            corner = block % 2
            row = pl.multiple_of(corner * BLK + (me ^ mask) * rows, rows)
            columns = slice(corner * BLK, (corner + 1) * BLK)
            basis_ref[block // 2, pl.ds(row, rows), columns] = ref[at]

    for pair, (ref, column) in enumerate(pairs_of(part, side, halves, act_ref, grad_ref)):
        projected = lax.dot_general(
            ref[:, pl.ds(column, PAIR)],
            basis_ref[pair],
            contract_inner,
            preferred_element_type=jnp.float32,
        )
        power = projected * projected
        power_ref[pair] = power
        sums = scale * jnp.sum(power, axis=0, keepdims=True)
        row = done + 2 * pair
        sums_ref[row : row + 1, :] = sums[:, :BLK]
        sums_ref[row + 1 : row + 2, :] = sums[:, BLK:]


def combine_kernel(halves, side_ref, *refs):
    *sums_refs, act_eigen_ref, grad_eigen_ref, eigen_ref, total_ref = refs
    side = side_ref[0]
    act_half, grad_half = act_eigen_ref.shape[0] // halves, grad_eigen_ref.shape[0] // halves
    eigen = sums_refs[0][...]
    for sums_ref in sums_refs[1:]:
        eigen = eigen + sums_ref[...]
    eigen_ref[...] = eigen
    act_total = jnp.zeros((1, BLK), jnp.float32)
    grad_total = jnp.zeros((1, BLK), jnp.float32)
    for part in range(halves):
        half = lax.rem(side + part, halves)
        first = part * (act_half + grad_half)
        act = eigen[first : first + act_half]
        grad = eigen[first + act_half : first + act_half + grad_half]
        act_total += jnp.sum(act, axis=0, keepdims=True)
        grad_total += jnp.sum(grad, axis=0, keepdims=True)
        act_eigen_ref[pl.ds(half * act_half, act_half), :] = act
        grad_eigen_ref[pl.ds(half * grad_half, grad_half), :] = grad
    total_ref[0:1, :] = act_total
    total_ref[1:2, :] = grad_total


def weight_kernel(halves, act_half, eigen_ref, *refs):
    *refs, weight_ref, inverse, act_sum, grad_sum = refs
    power_refs, total_refs = refs[:halves], refs[halves:]
    totals = total_refs[0][...]
    for total_ref in total_refs[1:]:
        totals = totals + total_ref[...]
    totals = jnp.sum(totals, axis=1, keepdims=True)
    blocks_half = eigen_ref.shape[0] // halves
    for part in range(halves):
        first = part * blocks_half
        act = slice(first, first + act_half)
        grad = slice(first + act_half, first + blocks_half)
        inverse[act] = 1.0 / (eigen_ref[act] + totals[0:1] * (damp_root / D))
        inverse[grad] = 1.0 / (eigen_ref[grad] + totals[1:2] * (damp_root / FF))
    tokens = act_sum.shape[0]

    @pl.loop(0, tokens // TILE)
    def _(tile):
        here = pl.ds(pl.multiple_of(tile * TILE, TILE), TILE)
        sums = [jnp.zeros((TILE, BLK), jnp.float32), jnp.zeros((TILE, BLK), jnp.float32)]
        for part, power_ref in enumerate(power_refs):
            for pair in range(power_ref.shape[0]):
                which = 0 if 2 * pair < act_half else 1
                for side in range(2):
                    row = part * blocks_half + 2 * pair + side
                    power = power_ref[pair, here, side * BLK : (side + 1) * BLK]
                    sums[which] += power * inverse[row : row + 1, :]
        act_sum[here, :], grad_sum[here, :] = sums

    ones = jnp.ones((8, BLK), jnp.float32)
    for index, total in enumerate((act_sum, grad_sum)):
        sums = lax.dot_general(
            ones,
            total[...],
            contract_lanes,
            precision=lax.Precision.HIGHEST,
            preferred_element_type=jnp.float32,
        )
        weight_ref[index : index + 1, :] = sums[0:1]


def score_kernel(*refs):
    *weight_refs, score_ref = refs
    weights = weight_refs[0][...]
    for weight_ref in weight_refs[1:]:
        weights = weights + weight_ref[...]
    score_ref[...] = weights[0:1] * weights[1:2] * (1.0 / (D * FF))


def swap(value, axis, mask):
    count = lax.axis_size(axis)
    return lax.ppermute(value, axis, [(i, i ^ mask) for i in range(count)])


def share(value, axis, direct):
    if not direct:
        return [lax.psum(value, axis)]
    return [value] + [swap(value, axis, mask) for mask in range(1, lax.axis_size(axis))]


def after(values, done):
    return list(lax.optimization_barrier((tuple(values), done))[0])


def local(activations, gradients, basis_act, basis_grad):
    tokens = activations.shape[0]
    act_blocks, grad_blocks = basis_act.shape[0], basis_grad.shape[0]
    blocks = act_blocks + grad_blocks
    dp, owners = lax.axis_size("dp"), lax.axis_size("owner")
    scale = 1.0 / (tokens * dp)
    direct = dp in (2, 4) and owners in (1, 2, 4)
    pieces = dp if direct else 1
    halves = 2 if pieces == 4 and lax.axis_size("groups") == 2 else 1
    rows = BLK // pieces
    me = jnp.full((1,), lax.axis_index("dp") if direct else 0, jnp.int32)
    side = jnp.full((1,), lax.axis_index("groups"), jnp.int32)
    macs = tokens * blocks * BLK * BLK
    input_bytes = 2 * tokens * blocks * BLK
    if direct:
        shards = call(
            pack_kernel,
            [bf16(blocks // part, rows, BLK) for part in range(1, halves + 1)],
            "pack_basis", 0, 2 * blocks * rows * BLK,
            [IN_SMEM, IN_HBM, IN_HBM], [pltpu.SemaphoreType.DMA((2 * halves,))],
        )(side, in_hbm(basis_act), in_hbm(basis_grad))
        near = [shards[0], swap(shards[0], "dp", 1)]
        far = {mask: swap(shards[-1], "dp", mask) for mask in range(pieces - 1, 1, -1)}
    else:
        near = [
            jnp.concatenate(
                [lax.all_gather(part, "dp", axis=1, tiled=True) for part in (basis_act, basis_grad)]
            )
        ]
        far = {}
    masks = [*range(len(near)), *far]

    early, beside, late = [], [], []
    if pieces == 4:
        early = [(1, 0, blocks)]
        beside = [(3, 0, blocks)]
        late = [(2, 0, blocks)]
    elif pieces == 2:
        late = [(1, 0, blocks)]
    messages = early + beside + late
    act_here, grad_here, own, *sent = call(
        functools.partial(gram_kernel, pieces, messages, scale),
        [
            bf16(*activations.shape),
            bf16(*gradients.shape),
            f32(blocks, rows, BLK),
            *[bf16((end - first) * rows + scale_rows(first, end), BLK) for _, first, end in messages],
        ],
        "partial_gram", 4 * macs, input_bytes,
        [IN_SMEM, IN_HBM, IN_HBM],
        [
            pltpu.VMEM((GROUP, BLK, BLK), jnp.float32),
            pltpu.VMEM((scale_rows(0, blocks), BLK), jnp.float32),
            pltpu.SemaphoreType.DMA((blocks // GROUP,)),
        ],
    )(me, in_hbm(activations), in_hbm(gradients))
    sent = dict(zip(messages, sent))
    if not direct:
        own = lax.psum_scatter(own, "dp", scatter_dimension=1, tiled=True)

    def send(messages, done=None):
        chunks = [sent[message] for message in messages]
        if done is not None:
            chunks = after(chunks, done)
        return [swap(chunk, "dp", message[0]) for chunk, message in zip(chunks, messages)]

    early_chunks, beside_chunks = send(early), send(beside)

    parts = [[*near, *far.values()]]
    if halves == 2:
        swapped = [own]
        for part in far.values():
            swapped.append(swap(after([part], swapped[-1])[0], "groups", 1))
        parts.append([*near, *swapped[1:]])
    powers, sums = [], []
    for part, shards in enumerate(parts):
        power, *sums = call(
            functools.partial(eigen_kernel, part, halves, masks, pieces, scale),
            [f32(blocks // halves // 2, tokens, PAIR), f32(blocks // halves * (part + 1), BLK)],
            "partial_eigen", 2 * macs // halves, input_bytes // halves,
            [IN_SMEM, IN_SMEM] + [IN_VMEM] * (2 + len(shards) + len(sums)),
            [pltpu.VMEM((blocks // halves // 2, PAIR, PAIR), jnp.bfloat16)],
        )(me, side, act_here, grad_here, *shards, *sums)
        powers.append(power)
    sums = share(after(sums, early_chunks)[0], "dp", direct)
    sums = after(sums, beside_chunks)
    act_eigen, grad_eigen, eigen, totals = call(
        functools.partial(combine_kernel, halves),
        [f32(act_blocks, BLK), f32(grad_blocks, BLK), f32(blocks, BLK), f32(2, BLK)],
        "combine_eigen", 0, 4 * blocks * BLK * pieces, [IN_SMEM] + [IN_VMEM] * len(sums),
    )(side, *sums)
    late_chunks = send(late, totals)
    totals = share(totals, "owner", direct)
    weights = call(
        functools.partial(weight_kernel, halves, act_blocks // halves),
        f32(2, tokens), "partial_weights", 0, 4 * tokens * blocks * BLK,
        [IN_VMEM] * (1 + halves + len(totals)),
        [
            pltpu.VMEM((blocks, BLK), jnp.float32),
            pltpu.VMEM((tokens, BLK), jnp.float32),
            pltpu.VMEM((tokens, BLK), jnp.float32),
        ],
    )(eigen, *powers, *totals)
    weights = share(weights, "owner", direct)
    token_scores = call(
        score_kernel, f32(1, tokens), "token_scores", 0, 8 * tokens * len(weights),
        [IN_VMEM] * len(weights),
    )(*weights)

    def tops_of(messages):
        return [pltpu.VMEM((scale_rows(first, end), BLK), jnp.float32) for _, first, end in messages]

    if early:
        own = call(
            functools.partial(add_kernel, early + beside), f32(*own.shape),
            "add_chunks", 0, 12 * own.size, [IN_VMEM] * (1 + len(early + beside)),
            tops_of(early + beside),
        )(own, *early_chunks, *beside_chunks)
    if late:
        covariance = call(
            functools.partial(last_add_kernel, late),
            [f32(act_blocks, rows, BLK), f32(grad_blocks, rows, BLK)],
            "add_last_chunk", 0, 10 * own.size, [IN_VMEM] * (1 + len(late)),
            [
                *tops_of(late),
                pltpu.VMEM(own.shape, jnp.float32),
                pltpu.SemaphoreType.DMA((blocks // GROUP,)),
            ],
            out_spec=pl.BlockSpec(memory_space=pl.ANY),
        )(own, *late_chunks)
    else:
        covariance = own[:act_blocks], own[act_blocks:]
    return (
        *covariance,
        act_eigen.reshape(-1),
        grad_eigen.reshape(-1),
        token_scores.reshape(-1),
    )


def solution(mesh):
    return jax.shard_map(
        local,
        mesh=mesh,
        in_specs=(
            P(("groups", "dp"), "owner"),
            P(("groups", "dp"), "owner"),
            P("owner", "dp", None),
            P("owner", "dp", None),
        ),
        out_specs=(
            P(("groups", "owner"), "dp", None),
            P(("groups", "owner"), "dp", None),
            P(("groups", "owner")),
            P(("groups", "owner")),
            P(("groups", "dp")),
        ),
        check_vma=False,
    )
```

```python
import functools

import jax
import jax.numpy as jnp
from jax import lax
from jax.experimental import pallas as pl
from jax.experimental.pallas import tpu as pltpu
from jax.sharding import PartitionSpec as P

D = 4096
FF = 14336
BLK = 128
PAIR = 2 * BLK
GROUP = 4
TILE = 64
VMEM_LIMIT = 24 * 1024 * 1024
CODE_TOP = 2.0**7.875
SMALLEST = 1e-36

damp_root = 0.31622776601683794
contract_rows = (((0,), (0,)), ((), ()))
contract_inner = (((1,), (0,)), ((), ()))
contract_lanes = (((1,), (1,)), ((), ()))

IN_VMEM = pl.BlockSpec(memory_space=pltpu.VMEM)
IN_SMEM = pl.BlockSpec(memory_space=pltpu.SMEM)
IN_HBM = pl.BlockSpec(memory_space=pltpu.HBM)


def scale_rows(first, end):
    return 16 * pl.cdiv(end - first, 16)


def call(
    kernel, out_shape, name, flops, bytes_accessed, in_specs, scratch_shapes=(),
    out_spec=IN_VMEM,
):
    return pl.pallas_call(
        kernel,
        out_shape=out_shape,
        in_specs=in_specs,
        out_specs=jax.tree.map(lambda _: out_spec, out_shape),
        scratch_shapes=scratch_shapes,
        compiler_params=pltpu.CompilerParams(vmem_limit_bytes=VMEM_LIMIT),
        cost_estimate=pl.CostEstimate(
            flops=flops, bytes_accessed=bytes_accessed, transcendentals=0
        ),
        name=name,
    )


def in_hbm(value):
    return pltpu.with_memory_space_constraint(value, pltpu.HBM)


def f32(*shape):
    return jax.ShapeDtypeStruct(shape, jnp.float32)


def bf16(*shape):
    return jax.ShapeDtypeStruct(shape, jnp.bfloat16)


def encode(values):
    power = values * values
    power = power * power
    power = power * power
    power = power * power
    return jnp.where(values < 0.0, -power, power).astype(jnp.bfloat16)


def top_of(values):
    top = jnp.maximum(jnp.max(jnp.abs(values), axis=0, keepdims=True), SMALLEST)
    return (top * (1.0 + 2.0**-8)).astype(jnp.bfloat16).astype(jnp.float32)


def decode(coded):
    coded = coded.astype(jnp.float32)
    root = jnp.abs(coded)
    for _ in range(4):
        root = lax.rsqrt(root)
    return jnp.where(coded > 0.0, root, jnp.where(coded < 0.0, -root, 0.0))


def pack_kernel(side_ref, act_ref, grad_ref, *refs):
    *out_refs, sems = refs
    side = side_ref[0]
    blocks = out_refs[0].shape[0]
    copies = []
    for out_ref in reversed(out_refs):
        halves = blocks // out_ref.shape[0]
        at = 0
        for ref in (act_ref, grad_ref):
            count = ref.shape[0] // halves
            copies.append(
                pltpu.make_async_copy(
                    ref.at[pl.ds(side * count if halves > 1 else 0, count)],
                    out_ref.at[pl.ds(at, count)],
                    sems.at[len(copies)],
                )
            )
            at += count
    for copy in copies:
        copy.start()
    for copy in copies:
        copy.wait()


def gram_kernel(pieces, messages, scale, me_ref, act_hbm, grad_hbm, act_ref, grad_ref, *refs):
    refs, (whole, tops, sems) = refs[:-3], refs[-3:]
    plain_refs, sent_refs = refs[: len(refs) - len(messages)], refs[len(refs) - len(messages) :]
    rows = BLK // pieces
    me = me_ref[0]
    steps = []
    for source, target in ((act_hbm, act_ref), (grad_hbm, grad_ref)):
        for first in range(0, source.shape[1], GROUP * BLK):
            columns = slice(first, first + GROUP * BLK)
            copy = pltpu.make_async_copy(
                source.at[:, columns], target.at[:, columns], sems.at[len(steps)]
            )
            copy.start()
            steps.append((target, columns, copy))
    tops[...] = jnp.zeros_like(tops)
    for step, (ref, columns, copy) in enumerate(steps):
        copy.wait()
        for offset in range(GROUP):
            block = step * GROUP + offset
            at = columns.start + offset * BLK
            values = ref[:, at : at + BLK]
            gram = scale * lax.dot_general(
                values, values, contract_rows, preferred_element_type=jnp.float32
            )
            if pieces == 1:
                plain_refs[0][block] = gram
                continue
            whole[offset] = gram
            for ref_at, mask in zip(plain_refs, (0, 2)):
                row = pl.multiple_of((me ^ mask) * rows, rows)
                ref_at[block] = whole[offset, pl.ds(row, rows), :]
            top = top_of(gram)
            tops[block : block + 1, :] = top
            gain = CODE_TOP / top
            for sent_ref, (mask, first, end) in zip(sent_refs, messages):
                if first <= block < end:
                    row = pl.multiple_of((me ^ mask) * rows, rows)
                    place = slice((block - first) * rows, (block - first + 1) * rows)
                    sent_ref[place, :] = encode(whole[offset, pl.ds(row, rows), :] * gain)
    for sent_ref, (_, first, end) in zip(sent_refs, messages):
        sent_ref[(end - first) * rows :, :] = tops[
            first : first + scale_rows(first, end), :
        ].astype(jnp.bfloat16)


def add_group(messages, rows, own_ref, sent_refs, tops_refs, step):
    for block in range(step * GROUP, (step + 1) * GROUP):
        total = own_ref[block]
        for (_, first, end), sent_ref, tops in zip(messages, sent_refs, tops_refs):
            if first <= block < end:
                at = block - first
                values = decode(sent_ref[at * rows : (at + 1) * rows, :])
                total = total + values * tops[at : at + 1, :]
        yield block, total


def load_tops(messages, rows, sent_refs, tops_refs):
    for (_, first, end), sent_ref, tops in zip(messages, sent_refs, tops_refs):
        tops[...] = sent_ref[(end - first) * rows :, :].astype(jnp.float32) * (1.0 / CODE_TOP)


def add_kernel(messages, own_ref, *refs):
    sent_refs, sum_ref, tops_refs = refs[: len(messages)], refs[len(messages)], refs[len(messages) + 1 :]
    blocks, rows, _ = own_ref.shape
    load_tops(messages, rows, sent_refs, tops_refs)
    for step in range(blocks // GROUP):
        for block, total in add_group(messages, rows, own_ref, sent_refs, tops_refs, step):
            sum_ref[block] = total


def relay_kernel(message, far_ref, relayed_ref, sent_ref, relayed_tops, tops):
    messages = (message,)
    blocks, rows, _ = far_ref.shape
    load_tops(messages, rows, (relayed_ref,), (relayed_tops,))
    tops[...] = jnp.zeros_like(tops)
    for step in range(blocks // GROUP):
        for block, total in add_group(
            messages, rows, far_ref, (relayed_ref,), (relayed_tops,), step
        ):
            top = top_of(total)
            tops[block : block + 1, :] = top
            sent_ref[block * rows : (block + 1) * rows, :] = encode(total * (CODE_TOP / top))
    sent_ref[blocks * rows :, :] = tops[...].astype(jnp.bfloat16)


def last_add_kernel(messages, own_ref, *refs):
    sent_refs, refs = refs[: len(messages)], refs[len(messages) :]
    act_ref, grad_ref, *tops_refs, sums, sems = refs
    blocks, rows, _ = own_ref.shape
    load_tops(messages, rows, sent_refs, tops_refs)
    copies = []
    for step in range(blocks // GROUP):
        for block, total in add_group(messages, rows, own_ref, sent_refs, tops_refs, step):
            sums[block] = total
        first = step * GROUP
        ref, at = act_ref, first
        if first >= act_ref.shape[0]:
            ref, at = grad_ref, first - act_ref.shape[0]
        copies.append(
            pltpu.make_async_copy(
                sums.at[pl.ds(first, GROUP)], ref.at[pl.ds(at, GROUP)], sems.at[step]
            )
        )
        copies[-1].start()
    for copy in copies:
        copy.wait()


def pairs_of(part, side, halves, act_ref, grad_ref):
    half = lax.rem(side + part, halves)
    for ref in (act_ref, grad_ref):
        count = ref.shape[1] // PAIR // halves
        for pair in range(count):
            yield ref, pl.multiple_of((half * count + pair) * PAIR, PAIR)


def eigen_kernel(part, halves, masks, pieces, scale, me_ref, side_ref, act_ref, grad_ref, *refs):
    *shard_refs, power_ref, sums_ref, basis_ref = refs
    me, side = me_ref[0], side_ref[0]
    rows = BLK // pieces
    done = 0
    if part:
        *shard_refs, done_ref = shard_refs
        done = done_ref.shape[0]
        sums_ref[:done] = done_ref[...]
    half = lax.rem(side + part, halves)
    act_half = act_ref.shape[1] // BLK // halves
    grad_half = grad_ref.shape[1] // BLK // halves
    basis_ref[...] = jnp.zeros_like(basis_ref)
    for mask, ref in zip(masks, shard_refs):
        whole = halves > 1 and ref.shape[0] == halves * (act_half + grad_half)
        for block in range(act_half + grad_half):
            at = block
            if whole and block < act_half:
                at = half * act_half + block
            elif whole:
                at = (halves - 1) * act_half + half * grad_half + block
            corner = block % 2
            row = pl.multiple_of(corner * BLK + (me ^ mask) * rows, rows)
            columns = slice(corner * BLK, (corner + 1) * BLK)
            basis_ref[block // 2, pl.ds(row, rows), columns] = ref[at]

    for pair, (ref, column) in enumerate(pairs_of(part, side, halves, act_ref, grad_ref)):
        projected = lax.dot_general(
            ref[:, pl.ds(column, PAIR)],
            basis_ref[pair],
            contract_inner,
            preferred_element_type=jnp.float32,
        )
        power = projected * projected
        power_ref[pair] = power
        sums = scale * jnp.sum(power, axis=0, keepdims=True)
        row = done + 2 * pair
        sums_ref[row : row + 1, :] = sums[:, :BLK]
        sums_ref[row + 1 : row + 2, :] = sums[:, BLK:]


def combine_kernel(halves, side_ref, *refs):
    *sums_refs, act_eigen_ref, grad_eigen_ref, eigen_ref, total_ref = refs
    side = side_ref[0]
    act_half, grad_half = act_eigen_ref.shape[0] // halves, grad_eigen_ref.shape[0] // halves
    eigen = sums_refs[0][...]
    for sums_ref in sums_refs[1:]:
        eigen = eigen + sums_ref[...]
    eigen_ref[...] = eigen
    act_total = jnp.zeros((1, BLK), jnp.float32)
    grad_total = jnp.zeros((1, BLK), jnp.float32)
    for part in range(halves):
        half = lax.rem(side + part, halves)
        first = part * (act_half + grad_half)
        act = eigen[first : first + act_half]
        grad = eigen[first + act_half : first + act_half + grad_half]
        act_total += jnp.sum(act, axis=0, keepdims=True)
        grad_total += jnp.sum(grad, axis=0, keepdims=True)
        act_eigen_ref[pl.ds(half * act_half, act_half), :] = act
        grad_eigen_ref[pl.ds(half * grad_half, grad_half), :] = grad
    total_ref[0:1, :] = act_total
    total_ref[1:2, :] = grad_total


def weight_kernel(halves, act_half, eigen_ref, *refs):
    *refs, weight_ref, inverse, act_sum, grad_sum = refs
    power_refs, total_refs = refs[:halves], refs[halves:]
    totals = total_refs[0][...]
    for total_ref in total_refs[1:]:
        totals = totals + total_ref[...]
    totals = jnp.sum(totals, axis=1, keepdims=True)
    blocks_half = eigen_ref.shape[0] // halves
    for part in range(halves):
        first = part * blocks_half
        act = slice(first, first + act_half)
        grad = slice(first + act_half, first + blocks_half)
        inverse[act] = 1.0 / (eigen_ref[act] + totals[0:1] * (damp_root / D))
        inverse[grad] = 1.0 / (eigen_ref[grad] + totals[1:2] * (damp_root / FF))
    tokens = act_sum.shape[0]

    @pl.loop(0, tokens // TILE)
    def _(tile):
        here = pl.ds(pl.multiple_of(tile * TILE, TILE), TILE)
        sums = [jnp.zeros((TILE, BLK), jnp.float32), jnp.zeros((TILE, BLK), jnp.float32)]
        for part, power_ref in enumerate(power_refs):
            for pair in range(power_ref.shape[0]):
                which = 0 if 2 * pair < act_half else 1
                for side in range(2):
                    row = part * blocks_half + 2 * pair + side
                    power = power_ref[pair, here, side * BLK : (side + 1) * BLK]
                    sums[which] += power * inverse[row : row + 1, :]
        act_sum[here, :], grad_sum[here, :] = sums

    ones = jnp.ones((8, BLK), jnp.float32)
    for index, total in enumerate((act_sum, grad_sum)):
        sums = lax.dot_general(
            ones,
            total[...],
            contract_lanes,
            precision=lax.Precision.HIGHEST,
            preferred_element_type=jnp.float32,
        )
        weight_ref[index : index + 1, :] = sums[0:1]


def score_kernel(*refs):
    *weight_refs, score_ref = refs
    weights = weight_refs[0][...]
    for weight_ref in weight_refs[1:]:
        weights = weights + weight_ref[...]
    score_ref[...] = weights[0:1] * weights[1:2] * (1.0 / (D * FF))


def swap(value, axis, mask):
    count = lax.axis_size(axis)
    return lax.ppermute(value, axis, [(i, i ^ mask) for i in range(count)])


def share(value, axis, direct):
    if not direct:
        return [lax.psum(value, axis)]
    return [value] + [swap(value, axis, mask) for mask in range(1, lax.axis_size(axis))]


def after(values, done):
    return list(lax.optimization_barrier((tuple(values), done))[0])


def local(activations, gradients, basis_act, basis_grad):
    tokens = activations.shape[0]
    act_blocks, grad_blocks = basis_act.shape[0], basis_grad.shape[0]
    blocks = act_blocks + grad_blocks
    dp, owners = lax.axis_size("dp"), lax.axis_size("owner")
    scale = 1.0 / (tokens * dp)
    direct = dp in (2, 4) and owners in (1, 2, 4)
    pieces = dp if direct else 1
    halves = 2 if pieces == 4 and lax.axis_size("groups") == 2 else 1
    rows = BLK // pieces
    me = jnp.full((1,), lax.axis_index("dp") if direct else 0, jnp.int32)
    side = jnp.full((1,), lax.axis_index("groups"), jnp.int32)
    macs = tokens * blocks * BLK * BLK
    input_bytes = 2 * tokens * blocks * BLK
    if direct:
        shards = call(
            pack_kernel,
            [bf16(blocks // part, rows, BLK) for part in range(1, halves + 1)],
            "pack_basis", 0, 2 * blocks * rows * BLK,
            [IN_SMEM, IN_HBM, IN_HBM], [pltpu.SemaphoreType.DMA((2 * halves,))],
        )(side, in_hbm(basis_act), in_hbm(basis_grad))
        near = [shards[0], swap(shards[0], "dp", 1)]
        far = {mask: swap(shards[-1], "dp", mask) for mask in range(pieces - 1, 1, -1)}
    else:
        near = [
            jnp.concatenate(
                [lax.all_gather(part, "dp", axis=1, tiled=True) for part in (basis_act, basis_grad)]
            )
        ]
        far = {}
    masks = [*range(len(near)), *far]

    message = bf16(blocks * rows + scale_rows(0, blocks), BLK)
    whole_range = (0, blocks)
    coded = {4: [(3, *whole_range), (1, *whole_range)], 2: [(1, *whole_range)], 1: []}[pieces]
    plain = 2 if pieces == 4 else 1
    act_here, grad_here, *grams = call(
        functools.partial(gram_kernel, pieces, coded, scale),
        [
            bf16(*activations.shape),
            bf16(*gradients.shape),
            *[f32(blocks, rows, BLK)] * plain,
            *[message] * len(coded),
        ],
        "partial_gram", 4 * macs, input_bytes,
        [IN_SMEM, IN_HBM, IN_HBM],
        [
            pltpu.VMEM((GROUP, BLK, BLK), jnp.float32),
            pltpu.VMEM((scale_rows(0, blocks), BLK), jnp.float32),
            pltpu.SemaphoreType.DMA((blocks // GROUP,)),
        ],
    )(me, in_hbm(activations), in_hbm(gradients))
    own = grams[0]
    sent = {message[0]: chunk for message, chunk in zip(coded, grams[plain:])}
    if not direct:
        own = lax.psum_scatter(own, "dp", scatter_dimension=1, tiled=True)
    if pieces == 4:
        middle = lax.ppermute(sent[3], "dp", [(1, 2), (2, 1)])
        relayed = lax.ppermute(sent[3], "dp", [(0, 1), (3, 2)])

    parts = [[*near, *far.values()]]
    if halves == 2:
        swapped = [swap(after([part], own)[0], "groups", 1) for part in far.values()]
        parts.append([*near, *swapped])
    powers, sums = [], []
    for part, shards in enumerate(parts):
        power, *sums = call(
            functools.partial(eigen_kernel, part, halves, masks, pieces, scale),
            [f32(blocks // halves // 2, tokens, PAIR), f32(blocks // halves * (part + 1), BLK)],
            "partial_eigen", 2 * macs // halves, input_bytes // halves,
            [IN_SMEM, IN_SMEM] + [IN_VMEM] * (2 + len(shards) + len(sums)),
            [pltpu.VMEM((blocks // halves // 2, PAIR, PAIR), jnp.bfloat16)],
        )(me, side, act_here, grad_here, *shards, *sums)
        powers.append(power)
    if pieces == 4:
        sent[2] = call(
            functools.partial(relay_kernel, coded[0]), message, "relay_chunk", 0, 12 * own.size,
            [IN_VMEM, IN_VMEM],
            [pltpu.VMEM((scale_rows(0, blocks), BLK), jnp.float32)] * 2,
        )(*after([grams[1], relayed], sums))
    sums = share(sums[0], "dp", direct)
    if pieces == 4:
        sums = after(sums, middle)
    act_eigen, grad_eigen, eigen, totals = call(
        functools.partial(combine_kernel, halves),
        [f32(act_blocks, BLK), f32(grad_blocks, BLK), f32(blocks, BLK), f32(2, BLK)],
        "combine_eigen", 0, 4 * blocks * BLK * pieces, [IN_SMEM] + [IN_VMEM] * len(sums),
    )(side, *sums)
    arrived = {}
    sent.pop(3, None)
    for mask in sent:
        arrived[mask] = swap(after([sent[mask]], totals)[0], "dp", mask)
    totals = share(totals, "owner", direct)
    weights = call(
        functools.partial(weight_kernel, halves, act_blocks // halves),
        f32(2, tokens), "partial_weights", 0, 4 * tokens * blocks * BLK,
        [IN_VMEM] * (1 + halves + len(totals)),
        [
            pltpu.VMEM((blocks, BLK), jnp.float32),
            pltpu.VMEM((tokens, BLK), jnp.float32),
            pltpu.VMEM((tokens, BLK), jnp.float32),
        ],
    )(eigen, *powers, *totals)
    weights = share(weights, "owner", direct)
    token_scores = call(
        score_kernel, f32(1, tokens), "token_scores", 0, 8 * tokens * len(weights),
        [IN_VMEM] * len(weights),
    )(*weights)

    def add(kernel, chunks, out_shape, scratch_shapes=(), **options):
        messages = [(None, *whole_range)] * len(chunks)
        return call(
            functools.partial(kernel, messages), out_shape, "add_chunks", 0, 12 * own.size,
            [IN_VMEM] * (1 + len(chunks)),
            [pltpu.VMEM((scale_rows(*whole_range), BLK), jnp.float32)] * len(chunks)
            + [*scratch_shapes],
            **options,
        )(own, *chunks)

    if pieces == 4:
        own = add(add_kernel, [middle, arrived.pop(1)], f32(*own.shape))
    if arrived:
        covariance = add(
            last_add_kernel, [*arrived.values()],
            [f32(act_blocks, rows, BLK), f32(grad_blocks, rows, BLK)],
            [pltpu.VMEM(own.shape, jnp.float32), pltpu.SemaphoreType.DMA((blocks // GROUP,))],
            out_spec=pl.BlockSpec(memory_space=pl.ANY),
        )
    else:
        covariance = own[:act_blocks], own[act_blocks:]
    return (
        *covariance,
        act_eigen.reshape(-1),
        grad_eigen.reshape(-1),
        token_scores.reshape(-1),
    )


def solution(mesh):
    return jax.shard_map(
        local,
        mesh=mesh,
        in_specs=(
            P(("groups", "dp"), "owner"),
            P(("groups", "dp"), "owner"),
            P("owner", "dp", None),
            P("owner", "dp", None),
        ),
        out_specs=(
            P(("groups", "owner"), "dp", None),
            P(("groups", "owner"), "dp", None),
            P(("groups", "owner")),
            P(("groups", "owner")),
            P(("groups", "dp")),
        ),
        check_vma=False,
    )
```

```python
import functools

import jax
import jax.numpy as jnp
from jax import lax
from jax.experimental import pallas as pl
from jax.experimental.pallas import tpu as pltpu
from jax.sharding import PartitionSpec as P

D = 4096
FF = 14336
BLK = 128
PAIR = 2 * BLK
GROUP = 4
TILE = 64
VMEM_LIMIT = 24 * 1024 * 1024
CODE_TOP = 2.0**7.875
SMALLEST = 1e-36

damp_root = 0.31622776601683794
contract_rows = (((0,), (0,)), ((), ()))
contract_inner = (((1,), (0,)), ((), ()))
contract_lanes = (((1,), (1,)), ((), ()))

IN_VMEM = pl.BlockSpec(memory_space=pltpu.VMEM)
IN_SMEM = pl.BlockSpec(memory_space=pltpu.SMEM)
IN_HBM = pl.BlockSpec(memory_space=pltpu.HBM)


def scale_rows(first, end):
    return 16 * pl.cdiv(end - first, 16)


def call(
    kernel, out_shape, name, flops, bytes_accessed, in_specs, scratch_shapes=(),
    out_spec=None,
):
    return pl.pallas_call(
        kernel,
        out_shape=out_shape,
        in_specs=in_specs,
        out_specs=out_spec or jax.tree.map(lambda _: IN_VMEM, out_shape),
        scratch_shapes=scratch_shapes,
        compiler_params=pltpu.CompilerParams(vmem_limit_bytes=VMEM_LIMIT),
        cost_estimate=pl.CostEstimate(
            flops=flops, bytes_accessed=bytes_accessed, transcendentals=0
        ),
        name=name,
    )


def in_hbm(value):
    return pltpu.with_memory_space_constraint(value, pltpu.HBM)


def f32(*shape):
    return jax.ShapeDtypeStruct(shape, jnp.float32)


def bf16(*shape):
    return jax.ShapeDtypeStruct(shape, jnp.bfloat16)


def encode(values):
    power = values * values
    power = power * power
    power = power * power
    power = power * power
    return jnp.where(values < 0.0, -power, power).astype(jnp.bfloat16)


def top_of(values):
    top = jnp.maximum(jnp.max(jnp.abs(values), axis=0, keepdims=True), SMALLEST)
    return (top * (1.0 + 2.0**-8)).astype(jnp.bfloat16).astype(jnp.float32)


def decode(coded):
    coded = coded.astype(jnp.float32)
    root = jnp.abs(coded)
    for _ in range(4):
        root = lax.rsqrt(root)
    return jnp.where(coded > 0.0, root, jnp.where(coded < 0.0, -root, 0.0))


def pack_kernel(side_ref, act_ref, grad_ref, *refs):
    *out_refs, sems = refs
    side = side_ref[0]
    blocks = out_refs[0].shape[0]
    copies = []
    for out_ref in reversed(out_refs):
        halves = blocks // out_ref.shape[0]
        at = 0
        for ref in (act_ref, grad_ref):
            count = ref.shape[0] // halves
            copies.append(
                pltpu.make_async_copy(
                    ref.at[pl.ds(side * count if halves > 1 else 0, count)],
                    out_ref.at[pl.ds(at, count)],
                    sems.at[len(copies)],
                )
            )
            at += count
    for copy in copies:
        copy.start()
    for copy in copies:
        copy.wait()


def gram_kernel(pieces, messages, scale, me_ref, act_hbm, grad_hbm, act_ref, grad_ref, *refs):
    refs, (whole, tops, sems) = refs[:-3], refs[-3:]
    plain_refs, sent_refs = refs[: len(refs) - len(messages)], refs[len(refs) - len(messages) :]
    rows = BLK // pieces
    me = me_ref[0]
    steps = []
    for source, target in ((act_hbm, act_ref), (grad_hbm, grad_ref)):
        for first in range(0, source.shape[1], GROUP * BLK):
            columns = slice(first, first + GROUP * BLK)
            copy = pltpu.make_async_copy(
                source.at[:, columns], target.at[:, columns], sems.at[len(steps)]
            )
            copy.start()
            steps.append((target, columns, copy))
    tops[...] = jnp.zeros_like(tops)
    for step, (ref, columns, copy) in enumerate(steps):
        copy.wait()
        for offset in range(GROUP):
            block = step * GROUP + offset
            at = columns.start + offset * BLK
            values = ref[:, at : at + BLK]
            gram = scale * lax.dot_general(
                values, values, contract_rows, preferred_element_type=jnp.float32
            )
            if pieces == 1:
                plain_refs[0][block] = gram
                continue
            whole[offset] = gram
            for ref_at, mask in zip(plain_refs, (0, 2)):
                row = pl.multiple_of((me ^ mask) * rows, rows)
                ref_at[block] = whole[offset, pl.ds(row, rows), :]
            top = top_of(gram)
            tops[block : block + 1, :] = top
            gain = CODE_TOP / top
            for sent_ref, (mask, first, end) in zip(sent_refs, messages):
                if first <= block < end:
                    row = pl.multiple_of((me ^ mask) * rows, rows)
                    place = slice((block - first) * rows, (block - first + 1) * rows)
                    sent_ref[place, :] = encode(whole[offset, pl.ds(row, rows), :] * gain)
    for sent_ref, (_, first, end) in zip(sent_refs, messages):
        sent_ref[(end - first) * rows :, :] = tops[
            first : first + scale_rows(first, end), :
        ].astype(jnp.bfloat16)


def add_group(messages, rows, own_ref, sent_refs, tops_refs, step):
    for block in range(step * GROUP, (step + 1) * GROUP):
        total = own_ref[block]
        for (_, first, end), sent_ref, tops in zip(messages, sent_refs, tops_refs):
            if first <= block < end:
                at = block - first
                values = decode(sent_ref[at * rows : (at + 1) * rows, :])
                total = total + values * tops[at : at + 1, :]
        yield block, total


def load_tops(messages, rows, sent_refs, tops_refs):
    for (_, first, end), sent_ref, tops in zip(messages, sent_refs, tops_refs):
        tops[...] = sent_ref[(end - first) * rows :, :].astype(jnp.float32) * (1.0 / CODE_TOP)


def add_kernel(messages, own_ref, *refs):
    sent_refs, sum_ref, tops_refs = refs[: len(messages)], refs[len(messages)], refs[len(messages) + 1 :]
    blocks, rows, _ = own_ref.shape
    load_tops(messages, rows, sent_refs, tops_refs)
    for step in range(blocks // GROUP):
        for block, total in add_group(messages, rows, own_ref, sent_refs, tops_refs, step):
            sum_ref[block] = total


def relay_kernel(message, far_ref, relayed_ref, sent_ref, relayed_tops, tops):
    messages = (message,)
    blocks, rows, _ = far_ref.shape
    load_tops(messages, rows, (relayed_ref,), (relayed_tops,))
    tops[...] = jnp.zeros_like(tops)
    for step in range(blocks // GROUP):
        for block, total in add_group(
            messages, rows, far_ref, (relayed_ref,), (relayed_tops,), step
        ):
            top = top_of(total)
            tops[block : block + 1, :] = top
            sent_ref[block * rows : (block + 1) * rows, :] = encode(total * (CODE_TOP / top))
    sent_ref[blocks * rows :, :] = tops[...].astype(jnp.bfloat16)


def last_add_kernel(messages, owners, own_ref, *refs):
    sent_refs, refs = refs[: len(messages)], refs[len(messages) :]
    weight_refs, refs = refs[:owners], refs[owners:]
    act_ref, grad_ref, score_ref, *tops_refs, sums, sems = refs
    blocks, rows, _ = own_ref.shape
    load_tops(messages, rows, sent_refs, tops_refs)
    copies = []
    for step in range(blocks // GROUP):
        for block, total in add_group(messages, rows, own_ref, sent_refs, tops_refs, step):
            sums[block] = total
        first = step * GROUP
        ref, at = act_ref, first
        if first >= act_ref.shape[0]:
            ref, at = grad_ref, first - act_ref.shape[0]
        copies.append(
            pltpu.make_async_copy(
                sums.at[pl.ds(first, GROUP)], ref.at[pl.ds(at, GROUP)], sems.at[step]
            )
        )
        copies[-1].start()
    score_kernel(weight_refs, score_ref)
    for copy in copies:
        copy.wait()


def pairs_of(part, side, halves, act_ref, grad_ref):
    half = lax.rem(side + part, halves)
    for ref in (act_ref, grad_ref):
        count = ref.shape[1] // PAIR // halves
        for pair in range(count):
            yield ref, pl.multiple_of((half * count + pair) * PAIR, PAIR)


def eigen_kernel(part, halves, masks, pieces, scale, me_ref, side_ref, act_ref, grad_ref, *refs):
    *shard_refs, power_ref, sums_ref, basis_ref = refs
    me, side = me_ref[0], side_ref[0]
    rows = BLK // pieces
    done = 0
    if part:
        *shard_refs, done_ref = shard_refs
        done = done_ref.shape[0]
        sums_ref[:done] = done_ref[...]
    half = lax.rem(side + part, halves)
    act_half = act_ref.shape[1] // BLK // halves
    grad_half = grad_ref.shape[1] // BLK // halves
    basis_ref[...] = jnp.zeros_like(basis_ref)
    for mask, ref in zip(masks, shard_refs):
        whole = halves > 1 and ref.shape[0] == halves * (act_half + grad_half)
        for block in range(act_half + grad_half):
            at = block
            if whole and block < act_half:
                at = half * act_half + block
            elif whole:
                at = (halves - 1) * act_half + half * grad_half + block
            corner = block % 2
            row = pl.multiple_of(corner * BLK + (me ^ mask) * rows, rows)
            columns = slice(corner * BLK, (corner + 1) * BLK)
            basis_ref[block // 2, pl.ds(row, rows), columns] = ref[at]

    for pair, (ref, column) in enumerate(pairs_of(part, side, halves, act_ref, grad_ref)):
        projected = lax.dot_general(
            ref[:, pl.ds(column, PAIR)],
            basis_ref[pair],
            contract_inner,
            preferred_element_type=jnp.float32,
        )
        power = projected * projected
        power_ref[pair] = power
        sums = scale * jnp.sum(power, axis=0, keepdims=True)
        row = done + 2 * pair
        sums_ref[row : row + 1, :] = sums[:, :BLK]
        sums_ref[row + 1 : row + 2, :] = sums[:, BLK:]


def combine_kernel(halves, side_ref, *refs):
    *sums_refs, act_eigen_ref, grad_eigen_ref, eigen_ref, total_ref = refs
    side = side_ref[0]
    act_half, grad_half = act_eigen_ref.shape[0] // halves, grad_eigen_ref.shape[0] // halves
    eigen = sums_refs[0][...]
    for sums_ref in sums_refs[1:]:
        eigen = eigen + sums_ref[...]
    eigen_ref[...] = eigen
    act_total = jnp.zeros((1, BLK), jnp.float32)
    grad_total = jnp.zeros((1, BLK), jnp.float32)
    for part in range(halves):
        half = lax.rem(side + part, halves)
        first = part * (act_half + grad_half)
        act = eigen[first : first + act_half]
        grad = eigen[first + act_half : first + act_half + grad_half]
        act_total += jnp.sum(act, axis=0, keepdims=True)
        grad_total += jnp.sum(grad, axis=0, keepdims=True)
        act_eigen_ref[pl.ds(half * act_half, act_half), :] = act
        grad_eigen_ref[pl.ds(half * grad_half, grad_half), :] = grad
    total_ref[0:1, :] = act_total
    total_ref[1:2, :] = grad_total


def weight_kernel(halves, act_half, eigen_ref, *refs):
    *refs, weight_ref, inverse, act_sum, grad_sum = refs
    power_refs, total_refs = refs[:halves], refs[halves:]
    totals = total_refs[0][...]
    for total_ref in total_refs[1:]:
        totals = totals + total_ref[...]
    totals = jnp.sum(totals, axis=1, keepdims=True)
    blocks_half = eigen_ref.shape[0] // halves
    for part in range(halves):
        first = part * blocks_half
        act = slice(first, first + act_half)
        grad = slice(first + act_half, first + blocks_half)
        inverse[act] = 1.0 / (eigen_ref[act] + totals[0:1] * (damp_root / D))
        inverse[grad] = 1.0 / (eigen_ref[grad] + totals[1:2] * (damp_root / FF))
    tokens = act_sum.shape[0]

    @pl.loop(0, tokens // TILE)
    def _(tile):
        here = pl.ds(pl.multiple_of(tile * TILE, TILE), TILE)
        sums = [jnp.zeros((TILE, BLK), jnp.float32), jnp.zeros((TILE, BLK), jnp.float32)]
        for part, power_ref in enumerate(power_refs):
            for pair in range(power_ref.shape[0]):
                which = 0 if 2 * pair < act_half else 1
                for side in range(2):
                    row = part * blocks_half + 2 * pair + side
                    power = power_ref[pair, here, side * BLK : (side + 1) * BLK]
                    sums[which] += power * inverse[row : row + 1, :]
        act_sum[here, :], grad_sum[here, :] = sums

    ones = jnp.ones((8, BLK), jnp.float32)
    for index, total in enumerate((act_sum, grad_sum)):
        sums = lax.dot_general(
            ones,
            total[...],
            contract_lanes,
            precision=lax.Precision.HIGHEST,
            preferred_element_type=jnp.float32,
        )
        weight_ref[index : index + 1, :] = sums[0:1]


def score_kernel(weight_refs, score_ref):
    weights = weight_refs[0][...]
    for weight_ref in weight_refs[1:]:
        weights = weights + weight_ref[...]
    score_ref[...] = weights[0:1] * weights[1:2] * (1.0 / (D * FF))


def swap(value, axis, mask):
    count = lax.axis_size(axis)
    return lax.ppermute(value, axis, [(i, i ^ mask) for i in range(count)])


def share(value, axis, direct):
    if not direct:
        return [lax.psum(value, axis)]
    return [value] + [swap(value, axis, mask) for mask in range(1, lax.axis_size(axis))]


def after(values, done):
    return list(lax.optimization_barrier((tuple(values), done))[0])


def local(activations, gradients, basis_act, basis_grad):
    tokens = activations.shape[0]
    act_blocks, grad_blocks = basis_act.shape[0], basis_grad.shape[0]
    blocks = act_blocks + grad_blocks
    dp, owners = lax.axis_size("dp"), lax.axis_size("owner")
    scale = 1.0 / (tokens * dp)
    direct = dp in (2, 4) and owners in (1, 2, 4)
    pieces = dp if direct else 1
    halves = 2 if pieces == 4 and lax.axis_size("groups") == 2 else 1
    rows = BLK // pieces
    me = jnp.full((1,), lax.axis_index("dp") if direct else 0, jnp.int32)
    side = jnp.full((1,), lax.axis_index("groups"), jnp.int32)
    macs = tokens * blocks * BLK * BLK
    input_bytes = 2 * tokens * blocks * BLK
    if direct:
        shards = call(
            pack_kernel,
            [bf16(blocks // part, rows, BLK) for part in range(1, halves + 1)],
            "pack_basis", 0, 2 * blocks * rows * BLK,
            [IN_SMEM, IN_HBM, IN_HBM], [pltpu.SemaphoreType.DMA((2 * halves,))],
        )(side, in_hbm(basis_act), in_hbm(basis_grad))
        near = [shards[0], swap(shards[0], "dp", 1)]
        far = {mask: swap(shards[-1], "dp", mask) for mask in range(pieces - 1, 1, -1)}
    else:
        near = [
            jnp.concatenate(
                [lax.all_gather(part, "dp", axis=1, tiled=True) for part in (basis_act, basis_grad)]
            )
        ]
        far = {}
    masks = [*range(len(near)), *far]

    message = bf16(blocks * rows + scale_rows(0, blocks), BLK)
    whole_range = (0, blocks)
    coded = {4: [(3, *whole_range), (1, *whole_range)], 2: [(1, *whole_range)], 1: []}[pieces]
    plain = 2 if pieces == 4 else 1
    act_here, grad_here, *grams = call(
        functools.partial(gram_kernel, pieces, coded, scale),
        [
            bf16(*activations.shape),
            bf16(*gradients.shape),
            *[f32(blocks, rows, BLK)] * plain,
            *[message] * len(coded),
        ],
        "partial_gram", 4 * macs, input_bytes,
        [IN_SMEM, IN_HBM, IN_HBM],
        [
            pltpu.VMEM((GROUP, BLK, BLK), jnp.float32),
            pltpu.VMEM((scale_rows(0, blocks), BLK), jnp.float32),
            pltpu.SemaphoreType.DMA((blocks // GROUP,)),
        ],
    )(me, in_hbm(activations), in_hbm(gradients))
    own = grams[0]
    sent = {message[0]: chunk for message, chunk in zip(coded, grams[plain:])}
    if not direct:
        own = lax.psum_scatter(own, "dp", scatter_dimension=1, tiled=True)
    if pieces == 4:
        middle = lax.ppermute(sent[3], "dp", [(1, 2), (2, 1)])
        relayed = lax.ppermute(sent[3], "dp", [(0, 1), (3, 2)])

    parts = [[*near, *far.values()]]
    if halves == 2:
        swapped = [swap(after([part], own)[0], "groups", 1) for part in far.values()]
        parts.append([*near, *swapped])
    powers, sums = [], []
    for part, shards in enumerate(parts):
        power, *sums = call(
            functools.partial(eigen_kernel, part, halves, masks, pieces, scale),
            [f32(blocks // halves // 2, tokens, PAIR), f32(blocks // halves * (part + 1), BLK)],
            "partial_eigen", 2 * macs // halves, input_bytes // halves,
            [IN_SMEM, IN_SMEM] + [IN_VMEM] * (2 + len(shards) + len(sums)),
            [pltpu.VMEM((blocks // halves // 2, PAIR, PAIR), jnp.bfloat16)],
        )(me, side, act_here, grad_here, *shards, *sums)
        powers.append(power)
    if pieces == 4:
        sent[2] = call(
            functools.partial(relay_kernel, coded[0]), message, "relay_chunk", 0, 12 * own.size,
            [IN_VMEM, IN_VMEM],
            [pltpu.VMEM((scale_rows(0, blocks), BLK), jnp.float32)] * 2,
        )(*after([grams[1], relayed], sums))
    sums = share(sums[0], "dp", direct)
    if pieces == 4:
        sums = after(sums, (middle, sent[2]))
    act_eigen, grad_eigen, eigen, totals = call(
        functools.partial(combine_kernel, halves),
        [f32(act_blocks, BLK), f32(grad_blocks, BLK), f32(blocks, BLK), f32(2, BLK)],
        "combine_eigen", 0, 4 * blocks * BLK * pieces, [IN_SMEM] + [IN_VMEM] * len(sums),
    )(side, *sums)
    arrived = {}
    sent.pop(3, None)
    totals = share(totals, "owner", direct)
    for mask in sent:
        arrived[mask] = swap(after([sent[mask]], totals[:2])[0], "dp", mask)
    weights = call(
        functools.partial(weight_kernel, halves, act_blocks // halves),
        f32(2, tokens), "partial_weights", 0, 4 * tokens * blocks * BLK,
        [IN_VMEM] * (1 + halves + len(totals)),
        [
            pltpu.VMEM((blocks, BLK), jnp.float32),
            pltpu.VMEM((tokens, BLK), jnp.float32),
            pltpu.VMEM((tokens, BLK), jnp.float32),
        ],
    )(eigen, *powers, *totals)
    weights = share(weights, "owner", direct)

    def tops_of(count):
        return [pltpu.VMEM((scale_rows(0, blocks), BLK), jnp.float32)] * count

    if pieces == 4:
        own = call(
            functools.partial(add_kernel, [(None, 0, blocks)] * 2),
            f32(*own.shape), "add_chunks", 0, 16 * own.size, [IN_VMEM] * 3, tops_of(2),
        )(own, middle, arrived.pop(1))
        weights[1:] = after(weights[1:], own)
    chunks = list(arrived.values())
    if chunks:
        anywhere = pl.BlockSpec(memory_space=pl.ANY)
        *covariance, token_scores = call(
            functools.partial(last_add_kernel, [(None, 0, blocks)] * len(chunks), len(weights)),
            [f32(act_blocks, rows, BLK), f32(grad_blocks, rows, BLK), f32(1, tokens)],
            "last_sums", 0, 12 * own.size, [IN_VMEM] * (1 + len(chunks) + len(weights)),
            [
                *tops_of(len(chunks)),
                pltpu.VMEM(own.shape, jnp.float32),
                pltpu.SemaphoreType.DMA((blocks // GROUP,)),
            ],
            out_spec=[anywhere, anywhere, IN_VMEM],
        )(own, *chunks, *weights)
    else:
        covariance = own[:act_blocks], own[act_blocks:]
        token_scores = call(
            lambda *refs: score_kernel(refs[:-1], refs[-1]),
            f32(1, tokens), "token_scores", 0, 8 * tokens, [IN_VMEM] * len(weights),
        )(*weights)
    return (
        *covariance,
        act_eigen.reshape(-1),
        grad_eigen.reshape(-1),
        token_scores.reshape(-1),
    )


def solution(mesh):
    return jax.shard_map(
        local,
        mesh=mesh,
        in_specs=(
            P(("groups", "dp"), "owner"),
            P(("groups", "dp"), "owner"),
            P("owner", "dp", None),
            P("owner", "dp", None),
        ),
        out_specs=(
            P(("groups", "owner"), "dp", None),
            P(("groups", "owner"), "dp", None),
            P(("groups", "owner")),
            P(("groups", "owner")),
            P(("groups", "dp")),
        ),
        check_vma=False,
    )
```

```python
import functools

import jax
import jax.numpy as jnp
from jax import lax
from jax.experimental import pallas as pl
from jax.experimental.pallas import tpu as pltpu
from jax.sharding import PartitionSpec as P

D = 4096
FF = 14336
BLK = 128
PAIR = 2 * BLK
GROUP = 4
TILE = 64
VMEM_LIMIT = 24 * 1024 * 1024
CODE_TOP = 2.0**7.875
SMALLEST = 1e-36

damp_root = 0.31622776601683794
contract_rows = (((0,), (0,)), ((), ()))
contract_inner = (((1,), (0,)), ((), ()))
contract_lanes = (((1,), (1,)), ((), ()))

IN_VMEM = pl.BlockSpec(memory_space=pltpu.VMEM)
IN_SMEM = pl.BlockSpec(memory_space=pltpu.SMEM)
IN_HBM = pl.BlockSpec(memory_space=pltpu.HBM)


def scale_rows(first, end):
    return 16 * pl.cdiv(end - first, 16)


def call(
    kernel, out_shape, name, flops, bytes_accessed, in_specs, scratch_shapes=(),
    out_spec=None,
):
    return pl.pallas_call(
        kernel,
        out_shape=out_shape,
        in_specs=in_specs,
        out_specs=out_spec or jax.tree.map(lambda _: IN_VMEM, out_shape),
        scratch_shapes=scratch_shapes,
        compiler_params=pltpu.CompilerParams(vmem_limit_bytes=VMEM_LIMIT),
        cost_estimate=pl.CostEstimate(
            flops=flops, bytes_accessed=bytes_accessed, transcendentals=0
        ),
        name=name,
    )


def in_hbm(value):
    return pltpu.with_memory_space_constraint(value, pltpu.HBM)


def f32(*shape):
    return jax.ShapeDtypeStruct(shape, jnp.float32)


def bf16(*shape):
    return jax.ShapeDtypeStruct(shape, jnp.bfloat16)


def encode(values):
    power = values * values
    power = power * power
    power = power * power
    power = power * power
    return jnp.where(values < 0.0, -power, power).astype(jnp.bfloat16)


def top_of(values):
    top = jnp.maximum(jnp.max(jnp.abs(values), axis=0, keepdims=True), SMALLEST)
    return (top * (1.0 + 2.0**-8)).astype(jnp.bfloat16).astype(jnp.float32)


def decode(coded):
    coded = coded.astype(jnp.float32)
    root = jnp.abs(coded)
    for _ in range(4):
        root = lax.rsqrt(root)
    return jnp.where(coded > 0.0, root, jnp.where(coded < 0.0, -root, 0.0))


def pack_kernel(side_ref, act_ref, grad_ref, *refs):
    *out_refs, sems = refs
    side = side_ref[0]
    blocks = out_refs[0].shape[0]
    copies = []
    for out_ref in reversed(out_refs):
        halves = blocks // out_ref.shape[0]
        at = 0
        for ref in (act_ref, grad_ref):
            count = ref.shape[0] // halves
            copies.append(
                pltpu.make_async_copy(
                    ref.at[pl.ds(side * count if halves > 1 else 0, count)],
                    out_ref.at[pl.ds(at, count)],
                    sems.at[len(copies)],
                )
            )
            at += count
    for copy in copies:
        copy.start()
    for copy in copies:
        copy.wait()


def gram_kernel(pieces, messages, scale, me_ref, act_hbm, grad_hbm, act_ref, grad_ref, *refs):
    refs, (whole, tops, sems) = refs[:-3], refs[-3:]
    plain_refs, sent_refs = refs[: len(refs) - len(messages)], refs[len(refs) - len(messages) :]
    rows = BLK // pieces
    me = me_ref[0]
    steps = []
    for source, target in ((act_hbm, act_ref), (grad_hbm, grad_ref)):
        for first in range(0, source.shape[1], GROUP * BLK):
            columns = slice(first, first + GROUP * BLK)
            copy = pltpu.make_async_copy(
                source.at[:, columns], target.at[:, columns], sems.at[len(steps)]
            )
            copy.start()
            steps.append((target, columns, copy))
    tops[...] = jnp.zeros_like(tops)
    for step, (ref, columns, copy) in enumerate(steps):
        copy.wait()
        for offset in range(GROUP):
            block = step * GROUP + offset
            at = columns.start + offset * BLK
            values = ref[:, at : at + BLK]
            gram = scale * lax.dot_general(
                values, values, contract_rows, preferred_element_type=jnp.float32
            )
            if pieces == 1:
                plain_refs[0][block] = gram
                continue
            whole[offset] = gram
            for ref_at, mask in zip(plain_refs, (0, 2)):
                row = pl.multiple_of((me ^ mask) * rows, rows)
                ref_at[block] = whole[offset, pl.ds(row, rows), :]
            top = top_of(gram)
            tops[block : block + 1, :] = top
            gain = CODE_TOP / top
            for sent_ref, (mask, first, end) in zip(sent_refs, messages):
                if first <= block < end:
                    row = pl.multiple_of((me ^ mask) * rows, rows)
                    place = slice((block - first) * rows, (block - first + 1) * rows)
                    sent_ref[place, :] = encode(whole[offset, pl.ds(row, rows), :] * gain)
    for sent_ref, (_, first, end) in zip(sent_refs, messages):
        sent_ref[(end - first) * rows :, :] = tops[
            first : first + scale_rows(first, end), :
        ].astype(jnp.bfloat16)


def add_group(messages, rows, own_ref, sent_refs, tops_refs, step):
    for block in range(step * GROUP, (step + 1) * GROUP):
        total = own_ref[block]
        for (_, first, end), sent_ref, tops in zip(messages, sent_refs, tops_refs):
            if first <= block < end:
                at = block - first
                values = decode(sent_ref[at * rows : (at + 1) * rows, :])
                total = total + values * tops[at : at + 1, :]
        yield block, total


def load_tops(messages, rows, sent_refs, tops_refs):
    for (_, first, end), sent_ref, tops in zip(messages, sent_refs, tops_refs):
        tops[...] = sent_ref[(end - first) * rows :, :].astype(jnp.float32) * (1.0 / CODE_TOP)


def add_kernel(messages, own_ref, *refs):
    sent_refs, sum_ref, tops_refs = refs[: len(messages)], refs[len(messages)], refs[len(messages) + 1 :]
    blocks, rows, _ = own_ref.shape
    load_tops(messages, rows, sent_refs, tops_refs)
    for step in range(blocks // GROUP):
        for block, total in add_group(messages, rows, own_ref, sent_refs, tops_refs, step):
            sum_ref[block] = total


def relay_kernel(message, far_ref, relayed_ref, sent_ref, relayed_tops, tops):
    messages = (message,)
    blocks, rows, _ = far_ref.shape
    load_tops(messages, rows, (relayed_ref,), (relayed_tops,))
    tops[...] = jnp.zeros_like(tops)
    for step in range(blocks // GROUP):
        for block, total in add_group(
            messages, rows, far_ref, (relayed_ref,), (relayed_tops,), step
        ):
            top = top_of(total)
            tops[block : block + 1, :] = top
            sent_ref[block * rows : (block + 1) * rows, :] = encode(total * (CODE_TOP / top))
    sent_ref[blocks * rows :, :] = tops[...].astype(jnp.bfloat16)


def last_add_kernel(messages, own_ref, *refs):
    sent_refs, refs = refs[: len(messages)], refs[len(messages) :]
    act_ref, grad_ref, *tops_refs, sums, sems = refs
    blocks, rows, _ = own_ref.shape
    load_tops(messages, rows, sent_refs, tops_refs)
    copies = []
    for step in range(blocks // GROUP):
        for block, total in add_group(messages, rows, own_ref, sent_refs, tops_refs, step):
            sums[block] = total
        first = step * GROUP
        ref, at = act_ref, first
        if first >= act_ref.shape[0]:
            ref, at = grad_ref, first - act_ref.shape[0]
        copies.append(
            pltpu.make_async_copy(
                sums.at[pl.ds(first, GROUP)], ref.at[pl.ds(at, GROUP)], sems.at[step]
            )
        )
        copies[-1].start()
    for copy in copies:
        copy.wait()


def pairs_of(part, side, halves, act_ref, grad_ref):
    half = lax.rem(side + part, halves)
    for ref in (act_ref, grad_ref):
        count = ref.shape[1] // PAIR // halves
        for pair in range(count):
            yield ref, pl.multiple_of((half * count + pair) * PAIR, PAIR)


def eigen_kernel(part, halves, masks, pieces, scale, me_ref, side_ref, act_ref, grad_ref, *refs):
    *shard_refs, power_ref, sums_ref, basis_ref = refs
    me, side = me_ref[0], side_ref[0]
    rows = BLK // pieces
    done = 0
    if part:
        *shard_refs, done_ref = shard_refs
        done = done_ref.shape[0]
        sums_ref[:done] = done_ref[...]
    half = lax.rem(side + part, halves)
    act_half = act_ref.shape[1] // BLK // halves
    grad_half = grad_ref.shape[1] // BLK // halves
    basis_ref[...] = jnp.zeros_like(basis_ref)
    for mask, ref in zip(masks, shard_refs):
        whole = halves > 1 and ref.shape[0] == halves * (act_half + grad_half)
        for block in range(act_half + grad_half):
            at = block
            if whole and block < act_half:
                at = half * act_half + block
            elif whole:
                at = (halves - 1) * act_half + half * grad_half + block
            corner = block % 2
            row = pl.multiple_of(corner * BLK + (me ^ mask) * rows, rows)
            columns = slice(corner * BLK, (corner + 1) * BLK)
            basis_ref[block // 2, pl.ds(row, rows), columns] = ref[at]

    for pair, (ref, column) in enumerate(pairs_of(part, side, halves, act_ref, grad_ref)):
        projected = lax.dot_general(
            ref[:, pl.ds(column, PAIR)],
            basis_ref[pair],
            contract_inner,
            preferred_element_type=jnp.float32,
        )
        power = projected * projected
        power_ref[pair] = power
        sums = scale * jnp.sum(power, axis=0, keepdims=True)
        row = done + 2 * pair
        sums_ref[row : row + 1, :] = sums[:, :BLK]
        sums_ref[row + 1 : row + 2, :] = sums[:, BLK:]


def combine_kernel(halves, side_ref, *refs):
    *sums_refs, act_eigen_ref, grad_eigen_ref, eigen_ref, total_ref = refs
    side = side_ref[0]
    act_half, grad_half = act_eigen_ref.shape[0] // halves, grad_eigen_ref.shape[0] // halves
    eigen = sums_refs[0][...]
    for sums_ref in sums_refs[1:]:
        eigen = eigen + sums_ref[...]
    eigen_ref[...] = eigen
    act_total = jnp.zeros((1, BLK), jnp.float32)
    grad_total = jnp.zeros((1, BLK), jnp.float32)
    for part in range(halves):
        half = lax.rem(side + part, halves)
        first = part * (act_half + grad_half)
        act = eigen[first : first + act_half]
        grad = eigen[first + act_half : first + act_half + grad_half]
        act_total += jnp.sum(act, axis=0, keepdims=True)
        grad_total += jnp.sum(grad, axis=0, keepdims=True)
        act_eigen_ref[pl.ds(half * act_half, act_half), :] = act
        grad_eigen_ref[pl.ds(half * grad_half, grad_half), :] = grad
    total_ref[0:1, :] = act_total
    total_ref[1:2, :] = grad_total


def weight_kernel(halves, act_half, eigen_ref, *refs):
    *refs, weight_ref, inverse, act_sum, grad_sum = refs
    power_refs, total_refs = refs[:halves], refs[halves:]
    totals = total_refs[0][...]
    for total_ref in total_refs[1:]:
        totals = totals + total_ref[...]
    totals = jnp.sum(totals, axis=1, keepdims=True)
    blocks_half = eigen_ref.shape[0] // halves
    for part in range(halves):
        first = part * blocks_half
        act = slice(first, first + act_half)
        grad = slice(first + act_half, first + blocks_half)
        inverse[act] = 1.0 / (eigen_ref[act] + totals[0:1] * (damp_root / D))
        inverse[grad] = 1.0 / (eigen_ref[grad] + totals[1:2] * (damp_root / FF))
    tokens = act_sum.shape[0]

    @pl.loop(0, tokens // TILE)
    def _(tile):
        here = pl.ds(pl.multiple_of(tile * TILE, TILE), TILE)
        sums = [jnp.zeros((TILE, BLK), jnp.float32), jnp.zeros((TILE, BLK), jnp.float32)]
        for part, power_ref in enumerate(power_refs):
            for pair in range(power_ref.shape[0]):
                which = 0 if 2 * pair < act_half else 1
                for side in range(2):
                    row = part * blocks_half + 2 * pair + side
                    power = power_ref[pair, here, side * BLK : (side + 1) * BLK]
                    sums[which] += power * inverse[row : row + 1, :]
        act_sum[here, :], grad_sum[here, :] = sums

    ones = jnp.ones((8, BLK), jnp.float32)
    for index, total in enumerate((act_sum, grad_sum)):
        sums = lax.dot_general(
            ones,
            total[...],
            contract_lanes,
            precision=lax.Precision.HIGHEST,
            preferred_element_type=jnp.float32,
        )
        weight_ref[index : index + 1, :] = sums[0:1]


def score_kernel(*refs):
    *weight_refs, score_ref = refs
    weights = weight_refs[0][...]
    for weight_ref in weight_refs[1:]:
        weights = weights + weight_ref[...]
    score_ref[...] = weights[0:1] * weights[1:2] * (1.0 / (D * FF))


def swap(value, axis, mask):
    count = lax.axis_size(axis)
    return lax.ppermute(value, axis, [(i, i ^ mask) for i in range(count)])


def share(value, axis, direct):
    if not direct:
        return [lax.psum(value, axis)]
    return [value] + [swap(value, axis, mask) for mask in range(1, lax.axis_size(axis))]


def after(values, done):
    return list(lax.optimization_barrier((tuple(values), done))[0])


def local(activations, gradients, basis_act, basis_grad):
    tokens = activations.shape[0]
    act_blocks, grad_blocks = basis_act.shape[0], basis_grad.shape[0]
    blocks = act_blocks + grad_blocks
    dp, owners = lax.axis_size("dp"), lax.axis_size("owner")
    scale = 1.0 / (tokens * dp)
    direct = dp in (2, 4) and owners in (1, 2, 4)
    pieces = dp if direct else 1
    halves = 2 if pieces == 4 and lax.axis_size("groups") == 2 else 1
    rows = BLK // pieces
    me = jnp.full((1,), lax.axis_index("dp") if direct else 0, jnp.int32)
    side = jnp.full((1,), lax.axis_index("groups"), jnp.int32)
    macs = tokens * blocks * BLK * BLK
    input_bytes = 2 * tokens * blocks * BLK
    if direct:
        shards = call(
            pack_kernel,
            [bf16(blocks // part, rows, BLK) for part in range(1, halves + 1)],
            "pack_basis", 0, 2 * blocks * rows * BLK,
            [IN_SMEM, IN_HBM, IN_HBM], [pltpu.SemaphoreType.DMA((2 * halves,))],
        )(side, in_hbm(basis_act), in_hbm(basis_grad))
        near = [shards[0], swap(shards[0], "dp", 1)]
        far = {mask: swap(shards[-1], "dp", mask) for mask in range(pieces - 1, 1, -1)}
    else:
        near = [
            jnp.concatenate(
                [lax.all_gather(part, "dp", axis=1, tiled=True) for part in (basis_act, basis_grad)]
            )
        ]
        far = {}
    masks = [*range(len(near)), *far]

    message = bf16(blocks * rows + scale_rows(0, blocks), BLK)
    whole_range = (0, blocks)
    coded = {4: [(3, *whole_range), (1, *whole_range)], 2: [(1, *whole_range)], 1: []}[pieces]
    plain = 2 if pieces == 4 else 1
    act_here, grad_here, *grams = call(
        functools.partial(gram_kernel, pieces, coded, scale),
        [
            bf16(*activations.shape),
            bf16(*gradients.shape),
            *[f32(blocks, rows, BLK)] * plain,
            *[message] * len(coded),
        ],
        "partial_gram", 4 * macs, input_bytes,
        [IN_SMEM, IN_HBM, IN_HBM],
        [
            pltpu.VMEM((GROUP, BLK, BLK), jnp.float32),
            pltpu.VMEM((scale_rows(0, blocks), BLK), jnp.float32),
            pltpu.SemaphoreType.DMA((blocks // GROUP,)),
        ],
    )(me, in_hbm(activations), in_hbm(gradients))
    own = grams[0]
    sent = {message[0]: chunk for message, chunk in zip(coded, grams[plain:])}
    if not direct:
        own = lax.psum_scatter(own, "dp", scatter_dimension=1, tiled=True)
    if pieces == 4:
        middle = lax.ppermute(sent[3], "dp", [(1, 2), (2, 1)])
        relayed = lax.ppermute(sent[3], "dp", [(0, 1), (3, 2)])

    parts = [[*near, *far.values()]]
    if halves == 2:
        swapped = [swap(after([part], own)[0], "groups", 1) for part in far.values()]
        parts.append([*near, *swapped])
    powers, sums = [], []
    for part, shards in enumerate(parts):
        power, *sums = call(
            functools.partial(eigen_kernel, part, halves, masks, pieces, scale),
            [f32(blocks // halves // 2, tokens, PAIR), f32(blocks // halves * (part + 1), BLK)],
            "partial_eigen", 2 * macs // halves, input_bytes // halves,
            [IN_SMEM, IN_SMEM] + [IN_VMEM] * (2 + len(shards) + len(sums)),
            [pltpu.VMEM((blocks // halves // 2, PAIR, PAIR), jnp.bfloat16)],
        )(me, side, act_here, grad_here, *shards, *sums)
        powers.append(power)
    if pieces == 4:
        sent[2] = call(
            functools.partial(relay_kernel, coded[0]), message, "relay_chunk", 0, 12 * own.size,
            [IN_VMEM, IN_VMEM],
            [pltpu.VMEM((scale_rows(0, blocks), BLK), jnp.float32)] * 2,
        )(*after([grams[1], relayed], sums))
    sums = share(sums[0], "dp", direct)
    if pieces == 4:
        sums = after(sums, (middle, sent[2]))
    act_eigen, grad_eigen, eigen, totals = call(
        functools.partial(combine_kernel, halves),
        [f32(act_blocks, BLK), f32(grad_blocks, BLK), f32(blocks, BLK), f32(2, BLK)],
        "combine_eigen", 0, 4 * blocks * BLK * pieces, [IN_SMEM] + [IN_VMEM] * len(sums),
    )(side, *sums)
    arrived = {}
    sent.pop(3, None)
    for mask in sent:
        arrived[mask] = swap(after([sent[mask]], totals)[0], "dp", mask)
    totals = share(totals, "owner", direct)
    weights = call(
        functools.partial(weight_kernel, halves, act_blocks // halves),
        f32(2, tokens), "partial_weights", 0, 4 * tokens * blocks * BLK,
        [IN_VMEM] * (1 + halves + len(totals)),
        [
            pltpu.VMEM((blocks, BLK), jnp.float32),
            pltpu.VMEM((tokens, BLK), jnp.float32),
            pltpu.VMEM((tokens, BLK), jnp.float32),
        ],
    )(eigen, *powers, *totals)
    weights = share(weights, "owner", direct)

    def tops_of(count):
        return [pltpu.VMEM((scale_rows(0, blocks), BLK), jnp.float32)] * count

    if pieces == 4:
        own = call(
            functools.partial(add_kernel, [(None, 0, blocks)] * 2),
            f32(*own.shape), "add_chunks", 0, 16 * own.size, [IN_VMEM] * 3, tops_of(2),
        )(own, middle, arrived.pop(1))
        weights[1:] = after(weights[1:], own)
    token_scores = call(
        score_kernel, f32(1, tokens), "token_scores", 0, 8 * tokens, [IN_VMEM] * len(weights)
    )(*weights)
    chunks = list(arrived.values())
    if chunks:
        covariance = call(
            functools.partial(last_add_kernel, [(None, 0, blocks)] * len(chunks)),
            [f32(act_blocks, rows, BLK), f32(grad_blocks, rows, BLK)],
            "add_last_chunk", 0, 12 * own.size, [IN_VMEM] * (1 + len(chunks)),
            [
                *tops_of(len(chunks)),
                pltpu.VMEM(own.shape, jnp.float32),
                pltpu.SemaphoreType.DMA((blocks // GROUP,)),
            ],
            out_spec=[pl.BlockSpec(memory_space=pl.ANY)] * 2,
        )(own, *chunks)
    else:
        covariance = own[:act_blocks], own[act_blocks:]
    return (
        *covariance,
        act_eigen.reshape(-1),
        grad_eigen.reshape(-1),
        token_scores.reshape(-1),
    )


def solution(mesh):
    return jax.shard_map(
        local,
        mesh=mesh,
        in_specs=(
            P(("groups", "dp"), "owner"),
            P(("groups", "dp"), "owner"),
            P("owner", "dp", None),
            P("owner", "dp", None),
        ),
        out_specs=(
            P(("groups", "owner"), "dp", None),
            P(("groups", "owner"), "dp", None),
            P(("groups", "owner")),
            P(("groups", "owner")),
            P(("groups", "dp")),
        ),
        check_vma=False,
    )
```

```python
import functools

import jax
import jax.numpy as jnp
from jax import lax
from jax.experimental import pallas as pl
from jax.experimental.pallas import tpu as pltpu
from jax.sharding import PartitionSpec as P

D = 4096
FF = 14336
BLK = 128
PAIR = 2 * BLK
GROUP = 4
TILE = 64
VMEM_LIMIT = 24 * 1024 * 1024
CODE_TOP = 2.0**7.875
SMALLEST = 1e-36

damp_root = 0.31622776601683794
contract_rows = (((0,), (0,)), ((), ()))
contract_inner = (((1,), (0,)), ((), ()))
contract_lanes = (((1,), (1,)), ((), ()))

IN_VMEM = pl.BlockSpec(memory_space=pltpu.VMEM)
IN_SMEM = pl.BlockSpec(memory_space=pltpu.SMEM)
IN_HBM = pl.BlockSpec(memory_space=pltpu.HBM)


def scale_rows(first, end):
    return 16 * pl.cdiv(end - first, 16)


def call(
    kernel, out_shape, name, flops, bytes_accessed, in_specs, scratch_shapes=(),
    out_spec=None,
):
    return pl.pallas_call(
        kernel,
        out_shape=out_shape,
        in_specs=in_specs,
        out_specs=out_spec or jax.tree.map(lambda _: IN_VMEM, out_shape),
        scratch_shapes=scratch_shapes,
        compiler_params=pltpu.CompilerParams(vmem_limit_bytes=VMEM_LIMIT),
        cost_estimate=pl.CostEstimate(
            flops=flops, bytes_accessed=bytes_accessed, transcendentals=0
        ),
        name=name,
    )


def in_hbm(value):
    return pltpu.with_memory_space_constraint(value, pltpu.HBM)


def f32(*shape):
    return jax.ShapeDtypeStruct(shape, jnp.float32)


def bf16(*shape):
    return jax.ShapeDtypeStruct(shape, jnp.bfloat16)


def encode(values):
    power = values * values
    power = power * power
    power = power * power
    power = power * power
    return jnp.where(values < 0.0, -power, power).astype(jnp.bfloat16)


def top_of(values):
    top = jnp.maximum(jnp.max(jnp.abs(values), axis=0, keepdims=True), SMALLEST)
    return (top * (1.0 + 2.0**-8)).astype(jnp.bfloat16).astype(jnp.float32)


def decode(coded):
    coded = coded.astype(jnp.float32)
    root = jnp.abs(coded)
    for _ in range(4):
        root = lax.rsqrt(root)
    return jnp.where(coded > 0.0, root, jnp.where(coded < 0.0, -root, 0.0))


def pack_kernel(side_ref, act_ref, grad_ref, *refs):
    *out_refs, sems = refs
    side = side_ref[0]
    blocks = out_refs[0].shape[0]
    copies = []
    for out_ref in reversed(out_refs):
        halves = blocks // out_ref.shape[0]
        at = 0
        for ref in (act_ref, grad_ref):
            count = ref.shape[0] // halves
            copies.append(
                pltpu.make_async_copy(
                    ref.at[pl.ds(side * count if halves > 1 else 0, count)],
                    out_ref.at[pl.ds(at, count)],
                    sems.at[len(copies)],
                )
            )
            at += count
    for copy in copies:
        copy.start()
    for copy in copies:
        copy.wait()


def gram_kernel(pieces, messages, scale, me_ref, act_hbm, grad_hbm, act_ref, grad_ref, *refs):
    refs, (whole, tops, sems) = refs[:-3], refs[-3:]
    plain_refs, sent_refs = refs[: len(refs) - len(messages)], refs[len(refs) - len(messages) :]
    rows = BLK // pieces
    me = me_ref[0]
    steps = []
    for source, target in ((act_hbm, act_ref), (grad_hbm, grad_ref)):
        for first in range(0, source.shape[1], GROUP * BLK):
            columns = slice(first, first + GROUP * BLK)
            copy = pltpu.make_async_copy(
                source.at[:, columns], target.at[:, columns], sems.at[len(steps)]
            )
            copy.start()
            steps.append((target, columns, copy))
    tops[...] = jnp.zeros_like(tops)
    for step, (ref, columns, copy) in enumerate(steps):
        copy.wait()
        for offset in range(GROUP):
            block = step * GROUP + offset
            at = columns.start + offset * BLK
            values = ref[:, at : at + BLK]
            gram = scale * lax.dot_general(
                values, values, contract_rows, preferred_element_type=jnp.float32
            )
            if pieces == 1:
                plain_refs[0][block] = gram
                continue
            whole[offset] = gram
            for ref_at, mask in zip(plain_refs, (0, 2)):
                row = pl.multiple_of((me ^ mask) * rows, rows)
                ref_at[block] = whole[offset, pl.ds(row, rows), :]
            top = top_of(gram)
            tops[block : block + 1, :] = top
            gain = CODE_TOP / top
            for sent_ref, (mask, first, end) in zip(sent_refs, messages):
                if first <= block < end:
                    row = pl.multiple_of((me ^ mask) * rows, rows)
                    place = slice((block - first) * rows, (block - first + 1) * rows)
                    sent_ref[place, :] = encode(whole[offset, pl.ds(row, rows), :] * gain)
    for sent_ref, (_, first, end) in zip(sent_refs, messages):
        sent_ref[(end - first) * rows :, :] = tops[
            first : first + scale_rows(first, end), :
        ].astype(jnp.bfloat16)


def add_group(messages, rows, own_ref, sent_refs, tops_refs, step):
    for block in range(step * GROUP, (step + 1) * GROUP):
        total = own_ref[block]
        for (_, first, end), sent_ref, tops in zip(messages, sent_refs, tops_refs):
            if first <= block < end:
                at = block - first
                values = decode(sent_ref[at * rows : (at + 1) * rows, :])
                total = total + values * tops[at : at + 1, :]
        yield block, total


def load_tops(messages, rows, sent_refs, tops_refs):
    for (_, first, end), sent_ref, tops in zip(messages, sent_refs, tops_refs):
        tops[...] = sent_ref[(end - first) * rows :, :].astype(jnp.float32) * (1.0 / CODE_TOP)


def add_kernel(messages, own_ref, *refs):
    sent_refs, sum_ref, tops_refs = refs[: len(messages)], refs[len(messages)], refs[len(messages) + 1 :]
    blocks, rows, _ = own_ref.shape
    load_tops(messages, rows, sent_refs, tops_refs)
    for step in range(blocks // GROUP):
        for block, total in add_group(messages, rows, own_ref, sent_refs, tops_refs, step):
            sum_ref[block] = total


def relay_kernel(message, far_ref, relayed_ref, sent_ref, relayed_tops, tops):
    messages = (message,)
    blocks, rows, _ = far_ref.shape
    load_tops(messages, rows, (relayed_ref,), (relayed_tops,))
    tops[...] = jnp.zeros_like(tops)
    for step in range(blocks // GROUP):
        for block, total in add_group(
            messages, rows, far_ref, (relayed_ref,), (relayed_tops,), step
        ):
            top = top_of(total)
            tops[block : block + 1, :] = top
            sent_ref[block * rows : (block + 1) * rows, :] = encode(total * (CODE_TOP / top))
    sent_ref[blocks * rows :, :] = tops[...].astype(jnp.bfloat16)


def last_add_kernel(messages, own_ref, *refs):
    sent_refs, refs = refs[: len(messages)], refs[len(messages) :]
    act_ref, grad_ref, *tops_refs, sums, sems = refs
    blocks, rows, _ = own_ref.shape
    load_tops(messages, rows, sent_refs, tops_refs)
    copies = []
    for step in range(blocks // GROUP):
        for block, total in add_group(messages, rows, own_ref, sent_refs, tops_refs, step):
            sums[block] = total
        first = step * GROUP
        ref, at = act_ref, first
        if first >= act_ref.shape[0]:
            ref, at = grad_ref, first - act_ref.shape[0]
        copies.append(
            pltpu.make_async_copy(
                sums.at[pl.ds(first, GROUP)], ref.at[pl.ds(at, GROUP)], sems.at[step]
            )
        )
        copies[-1].start()
    for copy in copies:
        copy.wait()


def pairs_of(part, side, halves, act_ref, grad_ref):
    half = lax.rem(side + part, halves)
    for ref in (act_ref, grad_ref):
        count = ref.shape[1] // PAIR // halves
        for pair in range(count):
            yield ref, pl.multiple_of((half * count + pair) * PAIR, PAIR)


def eigen_kernel(part, halves, masks, pieces, scale, me_ref, side_ref, act_ref, grad_ref, *refs):
    *shard_refs, power_ref, sums_ref, basis_ref = refs
    me, side = me_ref[0], side_ref[0]
    rows = BLK // pieces
    done = 0
    if part:
        *shard_refs, done_ref = shard_refs
        done = done_ref.shape[0]
        sums_ref[:done] = done_ref[...]
    half = lax.rem(side + part, halves)
    act_half = act_ref.shape[1] // BLK // halves
    grad_half = grad_ref.shape[1] // BLK // halves
    basis_ref[...] = jnp.zeros_like(basis_ref)
    for mask, ref in zip(masks, shard_refs):
        whole = halves > 1 and ref.shape[0] == halves * (act_half + grad_half)
        for block in range(act_half + grad_half):
            at = block
            if whole and block < act_half:
                at = half * act_half + block
            elif whole:
                at = (halves - 1) * act_half + half * grad_half + block
            corner = block % 2
            row = pl.multiple_of(corner * BLK + (me ^ mask) * rows, rows)
            columns = slice(corner * BLK, (corner + 1) * BLK)
            basis_ref[block // 2, pl.ds(row, rows), columns] = ref[at]

    for pair, (ref, column) in enumerate(pairs_of(part, side, halves, act_ref, grad_ref)):
        projected = lax.dot_general(
            ref[:, pl.ds(column, PAIR)],
            basis_ref[pair],
            contract_inner,
            preferred_element_type=jnp.float32,
        )
        power = projected * projected
        power_ref[pair] = power
        sums = scale * jnp.sum(power, axis=0, keepdims=True)
        row = done + 2 * pair
        sums_ref[row : row + 1, :] = sums[:, :BLK]
        sums_ref[row + 1 : row + 2, :] = sums[:, BLK:]


def pair_kernel(left_ref, right_ref, sum_ref):
    sum_ref[...] = left_ref[...] + right_ref[...]


def combine_kernel(halves, side_ref, *refs):
    *sums_refs, act_eigen_ref, grad_eigen_ref, eigen_ref, total_ref = refs
    side = side_ref[0]
    act_half, grad_half = act_eigen_ref.shape[0] // halves, grad_eigen_ref.shape[0] // halves
    eigen = sums_refs[0][...]
    for sums_ref in sums_refs[1:]:
        eigen = eigen + sums_ref[...]
    eigen_ref[...] = eigen
    act_total = jnp.zeros((1, BLK), jnp.float32)
    grad_total = jnp.zeros((1, BLK), jnp.float32)
    for part in range(halves):
        half = lax.rem(side + part, halves)
        first = part * (act_half + grad_half)
        act = eigen[first : first + act_half]
        grad = eigen[first + act_half : first + act_half + grad_half]
        act_total += jnp.sum(act, axis=0, keepdims=True)
        grad_total += jnp.sum(grad, axis=0, keepdims=True)
        act_eigen_ref[pl.ds(half * act_half, act_half), :] = act
        grad_eigen_ref[pl.ds(half * grad_half, grad_half), :] = grad
    total_ref[0:1, :] = act_total
    total_ref[1:2, :] = grad_total


def weight_kernel(halves, act_half, eigen_ref, *refs):
    *refs, weight_ref, inverse, act_sum, grad_sum = refs
    power_refs, total_refs = refs[:halves], refs[halves:]
    totals = total_refs[0][...]
    for total_ref in total_refs[1:]:
        totals = totals + total_ref[...]
    totals = jnp.sum(totals, axis=1, keepdims=True)
    blocks_half = eigen_ref.shape[0] // halves
    for part in range(halves):
        first = part * blocks_half
        act = slice(first, first + act_half)
        grad = slice(first + act_half, first + blocks_half)
        inverse[act] = 1.0 / (eigen_ref[act] + totals[0:1] * (damp_root / D))
        inverse[grad] = 1.0 / (eigen_ref[grad] + totals[1:2] * (damp_root / FF))
    tokens = act_sum.shape[0]

    @pl.loop(0, tokens // TILE)
    def _(tile):
        here = pl.ds(pl.multiple_of(tile * TILE, TILE), TILE)
        sums = [jnp.zeros((TILE, BLK), jnp.float32), jnp.zeros((TILE, BLK), jnp.float32)]
        for part, power_ref in enumerate(power_refs):
            for pair in range(power_ref.shape[0]):
                which = 0 if 2 * pair < act_half else 1
                for side in range(2):
                    row = part * blocks_half + 2 * pair + side
                    power = power_ref[pair, here, side * BLK : (side + 1) * BLK]
                    sums[which] += power * inverse[row : row + 1, :]
        act_sum[here, :], grad_sum[here, :] = sums

    ones = jnp.ones((8, BLK), jnp.float32)
    for index, total in enumerate((act_sum, grad_sum)):
        sums = lax.dot_general(
            ones,
            total[...],
            contract_lanes,
            precision=lax.Precision.HIGHEST,
            preferred_element_type=jnp.float32,
        )
        weight_ref[index : index + 1, :] = sums[0:1]


def score_kernel(*refs):
    *weight_refs, score_ref = refs
    weights = weight_refs[0][...]
    for weight_ref in weight_refs[1:]:
        weights = weights + weight_ref[...]
    score_ref[...] = weights[0:1] * weights[1:2] * (1.0 / (D * FF))


def swap(value, axis, mask):
    count = lax.axis_size(axis)
    return lax.ppermute(value, axis, [(i, i ^ mask) for i in range(count)])


def share(value, axis, direct):
    if not direct:
        return [lax.psum(value, axis)]
    return [value] + [swap(value, axis, mask) for mask in range(1, lax.axis_size(axis))]


def after(values, done):
    return list(lax.optimization_barrier((tuple(values), done))[0])


def local(activations, gradients, basis_act, basis_grad):
    tokens = activations.shape[0]
    act_blocks, grad_blocks = basis_act.shape[0], basis_grad.shape[0]
    blocks = act_blocks + grad_blocks
    dp, owners = lax.axis_size("dp"), lax.axis_size("owner")
    scale = 1.0 / (tokens * dp)
    direct = dp in (2, 4) and owners in (1, 2, 4)
    pieces = dp if direct else 1
    halves = 2 if pieces == 4 and lax.axis_size("groups") == 2 else 1
    rows = BLK // pieces
    me = jnp.full((1,), lax.axis_index("dp") if direct else 0, jnp.int32)
    side = jnp.full((1,), lax.axis_index("groups"), jnp.int32)
    macs = tokens * blocks * BLK * BLK
    input_bytes = 2 * tokens * blocks * BLK
    if direct:
        shards = call(
            pack_kernel,
            [bf16(blocks // part, rows, BLK) for part in range(1, halves + 1)],
            "pack_basis", 0, 2 * blocks * rows * BLK,
            [IN_SMEM, IN_HBM, IN_HBM], [pltpu.SemaphoreType.DMA((2 * halves,))],
        )(side, in_hbm(basis_act), in_hbm(basis_grad))
        near = [shards[0], swap(shards[0], "dp", 1)]
        far = {mask: swap(shards[-1], "dp", mask) for mask in range(pieces - 1, 1, -1)}
    else:
        near = [
            jnp.concatenate(
                [lax.all_gather(part, "dp", axis=1, tiled=True) for part in (basis_act, basis_grad)]
            )
        ]
        far = {}
    masks = [*range(len(near)), *far]

    message = bf16(blocks * rows + scale_rows(0, blocks), BLK)
    whole_range = (0, blocks)
    coded = {4: [(3, *whole_range), (1, *whole_range)], 2: [(1, *whole_range)], 1: []}[pieces]
    plain = 2 if pieces == 4 else 1
    act_here, grad_here, *grams = call(
        functools.partial(gram_kernel, pieces, coded, scale),
        [
            bf16(*activations.shape),
            bf16(*gradients.shape),
            *[f32(blocks, rows, BLK)] * plain,
            *[message] * len(coded),
        ],
        "partial_gram", 4 * macs, input_bytes,
        [IN_SMEM, IN_HBM, IN_HBM],
        [
            pltpu.VMEM((GROUP, BLK, BLK), jnp.float32),
            pltpu.VMEM((scale_rows(0, blocks), BLK), jnp.float32),
            pltpu.SemaphoreType.DMA((blocks // GROUP,)),
        ],
    )(me, in_hbm(activations), in_hbm(gradients))
    own = grams[0]
    sent = {message[0]: chunk for message, chunk in zip(coded, grams[plain:])}
    if not direct:
        own = lax.psum_scatter(own, "dp", scatter_dimension=1, tiled=True)
    if pieces == 4:
        middle = lax.ppermute(sent[3], "dp", [(1, 2), (2, 1)])
        relayed = lax.ppermute(sent[3], "dp", [(0, 1), (3, 2)])

    parts = [[*near, *far.values()]]
    if halves == 2:
        swapped = [swap(after([part], own)[0], "groups", 1) for part in far.values()]
        parts.append([*near, *swapped])
    powers, sums = [], []
    for part, shards in enumerate(parts):
        power, *sums = call(
            functools.partial(eigen_kernel, part, halves, masks, pieces, scale),
            [f32(blocks // halves // 2, tokens, PAIR), f32(blocks // halves * (part + 1), BLK)],
            "partial_eigen", 2 * macs // halves, input_bytes // halves,
            [IN_SMEM, IN_SMEM] + [IN_VMEM] * (2 + len(shards) + len(sums)),
            [pltpu.VMEM((blocks // halves // 2, PAIR, PAIR), jnp.bfloat16)],
        )(me, side, act_here, grad_here, *shards, *sums)
        powers.append(power)
    if pieces == 4:
        sent[2] = call(
            functools.partial(relay_kernel, coded[0]), message, "relay_chunk", 0, 12 * own.size,
            [IN_VMEM, IN_VMEM],
            [pltpu.VMEM((scale_rows(0, blocks), BLK), jnp.float32)] * 2,
        )(*after([grams[1], relayed], sums))
    if pieces == 4:
        pair = call(
            pair_kernel, f32(blocks, BLK), "pair_eigen", 0, 12 * blocks * BLK, [IN_VMEM] * 2
        )(sums[0], swap(sums[0], "dp", 1))
        sums = [pair, swap(pair, "dp", 2)]
    else:
        sums = share(sums[0], "dp", direct)
    if pieces == 4:
        sums = after(sums, (middle, sent[2]))
    act_eigen, grad_eigen, eigen, totals = call(
        functools.partial(combine_kernel, halves),
        [f32(act_blocks, BLK), f32(grad_blocks, BLK), f32(blocks, BLK), f32(2, BLK)],
        "combine_eigen", 0, 4 * blocks * BLK * pieces, [IN_SMEM] + [IN_VMEM] * len(sums),
    )(side, *sums)
    arrived = {}
    sent.pop(3, None)
    for mask in sent:
        arrived[mask] = swap(after([sent[mask]], totals)[0], "dp", mask)
    totals = share(totals, "owner", direct)
    weights = call(
        functools.partial(weight_kernel, halves, act_blocks // halves),
        f32(2, tokens), "partial_weights", 0, 4 * tokens * blocks * BLK,
        [IN_VMEM] * (1 + halves + len(totals)),
        [
            pltpu.VMEM((blocks, BLK), jnp.float32),
            pltpu.VMEM((tokens, BLK), jnp.float32),
            pltpu.VMEM((tokens, BLK), jnp.float32),
        ],
    )(eigen, *powers, *totals)
    weights = share(weights, "owner", direct)

    def tops_of(count):
        return [pltpu.VMEM((scale_rows(0, blocks), BLK), jnp.float32)] * count

    if pieces == 4:
        own = call(
            functools.partial(add_kernel, [(None, 0, blocks)] * 2),
            f32(*own.shape), "add_chunks", 0, 16 * own.size, [IN_VMEM] * 3, tops_of(2),
        )(own, middle, arrived.pop(1))
        weights[1:] = after(weights[1:], own)
    token_scores = call(
        score_kernel, f32(1, tokens), "token_scores", 0, 8 * tokens, [IN_VMEM] * len(weights)
    )(*weights)
    chunks = list(arrived.values())
    if chunks:
        covariance = call(
            functools.partial(last_add_kernel, [(None, 0, blocks)] * len(chunks)),
            [f32(act_blocks, rows, BLK), f32(grad_blocks, rows, BLK)],
            "add_last_chunk", 0, 12 * own.size, [IN_VMEM] * (1 + len(chunks)),
            [
                *tops_of(len(chunks)),
                pltpu.VMEM(own.shape, jnp.float32),
                pltpu.SemaphoreType.DMA((blocks // GROUP,)),
            ],
            out_spec=[pl.BlockSpec(memory_space=pl.ANY)] * 2,
        )(own, *chunks)
    else:
        covariance = own[:act_blocks], own[act_blocks:]
    return (
        *covariance,
        act_eigen.reshape(-1),
        grad_eigen.reshape(-1),
        token_scores.reshape(-1),
    )


def solution(mesh):
    return jax.shard_map(
        local,
        mesh=mesh,
        in_specs=(
            P(("groups", "dp"), "owner"),
            P(("groups", "dp"), "owner"),
            P("owner", "dp", None),
            P("owner", "dp", None),
        ),
        out_specs=(
            P(("groups", "owner"), "dp", None),
            P(("groups", "owner"), "dp", None),
            P(("groups", "owner")),
            P(("groups", "owner")),
            P(("groups", "dp")),
        ),
        check_vma=False,
    )
```

```python
import functools

import jax
import jax.numpy as jnp
from jax import lax
from jax.experimental import pallas as pl
from jax.experimental.pallas import tpu as pltpu
from jax.sharding import PartitionSpec as P

D = 4096
FF = 14336
BLK = 128
PAIR = 2 * BLK
GROUP = 4
TILE = 64
VMEM_LIMIT = 24 * 1024 * 1024
CODE_TOP = 2.0**7.875
SMALLEST = 1e-36

damp_root = 0.31622776601683794
contract_rows = (((0,), (0,)), ((), ()))
contract_inner = (((1,), (0,)), ((), ()))
contract_lanes = (((1,), (1,)), ((), ()))

IN_VMEM = pl.BlockSpec(memory_space=pltpu.VMEM)
IN_SMEM = pl.BlockSpec(memory_space=pltpu.SMEM)
IN_HBM = pl.BlockSpec(memory_space=pltpu.HBM)


def scale_rows(first, end):
    return 16 * pl.cdiv(end - first, 16)


def call(
    kernel, out_shape, name, flops, bytes_accessed, in_specs, scratch_shapes=(),
    out_spec=None,
):
    return pl.pallas_call(
        kernel,
        out_shape=out_shape,
        in_specs=in_specs,
        out_specs=out_spec or jax.tree.map(lambda _: IN_VMEM, out_shape),
        scratch_shapes=scratch_shapes,
        compiler_params=pltpu.CompilerParams(vmem_limit_bytes=VMEM_LIMIT),
        cost_estimate=pl.CostEstimate(
            flops=flops, bytes_accessed=bytes_accessed, transcendentals=0
        ),
        name=name,
    )


def in_hbm(value):
    return pltpu.with_memory_space_constraint(value, pltpu.HBM)


def f32(*shape):
    return jax.ShapeDtypeStruct(shape, jnp.float32)


def bf16(*shape):
    return jax.ShapeDtypeStruct(shape, jnp.bfloat16)


def encode(values):
    power = values * values
    power = power * power
    power = power * power
    power = power * power
    return jnp.where(values < 0.0, -power, power).astype(jnp.bfloat16)


def top_of(values):
    top = jnp.maximum(jnp.max(jnp.abs(values), axis=0, keepdims=True), SMALLEST)
    return (top * (1.0 + 2.0**-8)).astype(jnp.bfloat16).astype(jnp.float32)


def decode(coded):
    coded = coded.astype(jnp.float32)
    root = jnp.abs(coded)
    for _ in range(4):
        root = lax.rsqrt(root)
    return jnp.where(coded > 0.0, root, jnp.where(coded < 0.0, -root, 0.0))


def pack_kernel(side_ref, act_ref, grad_ref, *refs):
    *out_refs, sems = refs
    side = side_ref[0]
    blocks = out_refs[0].shape[0]
    copies = []
    for out_ref in reversed(out_refs):
        halves = blocks // out_ref.shape[0]
        at = 0
        for ref in (act_ref, grad_ref):
            count = ref.shape[0] // halves
            copies.append(
                pltpu.make_async_copy(
                    ref.at[pl.ds(side * count if halves > 1 else 0, count)],
                    out_ref.at[pl.ds(at, count)],
                    sems.at[len(copies)],
                )
            )
            at += count
    for copy in copies:
        copy.start()
    for copy in copies:
        copy.wait()


def gram_kernel(pieces, messages, scale, me_ref, act_hbm, grad_hbm, act_ref, grad_ref, *refs):
    refs, (whole, tops, sems) = refs[:-3], refs[-3:]
    plain_refs, sent_refs = refs[: len(refs) - len(messages)], refs[len(refs) - len(messages) :]
    rows = BLK // pieces
    me = me_ref[0]
    steps = []
    for source, target in ((act_hbm, act_ref), (grad_hbm, grad_ref)):
        for first in range(0, source.shape[1], GROUP * BLK):
            columns = slice(first, first + GROUP * BLK)
            copy = pltpu.make_async_copy(
                source.at[:, columns], target.at[:, columns], sems.at[len(steps)]
            )
            copy.start()
            steps.append((target, columns, copy))
    tops[...] = jnp.zeros_like(tops)
    for step, (ref, columns, copy) in enumerate(steps):
        copy.wait()
        for offset in range(GROUP):
            block = step * GROUP + offset
            at = columns.start + offset * BLK
            values = ref[:, at : at + BLK]
            gram = scale * lax.dot_general(
                values, values, contract_rows, preferred_element_type=jnp.float32
            )
            if pieces == 1:
                plain_refs[0][block] = gram
                continue
            whole[offset] = gram
            for ref_at, mask in zip(plain_refs, (0, 2)):
                row = pl.multiple_of((me ^ mask) * rows, rows)
                ref_at[block] = whole[offset, pl.ds(row, rows), :]
            top = top_of(gram)
            tops[block : block + 1, :] = top
            gain = CODE_TOP / top
            for sent_ref, (mask, first, end) in zip(sent_refs, messages):
                if first <= block < end:
                    row = pl.multiple_of((me ^ mask) * rows, rows)
                    place = slice((block - first) * rows, (block - first + 1) * rows)
                    sent_ref[place, :] = encode(whole[offset, pl.ds(row, rows), :] * gain)
    for sent_ref, (_, first, end) in zip(sent_refs, messages):
        sent_ref[(end - first) * rows :, :] = tops[
            first : first + scale_rows(first, end), :
        ].astype(jnp.bfloat16)


def add_group(messages, rows, own_ref, sent_refs, tops_refs, step):
    for block in range(step * GROUP, (step + 1) * GROUP):
        total = own_ref[block]
        for (_, first, end), sent_ref, tops in zip(messages, sent_refs, tops_refs):
            if first <= block < end:
                at = block - first
                values = decode(sent_ref[at * rows : (at + 1) * rows, :])
                total = total + values * tops[at : at + 1, :]
        yield block, total


def load_tops(messages, rows, sent_refs, tops_refs):
    for (_, first, end), sent_ref, tops in zip(messages, sent_refs, tops_refs):
        tops[...] = sent_ref[(end - first) * rows :, :].astype(jnp.float32) * (1.0 / CODE_TOP)


def add_kernel(messages, own_ref, *refs):
    sent_refs, sum_ref, tops_refs = refs[: len(messages)], refs[len(messages)], refs[len(messages) + 1 :]
    blocks, rows, _ = own_ref.shape
    load_tops(messages, rows, sent_refs, tops_refs)
    for step in range(blocks // GROUP):
        for block, total in add_group(messages, rows, own_ref, sent_refs, tops_refs, step):
            sum_ref[block] = total


def relay_kernel(message, far_ref, relayed_ref, sent_ref, relayed_tops, tops):
    messages = (message,)
    blocks, rows, _ = far_ref.shape
    load_tops(messages, rows, (relayed_ref,), (relayed_tops,))
    tops[...] = jnp.zeros_like(tops)
    for step in range(blocks // GROUP):
        for block, total in add_group(
            messages, rows, far_ref, (relayed_ref,), (relayed_tops,), step
        ):
            top = top_of(total)
            tops[block : block + 1, :] = top
            sent_ref[block * rows : (block + 1) * rows, :] = encode(total * (CODE_TOP / top))
    sent_ref[blocks * rows :, :] = tops[...].astype(jnp.bfloat16)


def last_add_kernel(messages, own_ref, *refs):
    sent_refs, refs = refs[: len(messages)], refs[len(messages) :]
    act_ref, grad_ref, *tops_refs, sums, sems = refs
    blocks, rows, _ = own_ref.shape
    load_tops(messages, rows, sent_refs, tops_refs)
    copies = []
    for step in range(blocks // GROUP):
        for block, total in add_group(messages, rows, own_ref, sent_refs, tops_refs, step):
            sums[block] = total
        first = step * GROUP
        ref, at = act_ref, first
        if first >= act_ref.shape[0]:
            ref, at = grad_ref, first - act_ref.shape[0]
        copies.append(
            pltpu.make_async_copy(
                sums.at[pl.ds(first, GROUP)], ref.at[pl.ds(at, GROUP)], sems.at[step]
            )
        )
        copies[-1].start()
    for copy in copies:
        copy.wait()


def pairs_of(part, side, halves, act_ref, grad_ref):
    half = lax.rem(side + part, halves)
    for ref in (act_ref, grad_ref):
        count = ref.shape[1] // PAIR // halves
        for pair in range(count):
            yield ref, pl.multiple_of((half * count + pair) * PAIR, PAIR)


def eigen_kernel(part, halves, masks, pieces, scale, me_ref, side_ref, act_ref, grad_ref, *refs):
    *shard_refs, power_ref, sums_ref, basis_ref = refs
    me, side = me_ref[0], side_ref[0]
    rows = BLK // pieces
    done = 0
    if part:
        *shard_refs, done_ref = shard_refs
        done = done_ref.shape[0]
        sums_ref[:done] = done_ref[...]
    half = lax.rem(side + part, halves)
    act_half = act_ref.shape[1] // BLK // halves
    grad_half = grad_ref.shape[1] // BLK // halves
    basis_ref[...] = jnp.zeros_like(basis_ref)
    for mask, ref in zip(masks, shard_refs):
        whole = halves > 1 and ref.shape[0] == halves * (act_half + grad_half)
        for block in range(act_half + grad_half):
            at = block
            if whole and block < act_half:
                at = half * act_half + block
            elif whole:
                at = (halves - 1) * act_half + half * grad_half + block
            corner = block % 2
            row = pl.multiple_of(corner * BLK + (me ^ mask) * rows, rows)
            columns = slice(corner * BLK, (corner + 1) * BLK)
            basis_ref[block // 2, pl.ds(row, rows), columns] = ref[at]

    for pair, (ref, column) in enumerate(pairs_of(part, side, halves, act_ref, grad_ref)):
        projected = lax.dot_general(
            ref[:, pl.ds(column, PAIR)],
            basis_ref[pair],
            contract_inner,
            preferred_element_type=jnp.float32,
        )
        power = projected * projected
        power_ref[pair] = power
        sums = scale * jnp.sum(power, axis=0, keepdims=True)
        row = done + 2 * pair
        sums_ref[row : row + 1, :] = sums[:, :BLK]
        sums_ref[row + 1 : row + 2, :] = sums[:, BLK:]


def combine_kernel(halves, side_ref, *refs):
    *sums_refs, act_eigen_ref, grad_eigen_ref, eigen_ref, total_ref = refs
    side = side_ref[0]
    act_half, grad_half = act_eigen_ref.shape[0] // halves, grad_eigen_ref.shape[0] // halves
    eigen = sums_refs[0][...]
    for sums_ref in sums_refs[1:]:
        eigen = eigen + sums_ref[...]
    eigen_ref[...] = eigen
    act_total = jnp.zeros((1, BLK), jnp.float32)
    grad_total = jnp.zeros((1, BLK), jnp.float32)
    for part in range(halves):
        half = lax.rem(side + part, halves)
        first = part * (act_half + grad_half)
        act = eigen[first : first + act_half]
        grad = eigen[first + act_half : first + act_half + grad_half]
        act_total += jnp.sum(act, axis=0, keepdims=True)
        grad_total += jnp.sum(grad, axis=0, keepdims=True)
        act_eigen_ref[pl.ds(half * act_half, act_half), :] = act
        grad_eigen_ref[pl.ds(half * grad_half, grad_half), :] = grad
    total_ref[0:1, :] = act_total
    total_ref[1:2, :] = grad_total


def weight_kernel(halves, act_half, eigen_ref, *refs):
    *refs, weight_ref, inverse, act_sum, grad_sum = refs
    power_refs, total_refs = refs[:halves], refs[halves:]
    totals = total_refs[0][...]
    for total_ref in total_refs[1:]:
        totals = totals + total_ref[...]
    totals = jnp.sum(totals, axis=1, keepdims=True)
    blocks_half = eigen_ref.shape[0] // halves
    for part in range(halves):
        first = part * blocks_half
        act = slice(first, first + act_half)
        grad = slice(first + act_half, first + blocks_half)
        inverse[act] = 1.0 / (eigen_ref[act] + totals[0:1] * (damp_root / D))
        inverse[grad] = 1.0 / (eigen_ref[grad] + totals[1:2] * (damp_root / FF))
    tokens = act_sum.shape[0]

    @pl.loop(0, tokens // TILE)
    def _(tile):
        here = pl.ds(pl.multiple_of(tile * TILE, TILE), TILE)
        sums = [jnp.zeros((TILE, BLK), jnp.float32), jnp.zeros((TILE, BLK), jnp.float32)]
        for part, power_ref in enumerate(power_refs):
            for pair in range(power_ref.shape[0]):
                which = 0 if 2 * pair < act_half else 1
                for side in range(2):
                    row = part * blocks_half + 2 * pair + side
                    power = power_ref[pair, here, side * BLK : (side + 1) * BLK]
                    sums[which] += power * inverse[row : row + 1, :]
        act_sum[here, :], grad_sum[here, :] = sums

    ones = jnp.ones((8, BLK), jnp.float32)
    for index, total in enumerate((act_sum, grad_sum)):
        sums = lax.dot_general(
            ones,
            total[...],
            contract_lanes,
            precision=lax.Precision.HIGHEST,
            preferred_element_type=jnp.float32,
        )
        weight_ref[index : index + 1, :] = sums[0:1]


def score_kernel(*refs):
    *weight_refs, score_ref = refs
    weights = weight_refs[0][...]
    for weight_ref in weight_refs[1:]:
        weights = weights + weight_ref[...]
    score_ref[...] = weights[0:1] * weights[1:2] * (1.0 / (D * FF))


def swap(value, axis, mask):
    count = lax.axis_size(axis)
    return lax.ppermute(value, axis, [(i, i ^ mask) for i in range(count)])


def share(value, axis, direct):
    if not direct:
        return [lax.psum(value, axis)]
    return [value] + [swap(value, axis, mask) for mask in reversed(range(1, lax.axis_size(axis)))]


def after(values, done):
    return list(lax.optimization_barrier((tuple(values), done))[0])


def local(activations, gradients, basis_act, basis_grad):
    tokens = activations.shape[0]
    act_blocks, grad_blocks = basis_act.shape[0], basis_grad.shape[0]
    blocks = act_blocks + grad_blocks
    dp, owners = lax.axis_size("dp"), lax.axis_size("owner")
    scale = 1.0 / (tokens * dp)
    direct = dp in (2, 4) and owners in (1, 2, 4)
    pieces = dp if direct else 1
    halves = 2 if pieces == 4 and lax.axis_size("groups") == 2 else 1
    rows = BLK // pieces
    me = jnp.full((1,), lax.axis_index("dp") if direct else 0, jnp.int32)
    side = jnp.full((1,), lax.axis_index("groups"), jnp.int32)
    macs = tokens * blocks * BLK * BLK
    input_bytes = 2 * tokens * blocks * BLK
    if direct:
        shards = call(
            pack_kernel,
            [bf16(blocks // part, rows, BLK) for part in range(1, halves + 1)],
            "pack_basis", 0, 2 * blocks * rows * BLK,
            [IN_SMEM, IN_HBM, IN_HBM], [pltpu.SemaphoreType.DMA((2 * halves,))],
        )(side, in_hbm(basis_act), in_hbm(basis_grad))
        near = [shards[0], swap(shards[0], "dp", 1)]
        far = {mask: swap(shards[-1], "dp", mask) for mask in range(pieces - 1, 1, -1)}
    else:
        near = [
            jnp.concatenate(
                [lax.all_gather(part, "dp", axis=1, tiled=True) for part in (basis_act, basis_grad)]
            )
        ]
        far = {}
    masks = [*range(len(near)), *far]

    message = bf16(blocks * rows + scale_rows(0, blocks), BLK)
    whole_range = (0, blocks)
    coded = {4: [(3, *whole_range), (1, *whole_range)], 2: [(1, *whole_range)], 1: []}[pieces]
    plain = 2 if pieces == 4 else 1
    act_here, grad_here, *grams = call(
        functools.partial(gram_kernel, pieces, coded, scale),
        [
            bf16(*activations.shape),
            bf16(*gradients.shape),
            *[f32(blocks, rows, BLK)] * plain,
            *[message] * len(coded),
        ],
        "partial_gram", 4 * macs, input_bytes,
        [IN_SMEM, IN_HBM, IN_HBM],
        [
            pltpu.VMEM((GROUP, BLK, BLK), jnp.float32),
            pltpu.VMEM((scale_rows(0, blocks), BLK), jnp.float32),
            pltpu.SemaphoreType.DMA((blocks // GROUP,)),
        ],
    )(me, in_hbm(activations), in_hbm(gradients))
    own = grams[0]
    sent = {message[0]: chunk for message, chunk in zip(coded, grams[plain:])}
    if not direct:
        own = lax.psum_scatter(own, "dp", scatter_dimension=1, tiled=True)
    if pieces == 4:
        middle = lax.ppermute(sent[3], "dp", [(1, 2), (2, 1)])
        relayed = lax.ppermute(sent[3], "dp", [(0, 1), (3, 2)])

    parts = [[*near, *far.values()]]
    if halves == 2:
        swapped = [swap(after([part], own)[0], "groups", 1) for part in far.values()]
        parts.append([*near, *swapped])
    powers, sums = [], []
    for part, shards in enumerate(parts):
        power, *sums = call(
            functools.partial(eigen_kernel, part, halves, masks, pieces, scale),
            [f32(blocks // halves // 2, tokens, PAIR), f32(blocks // halves * (part + 1), BLK)],
            "partial_eigen", 2 * macs // halves, input_bytes // halves,
            [IN_SMEM, IN_SMEM] + [IN_VMEM] * (2 + len(shards) + len(sums)),
            [pltpu.VMEM((blocks // halves // 2, PAIR, PAIR), jnp.bfloat16)],
        )(me, side, act_here, grad_here, *shards, *sums)
        powers.append(power)
    if pieces == 4:
        sent[2] = call(
            functools.partial(relay_kernel, coded[0]), message, "relay_chunk", 0, 12 * own.size,
            [IN_VMEM, IN_VMEM],
            [pltpu.VMEM((scale_rows(0, blocks), BLK), jnp.float32)] * 2,
        )(*after([grams[1], relayed], sums))
    sums = share(sums[0], "dp", direct)
    if pieces == 4:
        sums = after(sums, (middle, sent[2]))
    act_eigen, grad_eigen, eigen, totals = call(
        functools.partial(combine_kernel, halves),
        [f32(act_blocks, BLK), f32(grad_blocks, BLK), f32(blocks, BLK), f32(2, BLK)],
        "combine_eigen", 0, 4 * blocks * BLK * pieces, [IN_SMEM] + [IN_VMEM] * len(sums),
    )(side, *sums)
    arrived = {}
    sent.pop(3, None)
    for mask in sent:
        arrived[mask] = swap(after([sent[mask]], totals)[0], "dp", mask)
    totals = share(totals, "owner", direct)
    weights = call(
        functools.partial(weight_kernel, halves, act_blocks // halves),
        f32(2, tokens), "partial_weights", 0, 4 * tokens * blocks * BLK,
        [IN_VMEM] * (1 + halves + len(totals)),
        [
            pltpu.VMEM((blocks, BLK), jnp.float32),
            pltpu.VMEM((tokens, BLK), jnp.float32),
            pltpu.VMEM((tokens, BLK), jnp.float32),
        ],
    )(eigen, *powers, *totals)
    weights = share(weights, "owner", direct)

    def tops_of(count):
        return [pltpu.VMEM((scale_rows(0, blocks), BLK), jnp.float32)] * count

    if pieces == 4:
        own = call(
            functools.partial(add_kernel, [(None, 0, blocks)] * 2),
            f32(*own.shape), "add_chunks", 0, 16 * own.size, [IN_VMEM] * 3, tops_of(2),
        )(own, middle, arrived.pop(1))
        weights[1:] = after(weights[1:], own)
    token_scores = call(
        score_kernel, f32(1, tokens), "token_scores", 0, 8 * tokens, [IN_VMEM] * len(weights)
    )(*weights)
    chunks = list(arrived.values())
    if chunks:
        covariance = call(
            functools.partial(last_add_kernel, [(None, 0, blocks)] * len(chunks)),
            [f32(act_blocks, rows, BLK), f32(grad_blocks, rows, BLK)],
            "add_last_chunk", 0, 12 * own.size, [IN_VMEM] * (1 + len(chunks)),
            [
                *tops_of(len(chunks)),
                pltpu.VMEM(own.shape, jnp.float32),
                pltpu.SemaphoreType.DMA((blocks // GROUP,)),
            ],
            out_spec=[pl.BlockSpec(memory_space=pl.ANY)] * 2,
        )(own, *chunks)
    else:
        covariance = own[:act_blocks], own[act_blocks:]
    return (
        *covariance,
        act_eigen.reshape(-1),
        grad_eigen.reshape(-1),
        token_scores.reshape(-1),
    )


def solution(mesh):
    return jax.shard_map(
        local,
        mesh=mesh,
        in_specs=(
            P(("groups", "dp"), "owner"),
            P(("groups", "dp"), "owner"),
            P("owner", "dp", None),
            P("owner", "dp", None),
        ),
        out_specs=(
            P(("groups", "owner"), "dp", None),
            P(("groups", "owner"), "dp", None),
            P(("groups", "owner")),
            P(("groups", "owner")),
            P(("groups", "dp")),
        ),
        check_vma=False,
    )
```

```python
import functools

import jax
import jax.numpy as jnp
from jax import lax
from jax.experimental import pallas as pl
from jax.experimental.pallas import tpu as pltpu
from jax.sharding import PartitionSpec as P

D = 4096
FF = 14336
BLK = 128
PAIR = 2 * BLK
GROUP = 4
TILE = 64
VMEM_LIMIT = 24 * 1024 * 1024
CODE_TOP = 2.0**7.875
SMALLEST = 1e-36

damp_root = 0.31622776601683794
contract_rows = (((0,), (0,)), ((), ()))
contract_inner = (((1,), (0,)), ((), ()))
contract_lanes = (((1,), (1,)), ((), ()))

IN_VMEM = pl.BlockSpec(memory_space=pltpu.VMEM)
IN_SMEM = pl.BlockSpec(memory_space=pltpu.SMEM)
IN_HBM = pl.BlockSpec(memory_space=pltpu.HBM)


def scale_rows(blocks):
    return 16 * pl.cdiv(blocks, 16)


def call(
    kernel, out_shape, name, flops, bytes_accessed, in_specs, scratch_shapes=(),
    out_spec=None,
):
    return pl.pallas_call(
        kernel,
        out_shape=out_shape,
        in_specs=in_specs,
        out_specs=out_spec or jax.tree.map(lambda _: IN_VMEM, out_shape),
        scratch_shapes=scratch_shapes,
        compiler_params=pltpu.CompilerParams(vmem_limit_bytes=VMEM_LIMIT),
        cost_estimate=pl.CostEstimate(
            flops=flops, bytes_accessed=bytes_accessed, transcendentals=0
        ),
        name=name,
    )


def in_hbm(value):
    return pltpu.with_memory_space_constraint(value, pltpu.HBM)


def f32(*shape):
    return jax.ShapeDtypeStruct(shape, jnp.float32)


def bf16(*shape):
    return jax.ShapeDtypeStruct(shape, jnp.bfloat16)


def encode(values):
    power = values * values
    power = power * power
    power = power * power
    power = power * power
    return jnp.where(values < 0.0, -power, power).astype(jnp.bfloat16)


def top_of(values):
    top = jnp.maximum(jnp.max(jnp.abs(values), axis=0, keepdims=True), SMALLEST)
    return (top * (1.0 + 2.0**-8)).astype(jnp.bfloat16).astype(jnp.float32)


def decode(coded):
    coded = coded.astype(jnp.float32)
    root = jnp.abs(coded)
    for _ in range(4):
        root = lax.rsqrt(root)
    return jnp.where(coded > 0.0, root, jnp.where(coded < 0.0, -root, 0.0))


def pack_kernel(side_ref, act_ref, grad_ref, *refs):
    *out_refs, sems = refs
    side = side_ref[0]
    blocks = out_refs[0].shape[0]
    copies = []
    for out_ref in reversed(out_refs):
        halves = blocks // out_ref.shape[0]
        at = 0
        for ref in (act_ref, grad_ref):
            count = ref.shape[0] // halves
            copies.append(
                pltpu.make_async_copy(
                    ref.at[pl.ds(side * count if halves > 1 else 0, count)],
                    out_ref.at[pl.ds(at, count)],
                    sems.at[len(copies)],
                )
            )
            at += count
    for copy in copies:
        copy.start()
    for copy in copies:
        copy.wait()


def pick(me, masks):
    ends, middle = masks
    return me ^ ends if ends == middle else jnp.where(in_middle(me), me ^ middle, me ^ ends)


def in_middle(me):
    return jnp.logical_or(me == 1, me == 2)


def gram_kernel(pieces, plain, coded, scale, me_ref, act_hbm, grad_hbm, act_ref, grad_ref, *refs):
    refs, (whole, tops, sems) = refs[:-3], refs[-3:]
    plain_refs, sent_refs = refs[: len(plain)], refs[len(plain) :]
    rows = BLK // pieces
    me = me_ref[0]

    def first_row(masks):
        return pl.multiple_of(pick(me, masks) * rows, rows)

    steps = []
    for source, target in ((act_hbm, act_ref), (grad_hbm, grad_ref)):
        for first in range(0, source.shape[1], GROUP * BLK):
            columns = slice(first, first + GROUP * BLK)
            copy = pltpu.make_async_copy(
                source.at[:, columns], target.at[:, columns], sems.at[len(steps)]
            )
            copy.start()
            steps.append((target, columns, copy))
    tops[...] = jnp.zeros_like(tops)
    for step, (ref, columns, copy) in enumerate(steps):
        copy.wait()
        for offset in range(GROUP):
            block = step * GROUP + offset
            at = columns.start + offset * BLK
            values = ref[:, at : at + BLK]
            gram = scale * lax.dot_general(
                values, values, contract_rows, preferred_element_type=jnp.float32
            )
            if pieces == 1:
                plain_refs[0][block] = gram
                continue
            whole[offset] = gram
            for plain_ref, masks in zip(plain_refs, plain):
                plain_ref[block] = whole[offset, pl.ds(first_row(masks), rows), :]
            top = top_of(gram)
            tops[block : block + 1, :] = top
            gain = CODE_TOP / top
            for sent_ref, masks in zip(sent_refs, coded):
                sent_ref[block * rows : (block + 1) * rows, :] = encode(
                    whole[offset, pl.ds(first_row(masks), rows), :] * gain
                )
    for sent_ref in sent_refs:
        sent_ref[len(steps) * GROUP * rows :, :] = tops[...].astype(jnp.bfloat16)


def add_group(own_ref, sent_refs, tops_refs, step):
    rows = own_ref.shape[1]
    for block in range(step * GROUP, (step + 1) * GROUP):
        total = own_ref[block]
        for sent_ref, tops in zip(sent_refs, tops_refs):
            values = decode(sent_ref[block * rows : (block + 1) * rows, :])
            total = total + values * tops[block : block + 1, :]
        yield block, total


def load_tops(own_ref, sent_ref, tops, weight=1.0):
    blocks, rows, _ = own_ref.shape
    tops[...] = sent_ref[blocks * rows :, :].astype(jnp.float32) * (weight / CODE_TOP)


def add_kernel(me_ref, own_ref, *refs):
    count = len(refs) // 2
    sent_refs, sum_ref, tops_refs = refs[:count], refs[count], refs[count + 1 :]
    ends = 1.0 - in_middle(me_ref[0]).astype(jnp.float32)
    for index, (sent_ref, tops) in enumerate(zip(sent_refs, tops_refs)):
        load_tops(own_ref, sent_ref, tops, ends if index == 0 else 1.0)
    for step in range(own_ref.shape[0] // GROUP):
        for block, total in add_group(own_ref, sent_refs, tops_refs, step):
            sum_ref[block] = total


def relay_kernel(me_ref, far_ref, nearest_ref, sent_ref, relayed_tops, tops):
    blocks, rows, _ = far_ref.shape
    load_tops(far_ref, nearest_ref, relayed_tops, in_middle(me_ref[0]).astype(jnp.float32))
    tops[...] = jnp.zeros_like(tops)
    for step in range(blocks // GROUP):
        for block, total in add_group(far_ref, (nearest_ref,), (relayed_tops,), step):
            top = top_of(total)
            tops[block : block + 1, :] = top
            sent_ref[block * rows : (block + 1) * rows, :] = encode(total * (CODE_TOP / top))
    sent_ref[blocks * rows :, :] = tops[...].astype(jnp.bfloat16)


def last_add_kernel(own_ref, sent_ref, act_ref, grad_ref, tops, sums, sems):
    load_tops(own_ref, sent_ref, tops)
    copies = []
    for step in range(own_ref.shape[0] // GROUP):
        for block, total in add_group(own_ref, (sent_ref,), (tops,), step):
            sums[block] = total
        first = step * GROUP
        ref, at = act_ref, first
        if first >= act_ref.shape[0]:
            ref, at = grad_ref, first - act_ref.shape[0]
        copies.append(
            pltpu.make_async_copy(
                sums.at[pl.ds(first, GROUP)], ref.at[pl.ds(at, GROUP)], sems.at[step]
            )
        )
        copies[-1].start()
    for copy in copies:
        copy.wait()


def pairs_of(part, side, halves, act_ref, grad_ref):
    half = lax.rem(side + part, halves)
    for ref in (act_ref, grad_ref):
        count = ref.shape[1] // PAIR // halves
        for pair in range(count):
            yield ref, pl.multiple_of((half * count + pair) * PAIR, PAIR)


def eigen_kernel(part, halves, masks, pieces, scale, me_ref, side_ref, act_ref, grad_ref, *refs):
    *shard_refs, power_ref, sums_ref, basis_ref = refs
    me, side = me_ref[0], side_ref[0]
    rows = BLK // pieces
    done = 0
    if part:
        *shard_refs, done_ref = shard_refs
        done = done_ref.shape[0]
        sums_ref[:done] = done_ref[...]
    half = lax.rem(side + part, halves)
    act_half = act_ref.shape[1] // BLK // halves
    grad_half = grad_ref.shape[1] // BLK // halves
    basis_ref[...] = jnp.zeros_like(basis_ref)
    for mask, ref in zip(masks, shard_refs):
        whole = halves > 1 and ref.shape[0] == halves * (act_half + grad_half)
        for block in range(act_half + grad_half):
            at = block
            if whole and block < act_half:
                at = half * act_half + block
            elif whole:
                at = (halves - 1) * act_half + half * grad_half + block
            corner = block % 2
            row = pl.multiple_of(corner * BLK + (me ^ mask) * rows, rows)
            columns = slice(corner * BLK, (corner + 1) * BLK)
            basis_ref[block // 2, pl.ds(row, rows), columns] = ref[at]

    for pair, (ref, column) in enumerate(pairs_of(part, side, halves, act_ref, grad_ref)):
        projected = lax.dot_general(
            ref[:, pl.ds(column, PAIR)],
            basis_ref[pair],
            contract_inner,
            preferred_element_type=jnp.float32,
        )
        power = projected * projected
        power_ref[pair] = power
        sums = scale * jnp.sum(power, axis=0, keepdims=True)
        row = done + 2 * pair
        sums_ref[row : row + 1, :] = sums[:, :BLK]
        sums_ref[row + 1 : row + 2, :] = sums[:, BLK:]


def combine_kernel(halves, side_ref, *refs):
    *sums_refs, act_eigen_ref, grad_eigen_ref, eigen_ref, total_ref = refs
    side = side_ref[0]
    act_half, grad_half = act_eigen_ref.shape[0] // halves, grad_eigen_ref.shape[0] // halves
    eigen = sums_refs[0][...]
    for sums_ref in sums_refs[1:]:
        eigen = eigen + sums_ref[...]
    eigen_ref[...] = eigen
    act_total = jnp.zeros((1, BLK), jnp.float32)
    grad_total = jnp.zeros((1, BLK), jnp.float32)
    for part in range(halves):
        half = lax.rem(side + part, halves)
        first = part * (act_half + grad_half)
        act = eigen[first : first + act_half]
        grad = eigen[first + act_half : first + act_half + grad_half]
        act_total += jnp.sum(act, axis=0, keepdims=True)
        grad_total += jnp.sum(grad, axis=0, keepdims=True)
        act_eigen_ref[pl.ds(half * act_half, act_half), :] = act
        grad_eigen_ref[pl.ds(half * grad_half, grad_half), :] = grad
    total_ref[0:1, :] = act_total
    total_ref[1:2, :] = grad_total


def weight_kernel(halves, act_half, eigen_ref, *refs):
    *refs, weight_ref, inverse, act_sum, grad_sum = refs
    power_refs, total_refs = refs[:halves], refs[halves:]
    totals = total_refs[0][...]
    for total_ref in total_refs[1:]:
        totals = totals + total_ref[...]
    totals = jnp.sum(totals, axis=1, keepdims=True)
    blocks_half = eigen_ref.shape[0] // halves
    for part in range(halves):
        first = part * blocks_half
        act = slice(first, first + act_half)
        grad = slice(first + act_half, first + blocks_half)
        inverse[act] = 1.0 / (eigen_ref[act] + totals[0:1] * (damp_root / D))
        inverse[grad] = 1.0 / (eigen_ref[grad] + totals[1:2] * (damp_root / FF))
    tokens = act_sum.shape[0]

    @pl.loop(0, tokens // TILE)
    def _(tile):
        here = pl.ds(pl.multiple_of(tile * TILE, TILE), TILE)
        sums = [jnp.zeros((TILE, BLK), jnp.float32), jnp.zeros((TILE, BLK), jnp.float32)]
        for part, power_ref in enumerate(power_refs):
            for pair in range(power_ref.shape[0]):
                which = 0 if 2 * pair < act_half else 1
                for side in range(2):
                    row = part * blocks_half + 2 * pair + side
                    power = power_ref[pair, here, side * BLK : (side + 1) * BLK]
                    sums[which] += power * inverse[row : row + 1, :]
        act_sum[here, :], grad_sum[here, :] = sums

    ones = jnp.ones((8, BLK), jnp.float32)
    for index, total in enumerate((act_sum, grad_sum)):
        sums = lax.dot_general(
            ones,
            total[...],
            contract_lanes,
            precision=lax.Precision.HIGHEST,
            preferred_element_type=jnp.float32,
        )
        weight_ref[index : index + 1, :] = sums[0:1]


def score_kernel(*refs):
    *weight_refs, score_ref = refs
    weights = weight_refs[0][...]
    for weight_ref in weight_refs[1:]:
        weights = weights + weight_ref[...]
    score_ref[...] = weights[0:1] * weights[1:2] * (1.0 / (D * FF))


def swap(value, axis, mask):
    count = lax.axis_size(axis)
    return lax.ppermute(value, axis, [(i, i ^ mask) for i in range(count)])


def share(value, axis, direct):
    if not direct:
        return [lax.psum(value, axis)]
    return [value] + [swap(value, axis, mask) for mask in range(1, lax.axis_size(axis))]


def after(values, done):
    return list(lax.optimization_barrier((tuple(values), done))[0])


def local(activations, gradients, basis_act, basis_grad):
    tokens = activations.shape[0]
    act_blocks, grad_blocks = basis_act.shape[0], basis_grad.shape[0]
    blocks = act_blocks + grad_blocks
    dp, owners = lax.axis_size("dp"), lax.axis_size("owner")
    scale = 1.0 / (tokens * dp)
    direct = dp in (2, 4) and owners in (1, 2, 4)
    pieces = dp if direct else 1
    halves = 2 if pieces == 4 and lax.axis_size("groups") == 2 else 1
    rows = BLK // pieces
    me = jnp.full((1,), lax.axis_index("dp") if direct else 0, jnp.int32)
    side = jnp.full((1,), lax.axis_index("groups"), jnp.int32)
    macs = tokens * blocks * BLK * BLK
    input_bytes = 2 * tokens * blocks * BLK
    if direct:
        shards = call(
            pack_kernel,
            [bf16(blocks // part, rows, BLK) for part in range(1, halves + 1)],
            "pack_basis", 0, 2 * blocks * rows * BLK,
            [IN_SMEM, IN_HBM, IN_HBM], [pltpu.SemaphoreType.DMA((2 * halves,))],
        )(side, in_hbm(basis_act), in_hbm(basis_grad))
        near = [shards[0], swap(shards[0], "dp", 1)]
        far = {mask: swap(shards[-1], "dp", mask) for mask in range(pieces - 1, 1, -1)}
    else:
        near = [
            jnp.concatenate(
                [lax.all_gather(part, "dp", axis=1, tiled=True) for part in (basis_act, basis_grad)]
            )
        ]
        far = {}
    masks = [*range(len(near)), *far]

    plain = {4: [(0, 0), (1, 2)], 2: [(0, 0)], 1: [(0, 0)]}[pieces]
    coded = {4: [(3, 1), (3, 3), (2, 2)], 2: [(1, 1)], 1: []}[pieces]
    message = bf16(blocks * rows + scale_rows(blocks), BLK)
    tops = pltpu.VMEM((scale_rows(blocks), BLK), jnp.float32)
    act_here, grad_here, *grams = call(
        functools.partial(gram_kernel, pieces, plain, coded, scale),
        [
            bf16(*activations.shape),
            bf16(*gradients.shape),
            *[f32(blocks, rows, BLK)] * len(plain),
            *[message] * len(coded),
        ],
        "partial_gram", 4 * macs, input_bytes,
        [IN_SMEM, IN_HBM, IN_HBM],
        [
            pltpu.VMEM((GROUP, BLK, BLK), jnp.float32),
            tops,
            pltpu.SemaphoreType.DMA((blocks // GROUP,)),
        ],
    )(me, in_hbm(activations), in_hbm(gradients))
    own, sent = grams[0], grams[len(plain) :]
    if not direct:
        own = lax.psum_scatter(own, "dp", scatter_dimension=1, tiled=True)
    if pieces == 4:
        nearest = swap(sent[0], "dp", 1)
        middle = lax.ppermute(sent[1], "dp", [(1, 2), (2, 1)])

    parts = [[*near, *far.values()]]
    if halves == 2:
        swapped = [swap(after([part], own)[0], "groups", 1) for part in far.values()]
        parts.append([*near, *swapped])
    powers, sums = [], []
    for part, shards in enumerate(parts):
        power, *sums = call(
            functools.partial(eigen_kernel, part, halves, masks, pieces, scale),
            [f32(blocks // halves // 2, tokens, PAIR), f32(blocks // halves * (part + 1), BLK)],
            "partial_eigen", 2 * macs // halves, input_bytes // halves,
            [IN_SMEM, IN_SMEM] + [IN_VMEM] * (2 + len(shards) + len(sums)),
            [pltpu.VMEM((blocks // halves // 2, PAIR, PAIR), jnp.bfloat16)],
        )(me, side, act_here, grad_here, *shards, *sums)
        powers.append(power)
    if pieces == 4:
        last = call(
            relay_kernel, message, "relay_chunk", 0, 12 * own.size,
            [IN_SMEM, IN_VMEM, IN_VMEM], [tops, tops],
        )(me, *after([grams[1], nearest], sums))
    elif pieces == 2:
        last = sent[0]
    sums = share(sums[0], "dp", direct)
    if pieces == 4:
        sums = after(sums, (middle, last))
    act_eigen, grad_eigen, eigen, totals = call(
        functools.partial(combine_kernel, halves),
        [f32(act_blocks, BLK), f32(grad_blocks, BLK), f32(blocks, BLK), f32(2, BLK)],
        "combine_eigen", 0, 4 * blocks * BLK * pieces, [IN_SMEM] + [IN_VMEM] * len(sums),
    )(side, *sums)
    if pieces == 4:
        ends = lax.ppermute(after([sent[2]], totals)[0], "dp", [(0, 2), (3, 1)])
    if pieces > 1:
        ways = {4: [(0, 1), (3, 2), (1, 3), (2, 0)], 2: [(0, 1), (1, 0)]}[pieces]
        last = lax.ppermute(after([last], totals)[0], "dp", ways)
    totals = share(totals, "owner", direct)
    weights = call(
        functools.partial(weight_kernel, halves, act_blocks // halves),
        f32(2, tokens), "partial_weights", 0, 4 * tokens * blocks * BLK,
        [IN_VMEM] * (1 + halves + len(totals)),
        [
            pltpu.VMEM((blocks, BLK), jnp.float32),
            pltpu.VMEM((tokens, BLK), jnp.float32),
            pltpu.VMEM((tokens, BLK), jnp.float32),
        ],
    )(eigen, *powers, *totals)
    weights = share(weights, "owner", direct)

    if pieces == 4:
        own = call(
            add_kernel, f32(*own.shape), "add_chunks", 0, 20 * own.size,
            [IN_SMEM] + [IN_VMEM] * 4, [tops] * 3,
        )(me, own, nearest, middle, ends)
        weights[1:] = after(weights[1:], own)
    token_scores = call(
        score_kernel, f32(1, tokens), "token_scores", 0, 8 * tokens, [IN_VMEM] * len(weights)
    )(*weights)
    if pieces > 1:
        covariance = call(
            last_add_kernel,
            [f32(act_blocks, rows, BLK), f32(grad_blocks, rows, BLK)],
            "add_last_chunk", 0, 12 * own.size, [IN_VMEM] * 2,
            [tops, pltpu.VMEM(own.shape, jnp.float32), pltpu.SemaphoreType.DMA((blocks // GROUP,))],
            out_spec=[pl.BlockSpec(memory_space=pl.ANY)] * 2,
        )(own, last)
    else:
        covariance = own[:act_blocks], own[act_blocks:]
    return (
        *covariance,
        act_eigen.reshape(-1),
        grad_eigen.reshape(-1),
        token_scores.reshape(-1),
    )


def solution(mesh):
    return jax.shard_map(
        local,
        mesh=mesh,
        in_specs=(
            P(("groups", "dp"), "owner"),
            P(("groups", "dp"), "owner"),
            P("owner", "dp", None),
            P("owner", "dp", None),
        ),
        out_specs=(
            P(("groups", "owner"), "dp", None),
            P(("groups", "owner"), "dp", None),
            P(("groups", "owner")),
            P(("groups", "owner")),
            P(("groups", "dp")),
        ),
        check_vma=False,
    )
```

```python
import functools

import jax
import jax.numpy as jnp
from jax import lax
from jax.experimental import pallas as pl
from jax.experimental.pallas import tpu as pltpu
from jax.sharding import PartitionSpec as P

D = 4096
FF = 14336
BLK = 128
PAIR = 2 * BLK
GROUP = 4
TILE = 64
VMEM_LIMIT = 24 * 1024 * 1024
CODE_TOP = 2.0**7.875
SMALLEST = 1e-36

damp_root = 0.31622776601683794
contract_rows = (((0,), (0,)), ((), ()))
contract_inner = (((1,), (0,)), ((), ()))
contract_lanes = (((1,), (1,)), ((), ()))

IN_VMEM = pl.BlockSpec(memory_space=pltpu.VMEM)
IN_SMEM = pl.BlockSpec(memory_space=pltpu.SMEM)
IN_HBM = pl.BlockSpec(memory_space=pltpu.HBM)


def scale_rows(first, end):
    return 16 * pl.cdiv(end - first, 16)


def call(
    kernel, out_shape, name, flops, bytes_accessed, in_specs, scratch_shapes=(),
    out_spec=None,
):
    return pl.pallas_call(
        kernel,
        out_shape=out_shape,
        in_specs=in_specs,
        out_specs=out_spec or jax.tree.map(lambda _: IN_VMEM, out_shape),
        scratch_shapes=scratch_shapes,
        compiler_params=pltpu.CompilerParams(vmem_limit_bytes=VMEM_LIMIT),
        cost_estimate=pl.CostEstimate(
            flops=flops, bytes_accessed=bytes_accessed, transcendentals=0
        ),
        name=name,
    )


def in_hbm(value):
    return pltpu.with_memory_space_constraint(value, pltpu.HBM)


def f32(*shape):
    return jax.ShapeDtypeStruct(shape, jnp.float32)


def bf16(*shape):
    return jax.ShapeDtypeStruct(shape, jnp.bfloat16)


def encode(values):
    power = values * values
    power = power * power
    power = power * power
    power = power * power
    return jnp.where(values < 0.0, -power, power).astype(jnp.bfloat16)


def top_of(values):
    top = jnp.maximum(jnp.max(jnp.abs(values), axis=0, keepdims=True), SMALLEST)
    return (top * (1.0 + 2.0**-8)).astype(jnp.bfloat16).astype(jnp.float32)


def decode(coded):
    coded = coded.astype(jnp.float32)
    root = jnp.abs(coded)
    for _ in range(4):
        root = lax.rsqrt(root)
    return jnp.where(coded > 0.0, root, jnp.where(coded < 0.0, -root, 0.0))


def pack_kernel(side_ref, act_ref, grad_ref, *refs):
    *out_refs, sems = refs
    side = side_ref[0]
    blocks = out_refs[0].shape[0]
    copies = []
    for out_ref in reversed(out_refs):
        halves = blocks // out_ref.shape[0]
        at = 0
        for ref in (act_ref, grad_ref):
            count = ref.shape[0] // halves
            copies.append(
                pltpu.make_async_copy(
                    ref.at[pl.ds(side * count if halves > 1 else 0, count)],
                    out_ref.at[pl.ds(at, count)],
                    sems.at[len(copies)],
                )
            )
            at += count
    for copy in copies:
        copy.start()
    for copy in copies:
        copy.wait()


def gram_kernel(pieces, messages, scale, me_ref, act_hbm, grad_hbm, act_ref, grad_ref, *refs):
    refs, (whole, tops, sems) = refs[:-3], refs[-3:]
    plain_refs, sent_refs = refs[: len(refs) - len(messages)], refs[len(refs) - len(messages) :]
    rows = BLK // pieces
    me = me_ref[0]
    steps = []
    for source, target in ((act_hbm, act_ref), (grad_hbm, grad_ref)):
        for first in range(0, source.shape[1], GROUP * BLK):
            columns = slice(first, first + GROUP * BLK)
            copy = pltpu.make_async_copy(
                source.at[:, columns], target.at[:, columns], sems.at[len(steps)]
            )
            copy.start()
            steps.append((target, columns, copy))
    tops[...] = jnp.zeros_like(tops)
    for step, (ref, columns, copy) in enumerate(steps):
        copy.wait()
        for offset in range(GROUP):
            block = step * GROUP + offset
            at = columns.start + offset * BLK
            values = ref[:, at : at + BLK]
            gram = scale * lax.dot_general(
                values, values, contract_rows, preferred_element_type=jnp.float32
            )
            if pieces == 1:
                plain_refs[0][block] = gram
                continue
            whole[offset] = gram
            for ref_at, mask in zip(plain_refs, (0, 2)):
                row = pl.multiple_of((me ^ mask) * rows, rows)
                ref_at[block] = whole[offset, pl.ds(row, rows), :]
            top = top_of(gram)
            tops[block : block + 1, :] = top
            gain = CODE_TOP / top
            for sent_ref, (mask, first, end) in zip(sent_refs, messages):
                if first <= block < end:
                    row = pl.multiple_of((me ^ mask) * rows, rows)
                    place = slice((block - first) * rows, (block - first + 1) * rows)
                    sent_ref[place, :] = encode(whole[offset, pl.ds(row, rows), :] * gain)
    for sent_ref, (_, first, end) in zip(sent_refs, messages):
        sent_ref[(end - first) * rows :, :] = tops[
            first : first + scale_rows(first, end), :
        ].astype(jnp.bfloat16)


def add_group(messages, rows, own_ref, sent_refs, tops_refs, step):
    for block in range(step * GROUP, (step + 1) * GROUP):
        total = own_ref[block]
        for (_, first, end), sent_ref, tops in zip(messages, sent_refs, tops_refs):
            if first <= block < end:
                at = block - first
                values = decode(sent_ref[at * rows : (at + 1) * rows, :])
                total = total + values * tops[at : at + 1, :]
        yield block, total


def load_tops(messages, rows, sent_refs, tops_refs):
    for (_, first, end), sent_ref, tops in zip(messages, sent_refs, tops_refs):
        tops[...] = sent_ref[(end - first) * rows :, :].astype(jnp.float32) * (1.0 / CODE_TOP)


def add_kernel(messages, halves, side_ref, eigen_ref, own_ref, *refs):
    sent_refs, refs = refs[: len(messages)], refs[len(messages) :]
    sum_ref, act_eigen_ref, grad_eigen_ref, *tops_refs = refs
    order_kernel(halves, side_ref, eigen_ref, act_eigen_ref, grad_eigen_ref)
    blocks, rows, _ = own_ref.shape
    load_tops(messages, rows, sent_refs, tops_refs)
    for step in range(blocks // GROUP):
        for block, total in add_group(messages, rows, own_ref, sent_refs, tops_refs, step):
            sum_ref[block] = total


def relay_kernel(message, far_ref, relayed_ref, sent_ref, relayed_tops, tops):
    messages = (message,)
    blocks, rows, _ = far_ref.shape
    load_tops(messages, rows, (relayed_ref,), (relayed_tops,))
    tops[...] = jnp.zeros_like(tops)
    for step in range(blocks // GROUP):
        for block, total in add_group(
            messages, rows, far_ref, (relayed_ref,), (relayed_tops,), step
        ):
            top = top_of(total)
            tops[block : block + 1, :] = top
            sent_ref[block * rows : (block + 1) * rows, :] = encode(total * (CODE_TOP / top))
    sent_ref[blocks * rows :, :] = tops[...].astype(jnp.bfloat16)


def last_add_kernel(messages, owners, own_ref, *refs):
    sent_refs, refs = refs[: len(messages)], refs[len(messages) :]
    weight_refs, refs = refs[:owners], refs[owners:]
    act_ref, grad_ref, score_ref, *tops_refs, sums, scores, sems = refs
    blocks, rows, _ = own_ref.shape
    score_kernel(*weight_refs, scores)
    copies = [pltpu.make_async_copy(scores, score_ref, sems.at[blocks // GROUP])]
    copies[0].start()
    load_tops(messages, rows, sent_refs, tops_refs)
    for step in range(blocks // GROUP):
        for block, total in add_group(messages, rows, own_ref, sent_refs, tops_refs, step):
            sums[block] = total
        first = step * GROUP
        ref, at = act_ref, first
        if first >= act_ref.shape[0]:
            ref, at = grad_ref, first - act_ref.shape[0]
        copies.append(
            pltpu.make_async_copy(
                sums.at[pl.ds(first, GROUP)], ref.at[pl.ds(at, GROUP)], sems.at[step]
            )
        )
        copies[-1].start()
    for copy in copies:
        copy.wait()


def pairs_of(part, side, halves, act_ref, grad_ref):
    half = lax.rem(side + part, halves)
    for ref in (act_ref, grad_ref):
        count = ref.shape[1] // PAIR // halves
        for pair in range(count):
            yield ref, pl.multiple_of((half * count + pair) * PAIR, PAIR)


def eigen_kernel(part, halves, masks, pieces, scale, me_ref, side_ref, act_ref, grad_ref, *refs):
    *shard_refs, power_ref, sums_ref, basis_ref = refs
    me, side = me_ref[0], side_ref[0]
    rows = BLK // pieces
    done = 0
    if part:
        *shard_refs, done_ref = shard_refs
        done = done_ref.shape[0]
        sums_ref[:done] = done_ref[...]
    half = lax.rem(side + part, halves)
    act_half = act_ref.shape[1] // BLK // halves
    grad_half = grad_ref.shape[1] // BLK // halves
    basis_ref[...] = jnp.zeros_like(basis_ref)
    for mask, ref in zip(masks, shard_refs):
        whole = halves > 1 and ref.shape[0] == halves * (act_half + grad_half)
        for block in range(act_half + grad_half):
            at = block
            if whole and block < act_half:
                at = half * act_half + block
            elif whole:
                at = (halves - 1) * act_half + half * grad_half + block
            corner = block % 2
            row = pl.multiple_of(corner * BLK + (me ^ mask) * rows, rows)
            columns = slice(corner * BLK, (corner + 1) * BLK)
            basis_ref[block // 2, pl.ds(row, rows), columns] = ref[at]

    for pair, (ref, column) in enumerate(pairs_of(part, side, halves, act_ref, grad_ref)):
        projected = lax.dot_general(
            ref[:, pl.ds(column, PAIR)],
            basis_ref[pair],
            contract_inner,
            preferred_element_type=jnp.float32,
        )
        power = projected * projected
        power_ref[pair] = power
        sums = scale * jnp.sum(power, axis=0, keepdims=True)
        row = done + 2 * pair
        sums_ref[row : row + 1, :] = sums[:, :BLK]
        sums_ref[row + 1 : row + 2, :] = sums[:, BLK:]


def combine_kernel(halves, act_half, *refs):
    *sums_refs, eigen_ref, total_ref = refs
    eigen = sums_refs[0][...]
    for sums_ref in sums_refs[1:]:
        eigen = eigen + sums_ref[...]
    eigen_ref[...] = eigen
    blocks_half = eigen.shape[0] // halves
    act_total = jnp.zeros((1, BLK), jnp.float32)
    grad_total = jnp.zeros((1, BLK), jnp.float32)
    for part in range(halves):
        first = part * blocks_half
        act_total += jnp.sum(eigen[first : first + act_half], axis=0, keepdims=True)
        grad_total += jnp.sum(eigen[first + act_half : first + blocks_half], axis=0, keepdims=True)
    total_ref[0:1, :] = act_total
    total_ref[1:2, :] = grad_total


def order_kernel(halves, side_ref, eigen_ref, act_eigen_ref, grad_eigen_ref):
    side = side_ref[0]
    act_half, grad_half = act_eigen_ref.shape[0] // halves, grad_eigen_ref.shape[0] // halves
    for part in range(halves):
        half = lax.rem(side + part, halves)
        first = part * (act_half + grad_half)
        middle = first + act_half
        act_eigen_ref[pl.ds(half * act_half, act_half), :] = eigen_ref[first:middle]
        grad_eigen_ref[pl.ds(half * grad_half, grad_half), :] = eigen_ref[
            middle : middle + grad_half
        ]


def weight_kernel(halves, act_half, eigen_ref, *refs):
    *refs, weight_ref, inverse, act_sum, grad_sum = refs
    power_refs, total_refs = refs[:halves], refs[halves:]
    totals = total_refs[0][...]
    for total_ref in total_refs[1:]:
        totals = totals + total_ref[...]
    totals = jnp.sum(totals, axis=1, keepdims=True)
    blocks_half = eigen_ref.shape[0] // halves
    for part in range(halves):
        first = part * blocks_half
        act = slice(first, first + act_half)
        grad = slice(first + act_half, first + blocks_half)
        inverse[act] = 1.0 / (eigen_ref[act] + totals[0:1] * (damp_root / D))
        inverse[grad] = 1.0 / (eigen_ref[grad] + totals[1:2] * (damp_root / FF))
    tokens = act_sum.shape[0]

    @pl.loop(0, tokens // TILE)
    def _(tile):
        here = pl.ds(pl.multiple_of(tile * TILE, TILE), TILE)
        sums = [jnp.zeros((TILE, BLK), jnp.float32), jnp.zeros((TILE, BLK), jnp.float32)]
        for part, power_ref in enumerate(power_refs):
            for pair in range(power_ref.shape[0]):
                which = 0 if 2 * pair < act_half else 1
                for side in range(2):
                    row = part * blocks_half + 2 * pair + side
                    power = power_ref[pair, here, side * BLK : (side + 1) * BLK]
                    sums[which] += power * inverse[row : row + 1, :]
        act_sum[here, :], grad_sum[here, :] = sums

    ones = jnp.ones((8, BLK), jnp.float32)
    for index, total in enumerate((act_sum, grad_sum)):
        sums = lax.dot_general(
            ones,
            total[...],
            contract_lanes,
            precision=lax.Precision.HIGHEST,
            preferred_element_type=jnp.float32,
        )
        weight_ref[index : index + 1, :] = sums[0:1]


def score_kernel(*refs):
    *weight_refs, score_ref = refs
    weights = weight_refs[0][...]
    for weight_ref in weight_refs[1:]:
        weights = weights + weight_ref[...]
    score_ref[...] = weights[0:1] * weights[1:2] * (1.0 / (D * FF))


def swap(value, axis, mask):
    count = lax.axis_size(axis)
    return lax.ppermute(value, axis, [(i, i ^ mask) for i in range(count)])


def share(value, axis, direct):
    if not direct:
        return [lax.psum(value, axis)]
    return [value] + [swap(value, axis, mask) for mask in reversed(range(1, lax.axis_size(axis)))]


def after(values, done):
    return list(lax.optimization_barrier((tuple(values), done))[0])


def local(activations, gradients, basis_act, basis_grad):
    tokens = activations.shape[0]
    act_blocks, grad_blocks = basis_act.shape[0], basis_grad.shape[0]
    blocks = act_blocks + grad_blocks
    dp, owners = lax.axis_size("dp"), lax.axis_size("owner")
    scale = 1.0 / (tokens * dp)
    direct = dp in (2, 4) and owners in (1, 2, 4)
    pieces = dp if direct else 1
    halves = 2 if pieces == 4 and lax.axis_size("groups") == 2 else 1
    rows = BLK // pieces
    me = jnp.full((1,), lax.axis_index("dp") if direct else 0, jnp.int32)
    side = jnp.full((1,), lax.axis_index("groups"), jnp.int32)
    macs = tokens * blocks * BLK * BLK
    input_bytes = 2 * tokens * blocks * BLK
    if direct:
        shards = call(
            pack_kernel,
            [bf16(blocks // part, rows, BLK) for part in range(1, halves + 1)],
            "pack_basis", 0, 2 * blocks * rows * BLK,
            [IN_SMEM, IN_HBM, IN_HBM], [pltpu.SemaphoreType.DMA((2 * halves,))],
        )(side, in_hbm(basis_act), in_hbm(basis_grad))
        near = [shards[0], swap(shards[0], "dp", 1)]
        far = {mask: swap(shards[-1], "dp", mask) for mask in range(pieces - 1, 1, -1)}
    else:
        near = [
            jnp.concatenate(
                [lax.all_gather(part, "dp", axis=1, tiled=True) for part in (basis_act, basis_grad)]
            )
        ]
        far = {}
    masks = [*range(len(near)), *far]

    message = bf16(blocks * rows + scale_rows(0, blocks), BLK)
    whole_range = (0, blocks)
    coded = {4: [(3, *whole_range), (1, *whole_range)], 2: [(1, *whole_range)], 1: []}[pieces]
    plain = 2 if pieces == 4 else 1
    act_here, grad_here, *grams = call(
        functools.partial(gram_kernel, pieces, coded, scale),
        [
            bf16(*activations.shape),
            bf16(*gradients.shape),
            *[f32(blocks, rows, BLK)] * plain,
            *[message] * len(coded),
        ],
        "partial_gram", 4 * macs, input_bytes,
        [IN_SMEM, IN_HBM, IN_HBM],
        [
            pltpu.VMEM((GROUP, BLK, BLK), jnp.float32),
            pltpu.VMEM((scale_rows(0, blocks), BLK), jnp.float32),
            pltpu.SemaphoreType.DMA((blocks // GROUP,)),
        ],
    )(me, in_hbm(activations), in_hbm(gradients))
    own = grams[0]
    sent = {message[0]: chunk for message, chunk in zip(coded, grams[plain:])}
    if not direct:
        own = lax.psum_scatter(own, "dp", scatter_dimension=1, tiled=True)
    if pieces == 4:
        middle = lax.ppermute(sent[3], "dp", [(1, 2), (2, 1)])
        relayed = lax.ppermute(sent[3], "dp", [(0, 1), (3, 2)])

    parts = [[*near, *far.values()]]
    if halves == 2:
        swapped = [swap(after([part], own)[0], "groups", 1) for part in far.values()]
        parts.append([*near, *swapped])
    powers, sums = [], []
    for part, shards in enumerate(parts):
        power, *sums = call(
            functools.partial(eigen_kernel, part, halves, masks, pieces, scale),
            [f32(blocks // halves // 2, tokens, PAIR), f32(blocks // halves * (part + 1), BLK)],
            "partial_eigen", 2 * macs // halves, input_bytes // halves,
            [IN_SMEM, IN_SMEM] + [IN_VMEM] * (2 + len(shards) + len(sums)),
            [pltpu.VMEM((blocks // halves // 2, PAIR, PAIR), jnp.bfloat16)],
        )(me, side, act_here, grad_here, *shards, *sums)
        powers.append(power)
    if pieces == 4:
        sent[2] = call(
            functools.partial(relay_kernel, coded[0]), message, "relay_chunk", 0, 12 * own.size,
            [IN_VMEM, IN_VMEM],
            [pltpu.VMEM((scale_rows(0, blocks), BLK), jnp.float32)] * 2,
        )(*after([grams[1], relayed], sums))
    sums = share(sums[0], "dp", direct)
    if pieces == 4:
        sums = after(sums, (middle, sent[2]))
    eigen, totals = call(
        functools.partial(combine_kernel, halves, act_blocks // halves),
        [f32(blocks, BLK), f32(2, BLK)],
        "combine_eigen", 0, 4 * blocks * BLK * pieces, [IN_VMEM] * len(sums),
    )(*sums)
    arrived = {}
    sent.pop(3, None)
    for mask in sent:
        arrived[mask] = swap(after([sent[mask]], totals)[0], "dp", mask)
    totals = share(totals, "owner", direct)
    weights = call(
        functools.partial(weight_kernel, halves, act_blocks // halves),
        f32(2, tokens), "partial_weights", 0, 4 * tokens * blocks * BLK,
        [IN_VMEM] * (1 + halves + len(totals)),
        [
            pltpu.VMEM((blocks, BLK), jnp.float32),
            pltpu.VMEM((tokens, BLK), jnp.float32),
            pltpu.VMEM((tokens, BLK), jnp.float32),
        ],
    )(eigen, *powers, *totals)
    weights = share(weights, "owner", direct)

    def tops_of(count):
        return [pltpu.VMEM((scale_rows(0, blocks), BLK), jnp.float32)] * count

    eigens = [f32(act_blocks, BLK), f32(grad_blocks, BLK)]
    if pieces == 4:
        own, *eigens = call(
            functools.partial(add_kernel, [(None, 0, blocks)], halves),
            [f32(*own.shape), *eigens], "add_chunk", 0, 12 * own.size,
            [IN_SMEM] + [IN_VMEM] * 3, tops_of(1),
        )(side, eigen, own, middle)
        weights[1:] = after(weights[1:], own)
    else:
        eigens = call(
            functools.partial(order_kernel, halves), eigens, "order_eigen", 0,
            8 * blocks * BLK, [IN_SMEM, IN_VMEM],
        )(side, eigen)
    chunks = list(arrived.values())[::-1]
    if chunks:
        *covariance, token_scores = call(
            functools.partial(last_add_kernel, [(None, 0, blocks)] * len(chunks), len(weights)),
            [f32(act_blocks, rows, BLK), f32(grad_blocks, rows, BLK), f32(1, tokens)],
            "last_sums", 0, 16 * own.size, [IN_VMEM] * (1 + len(chunks) + len(weights)),
            [
                *tops_of(len(chunks)),
                pltpu.VMEM(own.shape, jnp.float32),
                pltpu.VMEM((1, tokens), jnp.float32),
                pltpu.SemaphoreType.DMA((blocks // GROUP + 1,)),
            ],
            out_spec=[pl.BlockSpec(memory_space=pl.ANY)] * 3,
        )(own, *chunks, *weights)
    else:
        covariance = own[:act_blocks], own[act_blocks:]
        token_scores = call(
            score_kernel, f32(1, tokens), "token_scores", 0, 8 * tokens, [IN_VMEM] * len(weights)
        )(*weights)
    return (
        *covariance,
        *[eigen.reshape(-1) for eigen in eigens],
        token_scores.reshape(-1),
    )


def solution(mesh):
    return jax.shard_map(
        local,
        mesh=mesh,
        in_specs=(
            P(("groups", "dp"), "owner"),
            P(("groups", "dp"), "owner"),
            P("owner", "dp", None),
            P("owner", "dp", None),
        ),
        out_specs=(
            P(("groups", "owner"), "dp", None),
            P(("groups", "owner"), "dp", None),
            P(("groups", "owner")),
            P(("groups", "owner")),
            P(("groups", "dp")),
        ),
        check_vma=False,
    )
```

```python
import functools

import jax
import jax.numpy as jnp
from jax import lax
from jax.experimental import pallas as pl
from jax.experimental.pallas import tpu as pltpu
from jax.sharding import PartitionSpec as P

D = 4096
FF = 14336
BLK = 128
PAIR = 2 * BLK
GROUP = 4
TILE = 64
VMEM_LIMIT = 24 * 1024 * 1024
CODE_TOP = 2.0**7.875
SMALLEST = 1e-36

damp_root = 0.31622776601683794
contract_rows = (((0,), (0,)), ((), ()))
contract_inner = (((1,), (0,)), ((), ()))
contract_lanes = (((1,), (1,)), ((), ()))

IN_VMEM = pl.BlockSpec(memory_space=pltpu.VMEM)
IN_SMEM = pl.BlockSpec(memory_space=pltpu.SMEM)
IN_HBM = pl.BlockSpec(memory_space=pltpu.HBM)


def scale_rows(first, end):
    return 16 * pl.cdiv(end - first, 16)


def call(
    kernel, out_shape, name, flops, bytes_accessed, in_specs, scratch_shapes=(),
    out_spec=None,
):
    return pl.pallas_call(
        kernel,
        out_shape=out_shape,
        in_specs=in_specs,
        out_specs=out_spec or jax.tree.map(lambda _: IN_VMEM, out_shape),
        scratch_shapes=scratch_shapes,
        compiler_params=pltpu.CompilerParams(vmem_limit_bytes=VMEM_LIMIT),
        cost_estimate=pl.CostEstimate(
            flops=flops, bytes_accessed=bytes_accessed, transcendentals=0
        ),
        name=name,
    )


def in_hbm(value):
    return pltpu.with_memory_space_constraint(value, pltpu.HBM)


def f32(*shape):
    return jax.ShapeDtypeStruct(shape, jnp.float32)


def bf16(*shape):
    return jax.ShapeDtypeStruct(shape, jnp.bfloat16)


def encode(values):
    power = values * values
    power = power * power
    power = power * power
    power = power * power
    return jnp.where(values < 0.0, -power, power).astype(jnp.bfloat16)


def top_of(values):
    top = jnp.maximum(jnp.max(jnp.abs(values), axis=0, keepdims=True), SMALLEST)
    return (top * (1.0 + 2.0**-8)).astype(jnp.bfloat16).astype(jnp.float32)


def decode(coded):
    coded = coded.astype(jnp.float32)
    root = jnp.abs(coded)
    for _ in range(4):
        root = lax.rsqrt(root)
    return jnp.where(coded > 0.0, root, jnp.where(coded < 0.0, -root, 0.0))


def pack_kernel(side_ref, act_ref, grad_ref, *refs):
    *out_refs, sems = refs
    side = side_ref[0]
    blocks = out_refs[0].shape[0]
    copies = []
    for out_ref in reversed(out_refs):
        halves = blocks // out_ref.shape[0]
        at = 0
        for ref in (act_ref, grad_ref):
            count = ref.shape[0] // halves
            copies.append(
                pltpu.make_async_copy(
                    ref.at[pl.ds(side * count if halves > 1 else 0, count)],
                    out_ref.at[pl.ds(at, count)],
                    sems.at[len(copies)],
                )
            )
            at += count
    for copy in copies:
        copy.start()
    for copy in copies:
        copy.wait()


def gram_kernel(pieces, messages, scale, me_ref, act_hbm, grad_hbm, act_ref, grad_ref, *refs):
    refs, (whole, tops, sems) = refs[:-3], refs[-3:]
    plain_refs, sent_refs = refs[: len(refs) - len(messages)], refs[len(refs) - len(messages) :]
    rows = BLK // pieces
    me = me_ref[0]
    steps = []
    for source, target in ((act_hbm, act_ref), (grad_hbm, grad_ref)):
        for first in range(0, source.shape[1], GROUP * BLK):
            columns = slice(first, first + GROUP * BLK)
            copy = pltpu.make_async_copy(
                source.at[:, columns], target.at[:, columns], sems.at[len(steps)]
            )
            copy.start()
            steps.append((target, columns, copy))
    tops[...] = jnp.zeros_like(tops)
    for step, (ref, columns, copy) in enumerate(steps):
        copy.wait()
        for offset in range(GROUP):
            block = step * GROUP + offset
            at = columns.start + offset * BLK
            values = ref[:, at : at + BLK]
            gram = scale * lax.dot_general(
                values, values, contract_rows, preferred_element_type=jnp.float32
            )
            if pieces == 1:
                plain_refs[0][block] = gram
                continue
            whole[offset] = gram
            for ref_at, mask in zip(plain_refs, (0, 2)):
                row = pl.multiple_of((me ^ mask) * rows, rows)
                ref_at[block] = whole[offset, pl.ds(row, rows), :]
            top = top_of(gram)
            tops[block : block + 1, :] = top
            gain = CODE_TOP / top
            for sent_ref, (mask, first, end) in zip(sent_refs, messages):
                if first <= block < end:
                    row = pl.multiple_of((me ^ mask) * rows, rows)
                    place = slice((block - first) * rows, (block - first + 1) * rows)
                    sent_ref[place, :] = encode(whole[offset, pl.ds(row, rows), :] * gain)
    for sent_ref, (_, first, end) in zip(sent_refs, messages):
        sent_ref[(end - first) * rows :, :] = tops[
            first : first + scale_rows(first, end), :
        ].astype(jnp.bfloat16)


def add_group(messages, rows, own_ref, sent_refs, tops_refs, step):
    for block in range(step * GROUP, (step + 1) * GROUP):
        total = own_ref[block]
        for (_, first, end), sent_ref, tops in zip(messages, sent_refs, tops_refs):
            if first <= block < end:
                at = block - first
                values = decode(sent_ref[at * rows : (at + 1) * rows, :])
                total = total + values * tops[at : at + 1, :]
        yield block, total


def load_tops(messages, rows, sent_refs, tops_refs):
    for (_, first, end), sent_ref, tops in zip(messages, sent_refs, tops_refs):
        tops[...] = sent_ref[(end - first) * rows :, :].astype(jnp.float32) * (1.0 / CODE_TOP)


def add_kernel(messages, halves, side_ref, eigen_ref, own_ref, *refs):
    sent_refs, refs = refs[: len(messages)], refs[len(messages) :]
    sum_ref, act_eigen_ref, grad_eigen_ref, *tops_refs = refs
    order_kernel(halves, side_ref, eigen_ref, act_eigen_ref, grad_eigen_ref)
    blocks, rows, _ = own_ref.shape
    load_tops(messages, rows, sent_refs, tops_refs)
    for step in range(blocks // GROUP):
        for block, total in add_group(messages, rows, own_ref, sent_refs, tops_refs, step):
            sum_ref[block] = total


def relay_kernel(message, far_ref, relayed_ref, sent_ref, relayed_tops, tops):
    messages = (message,)
    blocks, rows, _ = far_ref.shape
    load_tops(messages, rows, (relayed_ref,), (relayed_tops,))
    tops[...] = jnp.zeros_like(tops)
    for step in range(blocks // GROUP):
        for block, total in add_group(
            messages, rows, far_ref, (relayed_ref,), (relayed_tops,), step
        ):
            top = top_of(total)
            tops[block : block + 1, :] = top
            sent_ref[block * rows : (block + 1) * rows, :] = encode(total * (CODE_TOP / top))
    sent_ref[blocks * rows :, :] = tops[...].astype(jnp.bfloat16)


def last_add_kernel(messages, owners, own_ref, *refs):
    sent_refs, refs = refs[: len(messages)], refs[len(messages) :]
    weight_refs, refs = refs[:owners], refs[owners:]
    act_ref, grad_ref, score_ref, *tops_refs, sums, scores, sems = refs
    blocks, rows, _ = own_ref.shape
    score_kernel(*weight_refs, scores)
    copies = [pltpu.make_async_copy(scores, score_ref, sems.at[blocks // GROUP])]
    copies[0].start()
    load_tops(messages, rows, sent_refs, tops_refs)
    for step in range(blocks // GROUP):
        for block, total in add_group(messages, rows, own_ref, sent_refs, tops_refs, step):
            sums[block] = total
        first = step * GROUP
        ref, at = act_ref, first
        if first >= act_ref.shape[0]:
            ref, at = grad_ref, first - act_ref.shape[0]
        copies.append(
            pltpu.make_async_copy(
                sums.at[pl.ds(first, GROUP)], ref.at[pl.ds(at, GROUP)], sems.at[step]
            )
        )
        copies[-1].start()
    for copy in copies:
        copy.wait()


def pairs_of(part, side, halves, act_ref, grad_ref):
    half = lax.rem(side + part, halves)
    for ref in (act_ref, grad_ref):
        count = ref.shape[1] // PAIR // halves
        for pair in range(count):
            yield ref, pl.multiple_of((half * count + pair) * PAIR, PAIR)


def eigen_kernel(part, halves, masks, pieces, scale, me_ref, side_ref, act_ref, grad_ref, *refs):
    *shard_refs, power_ref, sums_ref, basis_ref = refs
    me, side = me_ref[0], side_ref[0]
    rows = BLK // pieces
    done = 0
    if part:
        *shard_refs, done_ref = shard_refs
        done = done_ref.shape[0]
        sums_ref[:done] = done_ref[...]
    half = lax.rem(side + part, halves)
    act_half = act_ref.shape[1] // BLK // halves
    grad_half = grad_ref.shape[1] // BLK // halves
    basis_ref[...] = jnp.zeros_like(basis_ref)
    for mask, ref in zip(masks, shard_refs):
        whole = halves > 1 and ref.shape[0] == halves * (act_half + grad_half)
        for block in range(act_half + grad_half):
            at = block
            if whole and block < act_half:
                at = half * act_half + block
            elif whole:
                at = (halves - 1) * act_half + half * grad_half + block
            corner = block % 2
            row = pl.multiple_of(corner * BLK + (me ^ mask) * rows, rows)
            columns = slice(corner * BLK, (corner + 1) * BLK)
            basis_ref[block // 2, pl.ds(row, rows), columns] = ref[at]

    for pair, (ref, column) in enumerate(pairs_of(part, side, halves, act_ref, grad_ref)):
        projected = lax.dot_general(
            ref[:, pl.ds(column, PAIR)],
            basis_ref[pair],
            contract_inner,
            preferred_element_type=jnp.float32,
        )
        power = projected * projected
        power_ref[pair] = power
        sums = scale * jnp.sum(power, axis=0, keepdims=True)
        row = done + 2 * pair
        sums_ref[row : row + 1, :] = sums[:, :BLK]
        sums_ref[row + 1 : row + 2, :] = sums[:, BLK:]


def combine_kernel(halves, act_half, *refs):
    *sums_refs, eigen_ref, total_ref = refs
    eigen = sums_refs[0][...]
    for sums_ref in sums_refs[1:]:
        eigen = eigen + sums_ref[...]
    eigen_ref[...] = eigen
    blocks_half = eigen.shape[0] // halves
    act_total = jnp.zeros((1, BLK), jnp.float32)
    grad_total = jnp.zeros((1, BLK), jnp.float32)
    for part in range(halves):
        first = part * blocks_half
        act_total += jnp.sum(eigen[first : first + act_half], axis=0, keepdims=True)
        grad_total += jnp.sum(eigen[first + act_half : first + blocks_half], axis=0, keepdims=True)
    total_ref[0:1, :] = act_total
    total_ref[1:2, :] = grad_total


def order_kernel(halves, side_ref, eigen_ref, act_eigen_ref, grad_eigen_ref):
    side = side_ref[0]
    act_half, grad_half = act_eigen_ref.shape[0] // halves, grad_eigen_ref.shape[0] // halves
    for part in range(halves):
        half = lax.rem(side + part, halves)
        first = part * (act_half + grad_half)
        middle = first + act_half
        act_eigen_ref[pl.ds(half * act_half, act_half), :] = eigen_ref[first:middle]
        grad_eigen_ref[pl.ds(half * grad_half, grad_half), :] = eigen_ref[
            middle : middle + grad_half
        ]


def weight_kernel(halves, act_half, eigen_ref, *refs):
    *refs, weight_ref, inverse, act_sum, grad_sum = refs
    power_refs, total_refs = refs[:halves], refs[halves:]
    totals = total_refs[0][...]
    for total_ref in total_refs[1:]:
        totals = totals + total_ref[...]
    totals = jnp.sum(totals, axis=1, keepdims=True)
    blocks_half = eigen_ref.shape[0] // halves
    for part in range(halves):
        first = part * blocks_half
        act = slice(first, first + act_half)
        grad = slice(first + act_half, first + blocks_half)
        inverse[act] = 1.0 / (eigen_ref[act] + totals[0:1] * (damp_root / D))
        inverse[grad] = 1.0 / (eigen_ref[grad] + totals[1:2] * (damp_root / FF))
    tokens = act_sum.shape[0]

    @pl.loop(0, tokens // TILE)
    def _(tile):
        here = pl.ds(pl.multiple_of(tile * TILE, TILE), TILE)
        sums = [jnp.zeros((TILE, BLK), jnp.float32), jnp.zeros((TILE, BLK), jnp.float32)]
        for part, power_ref in enumerate(power_refs):
            for pair in range(power_ref.shape[0]):
                which = 0 if 2 * pair < act_half else 1
                for side in range(2):
                    row = part * blocks_half + 2 * pair + side
                    power = power_ref[pair, here, side * BLK : (side + 1) * BLK]
                    sums[which] += power * inverse[row : row + 1, :]
        act_sum[here, :], grad_sum[here, :] = sums

    ones = jnp.ones((8, BLK), jnp.float32)
    for index, total in enumerate((act_sum, grad_sum)):
        sums = lax.dot_general(
            ones,
            total[...],
            contract_lanes,
            precision=lax.Precision.HIGHEST,
            preferred_element_type=jnp.float32,
        )
        weight_ref[index : index + 1, :] = sums[0:1]


def score_kernel(*refs):
    *weight_refs, score_ref = refs
    weights = weight_refs[0][...]
    for weight_ref in weight_refs[1:]:
        weights = weights + weight_ref[...]
    score_ref[...] = weights[0:1] * weights[1:2] * (1.0 / (D * FF))


def swap(value, axis, mask):
    count = lax.axis_size(axis)
    return lax.ppermute(value, axis, [(i, i ^ mask) for i in range(count)])


def share(value, axis, direct):
    if not direct:
        return [lax.psum(value, axis)]
    return [value] + [swap(value, axis, mask) for mask in reversed(range(1, lax.axis_size(axis)))]


def after(values, done):
    return list(lax.optimization_barrier((tuple(values), done))[0])


def local(activations, gradients, basis_act, basis_grad):
    tokens = activations.shape[0]
    act_blocks, grad_blocks = basis_act.shape[0], basis_grad.shape[0]
    blocks = act_blocks + grad_blocks
    dp, owners = lax.axis_size("dp"), lax.axis_size("owner")
    scale = 1.0 / (tokens * dp)
    direct = dp in (2, 4) and owners in (1, 2, 4)
    pieces = dp if direct else 1
    halves = 2 if pieces == 4 and lax.axis_size("groups") == 2 else 1
    rows = BLK // pieces
    me = jnp.full((1,), lax.axis_index("dp") if direct else 0, jnp.int32)
    side = jnp.full((1,), lax.axis_index("groups"), jnp.int32)
    macs = tokens * blocks * BLK * BLK
    input_bytes = 2 * tokens * blocks * BLK
    if direct:
        shards = call(
            pack_kernel,
            [bf16(blocks // part, rows, BLK) for part in range(1, halves + 1)],
            "pack_basis", 0, 2 * blocks * rows * BLK,
            [IN_SMEM, IN_HBM, IN_HBM], [pltpu.SemaphoreType.DMA((2 * halves,))],
        )(side, in_hbm(basis_act), in_hbm(basis_grad))
        near = [shards[0], swap(shards[0], "dp", 1)]
        far = {mask: swap(shards[-1], "dp", mask) for mask in range(pieces - 1, 1, -1)}
    else:
        near = [
            jnp.concatenate(
                [lax.all_gather(part, "dp", axis=1, tiled=True) for part in (basis_act, basis_grad)]
            )
        ]
        far = {}
    masks = [*range(len(near)), *far]

    message = bf16(blocks * rows + scale_rows(0, blocks), BLK)
    whole_range = (0, blocks)
    coded = {4: [(3, *whole_range), (1, *whole_range)], 2: [(1, *whole_range)], 1: []}[pieces]
    plain = 2 if pieces == 4 else 1
    act_here, grad_here, *grams = call(
        functools.partial(gram_kernel, pieces, coded, scale),
        [
            bf16(*activations.shape),
            bf16(*gradients.shape),
            *[f32(blocks, rows, BLK)] * plain,
            *[message] * len(coded),
        ],
        "partial_gram", 4 * macs, input_bytes,
        [IN_SMEM, IN_HBM, IN_HBM],
        [
            pltpu.VMEM((GROUP, BLK, BLK), jnp.float32),
            pltpu.VMEM((scale_rows(0, blocks), BLK), jnp.float32),
            pltpu.SemaphoreType.DMA((blocks // GROUP,)),
        ],
    )(me, in_hbm(activations), in_hbm(gradients))
    own = grams[0]
    sent = {message[0]: chunk for message, chunk in zip(coded, grams[plain:])}
    if not direct:
        own = lax.psum_scatter(own, "dp", scatter_dimension=1, tiled=True)
    if pieces == 4:
        middle = lax.ppermute(sent[3], "dp", [(1, 2), (2, 1)])
        relayed = lax.ppermute(sent[3], "dp", [(0, 1), (3, 2)])

    parts = [[*near, *far.values()]]
    if halves == 2:
        swapped = [swap(after([part], own)[0], "groups", 1) for part in far.values()]
        parts.append([*near, *swapped])
    powers, sums = [], []
    for part, shards in enumerate(parts):
        power, *sums = call(
            functools.partial(eigen_kernel, part, halves, masks, pieces, scale),
            [f32(blocks // halves // 2, tokens, PAIR), f32(blocks // halves * (part + 1), BLK)],
            "partial_eigen", 2 * macs // halves, input_bytes // halves,
            [IN_SMEM, IN_SMEM] + [IN_VMEM] * (2 + len(shards) + len(sums)),
            [pltpu.VMEM((blocks // halves // 2, PAIR, PAIR), jnp.bfloat16)],
        )(me, side, act_here, grad_here, *shards, *sums)
        powers.append(power)
    if pieces == 4:
        sent[2] = call(
            functools.partial(relay_kernel, coded[0]), message, "relay_chunk", 0, 12 * own.size,
            [IN_VMEM, IN_VMEM],
            [pltpu.VMEM((scale_rows(0, blocks), BLK), jnp.float32)] * 2,
        )(*after([grams[1], relayed], sums))
    sums = share(sums[0], "dp", direct)
    if pieces == 4:
        sums = after(sums, (middle, sent[2]))
    eigen, totals = call(
        functools.partial(combine_kernel, halves, act_blocks // halves),
        [f32(blocks, BLK), f32(2, BLK)],
        "combine_eigen", 0, 4 * blocks * BLK * pieces, [IN_VMEM] * len(sums),
    )(*sums)
    arrived = {}
    sent.pop(3, None)
    for mask in sent:
        arrived[mask] = swap(after([sent[mask]], totals)[0], "dp", mask)
    totals = share(totals, "owner", direct)
    weights = call(
        functools.partial(weight_kernel, halves, act_blocks // halves),
        f32(2, tokens), "partial_weights", 0, 4 * tokens * blocks * BLK,
        [IN_VMEM] * (1 + halves + len(totals)),
        [
            pltpu.VMEM((blocks, BLK), jnp.float32),
            pltpu.VMEM((tokens, BLK), jnp.float32),
            pltpu.VMEM((tokens, BLK), jnp.float32),
        ],
    )(eigen, *powers, *totals)
    weights = share(weights, "owner", direct)

    def tops_of(count):
        return [pltpu.VMEM((scale_rows(0, blocks), BLK), jnp.float32)] * count

    eigens = [f32(act_blocks, BLK), f32(grad_blocks, BLK)]
    if pieces == 4:
        own, *eigens = call(
            functools.partial(add_kernel, [(None, 0, blocks)], halves),
            [f32(*own.shape), *eigens], "add_chunk", 0, 12 * own.size,
            [IN_SMEM] + [IN_VMEM] * 3, tops_of(1),
        )(side, eigen, own, middle)
        weights[1:] = after(weights[1:], own)
    else:
        eigens = call(
            functools.partial(order_kernel, halves), eigens, "order_eigen", 0,
            8 * blocks * BLK, [IN_SMEM, IN_VMEM],
        )(side, eigen)
    chunks = list(arrived.values())
    if chunks:
        *covariance, token_scores = call(
            functools.partial(last_add_kernel, [(None, 0, blocks)] * len(chunks), len(weights)),
            [f32(act_blocks, rows, BLK), f32(grad_blocks, rows, BLK), f32(1, tokens)],
            "last_sums", 0, 16 * own.size, [IN_VMEM] * (1 + len(chunks) + len(weights)),
            [
                *tops_of(len(chunks)),
                pltpu.VMEM(own.shape, jnp.float32),
                pltpu.VMEM((1, tokens), jnp.float32),
                pltpu.SemaphoreType.DMA((blocks // GROUP + 1,)),
            ],
            out_spec=[pl.BlockSpec(memory_space=pl.ANY)] * 3,
        )(own, *chunks, *weights)
    else:
        covariance = own[:act_blocks], own[act_blocks:]
        token_scores = call(
            score_kernel, f32(1, tokens), "token_scores", 0, 8 * tokens, [IN_VMEM] * len(weights)
        )(*weights)
    return (
        *covariance,
        *[eigen.reshape(-1) for eigen in eigens],
        token_scores.reshape(-1),
    )


def solution(mesh):
    return jax.shard_map(
        local,
        mesh=mesh,
        in_specs=(
            P(("groups", "dp"), "owner"),
            P(("groups", "dp"), "owner"),
            P("owner", "dp", None),
            P("owner", "dp", None),
        ),
        out_specs=(
            P(("groups", "owner"), "dp", None),
            P(("groups", "owner"), "dp", None),
            P(("groups", "owner")),
            P(("groups", "owner")),
            P(("groups", "dp")),
        ),
        check_vma=False,
    )
```

```python
import functools

import jax
import jax.numpy as jnp
from jax import lax
from jax.experimental import pallas as pl
from jax.experimental.pallas import tpu as pltpu
from jax.sharding import PartitionSpec as P

D = 4096
FF = 14336
BLK = 128
PAIR = 2 * BLK
GROUP = 4
TILE = 64
VMEM_LIMIT = 24 * 1024 * 1024
CODE_TOP = 2.0**7.875
SMALLEST = 1e-36

damp_root = 0.31622776601683794
contract_rows = (((0,), (0,)), ((), ()))
contract_inner = (((1,), (0,)), ((), ()))
contract_lanes = (((1,), (1,)), ((), ()))

IN_VMEM = pl.BlockSpec(memory_space=pltpu.VMEM)
IN_SMEM = pl.BlockSpec(memory_space=pltpu.SMEM)
IN_HBM = pl.BlockSpec(memory_space=pltpu.HBM)


def scale_rows(first, end):
    return 16 * pl.cdiv(end - first, 16)


def call(
    kernel, out_shape, name, flops, bytes_accessed, in_specs, scratch_shapes=(),
    out_spec=None,
):
    return pl.pallas_call(
        kernel,
        out_shape=out_shape,
        in_specs=in_specs,
        out_specs=out_spec or jax.tree.map(lambda _: IN_VMEM, out_shape),
        scratch_shapes=scratch_shapes,
        compiler_params=pltpu.CompilerParams(vmem_limit_bytes=VMEM_LIMIT),
        cost_estimate=pl.CostEstimate(
            flops=flops, bytes_accessed=bytes_accessed, transcendentals=0
        ),
        name=name,
    )


def in_hbm(value):
    return pltpu.with_memory_space_constraint(value, pltpu.HBM)


def f32(*shape):
    return jax.ShapeDtypeStruct(shape, jnp.float32)


def bf16(*shape):
    return jax.ShapeDtypeStruct(shape, jnp.bfloat16)


def encode(values):
    power = values * values
    power = power * power
    power = power * power
    power = power * power
    return jnp.where(values < 0.0, -power, power).astype(jnp.bfloat16)


def top_of(values):
    top = jnp.maximum(jnp.max(jnp.abs(values), axis=0, keepdims=True), SMALLEST)
    return (top * (1.0 + 2.0**-8)).astype(jnp.bfloat16).astype(jnp.float32)


def decode(coded):
    coded = coded.astype(jnp.float32)
    root = jnp.abs(coded)
    for _ in range(4):
        root = lax.rsqrt(root)
    return jnp.where(coded > 0.0, root, jnp.where(coded < 0.0, -root, 0.0))


def pack_kernel(side_ref, act_ref, grad_ref, *refs):
    *out_refs, sems = refs
    side = side_ref[0]
    blocks = out_refs[0].shape[0]
    copies = []
    for out_ref in reversed(out_refs):
        halves = blocks // out_ref.shape[0]
        at = 0
        for ref in (act_ref, grad_ref):
            count = ref.shape[0] // halves
            copies.append(
                pltpu.make_async_copy(
                    ref.at[pl.ds(side * count if halves > 1 else 0, count)],
                    out_ref.at[pl.ds(at, count)],
                    sems.at[len(copies)],
                )
            )
            at += count
    for copy in copies:
        copy.start()
    for copy in copies:
        copy.wait()


def gram_kernel(pieces, messages, scale, me_ref, act_hbm, grad_hbm, act_ref, grad_ref, *refs):
    refs, (whole, tops, sems) = refs[:-3], refs[-3:]
    plain_refs, sent_refs = refs[: len(refs) - len(messages)], refs[len(refs) - len(messages) :]
    rows = BLK // pieces
    me = me_ref[0]
    steps = []
    for source, target in ((act_hbm, act_ref), (grad_hbm, grad_ref)):
        for first in range(0, source.shape[1], GROUP * BLK):
            columns = slice(first, first + GROUP * BLK)
            copy = pltpu.make_async_copy(
                source.at[:, columns], target.at[:, columns], sems.at[len(steps)]
            )
            copy.start()
            steps.append((target, columns, copy))
    tops[...] = jnp.zeros_like(tops)
    for step, (ref, columns, copy) in enumerate(steps):
        copy.wait()
        for offset in range(GROUP):
            block = step * GROUP + offset
            at = columns.start + offset * BLK
            values = ref[:, at : at + BLK]
            gram = scale * lax.dot_general(
                values, values, contract_rows, preferred_element_type=jnp.float32
            )
            if pieces == 1:
                plain_refs[0][block] = gram
                continue
            whole[offset] = gram
            for ref_at, mask in zip(plain_refs, (0, 2)):
                row = pl.multiple_of((me ^ mask) * rows, rows)
                ref_at[block] = whole[offset, pl.ds(row, rows), :]
            top = top_of(gram)
            tops[block : block + 1, :] = top
            gain = CODE_TOP / top
            for sent_ref, (mask, first, end) in zip(sent_refs, messages):
                if first <= block < end:
                    row = pl.multiple_of((me ^ mask) * rows, rows)
                    place = slice((block - first) * rows, (block - first + 1) * rows)
                    sent_ref[place, :] = encode(whole[offset, pl.ds(row, rows), :] * gain)
    for sent_ref, (_, first, end) in zip(sent_refs, messages):
        sent_ref[(end - first) * rows :, :] = tops[
            first : first + scale_rows(first, end), :
        ].astype(jnp.bfloat16)


def add_group(messages, rows, own_ref, sent_refs, tops_refs, step):
    for block in range(step * GROUP, (step + 1) * GROUP):
        total = own_ref[block]
        for (_, first, end), sent_ref, tops in zip(messages, sent_refs, tops_refs):
            if first <= block < end:
                at = block - first
                values = decode(sent_ref[at * rows : (at + 1) * rows, :])
                total = total + values * tops[at : at + 1, :]
        yield block, total


def load_tops(messages, rows, sent_refs, tops_refs):
    for (_, first, end), sent_ref, tops in zip(messages, sent_refs, tops_refs):
        tops[...] = sent_ref[(end - first) * rows :, :].astype(jnp.float32) * (1.0 / CODE_TOP)


def add_kernel(messages, halves, side_ref, eigen_ref, own_ref, *refs):
    sent_refs, refs = refs[: len(messages)], refs[len(messages) :]
    sum_ref, act_eigen_ref, grad_eigen_ref, *tops_refs = refs
    order_kernel(halves, side_ref, eigen_ref, act_eigen_ref, grad_eigen_ref)
    blocks, rows, _ = own_ref.shape
    load_tops(messages, rows, sent_refs, tops_refs)
    for step in range(blocks // GROUP):
        for block, total in add_group(messages, rows, own_ref, sent_refs, tops_refs, step):
            sum_ref[block] = total


def relay_kernel(message, far_ref, relayed_ref, sent_ref, relayed_tops, tops):
    messages = (message,)
    blocks, rows, _ = far_ref.shape
    load_tops(messages, rows, (relayed_ref,), (relayed_tops,))
    tops[...] = jnp.zeros_like(tops)
    for step in range(blocks // GROUP):
        for block, total in add_group(
            messages, rows, far_ref, (relayed_ref,), (relayed_tops,), step
        ):
            top = top_of(total)
            tops[block : block + 1, :] = top
            sent_ref[block * rows : (block + 1) * rows, :] = encode(total * (CODE_TOP / top))
    sent_ref[blocks * rows :, :] = tops[...].astype(jnp.bfloat16)


def last_add_kernel(messages, owners, own_ref, *refs):
    sent_refs, refs = refs[: len(messages)], refs[len(messages) :]
    weight_refs, refs = refs[:owners], refs[owners:]
    act_ref, grad_ref, score_ref, *tops_refs, sums, scores, sems = refs
    blocks, rows, _ = own_ref.shape
    score_kernel(*weight_refs, scores)
    copies = [pltpu.make_async_copy(scores, score_ref, sems.at[blocks // GROUP])]
    copies[0].start()
    load_tops(messages, rows, sent_refs, tops_refs)
    for step in range(blocks // GROUP):
        for block, total in add_group(messages, rows, own_ref, sent_refs, tops_refs, step):
            sums[block] = total
        first = step * GROUP
        ref, at = act_ref, first
        if first >= act_ref.shape[0]:
            ref, at = grad_ref, first - act_ref.shape[0]
        copies.append(
            pltpu.make_async_copy(
                sums.at[pl.ds(first, GROUP)], ref.at[pl.ds(at, GROUP)], sems.at[step]
            )
        )
        copies[-1].start()
    for copy in copies:
        copy.wait()


def pairs_of(part, side, halves, act_ref, grad_ref):
    half = lax.rem(side + part, halves)
    for ref in (act_ref, grad_ref):
        count = ref.shape[1] // PAIR // halves
        for pair in range(count):
            yield ref, pl.multiple_of((half * count + pair) * PAIR, PAIR)


def eigen_kernel(part, halves, masks, pieces, scale, me_ref, side_ref, act_ref, grad_ref, *refs):
    *shard_refs, power_ref, sums_ref, basis_ref = refs
    me, side = me_ref[0], side_ref[0]
    rows = BLK // pieces
    done = 0
    if part:
        *shard_refs, done_ref = shard_refs
        done = done_ref.shape[0]
        sums_ref[:done] = done_ref[...]
    half = lax.rem(side + part, halves)
    act_half = act_ref.shape[1] // BLK // halves
    grad_half = grad_ref.shape[1] // BLK // halves
    basis_ref[...] = jnp.zeros_like(basis_ref)
    for mask, ref in zip(masks, shard_refs):
        whole = halves > 1 and ref.shape[0] == halves * (act_half + grad_half)
        for block in range(act_half + grad_half):
            at = block
            if whole and block < act_half:
                at = half * act_half + block
            elif whole:
                at = (halves - 1) * act_half + half * grad_half + block
            corner = block % 2
            row = pl.multiple_of(corner * BLK + (me ^ mask) * rows, rows)
            columns = slice(corner * BLK, (corner + 1) * BLK)
            basis_ref[block // 2, pl.ds(row, rows), columns] = ref[at]

    for pair, (ref, column) in enumerate(pairs_of(part, side, halves, act_ref, grad_ref)):
        projected = lax.dot_general(
            ref[:, pl.ds(column, PAIR)],
            basis_ref[pair],
            contract_inner,
            preferred_element_type=jnp.float32,
        )
        power = projected * projected
        power_ref[pair] = power
        sums = scale * jnp.sum(power, axis=0, keepdims=True)
        row = done + 2 * pair
        sums_ref[row : row + 1, :] = sums[:, :BLK]
        sums_ref[row + 1 : row + 2, :] = sums[:, BLK:]


def combine_kernel(halves, act_half, *refs):
    *sums_refs, eigen_ref, total_ref = refs
    eigen = sums_refs[0][...]
    for sums_ref in sums_refs[1:]:
        eigen = eigen + sums_ref[...]
    eigen_ref[...] = eigen
    blocks_half = eigen.shape[0] // halves
    act_total = jnp.zeros((1, BLK), jnp.float32)
    grad_total = jnp.zeros((1, BLK), jnp.float32)
    for part in range(halves):
        first = part * blocks_half
        act_total += jnp.sum(eigen[first : first + act_half], axis=0, keepdims=True)
        grad_total += jnp.sum(eigen[first + act_half : first + blocks_half], axis=0, keepdims=True)
    total_ref[0:1, :] = act_total
    total_ref[1:2, :] = grad_total


def order_kernel(halves, side_ref, eigen_ref, act_eigen_ref, grad_eigen_ref):
    side = side_ref[0]
    act_half, grad_half = act_eigen_ref.shape[0] // halves, grad_eigen_ref.shape[0] // halves
    for part in range(halves):
        half = lax.rem(side + part, halves)
        first = part * (act_half + grad_half)
        middle = first + act_half
        act_eigen_ref[pl.ds(half * act_half, act_half), :] = eigen_ref[first:middle]
        grad_eigen_ref[pl.ds(half * grad_half, grad_half), :] = eigen_ref[
            middle : middle + grad_half
        ]


def weight_kernel(halves, act_half, eigen_ref, *refs):
    *refs, weight_ref, inverse, act_sum, grad_sum = refs
    power_refs, total_refs = refs[:halves], refs[halves:]
    totals = total_refs[0][...]
    for total_ref in total_refs[1:]:
        totals = totals + total_ref[...]
    totals = jnp.sum(totals, axis=1, keepdims=True)
    blocks_half = eigen_ref.shape[0] // halves
    for part in range(halves):
        first = part * blocks_half
        act = slice(first, first + act_half)
        grad = slice(first + act_half, first + blocks_half)
        inverse[act] = 1.0 / (eigen_ref[act] + totals[0:1] * (damp_root / D))
        inverse[grad] = 1.0 / (eigen_ref[grad] + totals[1:2] * (damp_root / FF))
    tokens = act_sum.shape[0]

    @pl.loop(0, tokens // TILE)
    def _(tile):
        here = pl.ds(pl.multiple_of(tile * TILE, TILE), TILE)
        sums = [jnp.zeros((TILE, BLK), jnp.float32), jnp.zeros((TILE, BLK), jnp.float32)]
        for part, power_ref in enumerate(power_refs):
            for pair in range(power_ref.shape[0]):
                which = 0 if 2 * pair < act_half else 1
                for side in range(2):
                    row = part * blocks_half + 2 * pair + side
                    power = power_ref[pair, here, side * BLK : (side + 1) * BLK]
                    sums[which] += power * inverse[row : row + 1, :]
        act_sum[here, :], grad_sum[here, :] = sums

    ones = jnp.ones((8, BLK), jnp.float32)
    for index, total in enumerate((act_sum, grad_sum)):
        sums = lax.dot_general(
            ones,
            total[...],
            contract_lanes,
            precision=lax.Precision.HIGHEST,
            preferred_element_type=jnp.float32,
        )
        weight_ref[index : index + 1, :] = sums[0:1]


def score_kernel(*refs):
    *weight_refs, score_ref = refs
    weights = weight_refs[0][...]
    for weight_ref in weight_refs[1:]:
        weights = weights + weight_ref[...]
    score_ref[...] = weights[0:1] * weights[1:2] * (1.0 / (D * FF))


def swap(value, axis, mask):
    count = lax.axis_size(axis)
    return lax.ppermute(value, axis, [(i, i ^ mask) for i in range(count)])


def share(value, axis, direct):
    if not direct:
        return [lax.psum(value, axis)]
    return [value] + [swap(value, axis, mask) for mask in reversed(range(1, lax.axis_size(axis)))]


def after(values, done):
    return list(lax.optimization_barrier((tuple(values), done))[0])


def local(activations, gradients, basis_act, basis_grad):
    tokens = activations.shape[0]
    act_blocks, grad_blocks = basis_act.shape[0], basis_grad.shape[0]
    blocks = act_blocks + grad_blocks
    dp, owners = lax.axis_size("dp"), lax.axis_size("owner")
    scale = 1.0 / (tokens * dp)
    direct = dp in (2, 4) and owners in (1, 2, 4)
    pieces = dp if direct else 1
    halves = 2 if pieces == 4 and lax.axis_size("groups") == 2 else 1
    rows = BLK // pieces
    me = jnp.full((1,), lax.axis_index("dp") if direct else 0, jnp.int32)
    side = jnp.full((1,), lax.axis_index("groups"), jnp.int32)
    macs = tokens * blocks * BLK * BLK
    input_bytes = 2 * tokens * blocks * BLK
    if direct:
        shards = call(
            pack_kernel,
            [bf16(blocks // part, rows, BLK) for part in range(1, halves + 1)],
            "pack_basis", 0, 2 * blocks * rows * BLK,
            [IN_SMEM, IN_HBM, IN_HBM], [pltpu.SemaphoreType.DMA((2 * halves,))],
        )(side, in_hbm(basis_act), in_hbm(basis_grad))
        near = [shards[0]]
        far = {mask: swap(shards[-1], "dp", mask) for mask in range(pieces - 1, 0, -1)}
    else:
        near = [
            jnp.concatenate(
                [lax.all_gather(part, "dp", axis=1, tiled=True) for part in (basis_act, basis_grad)]
            )
        ]
        far = {}
    masks = [*range(len(near)), *far]

    message = bf16(blocks * rows + scale_rows(0, blocks), BLK)
    whole_range = (0, blocks)
    coded = {4: [(3, *whole_range), (1, *whole_range)], 2: [(1, *whole_range)], 1: []}[pieces]
    plain = 2 if pieces == 4 else 1
    act_here, grad_here, *grams = call(
        functools.partial(gram_kernel, pieces, coded, scale),
        [
            bf16(*activations.shape),
            bf16(*gradients.shape),
            *[f32(blocks, rows, BLK)] * plain,
            *[message] * len(coded),
        ],
        "partial_gram", 4 * macs, input_bytes,
        [IN_SMEM, IN_HBM, IN_HBM],
        [
            pltpu.VMEM((GROUP, BLK, BLK), jnp.float32),
            pltpu.VMEM((scale_rows(0, blocks), BLK), jnp.float32),
            pltpu.SemaphoreType.DMA((blocks // GROUP,)),
        ],
    )(me, in_hbm(activations), in_hbm(gradients))
    own = grams[0]
    sent = {message[0]: chunk for message, chunk in zip(coded, grams[plain:])}
    if not direct:
        own = lax.psum_scatter(own, "dp", scatter_dimension=1, tiled=True)
    if pieces == 4:
        middle = lax.ppermute(sent[3], "dp", [(1, 2), (2, 1)])
        relayed = lax.ppermute(sent[3], "dp", [(0, 1), (3, 2)])

    parts = [[*near, *far.values()]]
    if halves == 2:
        swapped = [swap(after([part], own)[0], "groups", 1) for part in far.values()]
        parts.append([*near, *swapped])
    powers, sums = [], []
    for part, shards in enumerate(parts):
        power, *sums = call(
            functools.partial(eigen_kernel, part, halves, masks, pieces, scale),
            [f32(blocks // halves // 2, tokens, PAIR), f32(blocks // halves * (part + 1), BLK)],
            "partial_eigen", 2 * macs // halves, input_bytes // halves,
            [IN_SMEM, IN_SMEM] + [IN_VMEM] * (2 + len(shards) + len(sums)),
            [pltpu.VMEM((blocks // halves // 2, PAIR, PAIR), jnp.bfloat16)],
        )(me, side, act_here, grad_here, *shards, *sums)
        powers.append(power)
    if pieces == 4:
        sent[2] = call(
            functools.partial(relay_kernel, coded[0]), message, "relay_chunk", 0, 12 * own.size,
            [IN_VMEM, IN_VMEM],
            [pltpu.VMEM((scale_rows(0, blocks), BLK), jnp.float32)] * 2,
        )(*after([grams[1], relayed], sums))
    sums = share(sums[0], "dp", direct)
    if pieces == 4:
        sums = after(sums, (middle, sent[2]))
    eigen, totals = call(
        functools.partial(combine_kernel, halves, act_blocks // halves),
        [f32(blocks, BLK), f32(2, BLK)],
        "combine_eigen", 0, 4 * blocks * BLK * pieces, [IN_VMEM] * len(sums),
    )(*sums)
    arrived = {}
    sent.pop(3, None)
    for mask in sent:
        arrived[mask] = swap(after([sent[mask]], totals)[0], "dp", mask)
    totals = share(totals, "owner", direct)
    weights = call(
        functools.partial(weight_kernel, halves, act_blocks // halves),
        f32(2, tokens), "partial_weights", 0, 4 * tokens * blocks * BLK,
        [IN_VMEM] * (1 + halves + len(totals)),
        [
            pltpu.VMEM((blocks, BLK), jnp.float32),
            pltpu.VMEM((tokens, BLK), jnp.float32),
            pltpu.VMEM((tokens, BLK), jnp.float32),
        ],
    )(eigen, *powers, *totals)
    weights = share(weights, "owner", direct)

    def tops_of(count):
        return [pltpu.VMEM((scale_rows(0, blocks), BLK), jnp.float32)] * count

    eigens = [f32(act_blocks, BLK), f32(grad_blocks, BLK)]
    if pieces == 4:
        own, *eigens = call(
            functools.partial(add_kernel, [(None, 0, blocks)], halves),
            [f32(*own.shape), *eigens], "add_chunk", 0, 12 * own.size,
            [IN_SMEM] + [IN_VMEM] * 3, tops_of(1),
        )(side, eigen, own, middle)
        weights[1:] = after(weights[1:], own)
    else:
        eigens = call(
            functools.partial(order_kernel, halves), eigens, "order_eigen", 0,
            8 * blocks * BLK, [IN_SMEM, IN_VMEM],
        )(side, eigen)
    chunks = list(arrived.values())[::-1]
    if chunks:
        *covariance, token_scores = call(
            functools.partial(last_add_kernel, [(None, 0, blocks)] * len(chunks), len(weights)),
            [f32(act_blocks, rows, BLK), f32(grad_blocks, rows, BLK), f32(1, tokens)],
            "last_sums", 0, 16 * own.size, [IN_VMEM] * (1 + len(chunks) + len(weights)),
            [
                *tops_of(len(chunks)),
                pltpu.VMEM(own.shape, jnp.float32),
                pltpu.VMEM((1, tokens), jnp.float32),
                pltpu.SemaphoreType.DMA((blocks // GROUP + 1,)),
            ],
            out_spec=[pl.BlockSpec(memory_space=pl.ANY)] * 3,
        )(own, *chunks, *weights)
    else:
        covariance = own[:act_blocks], own[act_blocks:]
        token_scores = call(
            score_kernel, f32(1, tokens), "token_scores", 0, 8 * tokens, [IN_VMEM] * len(weights)
        )(*weights)
    return (
        *covariance,
        *[eigen.reshape(-1) for eigen in eigens],
        token_scores.reshape(-1),
    )


def solution(mesh):
    return jax.shard_map(
        local,
        mesh=mesh,
        in_specs=(
            P(("groups", "dp"), "owner"),
            P(("groups", "dp"), "owner"),
            P("owner", "dp", None),
            P("owner", "dp", None),
        ),
        out_specs=(
            P(("groups", "owner"), "dp", None),
            P(("groups", "owner"), "dp", None),
            P(("groups", "owner")),
            P(("groups", "owner")),
            P(("groups", "dp")),
        ),
        check_vma=False,
    )
```

```python
import functools

import jax
import jax.numpy as jnp
from jax import lax
from jax.experimental import pallas as pl
from jax.experimental.pallas import tpu as pltpu
from jax.sharding import PartitionSpec as P

D = 4096
FF = 14336
BLK = 128
PAIR = 2 * BLK
GROUP = 4
TILE = 64
VMEM_LIMIT = 24 * 1024 * 1024
CODE_TOP = 2.0**7.875
SMALLEST = 1e-36

damp_root = 0.31622776601683794
contract_rows = (((0,), (0,)), ((), ()))
contract_inner = (((1,), (0,)), ((), ()))
contract_lanes = (((1,), (1,)), ((), ()))

IN_VMEM = pl.BlockSpec(memory_space=pltpu.VMEM)
IN_SMEM = pl.BlockSpec(memory_space=pltpu.SMEM)
IN_HBM = pl.BlockSpec(memory_space=pltpu.HBM)


def scale_rows(first, end):
    return 16 * pl.cdiv(end - first, 16)


def call(
    kernel, out_shape, name, flops, bytes_accessed, in_specs, scratch_shapes=(),
    out_spec=None,
):
    return pl.pallas_call(
        kernel,
        out_shape=out_shape,
        in_specs=in_specs,
        out_specs=out_spec or jax.tree.map(lambda _: IN_VMEM, out_shape),
        scratch_shapes=scratch_shapes,
        compiler_params=pltpu.CompilerParams(vmem_limit_bytes=VMEM_LIMIT),
        cost_estimate=pl.CostEstimate(
            flops=flops, bytes_accessed=bytes_accessed, transcendentals=0
        ),
        name=name,
    )


def in_hbm(value):
    return pltpu.with_memory_space_constraint(value, pltpu.HBM)


def f32(*shape):
    return jax.ShapeDtypeStruct(shape, jnp.float32)


def bf16(*shape):
    return jax.ShapeDtypeStruct(shape, jnp.bfloat16)


def encode(values):
    power = values * values
    power = power * power
    power = power * power
    power = power * power
    return jnp.where(values < 0.0, -power, power).astype(jnp.bfloat16)


def top_of(values):
    top = jnp.maximum(jnp.max(jnp.abs(values), axis=0, keepdims=True), SMALLEST)
    return (top * (1.0 + 2.0**-8)).astype(jnp.bfloat16).astype(jnp.float32)


def decode(coded):
    coded = coded.astype(jnp.float32)
    root = jnp.abs(coded)
    for _ in range(4):
        root = lax.rsqrt(root)
    return jnp.where(coded > 0.0, root, jnp.where(coded < 0.0, -root, 0.0))


def pack_kernel(side_ref, act_ref, grad_ref, *refs):
    *out_refs, sems = refs
    side = side_ref[0]
    blocks = out_refs[0].shape[0]
    copies = []
    for out_ref in reversed(out_refs):
        halves = blocks // out_ref.shape[0]
        at = 0
        for ref in (act_ref, grad_ref):
            count = ref.shape[0] // halves
            copies.append(
                pltpu.make_async_copy(
                    ref.at[pl.ds(side * count if halves > 1 else 0, count)],
                    out_ref.at[pl.ds(at, count)],
                    sems.at[len(copies)],
                )
            )
            at += count
    for copy in copies:
        copy.start()
    for copy in copies:
        copy.wait()


def gram_kernel(pieces, messages, scale, me_ref, act_hbm, grad_hbm, act_ref, grad_ref, *refs):
    refs, (whole, tops, sems) = refs[:-3], refs[-3:]
    plain_refs, sent_refs = refs[: len(refs) - len(messages)], refs[len(refs) - len(messages) :]
    rows = BLK // pieces
    me = me_ref[0]
    steps = []
    for source, target in ((act_hbm, act_ref), (grad_hbm, grad_ref)):
        for first in range(0, source.shape[1], GROUP * BLK):
            columns = slice(first, first + GROUP * BLK)
            copy = pltpu.make_async_copy(
                source.at[:, columns], target.at[:, columns], sems.at[len(steps)]
            )
            copy.start()
            steps.append((target, columns, copy))
    tops[...] = jnp.zeros_like(tops)
    for step, (ref, columns, copy) in enumerate(steps):
        copy.wait()
        for offset in range(GROUP):
            block = step * GROUP + offset
            at = columns.start + offset * BLK
            values = ref[:, at : at + BLK]
            gram = scale * lax.dot_general(
                values, values, contract_rows, preferred_element_type=jnp.float32
            )
            if pieces == 1:
                plain_refs[0][block] = gram
                continue
            whole[offset] = gram
            for ref_at, mask in zip(plain_refs, (0, 2)):
                row = pl.multiple_of((me ^ mask) * rows, rows)
                ref_at[block] = whole[offset, pl.ds(row, rows), :]
            top = top_of(gram)
            tops[block : block + 1, :] = top
            gain = CODE_TOP / top
            for sent_ref, (mask, first, end) in zip(sent_refs, messages):
                if first <= block < end:
                    row = pl.multiple_of((me ^ mask) * rows, rows)
                    place = slice((block - first) * rows, (block - first + 1) * rows)
                    sent_ref[place, :] = encode(whole[offset, pl.ds(row, rows), :] * gain)
    for sent_ref, (_, first, end) in zip(sent_refs, messages):
        sent_ref[(end - first) * rows :, :] = tops[
            first : first + scale_rows(first, end), :
        ].astype(jnp.bfloat16)


def add_group(messages, rows, own_ref, sent_refs, tops_refs, step):
    for block in range(step * GROUP, (step + 1) * GROUP):
        total = own_ref[block]
        for (_, first, end), sent_ref, tops in zip(messages, sent_refs, tops_refs):
            if first <= block < end:
                at = block - first
                values = decode(sent_ref[at * rows : (at + 1) * rows, :])
                total = total + values * tops[at : at + 1, :]
        yield block, total


def load_tops(messages, rows, sent_refs, tops_refs):
    for (_, first, end), sent_ref, tops in zip(messages, sent_refs, tops_refs):
        tops[...] = sent_ref[(end - first) * rows :, :].astype(jnp.float32) * (1.0 / CODE_TOP)


def add_kernel(messages, halves, side_ref, eigen_ref, own_ref, *refs):
    sent_refs, refs = refs[: len(messages)], refs[len(messages) :]
    sum_ref, act_eigen_ref, grad_eigen_ref, *tops_refs = refs
    order_kernel(halves, side_ref, eigen_ref, act_eigen_ref, grad_eigen_ref)
    blocks, rows, _ = own_ref.shape
    load_tops(messages, rows, sent_refs, tops_refs)
    for step in range(blocks // GROUP):
        for block, total in add_group(messages, rows, own_ref, sent_refs, tops_refs, step):
            sum_ref[block] = total


def relay_kernel(message, core_ref, far_ref, relayed_ref, near_ref, first_ref, second_ref, *refs):
    summed, relayed_tops, tops = refs
    messages = (message,)
    blocks, rows, _ = far_ref.shape
    load_tops(messages, rows, (relayed_ref,), (relayed_tops,))
    tops[...] = jnp.zeros_like(tops)
    for step in range(blocks // GROUP):
        for block, total in add_group(
            messages, rows, far_ref, (relayed_ref,), (relayed_tops,), step
        ):
            top = top_of(total)
            tops[block : block + 1, :] = top
            summed[block * rows : (block + 1) * rows, :] = encode(total * (CODE_TOP / top))
    summed[blocks * rows :, :] = tops[...].astype(jnp.bfloat16)

    @pl.when(core_ref[0] == 0)
    def _():
        first_ref[...] = summed[...]
        second_ref[...] = near_ref[...]

    @pl.when(core_ref[0] != 0)
    def _():
        first_ref[...] = near_ref[...]
        second_ref[...] = summed[...]


def last_add_kernel(messages, owners, own_ref, *refs):
    sent_refs, refs = refs[: len(messages)], refs[len(messages) :]
    weight_refs, refs = refs[:owners], refs[owners:]
    act_ref, grad_ref, score_ref, *tops_refs, sums, scores, sems = refs
    blocks, rows, _ = own_ref.shape
    score_kernel(*weight_refs, scores)
    copies = [pltpu.make_async_copy(scores, score_ref, sems.at[blocks // GROUP])]
    copies[0].start()
    load_tops(messages, rows, sent_refs, tops_refs)
    for step in range(blocks // GROUP):
        for block, total in add_group(messages, rows, own_ref, sent_refs, tops_refs, step):
            sums[block] = total
        first = step * GROUP
        ref, at = act_ref, first
        if first >= act_ref.shape[0]:
            ref, at = grad_ref, first - act_ref.shape[0]
        copies.append(
            pltpu.make_async_copy(
                sums.at[pl.ds(first, GROUP)], ref.at[pl.ds(at, GROUP)], sems.at[step]
            )
        )
        copies[-1].start()
    for copy in copies:
        copy.wait()


def pairs_of(part, side, halves, act_ref, grad_ref):
    half = lax.rem(side + part, halves)
    for ref in (act_ref, grad_ref):
        count = ref.shape[1] // PAIR // halves
        for pair in range(count):
            yield ref, pl.multiple_of((half * count + pair) * PAIR, PAIR)


def eigen_kernel(part, halves, masks, pieces, scale, me_ref, side_ref, act_ref, grad_ref, *refs):
    *shard_refs, power_ref, sums_ref, basis_ref = refs
    me, side = me_ref[0], side_ref[0]
    rows = BLK // pieces
    done = 0
    if part:
        *shard_refs, done_ref = shard_refs
        done = done_ref.shape[0]
        sums_ref[:done] = done_ref[...]
    half = lax.rem(side + part, halves)
    act_half = act_ref.shape[1] // BLK // halves
    grad_half = grad_ref.shape[1] // BLK // halves
    basis_ref[...] = jnp.zeros_like(basis_ref)
    for mask, ref in zip(masks, shard_refs):
        whole = halves > 1 and ref.shape[0] == halves * (act_half + grad_half)
        for block in range(act_half + grad_half):
            at = block
            if whole and block < act_half:
                at = half * act_half + block
            elif whole:
                at = (halves - 1) * act_half + half * grad_half + block
            corner = block % 2
            row = pl.multiple_of(corner * BLK + (me ^ mask) * rows, rows)
            columns = slice(corner * BLK, (corner + 1) * BLK)
            basis_ref[block // 2, pl.ds(row, rows), columns] = ref[at]

    for pair, (ref, column) in enumerate(pairs_of(part, side, halves, act_ref, grad_ref)):
        projected = lax.dot_general(
            ref[:, pl.ds(column, PAIR)],
            basis_ref[pair],
            contract_inner,
            preferred_element_type=jnp.float32,
        )
        power = projected * projected
        power_ref[pair] = power
        sums = scale * jnp.sum(power, axis=0, keepdims=True)
        row = done + 2 * pair
        sums_ref[row : row + 1, :] = sums[:, :BLK]
        sums_ref[row + 1 : row + 2, :] = sums[:, BLK:]


def combine_kernel(halves, act_half, *refs):
    *sums_refs, eigen_ref, total_ref = refs
    eigen = sums_refs[0][...]
    for sums_ref in sums_refs[1:]:
        eigen = eigen + sums_ref[...]
    eigen_ref[...] = eigen
    blocks_half = eigen.shape[0] // halves
    act_total = jnp.zeros((1, BLK), jnp.float32)
    grad_total = jnp.zeros((1, BLK), jnp.float32)
    for part in range(halves):
        first = part * blocks_half
        act_total += jnp.sum(eigen[first : first + act_half], axis=0, keepdims=True)
        grad_total += jnp.sum(eigen[first + act_half : first + blocks_half], axis=0, keepdims=True)
    total_ref[0:1, :] = act_total
    total_ref[1:2, :] = grad_total


def order_kernel(halves, side_ref, eigen_ref, act_eigen_ref, grad_eigen_ref):
    side = side_ref[0]
    act_half, grad_half = act_eigen_ref.shape[0] // halves, grad_eigen_ref.shape[0] // halves
    for part in range(halves):
        half = lax.rem(side + part, halves)
        first = part * (act_half + grad_half)
        middle = first + act_half
        act_eigen_ref[pl.ds(half * act_half, act_half), :] = eigen_ref[first:middle]
        grad_eigen_ref[pl.ds(half * grad_half, grad_half), :] = eigen_ref[
            middle : middle + grad_half
        ]


def weight_kernel(halves, act_half, eigen_ref, *refs):
    *refs, weight_ref, inverse, act_sum, grad_sum = refs
    power_refs, total_refs = refs[:halves], refs[halves:]
    totals = total_refs[0][...]
    for total_ref in total_refs[1:]:
        totals = totals + total_ref[...]
    totals = jnp.sum(totals, axis=1, keepdims=True)
    blocks_half = eigen_ref.shape[0] // halves
    for part in range(halves):
        first = part * blocks_half
        act = slice(first, first + act_half)
        grad = slice(first + act_half, first + blocks_half)
        inverse[act] = 1.0 / (eigen_ref[act] + totals[0:1] * (damp_root / D))
        inverse[grad] = 1.0 / (eigen_ref[grad] + totals[1:2] * (damp_root / FF))
    tokens = act_sum.shape[0]

    @pl.loop(0, tokens // TILE)
    def _(tile):
        here = pl.ds(pl.multiple_of(tile * TILE, TILE), TILE)
        sums = [jnp.zeros((TILE, BLK), jnp.float32), jnp.zeros((TILE, BLK), jnp.float32)]
        for part, power_ref in enumerate(power_refs):
            for pair in range(power_ref.shape[0]):
                which = 0 if 2 * pair < act_half else 1
                for side in range(2):
                    row = part * blocks_half + 2 * pair + side
                    power = power_ref[pair, here, side * BLK : (side + 1) * BLK]
                    sums[which] += power * inverse[row : row + 1, :]
        act_sum[here, :], grad_sum[here, :] = sums

    ones = jnp.ones((8, BLK), jnp.float32)
    for index, total in enumerate((act_sum, grad_sum)):
        sums = lax.dot_general(
            ones,
            total[...],
            contract_lanes,
            precision=lax.Precision.HIGHEST,
            preferred_element_type=jnp.float32,
        )
        weight_ref[index : index + 1, :] = sums[0:1]


def score_kernel(*refs):
    *weight_refs, score_ref = refs
    weights = weight_refs[0][...]
    for weight_ref in weight_refs[1:]:
        weights = weights + weight_ref[...]
    score_ref[...] = weights[0:1] * weights[1:2] * (1.0 / (D * FF))


def swap(value, axis, mask):
    count = lax.axis_size(axis)
    return lax.ppermute(value, axis, [(i, i ^ mask) for i in range(count)])


def share(value, axis, direct):
    if not direct:
        return [lax.psum(value, axis)]
    return [value] + [swap(value, axis, mask) for mask in reversed(range(1, lax.axis_size(axis)))]


def after(values, done):
    return list(lax.optimization_barrier((tuple(values), done))[0])


def local(activations, gradients, basis_act, basis_grad):
    tokens = activations.shape[0]
    act_blocks, grad_blocks = basis_act.shape[0], basis_grad.shape[0]
    blocks = act_blocks + grad_blocks
    dp, owners = lax.axis_size("dp"), lax.axis_size("owner")
    scale = 1.0 / (tokens * dp)
    direct = dp in (2, 4) and owners in (1, 2, 4)
    pieces = dp if direct else 1
    halves = 2 if pieces == 4 and lax.axis_size("groups") == 2 else 1
    rows = BLK // pieces
    me = jnp.full((1,), lax.axis_index("dp") if direct else 0, jnp.int32)
    side = jnp.full((1,), lax.axis_index("groups"), jnp.int32)
    macs = tokens * blocks * BLK * BLK
    input_bytes = 2 * tokens * blocks * BLK
    if direct:
        shards = call(
            pack_kernel,
            [bf16(blocks // part, rows, BLK) for part in range(1, halves + 1)],
            "pack_basis", 0, 2 * blocks * rows * BLK,
            [IN_SMEM, IN_HBM, IN_HBM], [pltpu.SemaphoreType.DMA((2 * halves,))],
        )(side, in_hbm(basis_act), in_hbm(basis_grad))
        near = [shards[0], swap(shards[0], "dp", 1)]
        far = {mask: swap(shards[-1], "dp", mask) for mask in range(pieces - 1, 1, -1)}
    else:
        near = [
            jnp.concatenate(
                [lax.all_gather(part, "dp", axis=1, tiled=True) for part in (basis_act, basis_grad)]
            )
        ]
        far = {}
    masks = [*range(len(near)), *far]

    message = bf16(blocks * rows + scale_rows(0, blocks), BLK)
    whole_range = (0, blocks)
    coded = {4: [(3, *whole_range), (1, *whole_range)], 2: [(1, *whole_range)], 1: []}[pieces]
    plain = 2 if pieces == 4 else 1
    act_here, grad_here, *grams = call(
        functools.partial(gram_kernel, pieces, coded, scale),
        [
            bf16(*activations.shape),
            bf16(*gradients.shape),
            *[f32(blocks, rows, BLK)] * plain,
            *[message] * len(coded),
        ],
        "partial_gram", 4 * macs, input_bytes,
        [IN_SMEM, IN_HBM, IN_HBM],
        [
            pltpu.VMEM((GROUP, BLK, BLK), jnp.float32),
            pltpu.VMEM((scale_rows(0, blocks), BLK), jnp.float32),
            pltpu.SemaphoreType.DMA((blocks // GROUP,)),
        ],
    )(me, in_hbm(activations), in_hbm(gradients))
    own = grams[0]
    sent = {message[0]: chunk for message, chunk in zip(coded, grams[plain:])}
    if not direct:
        own = lax.psum_scatter(own, "dp", scatter_dimension=1, tiled=True)
    if pieces == 4:
        middle = lax.ppermute(sent[3], "dp", [(1, 2), (2, 1)])
        relayed = lax.ppermute(sent[3], "dp", [(0, 1), (3, 2)])

    parts = [[*near, *far.values()]]
    if halves == 2:
        swapped = [swap(after([part], own)[0], "groups", 1) for part in far.values()]
        parts.append([*near, *swapped])
    powers, sums = [], []
    for part, shards in enumerate(parts):
        power, *sums = call(
            functools.partial(eigen_kernel, part, halves, masks, pieces, scale),
            [f32(blocks // halves // 2, tokens, PAIR), f32(blocks // halves * (part + 1), BLK)],
            "partial_eigen", 2 * macs // halves, input_bytes // halves,
            [IN_SMEM, IN_SMEM] + [IN_VMEM] * (2 + len(shards) + len(sums)),
            [pltpu.VMEM((blocks // halves // 2, PAIR, PAIR), jnp.bfloat16)],
        )(me, side, act_here, grad_here, *shards, *sums)
        powers.append(power)
    if pieces == 4:
        core = jnp.full((1,), lax.axis_index("owner") % 2, jnp.int32)
        far_chunk, relayed = after([grams[1], relayed], sums)
        late = call(
            functools.partial(relay_kernel, coded[0]), [message] * 2, "relay_chunk", 0, 16 * own.size,
            [IN_SMEM, IN_VMEM, IN_VMEM, IN_VMEM],
            [pltpu.VMEM(message.shape, jnp.bfloat16)]
            + [pltpu.VMEM((scale_rows(0, blocks), BLK), jnp.float32)] * 2,
        )(core, far_chunk, relayed, sent[1])
    sums = share(sums[0], "dp", direct)
    if pieces == 4:
        sums = after(sums, (middle, late))
    eigen, totals = call(
        functools.partial(combine_kernel, halves, act_blocks // halves),
        [f32(blocks, BLK), f32(2, BLK)],
        "combine_eigen", 0, 4 * blocks * BLK * pieces, [IN_VMEM] * len(sums),
    )(*sums)
    chunks = []
    if pieces == 4:
        for chunk, order in zip(late, ((2, 1), (1, 2))):
            ways = [
                (at * owners + owner, (at ^ order[owner % 2]) * owners + owner)
                for at in range(dp)
                for owner in range(owners)
            ]
            chunks.append(lax.ppermute(after([chunk], totals)[0], ("dp", "owner"), ways))
    elif pieces == 2:
        chunks.append(swap(after([sent[1]], totals)[0], "dp", 1))
    totals = share(totals, "owner", direct)
    weights = call(
        functools.partial(weight_kernel, halves, act_blocks // halves),
        f32(2, tokens), "partial_weights", 0, 4 * tokens * blocks * BLK,
        [IN_VMEM] * (1 + halves + len(totals)),
        [
            pltpu.VMEM((blocks, BLK), jnp.float32),
            pltpu.VMEM((tokens, BLK), jnp.float32),
            pltpu.VMEM((tokens, BLK), jnp.float32),
        ],
    )(eigen, *powers, *totals)
    weights = share(weights, "owner", direct)

    def tops_of(count):
        return [pltpu.VMEM((scale_rows(0, blocks), BLK), jnp.float32)] * count

    eigens = [f32(act_blocks, BLK), f32(grad_blocks, BLK)]
    if pieces == 4:
        own, *eigens = call(
            functools.partial(add_kernel, [(None, 0, blocks)], halves),
            [f32(*own.shape), *eigens], "add_chunk", 0, 12 * own.size,
            [IN_SMEM] + [IN_VMEM] * 3, tops_of(1),
        )(side, eigen, own, middle)
        weights[1:] = after(weights[1:], own)
    else:
        eigens = call(
            functools.partial(order_kernel, halves), eigens, "order_eigen", 0,
            8 * blocks * BLK, [IN_SMEM, IN_VMEM],
        )(side, eigen)
    chunks = chunks[::-1]
    if chunks:
        *covariance, token_scores = call(
            functools.partial(last_add_kernel, [(None, 0, blocks)] * len(chunks), len(weights)),
            [f32(act_blocks, rows, BLK), f32(grad_blocks, rows, BLK), f32(1, tokens)],
            "last_sums", 0, 16 * own.size, [IN_VMEM] * (1 + len(chunks) + len(weights)),
            [
                *tops_of(len(chunks)),
                pltpu.VMEM(own.shape, jnp.float32),
                pltpu.VMEM((1, tokens), jnp.float32),
                pltpu.SemaphoreType.DMA((blocks // GROUP + 1,)),
            ],
            out_spec=[pl.BlockSpec(memory_space=pl.ANY)] * 3,
        )(own, *chunks, *weights)
    else:
        covariance = own[:act_blocks], own[act_blocks:]
        token_scores = call(
            score_kernel, f32(1, tokens), "token_scores", 0, 8 * tokens, [IN_VMEM] * len(weights)
        )(*weights)
    return (
        *covariance,
        *[eigen.reshape(-1) for eigen in eigens],
        token_scores.reshape(-1),
    )


def solution(mesh):
    return jax.shard_map(
        local,
        mesh=mesh,
        in_specs=(
            P(("groups", "dp"), "owner"),
            P(("groups", "dp"), "owner"),
            P("owner", "dp", None),
            P("owner", "dp", None),
        ),
        out_specs=(
            P(("groups", "owner"), "dp", None),
            P(("groups", "owner"), "dp", None),
            P(("groups", "owner")),
            P(("groups", "owner")),
            P(("groups", "dp")),
        ),
        check_vma=False,
    )
```

```python
import functools

import jax
import jax.numpy as jnp
from jax import lax
from jax.experimental import pallas as pl
from jax.experimental.pallas import tpu as pltpu
from jax.sharding import PartitionSpec as P

D = 4096
FF = 14336
BLK = 128
PAIR = 2 * BLK
GROUP = 4
TILE = 64
VMEM_LIMIT = 24 * 1024 * 1024
CODE_TOP = 2.0**7.875
SMALLEST = 1e-36

damp_root = 0.31622776601683794
contract_rows = (((0,), (0,)), ((), ()))
contract_inner = (((1,), (0,)), ((), ()))
contract_lanes = (((1,), (1,)), ((), ()))

IN_VMEM = pl.BlockSpec(memory_space=pltpu.VMEM)
IN_SMEM = pl.BlockSpec(memory_space=pltpu.SMEM)
IN_HBM = pl.BlockSpec(memory_space=pltpu.HBM)


def scale_rows(first, end):
    return 16 * pl.cdiv(end - first, 16)


def call(
    kernel, out_shape, name, flops, bytes_accessed, in_specs, scratch_shapes=(),
    out_spec=None,
):
    return pl.pallas_call(
        kernel,
        out_shape=out_shape,
        in_specs=in_specs,
        out_specs=out_spec or jax.tree.map(lambda _: IN_VMEM, out_shape),
        scratch_shapes=scratch_shapes,
        compiler_params=pltpu.CompilerParams(vmem_limit_bytes=VMEM_LIMIT),
        cost_estimate=pl.CostEstimate(
            flops=flops, bytes_accessed=bytes_accessed, transcendentals=0
        ),
        name=name,
    )


def in_hbm(value):
    return pltpu.with_memory_space_constraint(value, pltpu.HBM)


def f32(*shape):
    return jax.ShapeDtypeStruct(shape, jnp.float32)


def bf16(*shape):
    return jax.ShapeDtypeStruct(shape, jnp.bfloat16)


def encode(values):
    power = values * values
    power = power * power
    power = power * power
    power = power * power
    return jnp.where(values < 0.0, -power, power).astype(jnp.bfloat16)


def top_of(values):
    top = jnp.maximum(jnp.max(jnp.abs(values), axis=0, keepdims=True), SMALLEST)
    return (top * (1.0 + 2.0**-8)).astype(jnp.bfloat16).astype(jnp.float32)


def decode(coded):
    coded = coded.astype(jnp.float32)
    root = jnp.abs(coded)
    for _ in range(4):
        root = lax.rsqrt(root)
    return jnp.where(coded > 0.0, root, jnp.where(coded < 0.0, -root, 0.0))


def pack_kernel(side_ref, owner_ref, act_ref, grad_ref, *refs):
    *out_refs, sems = refs
    side = side_ref[0]
    blocks = out_refs[0].shape[0]
    copies = []
    for out_ref in reversed(out_refs):
        halves = blocks // out_ref.shape[0]
        at = 0
        for ref in (act_ref, grad_ref):
            count = ref.shape[0] // halves
            copies.append(
                pltpu.make_async_copy(
                    ref.at[pl.ds(side * count if halves > 1 else 0, count)],
                    out_ref.at[pl.ds(at, count)],
                    sems.at[len(copies)],
                )
            )
            at += count
    for copy in copies:
        copy.start()
    for copy in copies:
        copy.wait()


def gram_kernel(pieces, messages, scale, me_ref, act_hbm, grad_hbm, act_ref, grad_ref, *refs):
    refs, (whole, tops, sems) = refs[:-3], refs[-3:]
    plain_refs, sent_refs = refs[: len(refs) - len(messages)], refs[len(refs) - len(messages) :]
    rows = BLK // pieces
    me = me_ref[0]
    steps = []
    for source, target in ((act_hbm, act_ref), (grad_hbm, grad_ref)):
        for first in range(0, source.shape[1], GROUP * BLK):
            columns = slice(first, first + GROUP * BLK)
            copy = pltpu.make_async_copy(
                source.at[:, columns], target.at[:, columns], sems.at[len(steps)]
            )
            copy.start()
            steps.append((target, columns, copy))
    tops[...] = jnp.zeros_like(tops)
    for step, (ref, columns, copy) in enumerate(steps):
        copy.wait()
        for offset in range(GROUP):
            block = step * GROUP + offset
            at = columns.start + offset * BLK
            values = ref[:, at : at + BLK]
            gram = scale * lax.dot_general(
                values, values, contract_rows, preferred_element_type=jnp.float32
            )
            if pieces == 1:
                plain_refs[0][block] = gram
                continue
            whole[offset] = gram
            for ref_at, mask in zip(plain_refs, (0, 2)):
                row = pl.multiple_of((me ^ mask) * rows, rows)
                ref_at[block] = whole[offset, pl.ds(row, rows), :]
            top = top_of(gram)
            tops[block : block + 1, :] = top
            gain = CODE_TOP / top
            for sent_ref, (mask, first, end) in zip(sent_refs, messages):
                if first <= block < end:
                    row = pl.multiple_of((me ^ mask) * rows, rows)
                    place = slice((block - first) * rows, (block - first + 1) * rows)
                    sent_ref[place, :] = encode(whole[offset, pl.ds(row, rows), :] * gain)
    for sent_ref, (_, first, end) in zip(sent_refs, messages):
        sent_ref[(end - first) * rows :, :] = tops[
            first : first + scale_rows(first, end), :
        ].astype(jnp.bfloat16)


def add_group(messages, rows, own_ref, sent_refs, tops_refs, step):
    for block in range(step * GROUP, (step + 1) * GROUP):
        total = own_ref[block]
        for (_, first, end), sent_ref, tops in zip(messages, sent_refs, tops_refs):
            if first <= block < end:
                at = block - first
                values = decode(sent_ref[at * rows : (at + 1) * rows, :])
                total = total + values * tops[at : at + 1, :]
        yield block, total


def load_tops(messages, rows, sent_refs, tops_refs):
    for (_, first, end), sent_ref, tops in zip(messages, sent_refs, tops_refs):
        tops[...] = sent_ref[(end - first) * rows :, :].astype(jnp.float32) * (1.0 / CODE_TOP)


def add_kernel(messages, halves, side_ref, eigen_ref, own_ref, *refs):
    sent_refs, refs = refs[: len(messages)], refs[len(messages) :]
    sum_ref, act_eigen_ref, grad_eigen_ref, *tops_refs = refs
    order_kernel(halves, side_ref, eigen_ref, act_eigen_ref, grad_eigen_ref)
    blocks, rows, _ = own_ref.shape
    load_tops(messages, rows, sent_refs, tops_refs)
    for step in range(blocks // GROUP):
        for block, total in add_group(messages, rows, own_ref, sent_refs, tops_refs, step):
            sum_ref[block] = total


def relay_kernel(message, owner_ref, far_ref, relayed_ref, near_ref, first_ref, second_ref, *refs):
    summed, relayed_tops, tops = refs
    messages = (message,)
    blocks, rows, _ = far_ref.shape
    load_tops(messages, rows, (relayed_ref,), (relayed_tops,))
    tops[...] = jnp.zeros_like(tops)
    for step in range(blocks // GROUP):
        for block, total in add_group(
            messages, rows, far_ref, (relayed_ref,), (relayed_tops,), step
        ):
            top = top_of(total)
            tops[block : block + 1, :] = top
            summed[block * rows : (block + 1) * rows, :] = encode(total * (CODE_TOP / top))
    summed[blocks * rows :, :] = tops[...].astype(jnp.bfloat16)

    core = owner_ref[0] & 1

    @pl.when(core == 0)
    def _():
        first_ref[...] = summed[...]
        second_ref[...] = near_ref[...]

    @pl.when(core != 0)
    def _():
        first_ref[...] = near_ref[...]
        second_ref[...] = summed[...]


def last_add_kernel(messages, owners, own_ref, *refs):
    sent_refs, refs = refs[: len(messages)], refs[len(messages) :]
    weight_refs, refs = refs[:owners], refs[owners:]
    act_ref, grad_ref, score_ref, *tops_refs, sums, scores, sems = refs
    blocks, rows, _ = own_ref.shape
    score_kernel(*weight_refs, scores)
    copies = [pltpu.make_async_copy(scores, score_ref, sems.at[blocks // GROUP])]
    copies[0].start()
    load_tops(messages, rows, sent_refs, tops_refs)
    for step in range(blocks // GROUP):
        for block, total in add_group(messages, rows, own_ref, sent_refs, tops_refs, step):
            sums[block] = total
        first = step * GROUP
        ref, at = act_ref, first
        if first >= act_ref.shape[0]:
            ref, at = grad_ref, first - act_ref.shape[0]
        copies.append(
            pltpu.make_async_copy(
                sums.at[pl.ds(first, GROUP)], ref.at[pl.ds(at, GROUP)], sems.at[step]
            )
        )
        copies[-1].start()
    for copy in copies:
        copy.wait()


def pairs_of(part, side, halves, act_ref, grad_ref):
    half = lax.rem(side + part, halves)
    for ref in (act_ref, grad_ref):
        count = ref.shape[1] // PAIR // halves
        for pair in range(count):
            yield ref, pl.multiple_of((half * count + pair) * PAIR, PAIR)


def eigen_kernel(part, halves, masks, pieces, scale, me_ref, side_ref, act_ref, grad_ref, *refs):
    *shard_refs, power_ref, sums_ref, basis_ref = refs
    me, side = me_ref[0], side_ref[0]
    rows = BLK // pieces
    done = 0
    if part:
        *shard_refs, done_ref = shard_refs
        done = done_ref.shape[0]
        sums_ref[:done] = done_ref[...]
    half = lax.rem(side + part, halves)
    act_half = act_ref.shape[1] // BLK // halves
    grad_half = grad_ref.shape[1] // BLK // halves
    basis_ref[...] = jnp.zeros_like(basis_ref)
    for mask, ref in zip(masks, shard_refs):
        whole = halves > 1 and ref.shape[0] == halves * (act_half + grad_half)
        for block in range(act_half + grad_half):
            at = block
            if whole and block < act_half:
                at = half * act_half + block
            elif whole:
                at = (halves - 1) * act_half + half * grad_half + block
            corner = block % 2
            row = pl.multiple_of(corner * BLK + (me ^ mask) * rows, rows)
            columns = slice(corner * BLK, (corner + 1) * BLK)
            basis_ref[block // 2, pl.ds(row, rows), columns] = ref[at]

    for pair, (ref, column) in enumerate(pairs_of(part, side, halves, act_ref, grad_ref)):
        projected = lax.dot_general(
            ref[:, pl.ds(column, PAIR)],
            basis_ref[pair],
            contract_inner,
            preferred_element_type=jnp.float32,
        )
        power = projected * projected
        power_ref[pair] = power
        sums = scale * jnp.sum(power, axis=0, keepdims=True)
        row = done + 2 * pair
        sums_ref[row : row + 1, :] = sums[:, :BLK]
        sums_ref[row + 1 : row + 2, :] = sums[:, BLK:]


def combine_kernel(halves, act_half, *refs):
    *sums_refs, eigen_ref, total_ref = refs
    eigen = sums_refs[0][...]
    for sums_ref in sums_refs[1:]:
        eigen = eigen + sums_ref[...]
    eigen_ref[...] = eigen
    blocks_half = eigen.shape[0] // halves
    act_total = jnp.zeros((1, BLK), jnp.float32)
    grad_total = jnp.zeros((1, BLK), jnp.float32)
    for part in range(halves):
        first = part * blocks_half
        act_total += jnp.sum(eigen[first : first + act_half], axis=0, keepdims=True)
        grad_total += jnp.sum(eigen[first + act_half : first + blocks_half], axis=0, keepdims=True)
    total_ref[0:1, :] = act_total
    total_ref[1:2, :] = grad_total


def order_kernel(halves, side_ref, eigen_ref, act_eigen_ref, grad_eigen_ref):
    side = side_ref[0]
    act_half, grad_half = act_eigen_ref.shape[0] // halves, grad_eigen_ref.shape[0] // halves
    for part in range(halves):
        half = lax.rem(side + part, halves)
        first = part * (act_half + grad_half)
        middle = first + act_half
        act_eigen_ref[pl.ds(half * act_half, act_half), :] = eigen_ref[first:middle]
        grad_eigen_ref[pl.ds(half * grad_half, grad_half), :] = eigen_ref[
            middle : middle + grad_half
        ]


def weight_kernel(halves, act_half, eigen_ref, *refs):
    *refs, weight_ref, inverse, act_sum, grad_sum = refs
    power_refs, total_refs = refs[:halves], refs[halves:]
    totals = total_refs[0][...]
    for total_ref in total_refs[1:]:
        totals = totals + total_ref[...]
    totals = jnp.sum(totals, axis=1, keepdims=True)
    blocks_half = eigen_ref.shape[0] // halves
    for part in range(halves):
        first = part * blocks_half
        act = slice(first, first + act_half)
        grad = slice(first + act_half, first + blocks_half)
        inverse[act] = 1.0 / (eigen_ref[act] + totals[0:1] * (damp_root / D))
        inverse[grad] = 1.0 / (eigen_ref[grad] + totals[1:2] * (damp_root / FF))
    tokens = act_sum.shape[0]

    @pl.loop(0, tokens // TILE)
    def _(tile):
        here = pl.ds(pl.multiple_of(tile * TILE, TILE), TILE)
        sums = [jnp.zeros((TILE, BLK), jnp.float32), jnp.zeros((TILE, BLK), jnp.float32)]
        for part, power_ref in enumerate(power_refs):
            for pair in range(power_ref.shape[0]):
                which = 0 if 2 * pair < act_half else 1
                for side in range(2):
                    row = part * blocks_half + 2 * pair + side
                    power = power_ref[pair, here, side * BLK : (side + 1) * BLK]
                    sums[which] += power * inverse[row : row + 1, :]
        act_sum[here, :], grad_sum[here, :] = sums

    ones = jnp.ones((8, BLK), jnp.float32)
    for index, total in enumerate((act_sum, grad_sum)):
        sums = lax.dot_general(
            ones,
            total[...],
            contract_lanes,
            precision=lax.Precision.HIGHEST,
            preferred_element_type=jnp.float32,
        )
        weight_ref[index : index + 1, :] = sums[0:1]


def score_kernel(*refs):
    *weight_refs, score_ref = refs
    weights = weight_refs[0][...]
    for weight_ref in weight_refs[1:]:
        weights = weights + weight_ref[...]
    score_ref[...] = weights[0:1] * weights[1:2] * (1.0 / (D * FF))


def swap(value, axis, mask):
    count = lax.axis_size(axis)
    return lax.ppermute(value, axis, [(i, i ^ mask) for i in range(count)])


def share(value, axis, direct):
    if not direct:
        return [lax.psum(value, axis)]
    return [value] + [swap(value, axis, mask) for mask in reversed(range(1, lax.axis_size(axis)))]


def after(values, done):
    return list(lax.optimization_barrier((tuple(values), done))[0])


def local(activations, gradients, basis_act, basis_grad):
    tokens = activations.shape[0]
    act_blocks, grad_blocks = basis_act.shape[0], basis_grad.shape[0]
    blocks = act_blocks + grad_blocks
    dp, owners = lax.axis_size("dp"), lax.axis_size("owner")
    scale = 1.0 / (tokens * dp)
    direct = dp in (2, 4) and owners in (1, 2, 4)
    pieces = dp if direct else 1
    halves = 2 if pieces == 4 and lax.axis_size("groups") == 2 else 1
    rows = BLK // pieces
    me = jnp.full((1,), lax.axis_index("dp") if direct else 0, jnp.int32)
    side = jnp.full((1,), lax.axis_index("groups"), jnp.int32)
    owner = jnp.full((1,), lax.axis_index("owner"), jnp.int32)
    macs = tokens * blocks * BLK * BLK
    input_bytes = 2 * tokens * blocks * BLK
    if direct:
        shards = call(
            pack_kernel,
            [bf16(blocks // part, rows, BLK) for part in range(1, halves + 1)],
            "pack_basis", 0, 2 * blocks * rows * BLK,
            [IN_SMEM, IN_SMEM, IN_HBM, IN_HBM], [pltpu.SemaphoreType.DMA((2 * halves,))],
        )(side, owner, in_hbm(basis_act), in_hbm(basis_grad))
        near = [shards[0], swap(shards[0], "dp", 1)]
        far = {mask: swap(shards[-1], "dp", mask) for mask in range(pieces - 1, 1, -1)}
    else:
        near = [
            jnp.concatenate(
                [lax.all_gather(part, "dp", axis=1, tiled=True) for part in (basis_act, basis_grad)]
            )
        ]
        far = {}
    masks = [*range(len(near)), *far]

    message = bf16(blocks * rows + scale_rows(0, blocks), BLK)
    whole_range = (0, blocks)
    coded = {4: [(3, *whole_range), (1, *whole_range)], 2: [(1, *whole_range)], 1: []}[pieces]
    plain = 2 if pieces == 4 else 1
    act_here, grad_here, *grams = call(
        functools.partial(gram_kernel, pieces, coded, scale),
        [
            bf16(*activations.shape),
            bf16(*gradients.shape),
            *[f32(blocks, rows, BLK)] * plain,
            *[message] * len(coded),
        ],
        "partial_gram", 4 * macs, input_bytes,
        [IN_SMEM, IN_HBM, IN_HBM],
        [
            pltpu.VMEM((GROUP, BLK, BLK), jnp.float32),
            pltpu.VMEM((scale_rows(0, blocks), BLK), jnp.float32),
            pltpu.SemaphoreType.DMA((blocks // GROUP,)),
        ],
    )(me, in_hbm(activations), in_hbm(gradients))
    own = grams[0]
    sent = {message[0]: chunk for message, chunk in zip(coded, grams[plain:])}
    if not direct:
        own = lax.psum_scatter(own, "dp", scatter_dimension=1, tiled=True)
    if pieces == 4:
        middle = lax.ppermute(sent[3], "dp", [(1, 2), (2, 1)])
        relayed = lax.ppermute(sent[3], "dp", [(0, 1), (3, 2)])

    parts = [[*near, *far.values()]]
    if halves == 2:
        swapped = [swap(after([part], own)[0], "groups", 1) for part in far.values()]
        parts.append([*near, *swapped])
    powers, sums = [], []
    for part, shards in enumerate(parts):
        power, *sums = call(
            functools.partial(eigen_kernel, part, halves, masks, pieces, scale),
            [f32(blocks // halves // 2, tokens, PAIR), f32(blocks // halves * (part + 1), BLK)],
            "partial_eigen", 2 * macs // halves, input_bytes // halves,
            [IN_SMEM, IN_SMEM] + [IN_VMEM] * (2 + len(shards) + len(sums)),
            [pltpu.VMEM((blocks // halves // 2, PAIR, PAIR), jnp.bfloat16)],
        )(me, side, act_here, grad_here, *shards, *sums)
        powers.append(power)
    if pieces == 4:
        far_chunk, relayed = after([grams[1], relayed], sums)
        late = call(
            functools.partial(relay_kernel, coded[0]), [message] * 2, "relay_chunk", 0, 16 * own.size,
            [IN_SMEM, IN_VMEM, IN_VMEM, IN_VMEM],
            [pltpu.VMEM(message.shape, jnp.bfloat16)]
            + [pltpu.VMEM((scale_rows(0, blocks), BLK), jnp.float32)] * 2,
        )(owner, far_chunk, relayed, sent[1])
    sums = share(sums[0], "dp", direct)
    if pieces == 4:
        sums = after(sums, (middle, late))
    eigen, totals = call(
        functools.partial(combine_kernel, halves, act_blocks // halves),
        [f32(blocks, BLK), f32(2, BLK)],
        "combine_eigen", 0, 4 * blocks * BLK * pieces, [IN_VMEM] * len(sums),
    )(*sums)
    chunks = []
    if pieces == 4:
        for chunk, order in zip(late, ((2, 1), (1, 2))):
            ways = [
                (at * owners + owner, (at ^ order[owner % 2]) * owners + owner)
                for at in range(dp)
                for owner in range(owners)
            ]
            chunks.append(lax.ppermute(after([chunk], totals)[0], ("dp", "owner"), ways))
    elif pieces == 2:
        chunks.append(swap(after([sent[1]], totals)[0], "dp", 1))
    totals = share(totals, "owner", direct)
    weights = call(
        functools.partial(weight_kernel, halves, act_blocks // halves),
        f32(2, tokens), "partial_weights", 0, 4 * tokens * blocks * BLK,
        [IN_VMEM] * (1 + halves + len(totals)),
        [
            pltpu.VMEM((blocks, BLK), jnp.float32),
            pltpu.VMEM((tokens, BLK), jnp.float32),
            pltpu.VMEM((tokens, BLK), jnp.float32),
        ],
    )(eigen, *powers, *totals)
    weights = share(weights, "owner", direct)

    def tops_of(count):
        return [pltpu.VMEM((scale_rows(0, blocks), BLK), jnp.float32)] * count

    eigens = [f32(act_blocks, BLK), f32(grad_blocks, BLK)]
    if pieces == 4:
        own, *eigens = call(
            functools.partial(add_kernel, [(None, 0, blocks)], halves),
            [f32(*own.shape), *eigens], "add_chunk", 0, 12 * own.size,
            [IN_SMEM] + [IN_VMEM] * 3, tops_of(1),
        )(side, eigen, own, middle)
        weights[1:] = after(weights[1:], own)
    else:
        eigens = call(
            functools.partial(order_kernel, halves), eigens, "order_eigen", 0,
            8 * blocks * BLK, [IN_SMEM, IN_VMEM],
        )(side, eigen)
    chunks = chunks[::-1]
    if chunks:
        *covariance, token_scores = call(
            functools.partial(last_add_kernel, [(None, 0, blocks)] * len(chunks), len(weights)),
            [f32(act_blocks, rows, BLK), f32(grad_blocks, rows, BLK), f32(1, tokens)],
            "last_sums", 0, 16 * own.size, [IN_VMEM] * (1 + len(chunks) + len(weights)),
            [
                *tops_of(len(chunks)),
                pltpu.VMEM(own.shape, jnp.float32),
                pltpu.VMEM((1, tokens), jnp.float32),
                pltpu.SemaphoreType.DMA((blocks // GROUP + 1,)),
            ],
            out_spec=[pl.BlockSpec(memory_space=pl.ANY)] * 3,
        )(own, *chunks, *weights)
    else:
        covariance = own[:act_blocks], own[act_blocks:]
        token_scores = call(
            score_kernel, f32(1, tokens), "token_scores", 0, 8 * tokens, [IN_VMEM] * len(weights)
        )(*weights)
    return (
        *covariance,
        *[eigen.reshape(-1) for eigen in eigens],
        token_scores.reshape(-1),
    )


def solution(mesh):
    return jax.shard_map(
        local,
        mesh=mesh,
        in_specs=(
            P(("groups", "dp"), "owner"),
            P(("groups", "dp"), "owner"),
            P("owner", "dp", None),
            P("owner", "dp", None),
        ),
        out_specs=(
            P(("groups", "owner"), "dp", None),
            P(("groups", "owner"), "dp", None),
            P(("groups", "owner")),
            P(("groups", "owner")),
            P(("groups", "dp")),
        ),
        check_vma=False,
    )
```

```python
import functools
import math

import jax
import jax.numpy as jnp
from jax import lax
from jax.experimental import pallas as pl
from jax.experimental.pallas import tpu as pltpu
from jax.sharding import PartitionSpec as P

D = 4096
FF = 14336
BLK = 128
PAIR = 2 * BLK
GROUP = 4
TILE = 64
VMEM_LIMIT = 24 * 1024 * 1024
CODE_TOP = 2.0**7.875
SMALLEST = 1e-36
SIXTEENTH = 1.0 / (16.0 * math.log(2.0))

damp_root = 0.31622776601683794
contract_rows = (((0,), (0,)), ((), ()))
contract_inner = (((1,), (0,)), ((), ()))
contract_lanes = (((1,), (1,)), ((), ()))

IN_VMEM = pl.BlockSpec(memory_space=pltpu.VMEM)
IN_SMEM = pl.BlockSpec(memory_space=pltpu.SMEM)
IN_HBM = pl.BlockSpec(memory_space=pltpu.HBM)


def scale_rows(first, end):
    return 16 * pl.cdiv(end - first, 16)


def call(
    kernel, out_shape, name, flops, bytes_accessed, in_specs, scratch_shapes=(),
    out_spec=None,
):
    return pl.pallas_call(
        kernel,
        out_shape=out_shape,
        in_specs=in_specs,
        out_specs=out_spec or jax.tree.map(lambda _: IN_VMEM, out_shape),
        scratch_shapes=scratch_shapes,
        compiler_params=pltpu.CompilerParams(vmem_limit_bytes=VMEM_LIMIT),
        cost_estimate=pl.CostEstimate(
            flops=flops, bytes_accessed=bytes_accessed, transcendentals=0
        ),
        name=name,
    )


def in_hbm(value):
    return pltpu.with_memory_space_constraint(value, pltpu.HBM)


def f32(*shape):
    return jax.ShapeDtypeStruct(shape, jnp.float32)


def bf16(*shape):
    return jax.ShapeDtypeStruct(shape, jnp.bfloat16)


def encode(values):
    power = values * values
    power = power * power
    power = power * power
    power = power * power
    return jnp.where(values < 0.0, -power, power).astype(jnp.bfloat16)


def top_of(values):
    top = jnp.maximum(jnp.max(jnp.abs(values), axis=0, keepdims=True), SMALLEST)
    return (top * (1.0 + 2.0**-8)).astype(jnp.bfloat16).astype(jnp.float32)


def decode(coded):
    coded = coded.astype(jnp.float32)
    root = jnp.exp2(jnp.log(jnp.abs(coded)) * SIXTEENTH)
    return jnp.where(coded > 0.0, root, jnp.where(coded < 0.0, -root, 0.0))


def pack_kernel(side_ref, act_ref, grad_ref, *refs):
    *out_refs, sems = refs
    side = side_ref[0]
    blocks = out_refs[0].shape[0]
    copies = []
    for out_ref in reversed(out_refs):
        halves = blocks // out_ref.shape[0]
        at = 0
        for ref in (act_ref, grad_ref):
            count = ref.shape[0] // halves
            copies.append(
                pltpu.make_async_copy(
                    ref.at[pl.ds(side * count if halves > 1 else 0, count)],
                    out_ref.at[pl.ds(at, count)],
                    sems.at[len(copies)],
                )
            )
            at += count
    for copy in copies:
        copy.start()
    for copy in copies:
        copy.wait()


def gram_kernel(pieces, messages, scale, me_ref, act_hbm, grad_hbm, act_ref, grad_ref, *refs):
    refs, (whole, tops, sems) = refs[:-3], refs[-3:]
    plain_refs, sent_refs = refs[: len(refs) - len(messages)], refs[len(refs) - len(messages) :]
    rows = BLK // pieces
    me = me_ref[0]
    steps = []
    for source, target in ((act_hbm, act_ref), (grad_hbm, grad_ref)):
        for first in range(0, source.shape[1], GROUP * BLK):
            columns = slice(first, first + GROUP * BLK)
            copy = pltpu.make_async_copy(
                source.at[:, columns], target.at[:, columns], sems.at[len(steps)]
            )
            copy.start()
            steps.append((target, columns, copy))
    tops[...] = jnp.zeros_like(tops)
    for step, (ref, columns, copy) in enumerate(steps):
        copy.wait()
        for offset in range(GROUP):
            block = step * GROUP + offset
            at = columns.start + offset * BLK
            values = ref[:, at : at + BLK]
            gram = scale * lax.dot_general(
                values, values, contract_rows, preferred_element_type=jnp.float32
            )
            if pieces == 1:
                plain_refs[0][block] = gram
                continue
            whole[offset] = gram
            for ref_at, mask in zip(plain_refs, (0, 2)):
                row = pl.multiple_of((me ^ mask) * rows, rows)
                ref_at[block] = whole[offset, pl.ds(row, rows), :]
            top = top_of(gram)
            tops[block : block + 1, :] = top
            gain = CODE_TOP / top
            for sent_ref, (mask, first, end) in zip(sent_refs, messages):
                if first <= block < end:
                    row = pl.multiple_of((me ^ mask) * rows, rows)
                    place = slice((block - first) * rows, (block - first + 1) * rows)
                    sent_ref[place, :] = encode(whole[offset, pl.ds(row, rows), :] * gain)
    for sent_ref, (_, first, end) in zip(sent_refs, messages):
        sent_ref[(end - first) * rows :, :] = tops[
            first : first + scale_rows(first, end), :
        ].astype(jnp.bfloat16)


def add_group(messages, rows, own_ref, sent_refs, tops_refs, step):
    for block in range(step * GROUP, (step + 1) * GROUP):
        total = own_ref[block]
        for (_, first, end), sent_ref, tops in zip(messages, sent_refs, tops_refs):
            if first <= block < end:
                at = block - first
                values = decode(sent_ref[at * rows : (at + 1) * rows, :])
                total = total + values * tops[at : at + 1, :]
        yield block, total


def load_tops(messages, rows, sent_refs, tops_refs):
    for (_, first, end), sent_ref, tops in zip(messages, sent_refs, tops_refs):
        tops[...] = sent_ref[(end - first) * rows :, :].astype(jnp.float32) * (1.0 / CODE_TOP)


def add_kernel(messages, halves, side_ref, eigen_ref, own_ref, *refs):
    sent_refs, refs = refs[: len(messages)], refs[len(messages) :]
    sum_ref, act_eigen_ref, grad_eigen_ref, *tops_refs = refs
    order_kernel(halves, side_ref, eigen_ref, act_eigen_ref, grad_eigen_ref)
    blocks, rows, _ = own_ref.shape
    load_tops(messages, rows, sent_refs, tops_refs)
    for step in range(blocks // GROUP):
        for block, total in add_group(messages, rows, own_ref, sent_refs, tops_refs, step):
            sum_ref[block] = total


def relay_kernel(message, far_ref, relayed_ref, sent_ref, relayed_tops, tops):
    messages = (message,)
    blocks, rows, _ = far_ref.shape
    load_tops(messages, rows, (relayed_ref,), (relayed_tops,))
    tops[...] = jnp.zeros_like(tops)
    for step in range(blocks // GROUP):
        for block, total in add_group(
            messages, rows, far_ref, (relayed_ref,), (relayed_tops,), step
        ):
            top = top_of(total)
            tops[block : block + 1, :] = top
            sent_ref[block * rows : (block + 1) * rows, :] = encode(total * (CODE_TOP / top))
    sent_ref[blocks * rows :, :] = tops[...].astype(jnp.bfloat16)


def last_add_kernel(messages, owners, own_ref, *refs):
    sent_refs, refs = refs[: len(messages)], refs[len(messages) :]
    weight_refs, refs = refs[:owners], refs[owners:]
    act_ref, grad_ref, score_ref, *tops_refs, sums, scores, sems = refs
    blocks, rows, _ = own_ref.shape
    score_kernel(*weight_refs, scores)
    copies = [pltpu.make_async_copy(scores, score_ref, sems.at[blocks // GROUP])]
    copies[0].start()
    load_tops(messages, rows, sent_refs, tops_refs)
    for step in range(blocks // GROUP):
        for block, total in add_group(messages, rows, own_ref, sent_refs, tops_refs, step):
            sums[block] = total
        first = step * GROUP
        ref, at = act_ref, first
        if first >= act_ref.shape[0]:
            ref, at = grad_ref, first - act_ref.shape[0]
        copies.append(
            pltpu.make_async_copy(
                sums.at[pl.ds(first, GROUP)], ref.at[pl.ds(at, GROUP)], sems.at[step]
            )
        )
        copies[-1].start()
    for copy in copies:
        copy.wait()


def pairs_of(part, side, halves, act_ref, grad_ref):
    half = lax.rem(side + part, halves)
    for ref in (act_ref, grad_ref):
        count = ref.shape[1] // PAIR // halves
        for pair in range(count):
            yield ref, pl.multiple_of((half * count + pair) * PAIR, PAIR)


def eigen_kernel(part, halves, masks, pieces, scale, me_ref, side_ref, act_ref, grad_ref, *refs):
    *shard_refs, power_ref, sums_ref, basis_ref = refs
    me, side = me_ref[0], side_ref[0]
    rows = BLK // pieces
    done = 0
    if part:
        *shard_refs, done_ref = shard_refs
        done = done_ref.shape[0]
        sums_ref[:done] = done_ref[...]
    half = lax.rem(side + part, halves)
    act_half = act_ref.shape[1] // BLK // halves
    grad_half = grad_ref.shape[1] // BLK // halves
    basis_ref[...] = jnp.zeros_like(basis_ref)
    for mask, ref in zip(masks, shard_refs):
        whole = halves > 1 and ref.shape[0] == halves * (act_half + grad_half)
        for block in range(act_half + grad_half):
            at = block
            if whole and block < act_half:
                at = half * act_half + block
            elif whole:
                at = (halves - 1) * act_half + half * grad_half + block
            corner = block % 2
            row = pl.multiple_of(corner * BLK + (me ^ mask) * rows, rows)
            columns = slice(corner * BLK, (corner + 1) * BLK)
            basis_ref[block // 2, pl.ds(row, rows), columns] = ref[at]

    for pair, (ref, column) in enumerate(pairs_of(part, side, halves, act_ref, grad_ref)):
        projected = lax.dot_general(
            ref[:, pl.ds(column, PAIR)],
            basis_ref[pair],
            contract_inner,
            preferred_element_type=jnp.float32,
        )
        power = projected * projected
        power_ref[pair] = power
        sums = scale * jnp.sum(power, axis=0, keepdims=True)
        row = done + 2 * pair
        sums_ref[row : row + 1, :] = sums[:, :BLK]
        sums_ref[row + 1 : row + 2, :] = sums[:, BLK:]


def combine_kernel(halves, act_half, *refs):
    *sums_refs, eigen_ref, total_ref = refs
    eigen = sums_refs[0][...]
    for sums_ref in sums_refs[1:]:
        eigen = eigen + sums_ref[...]
    eigen_ref[...] = eigen
    blocks_half = eigen.shape[0] // halves
    act_total = jnp.zeros((1, BLK), jnp.float32)
    grad_total = jnp.zeros((1, BLK), jnp.float32)
    for part in range(halves):
        first = part * blocks_half
        act_total += jnp.sum(eigen[first : first + act_half], axis=0, keepdims=True)
        grad_total += jnp.sum(eigen[first + act_half : first + blocks_half], axis=0, keepdims=True)
    total_ref[0:1, :] = act_total
    total_ref[1:2, :] = grad_total


def order_kernel(halves, side_ref, eigen_ref, act_eigen_ref, grad_eigen_ref):
    side = side_ref[0]
    act_half, grad_half = act_eigen_ref.shape[0] // halves, grad_eigen_ref.shape[0] // halves
    for part in range(halves):
        half = lax.rem(side + part, halves)
        first = part * (act_half + grad_half)
        middle = first + act_half
        act_eigen_ref[pl.ds(half * act_half, act_half), :] = eigen_ref[first:middle]
        grad_eigen_ref[pl.ds(half * grad_half, grad_half), :] = eigen_ref[
            middle : middle + grad_half
        ]


def weight_kernel(halves, act_half, eigen_ref, *refs):
    *refs, weight_ref, inverse, act_sum, grad_sum = refs
    power_refs, total_refs = refs[:halves], refs[halves:]
    totals = total_refs[0][...]
    for total_ref in total_refs[1:]:
        totals = totals + total_ref[...]
    totals = jnp.sum(totals, axis=1, keepdims=True)
    blocks_half = eigen_ref.shape[0] // halves
    for part in range(halves):
        first = part * blocks_half
        act = slice(first, first + act_half)
        grad = slice(first + act_half, first + blocks_half)
        inverse[act] = 1.0 / (eigen_ref[act] + totals[0:1] * (damp_root / D))
        inverse[grad] = 1.0 / (eigen_ref[grad] + totals[1:2] * (damp_root / FF))
    tokens = act_sum.shape[0]

    @pl.loop(0, tokens // TILE)
    def _(tile):
        here = pl.ds(pl.multiple_of(tile * TILE, TILE), TILE)
        sums = [jnp.zeros((TILE, BLK), jnp.float32), jnp.zeros((TILE, BLK), jnp.float32)]
        for part, power_ref in enumerate(power_refs):
            for pair in range(power_ref.shape[0]):
                which = 0 if 2 * pair < act_half else 1
                for side in range(2):
                    row = part * blocks_half + 2 * pair + side
                    power = power_ref[pair, here, side * BLK : (side + 1) * BLK]
                    sums[which] += power * inverse[row : row + 1, :]
        act_sum[here, :], grad_sum[here, :] = sums

    ones = jnp.ones((8, BLK), jnp.float32)
    for index, total in enumerate((act_sum, grad_sum)):
        sums = lax.dot_general(
            ones,
            total[...],
            contract_lanes,
            precision=lax.Precision.HIGHEST,
            preferred_element_type=jnp.float32,
        )
        weight_ref[index : index + 1, :] = sums[0:1]


def score_kernel(*refs):
    *weight_refs, score_ref = refs
    weights = weight_refs[0][...]
    for weight_ref in weight_refs[1:]:
        weights = weights + weight_ref[...]
    score_ref[...] = weights[0:1] * weights[1:2] * (1.0 / (D * FF))


def swap(value, axis, mask):
    count = lax.axis_size(axis)
    return lax.ppermute(value, axis, [(i, i ^ mask) for i in range(count)])


def share(value, axis, direct):
    if not direct:
        return [lax.psum(value, axis)]
    return [value] + [swap(value, axis, mask) for mask in reversed(range(1, lax.axis_size(axis)))]


def after(values, done):
    return list(lax.optimization_barrier((tuple(values), done))[0])


def local(activations, gradients, basis_act, basis_grad):
    tokens = activations.shape[0]
    act_blocks, grad_blocks = basis_act.shape[0], basis_grad.shape[0]
    blocks = act_blocks + grad_blocks
    dp, owners = lax.axis_size("dp"), lax.axis_size("owner")
    scale = 1.0 / (tokens * dp)
    direct = dp in (2, 4) and owners in (1, 2, 4)
    pieces = dp if direct else 1
    halves = 2 if pieces == 4 and lax.axis_size("groups") == 2 else 1
    rows = BLK // pieces
    me = jnp.full((1,), lax.axis_index("dp") if direct else 0, jnp.int32)
    side = jnp.full((1,), lax.axis_index("groups"), jnp.int32)
    macs = tokens * blocks * BLK * BLK
    input_bytes = 2 * tokens * blocks * BLK
    if direct:
        shards = call(
            pack_kernel,
            [bf16(blocks // part, rows, BLK) for part in range(1, halves + 1)],
            "pack_basis", 0, 2 * blocks * rows * BLK,
            [IN_SMEM, IN_HBM, IN_HBM], [pltpu.SemaphoreType.DMA((2 * halves,))],
        )(side, in_hbm(basis_act), in_hbm(basis_grad))
        near = [shards[0], swap(shards[0], "dp", 1)]
        far = {mask: swap(shards[-1], "dp", mask) for mask in range(pieces - 1, 1, -1)}
    else:
        near = [
            jnp.concatenate(
                [lax.all_gather(part, "dp", axis=1, tiled=True) for part in (basis_act, basis_grad)]
            )
        ]
        far = {}
    masks = [*range(len(near)), *far]

    message = bf16(blocks * rows + scale_rows(0, blocks), BLK)
    whole_range = (0, blocks)
    coded = {4: [(3, *whole_range), (1, *whole_range)], 2: [(1, *whole_range)], 1: []}[pieces]
    plain = 2 if pieces == 4 else 1
    act_here, grad_here, *grams = call(
        functools.partial(gram_kernel, pieces, coded, scale),
        [
            bf16(*activations.shape),
            bf16(*gradients.shape),
            *[f32(blocks, rows, BLK)] * plain,
            *[message] * len(coded),
        ],
        "partial_gram", 4 * macs, input_bytes,
        [IN_SMEM, IN_HBM, IN_HBM],
        [
            pltpu.VMEM((GROUP, BLK, BLK), jnp.float32),
            pltpu.VMEM((scale_rows(0, blocks), BLK), jnp.float32),
            pltpu.SemaphoreType.DMA((blocks // GROUP,)),
        ],
    )(me, in_hbm(activations), in_hbm(gradients))
    own = grams[0]
    sent = {message[0]: chunk for message, chunk in zip(coded, grams[plain:])}
    if not direct:
        own = lax.psum_scatter(own, "dp", scatter_dimension=1, tiled=True)
    if pieces == 4:
        middle = lax.ppermute(sent[3], "dp", [(1, 2), (2, 1)])
        relayed = lax.ppermute(sent[3], "dp", [(0, 1), (3, 2)])

    parts = [[*near, *far.values()]]
    if halves == 2:
        swapped = [swap(after([part], own)[0], "groups", 1) for part in far.values()]
        parts.append([*near, *swapped])
    powers, sums = [], []
    for part, shards in enumerate(parts):
        power, *sums = call(
            functools.partial(eigen_kernel, part, halves, masks, pieces, scale),
            [f32(blocks // halves // 2, tokens, PAIR), f32(blocks // halves * (part + 1), BLK)],
            "partial_eigen", 2 * macs // halves, input_bytes // halves,
            [IN_SMEM, IN_SMEM] + [IN_VMEM] * (2 + len(shards) + len(sums)),
            [pltpu.VMEM((blocks // halves // 2, PAIR, PAIR), jnp.bfloat16)],
        )(me, side, act_here, grad_here, *shards, *sums)
        powers.append(power)
    if pieces == 4:
        sent[2] = call(
            functools.partial(relay_kernel, coded[0]), message, "relay_chunk", 0, 12 * own.size,
            [IN_VMEM, IN_VMEM],
            [pltpu.VMEM((scale_rows(0, blocks), BLK), jnp.float32)] * 2,
        )(*after([grams[1], relayed], sums))
    sums = share(sums[0], "dp", direct)
    if pieces == 4:
        sums = after(sums, (middle, sent[2]))
    eigen, totals = call(
        functools.partial(combine_kernel, halves, act_blocks // halves),
        [f32(blocks, BLK), f32(2, BLK)],
        "combine_eigen", 0, 4 * blocks * BLK * pieces, [IN_VMEM] * len(sums),
    )(*sums)
    arrived = {}
    sent.pop(3, None)
    for mask in sent:
        arrived[mask] = swap(after([sent[mask]], totals)[0], "dp", mask)
    totals = share(totals, "owner", direct)
    weights = call(
        functools.partial(weight_kernel, halves, act_blocks // halves),
        f32(2, tokens), "partial_weights", 0, 4 * tokens * blocks * BLK,
        [IN_VMEM] * (1 + halves + len(totals)),
        [
            pltpu.VMEM((blocks, BLK), jnp.float32),
            pltpu.VMEM((tokens, BLK), jnp.float32),
            pltpu.VMEM((tokens, BLK), jnp.float32),
        ],
    )(eigen, *powers, *totals)
    weights = share(weights, "owner", direct)

    def tops_of(count):
        return [pltpu.VMEM((scale_rows(0, blocks), BLK), jnp.float32)] * count

    eigens = [f32(act_blocks, BLK), f32(grad_blocks, BLK)]
    if pieces == 4:
        own, *eigens = call(
            functools.partial(add_kernel, [(None, 0, blocks)], halves),
            [f32(*own.shape), *eigens], "add_chunk", 0, 12 * own.size,
            [IN_SMEM] + [IN_VMEM] * 3, tops_of(1),
        )(side, eigen, own, middle)
        weights[1:] = after(weights[1:], own)
    else:
        eigens = call(
            functools.partial(order_kernel, halves), eigens, "order_eigen", 0,
            8 * blocks * BLK, [IN_SMEM, IN_VMEM],
        )(side, eigen)
    chunks = list(arrived.values())[::-1]
    if chunks:
        *covariance, token_scores = call(
            functools.partial(last_add_kernel, [(None, 0, blocks)] * len(chunks), len(weights)),
            [f32(act_blocks, rows, BLK), f32(grad_blocks, rows, BLK), f32(1, tokens)],
            "last_sums", 0, 16 * own.size, [IN_VMEM] * (1 + len(chunks) + len(weights)),
            [
                *tops_of(len(chunks)),
                pltpu.VMEM(own.shape, jnp.float32),
                pltpu.VMEM((1, tokens), jnp.float32),
                pltpu.SemaphoreType.DMA((blocks // GROUP + 1,)),
            ],
            out_spec=[pl.BlockSpec(memory_space=pl.ANY)] * 3,
        )(own, *chunks, *weights)
    else:
        covariance = own[:act_blocks], own[act_blocks:]
        token_scores = call(
            score_kernel, f32(1, tokens), "token_scores", 0, 8 * tokens, [IN_VMEM] * len(weights)
        )(*weights)
    return (
        *covariance,
        *[eigen.reshape(-1) for eigen in eigens],
        token_scores.reshape(-1),
    )


def solution(mesh):
    return jax.shard_map(
        local,
        mesh=mesh,
        in_specs=(
            P(("groups", "dp"), "owner"),
            P(("groups", "dp"), "owner"),
            P("owner", "dp", None),
            P("owner", "dp", None),
        ),
        out_specs=(
            P(("groups", "owner"), "dp", None),
            P(("groups", "owner"), "dp", None),
            P(("groups", "owner")),
            P(("groups", "owner")),
            P(("groups", "dp")),
        ),
        check_vma=False,
    )
```

```python
import functools

import jax
import jax.numpy as jnp
from jax import lax
from jax.experimental import pallas as pl
from jax.experimental.pallas import tpu as pltpu
from jax.sharding import PartitionSpec as P

D = 4096
FF = 14336
BLK = 128
PAIR = 2 * BLK
GROUP = 4
TILE = 64
VMEM_LIMIT = 24 * 1024 * 1024
CODE_TOP = 2.0**7.875
SMALLEST = 1e-36

damp_root = 0.31622776601683794
contract_rows = (((0,), (0,)), ((), ()))
contract_inner = (((1,), (0,)), ((), ()))
contract_lanes = (((1,), (1,)), ((), ()))

IN_VMEM = pl.BlockSpec(memory_space=pltpu.VMEM)
IN_SMEM = pl.BlockSpec(memory_space=pltpu.SMEM)
IN_HBM = pl.BlockSpec(memory_space=pltpu.HBM)


def scale_rows(first, end):
    return 16 * pl.cdiv(end - first, 16)


def call(
    kernel, out_shape, name, flops, bytes_accessed, in_specs, scratch_shapes=(),
    out_spec=None,
):
    return pl.pallas_call(
        kernel,
        out_shape=out_shape,
        in_specs=in_specs,
        out_specs=out_spec or jax.tree.map(lambda _: IN_VMEM, out_shape),
        scratch_shapes=scratch_shapes,
        compiler_params=pltpu.CompilerParams(vmem_limit_bytes=VMEM_LIMIT),
        cost_estimate=pl.CostEstimate(
            flops=flops, bytes_accessed=bytes_accessed, transcendentals=0
        ),
        name=name,
    )


def in_hbm(value):
    return pltpu.with_memory_space_constraint(value, pltpu.HBM)


def f32(*shape):
    return jax.ShapeDtypeStruct(shape, jnp.float32)


def bf16(*shape):
    return jax.ShapeDtypeStruct(shape, jnp.bfloat16)


def encode(values):
    power = values * values
    power = power * power
    power = power * power
    power = power * power
    return jnp.where(values < 0.0, -power, power).astype(jnp.bfloat16)


def top_of(values):
    top = jnp.maximum(jnp.max(jnp.abs(values), axis=0, keepdims=True), SMALLEST)
    return (top * (1.0 + 2.0**-8)).astype(jnp.bfloat16).astype(jnp.float32)


def decode(coded):
    coded = coded.astype(jnp.float32)
    root = jnp.abs(coded)
    for _ in range(4):
        root = lax.rsqrt(root)
    return jnp.where(coded > 0.0, root, jnp.where(coded < 0.0, -root, 0.0))


def pack_kernel(side_ref, act_ref, grad_ref, *refs):
    *out_refs, sems = refs
    side = side_ref[0]
    blocks = out_refs[0].shape[0]
    copies = []
    for out_ref in reversed(out_refs):
        halves = blocks // out_ref.shape[0]
        at = 0
        for ref in (act_ref, grad_ref):
            count = ref.shape[0] // halves
            copies.append(
                pltpu.make_async_copy(
                    ref.at[pl.ds(side * count if halves > 1 else 0, count)],
                    out_ref.at[pl.ds(at, count)],
                    sems.at[len(copies)],
                )
            )
            at += count
    for copy in copies:
        copy.start()
    for copy in copies:
        copy.wait()


def gram_kernel(pieces, messages, scale, me_ref, act_hbm, grad_hbm, act_ref, grad_ref, *refs):
    refs, (whole, tops, sems) = refs[:-3], refs[-3:]
    plain_refs, sent_refs = refs[: len(refs) - len(messages)], refs[len(refs) - len(messages) :]
    rows = BLK // pieces
    me = me_ref[0]
    steps = []
    for source, target in ((act_hbm, act_ref), (grad_hbm, grad_ref)):
        for first in range(0, source.shape[1], GROUP * BLK):
            columns = slice(first, first + GROUP * BLK)
            copy = pltpu.make_async_copy(
                source.at[:, columns], target.at[:, columns], sems.at[len(steps)]
            )
            copy.start()
            steps.append((target, columns, copy))
    tops[...] = jnp.zeros_like(tops)
    for step, (ref, columns, copy) in enumerate(steps):
        copy.wait()
        for offset in range(GROUP):
            block = step * GROUP + offset
            at = columns.start + offset * BLK
            values = ref[:, at : at + BLK]
            gram = scale * lax.dot_general(
                values, values, contract_rows, preferred_element_type=jnp.float32
            )
            if pieces == 1:
                plain_refs[0][block] = gram
                continue
            whole[offset] = gram
            for ref_at, mask in zip(plain_refs, (0, 2)):
                row = pl.multiple_of((me ^ mask) * rows, rows)
                ref_at[block] = whole[offset, pl.ds(row, rows), :]
            top = top_of(gram)
            tops[block : block + 1, :] = top
            gain = CODE_TOP / top
            for sent_ref, (mask, first, end) in zip(sent_refs, messages):
                if first <= block < end:
                    row = pl.multiple_of((me ^ mask) * rows, rows)
                    place = slice((block - first) * rows, (block - first + 1) * rows)
                    sent_ref[place, :] = encode(whole[offset, pl.ds(row, rows), :] * gain)
    for sent_ref, (_, first, end) in zip(sent_refs, messages):
        sent_ref[(end - first) * rows :, :] = tops[
            first : first + scale_rows(first, end), :
        ].astype(jnp.bfloat16)


def add_group(messages, rows, own_ref, sent_refs, tops_refs, step):
    for block in range(step * GROUP, (step + 1) * GROUP):
        total = own_ref[block]
        for (_, first, end), sent_ref, tops in zip(messages, sent_refs, tops_refs):
            if first <= block < end:
                at = block - first
                values = decode(sent_ref[at * rows : (at + 1) * rows, :])
                total = total + values * tops[at : at + 1, :]
        yield block, total


def load_tops(messages, rows, sent_refs, tops_refs):
    for (_, first, end), sent_ref, tops in zip(messages, sent_refs, tops_refs):
        tops[...] = sent_ref[(end - first) * rows :, :].astype(jnp.float32) * (1.0 / CODE_TOP)


def add_kernel(messages, halves, side_ref, eigen_ref, own_ref, *refs):
    sent_refs, refs = refs[: len(messages)], refs[len(messages) :]
    sum_ref, act_eigen_ref, grad_eigen_ref, *tops_refs = refs
    order_kernel(halves, side_ref, eigen_ref, act_eigen_ref, grad_eigen_ref)
    blocks, rows, _ = own_ref.shape
    load_tops(messages, rows, sent_refs, tops_refs)
    for step in range(blocks // GROUP):
        for block, total in add_group(messages, rows, own_ref, sent_refs, tops_refs, step):
            sum_ref[block] = total


def relay_kernel(message, far_ref, relayed_ref, sent_ref, relayed_tops, tops):
    messages = (message,)
    blocks, rows, _ = far_ref.shape
    load_tops(messages, rows, (relayed_ref,), (relayed_tops,))
    tops[...] = jnp.zeros_like(tops)
    for step in range(blocks // GROUP):
        for block, total in add_group(
            messages, rows, far_ref, (relayed_ref,), (relayed_tops,), step
        ):
            top = top_of(total)
            tops[block : block + 1, :] = top
            sent_ref[block * rows : (block + 1) * rows, :] = encode(total * (CODE_TOP / top))
    sent_ref[blocks * rows :, :] = tops[...].astype(jnp.bfloat16)


def last_add_kernel(messages, owners, own_ref, *refs):
    sent_refs, refs = refs[: len(messages)], refs[len(messages) :]
    weight_refs, refs = refs[:owners], refs[owners:]
    act_ref, grad_ref, score_ref, *tops_refs, sums, scores, sems = refs
    blocks, rows, _ = own_ref.shape
    score_kernel(*weight_refs, scores)
    copies = [pltpu.make_async_copy(scores, score_ref, sems.at[blocks // GROUP])]
    copies[0].start()
    load_tops(messages, rows, sent_refs, tops_refs)
    for step in range(blocks // GROUP):
        for block, total in add_group(messages, rows, own_ref, sent_refs, tops_refs, step):
            sums[block] = total
        first = step * GROUP
        ref, at = act_ref, first
        if first >= act_ref.shape[0]:
            ref, at = grad_ref, first - act_ref.shape[0]
        copies.append(
            pltpu.make_async_copy(
                sums.at[pl.ds(first, GROUP)], ref.at[pl.ds(at, GROUP)], sems.at[step]
            )
        )
        copies[-1].start()
    for copy in copies:
        copy.wait()


def pairs_of(part, side, halves, act_ref, grad_ref):
    half = lax.rem(side + part, halves)
    for ref in (act_ref, grad_ref):
        count = ref.shape[1] // PAIR // halves
        for pair in range(count):
            yield ref, pl.multiple_of((half * count + pair) * PAIR, PAIR)


def eigen_kernel(part, halves, masks, pieces, scale, me_ref, side_ref, act_ref, grad_ref, *refs):
    *shard_refs, power_ref, sums_ref, basis_ref = refs
    me, side = me_ref[0], side_ref[0]
    rows = BLK // pieces
    done = 0
    if part:
        *shard_refs, done_ref = shard_refs
        done = done_ref.shape[0]
        sums_ref[:done] = done_ref[...]
    half = lax.rem(side + part, halves)
    act_half = act_ref.shape[1] // BLK // halves
    grad_half = grad_ref.shape[1] // BLK // halves
    basis_ref[...] = jnp.zeros_like(basis_ref)
    for mask, ref in zip(masks, shard_refs):
        whole = halves > 1 and ref.shape[0] == halves * (act_half + grad_half)
        for block in range(act_half + grad_half):
            at = block
            if whole and block < act_half:
                at = half * act_half + block
            elif whole:
                at = (halves - 1) * act_half + half * grad_half + block
            corner = block % 2
            row = pl.multiple_of(corner * BLK + (me ^ mask) * rows, rows)
            columns = slice(corner * BLK, (corner + 1) * BLK)
            basis_ref[block // 2, pl.ds(row, rows), columns] = ref[at]

    for pair, (ref, column) in enumerate(pairs_of(part, side, halves, act_ref, grad_ref)):
        projected = lax.dot_general(
            ref[:, pl.ds(column, PAIR)],
            basis_ref[pair],
            contract_inner,
            preferred_element_type=jnp.float32,
        )
        power = projected * projected
        power_ref[pair] = power
        sums = scale * jnp.sum(power, axis=0, keepdims=True)
        row = done + 2 * pair
        sums_ref[row : row + 1, :] = sums[:, :BLK]
        sums_ref[row + 1 : row + 2, :] = sums[:, BLK:]


def combine_kernel(halves, act_half, *refs):
    *sums_refs, eigen_ref, total_ref = refs
    eigen = sums_refs[0][...]
    for sums_ref in sums_refs[1:]:
        eigen = eigen + sums_ref[...]
    eigen_ref[...] = eigen
    blocks_half = eigen.shape[0] // halves
    act_total = jnp.zeros((1, BLK), jnp.float32)
    grad_total = jnp.zeros((1, BLK), jnp.float32)
    for part in range(halves):
        first = part * blocks_half
        act_total += jnp.sum(eigen[first : first + act_half], axis=0, keepdims=True)
        grad_total += jnp.sum(eigen[first + act_half : first + blocks_half], axis=0, keepdims=True)
    total_ref[0:1, :] = act_total
    total_ref[1:2, :] = grad_total


def order_kernel(halves, side_ref, eigen_ref, act_eigen_ref, grad_eigen_ref):
    side = side_ref[0]
    act_half, grad_half = act_eigen_ref.shape[0] // halves, grad_eigen_ref.shape[0] // halves
    for part in range(halves):
        half = lax.rem(side + part, halves)
        first = part * (act_half + grad_half)
        middle = first + act_half
        act_eigen_ref[pl.ds(half * act_half, act_half), :] = eigen_ref[first:middle]
        grad_eigen_ref[pl.ds(half * grad_half, grad_half), :] = eigen_ref[
            middle : middle + grad_half
        ]


def weight_kernel(halves, act_half, eigen_ref, *refs):
    *refs, weight_ref, inverse, act_sum, grad_sum = refs
    power_refs, total_refs = refs[:halves], refs[halves:]
    totals = total_refs[0][...]
    for total_ref in total_refs[1:]:
        totals = totals + total_ref[...]
    totals = jnp.sum(totals, axis=1, keepdims=True)
    blocks_half = eigen_ref.shape[0] // halves
    for part in range(halves):
        first = part * blocks_half
        act = slice(first, first + act_half)
        grad = slice(first + act_half, first + blocks_half)
        inverse[act] = 1.0 / (eigen_ref[act] + totals[0:1] * (damp_root / D))
        inverse[grad] = 1.0 / (eigen_ref[grad] + totals[1:2] * (damp_root / FF))
    tokens = act_sum.shape[0]

    @pl.loop(0, tokens // TILE)
    def _(tile):
        here = pl.ds(pl.multiple_of(tile * TILE, TILE), TILE)
        sums = [jnp.zeros((TILE, BLK), jnp.float32), jnp.zeros((TILE, BLK), jnp.float32)]
        for part, power_ref in enumerate(power_refs):
            for pair in range(power_ref.shape[0]):
                which = 0 if 2 * pair < act_half else 1
                for side in range(2):
                    row = part * blocks_half + 2 * pair + side
                    power = power_ref[pair, here, side * BLK : (side + 1) * BLK]
                    sums[which] += power * inverse[row : row + 1, :]
        act_sum[here, :], grad_sum[here, :] = sums

    ones = jnp.ones((8, BLK), jnp.float32)
    for index, total in enumerate((act_sum, grad_sum)):
        sums = lax.dot_general(
            ones,
            total[...],
            contract_lanes,
            precision=lax.Precision.HIGHEST,
            preferred_element_type=jnp.float32,
        )
        weight_ref[index : index + 1, :] = sums[0:1]


def score_kernel(*refs):
    *weight_refs, score_ref = refs
    weights = weight_refs[0][...]
    for weight_ref in weight_refs[1:]:
        weights = weights + weight_ref[...]
    score_ref[...] = weights[0:1] * weights[1:2] * (1.0 / (D * FF))


def swap(value, axis, mask):
    count = lax.axis_size(axis)
    return lax.ppermute(value, axis, [(i, i ^ mask) for i in range(count)])


def share(value, axis, direct):
    if not direct:
        return [lax.psum(value, axis)]
    return [value] + [swap(value, axis, mask) for mask in reversed(range(1, lax.axis_size(axis)))]


def after(values, done):
    return list(lax.optimization_barrier((tuple(values), done))[0])


def local(activations, gradients, basis_act, basis_grad):
    tokens = activations.shape[0]
    act_blocks, grad_blocks = basis_act.shape[0], basis_grad.shape[0]
    blocks = act_blocks + grad_blocks
    dp, owners = lax.axis_size("dp"), lax.axis_size("owner")
    scale = 1.0 / (tokens * dp)
    direct = dp in (2, 4) and owners in (1, 2, 4)
    pieces = dp if direct else 1
    halves = 2 if pieces == 4 and lax.axis_size("groups") == 2 else 1
    rows = BLK // pieces
    me = jnp.full((1,), lax.axis_index("dp") if direct else 0, jnp.int32)
    side = jnp.full((1,), lax.axis_index("groups"), jnp.int32)
    macs = tokens * blocks * BLK * BLK
    input_bytes = 2 * tokens * blocks * BLK
    if direct:
        shards = call(
            pack_kernel,
            [bf16(blocks // part, rows, BLK) for part in range(1, halves + 1)],
            "pack_basis", 0, 2 * blocks * rows * BLK,
            [IN_SMEM, IN_HBM, IN_HBM], [pltpu.SemaphoreType.DMA((2 * halves,))],
        )(side, in_hbm(basis_act), in_hbm(basis_grad))
        near = [shards[0], swap(shards[0], "dp", 1)]
        far = {mask: swap(shards[-1], "dp", mask) for mask in range(pieces - 1, 1, -1)}
    else:
        near = [
            jnp.concatenate(
                [lax.all_gather(part, "dp", axis=1, tiled=True) for part in (basis_act, basis_grad)]
            )
        ]
        far = {}
    masks = [*range(len(near)), *far]

    message = bf16(blocks * rows + scale_rows(0, blocks), BLK)
    whole_range = (0, blocks)
    coded = {4: [(3, *whole_range), (1, *whole_range)], 2: [(1, *whole_range)], 1: []}[pieces]
    plain = 2 if pieces == 4 else 1
    act_here, grad_here, *grams = call(
        functools.partial(gram_kernel, pieces, coded, scale),
        [
            bf16(*activations.shape),
            bf16(*gradients.shape),
            *[f32(blocks, rows, BLK)] * plain,
            *[message] * len(coded),
        ],
        "partial_gram", 4 * macs, input_bytes,
        [IN_SMEM, IN_HBM, IN_HBM],
        [
            pltpu.VMEM((GROUP, BLK, BLK), jnp.float32),
            pltpu.VMEM((scale_rows(0, blocks), BLK), jnp.float32),
            pltpu.SemaphoreType.DMA((blocks // GROUP,)),
        ],
    )(me, in_hbm(activations), in_hbm(gradients))
    own = grams[0]
    sent = {message[0]: chunk for message, chunk in zip(coded, grams[plain:])}
    if not direct:
        own = lax.psum_scatter(own, "dp", scatter_dimension=1, tiled=True)
    if pieces == 4:
        middle = lax.ppermute(sent[3], "dp", [(1, 2), (2, 1)])
        relayed = lax.ppermute(sent[3], "dp", [(0, 1), (3, 2)])

    parts = [[*near, *far.values()]]
    if halves == 2:
        swapped = [swap(after([part], own)[0], "groups", 1) for part in far.values()]
        parts.append([*near, *swapped])
    powers, sums = [], []
    for part, shards in enumerate(parts):
        power, *sums = call(
            functools.partial(eigen_kernel, part, halves, masks, pieces, scale),
            [f32(blocks // halves // 2, tokens, PAIR), f32(blocks // halves * (part + 1), BLK)],
            "partial_eigen", 2 * macs // halves, input_bytes // halves,
            [IN_SMEM, IN_SMEM] + [IN_VMEM] * (2 + len(shards) + len(sums)),
            [pltpu.VMEM((blocks // halves // 2, PAIR, PAIR), jnp.bfloat16)],
        )(me, side, act_here, grad_here, *shards, *sums)
        powers.append(power)
    if pieces == 4:
        sent[2] = call(
            functools.partial(relay_kernel, coded[0]), message, "relay_chunk", 0, 12 * own.size,
            [IN_VMEM, IN_VMEM],
            [pltpu.VMEM((scale_rows(0, blocks), BLK), jnp.float32)] * 2,
        )(*after([grams[1], relayed], (sums, middle)))
    sums = share(sums[0], "dp", direct)
    if pieces == 4:
        sums = after(sums, (middle, sent[2]))
    eigen, totals = call(
        functools.partial(combine_kernel, halves, act_blocks // halves),
        [f32(blocks, BLK), f32(2, BLK)],
        "combine_eigen", 0, 4 * blocks * BLK * pieces, [IN_VMEM] * len(sums),
    )(*sums)
    arrived = {}
    sent.pop(3, None)
    for mask in sent:
        arrived[mask] = swap(after([sent[mask]], totals)[0], "dp", mask)
    totals = share(totals, "owner", direct)
    weights = call(
        functools.partial(weight_kernel, halves, act_blocks // halves),
        f32(2, tokens), "partial_weights", 0, 4 * tokens * blocks * BLK,
        [IN_VMEM] * (1 + halves + len(totals)),
        [
            pltpu.VMEM((blocks, BLK), jnp.float32),
            pltpu.VMEM((tokens, BLK), jnp.float32),
            pltpu.VMEM((tokens, BLK), jnp.float32),
        ],
    )(eigen, *powers, *totals)
    weights = share(weights, "owner", direct)

    def tops_of(count):
        return [pltpu.VMEM((scale_rows(0, blocks), BLK), jnp.float32)] * count

    eigens = [f32(act_blocks, BLK), f32(grad_blocks, BLK)]
    if pieces == 4:
        own, *eigens = call(
            functools.partial(add_kernel, [(None, 0, blocks)], halves),
            [f32(*own.shape), *eigens], "add_chunk", 0, 12 * own.size,
            [IN_SMEM] + [IN_VMEM] * 3, tops_of(1),
        )(side, eigen, own, middle)
        weights[1:] = after(weights[1:], own)
    else:
        eigens = call(
            functools.partial(order_kernel, halves), eigens, "order_eigen", 0,
            8 * blocks * BLK, [IN_SMEM, IN_VMEM],
        )(side, eigen)
    chunks = list(arrived.values())[::-1]
    if chunks:
        *covariance, token_scores = call(
            functools.partial(last_add_kernel, [(None, 0, blocks)] * len(chunks), len(weights)),
            [f32(act_blocks, rows, BLK), f32(grad_blocks, rows, BLK), f32(1, tokens)],
            "last_sums", 0, 16 * own.size, [IN_VMEM] * (1 + len(chunks) + len(weights)),
            [
                *tops_of(len(chunks)),
                pltpu.VMEM(own.shape, jnp.float32),
                pltpu.VMEM((1, tokens), jnp.float32),
                pltpu.SemaphoreType.DMA((blocks // GROUP + 1,)),
            ],
            out_spec=[pl.BlockSpec(memory_space=pl.ANY)] * 3,
        )(own, *chunks, *weights)
    else:
        covariance = own[:act_blocks], own[act_blocks:]
        token_scores = call(
            score_kernel, f32(1, tokens), "token_scores", 0, 8 * tokens, [IN_VMEM] * len(weights)
        )(*weights)
    return (
        *covariance,
        *[eigen.reshape(-1) for eigen in eigens],
        token_scores.reshape(-1),
    )


def solution(mesh):
    return jax.shard_map(
        local,
        mesh=mesh,
        in_specs=(
            P(("groups", "dp"), "owner"),
            P(("groups", "dp"), "owner"),
            P("owner", "dp", None),
            P("owner", "dp", None),
        ),
        out_specs=(
            P(("groups", "owner"), "dp", None),
            P(("groups", "owner"), "dp", None),
            P(("groups", "owner")),
            P(("groups", "owner")),
            P(("groups", "dp")),
        ),
        check_vma=False,
    )
```

```python
import functools
import math

import jax
import jax.numpy as jnp
from jax import lax
from jax.experimental import pallas as pl
from jax.experimental.pallas import tpu as pltpu
from jax.sharding import PartitionSpec as P

D = 4096
FF = 14336
BLK = 128
PAIR = 2 * BLK
GROUP = 4
TILE = 64
VMEM_LIMIT = 24 * 1024 * 1024
CODE_TOP = 2.0**7.875
SMALLEST = 1e-36
SIXTEENTH = 1.0 / (16.0 * math.log(2.0))

damp_root = 0.31622776601683794
contract_rows = (((0,), (0,)), ((), ()))
contract_inner = (((1,), (0,)), ((), ()))
contract_lanes = (((1,), (1,)), ((), ()))

IN_VMEM = pl.BlockSpec(memory_space=pltpu.VMEM)
IN_SMEM = pl.BlockSpec(memory_space=pltpu.SMEM)
IN_HBM = pl.BlockSpec(memory_space=pltpu.HBM)


def scale_rows(first, end):
    return 16 * pl.cdiv(end - first, 16)


def call(
    kernel, out_shape, name, flops, bytes_accessed, in_specs, scratch_shapes=(),
    out_spec=None,
):
    return pl.pallas_call(
        kernel,
        out_shape=out_shape,
        in_specs=in_specs,
        out_specs=out_spec or jax.tree.map(lambda _: IN_VMEM, out_shape),
        scratch_shapes=scratch_shapes,
        compiler_params=pltpu.CompilerParams(vmem_limit_bytes=VMEM_LIMIT),
        cost_estimate=pl.CostEstimate(
            flops=flops, bytes_accessed=bytes_accessed, transcendentals=0
        ),
        name=name,
    )


def in_hbm(value):
    return pltpu.with_memory_space_constraint(value, pltpu.HBM)


def f32(*shape):
    return jax.ShapeDtypeStruct(shape, jnp.float32)


def bf16(*shape):
    return jax.ShapeDtypeStruct(shape, jnp.bfloat16)


def encode(values):
    power = values * values
    power = power * power
    power = power * power
    power = power * power
    return jnp.where(values < 0.0, -power, power).astype(jnp.bfloat16)


def top_of(values):
    top = jnp.maximum(jnp.max(jnp.abs(values), axis=0, keepdims=True), SMALLEST)
    return (top * (1.0 + 2.0**-8)).astype(jnp.bfloat16).astype(jnp.float32)


def decode(coded):
    coded = coded.astype(jnp.float32)
    root = jnp.exp2(jnp.log(jnp.abs(coded)) * SIXTEENTH)
    return jnp.where(coded > 0.0, root, jnp.where(coded < 0.0, -root, 0.0))


def pack_kernel(side_ref, act_ref, grad_ref, *refs):
    *out_refs, sems = refs
    side = side_ref[0]
    blocks = out_refs[0].shape[0]
    copies = []
    for out_ref in reversed(out_refs):
        halves = blocks // out_ref.shape[0]
        at = 0
        for ref in (act_ref, grad_ref):
            count = ref.shape[0] // halves
            copies.append(
                pltpu.make_async_copy(
                    ref.at[pl.ds(side * count if halves > 1 else 0, count)],
                    out_ref.at[pl.ds(at, count)],
                    sems.at[len(copies)],
                )
            )
            at += count
    for copy in copies:
        copy.start()
    for copy in copies:
        copy.wait()


def gram_kernel(pieces, messages, scale, me_ref, act_hbm, grad_hbm, act_ref, grad_ref, *refs):
    refs, (whole, tops, sems) = refs[:-3], refs[-3:]
    plain_refs, sent_refs = refs[: len(refs) - len(messages)], refs[len(refs) - len(messages) :]
    rows = BLK // pieces
    me = me_ref[0]
    steps = []
    for source, target in ((act_hbm, act_ref), (grad_hbm, grad_ref)):
        for first in range(0, source.shape[1], GROUP * BLK):
            columns = slice(first, first + GROUP * BLK)
            copy = pltpu.make_async_copy(
                source.at[:, columns], target.at[:, columns], sems.at[len(steps)]
            )
            copy.start()
            steps.append((target, columns, copy))
    tops[...] = jnp.zeros_like(tops)
    for step, (ref, columns, copy) in enumerate(steps):
        copy.wait()
        for offset in range(GROUP):
            block = step * GROUP + offset
            at = columns.start + offset * BLK
            values = ref[:, at : at + BLK]
            gram = scale * lax.dot_general(
                values, values, contract_rows, preferred_element_type=jnp.float32
            )
            if pieces == 1:
                plain_refs[0][block] = gram
                continue
            whole[offset] = gram
            for ref_at, mask in zip(plain_refs, (0, 2)):
                row = pl.multiple_of((me ^ mask) * rows, rows)
                ref_at[block] = whole[offset, pl.ds(row, rows), :]
            top = top_of(gram)
            tops[block : block + 1, :] = top
            gain = CODE_TOP / top
            for sent_ref, (mask, first, end) in zip(sent_refs, messages):
                if first <= block < end:
                    row = pl.multiple_of((me ^ mask) * rows, rows)
                    place = slice((block - first) * rows, (block - first + 1) * rows)
                    sent_ref[place, :] = encode(whole[offset, pl.ds(row, rows), :] * gain)
    for sent_ref, (_, first, end) in zip(sent_refs, messages):
        sent_ref[(end - first) * rows :, :] = tops[
            first : first + scale_rows(first, end), :
        ].astype(jnp.bfloat16)


def add_group(messages, rows, own_ref, sent_refs, tops_refs, step):
    for block in range(step * GROUP, (step + 1) * GROUP):
        total = own_ref[block]
        for (_, first, end), sent_ref, tops in zip(messages, sent_refs, tops_refs):
            if first <= block < end:
                at = block - first
                values = decode(sent_ref[at * rows : (at + 1) * rows, :])
                total = total + values * tops[at : at + 1, :]
        yield block, total


def load_tops(messages, rows, sent_refs, tops_refs):
    for (_, first, end), sent_ref, tops in zip(messages, sent_refs, tops_refs):
        tops[...] = sent_ref[(end - first) * rows :, :].astype(jnp.float32) * (1.0 / CODE_TOP)


def add_kernel(messages, halves, side_ref, eigen_ref, own_ref, *refs):
    sent_refs, refs = refs[: len(messages)], refs[len(messages) :]
    sum_ref, act_eigen_ref, grad_eigen_ref, *tops_refs = refs
    order_kernel(halves, side_ref, eigen_ref, act_eigen_ref, grad_eigen_ref)
    blocks, rows, _ = own_ref.shape
    load_tops(messages, rows, sent_refs, tops_refs)
    for step in range(blocks // GROUP):
        for block, total in add_group(messages, rows, own_ref, sent_refs, tops_refs, step):
            sum_ref[block] = total


def near_kernel(messages, own_ref, sent_ref, sum_ref, tops):
    blocks, rows, _ = own_ref.shape
    load_tops(messages, rows, (sent_ref,), (tops,))
    for step in range(blocks // GROUP):
        for block, total in add_group(messages, rows, own_ref, (sent_ref,), (tops,), step):
            sum_ref[block] = total


def relay_kernel(message, far_ref, relayed_ref, sent_ref, relayed_tops, tops):
    messages = (message,)
    blocks, rows, _ = far_ref.shape
    load_tops(messages, rows, (relayed_ref,), (relayed_tops,))
    tops[...] = jnp.zeros_like(tops)
    for step in range(blocks // GROUP):
        for block, total in add_group(
            messages, rows, far_ref, (relayed_ref,), (relayed_tops,), step
        ):
            top = top_of(total)
            tops[block : block + 1, :] = top
            sent_ref[block * rows : (block + 1) * rows, :] = encode(total * (CODE_TOP / top))
    sent_ref[blocks * rows :, :] = tops[...].astype(jnp.bfloat16)


def last_add_kernel(messages, owners, own_ref, *refs):
    sent_refs, refs = refs[: len(messages)], refs[len(messages) :]
    weight_refs, refs = refs[:owners], refs[owners:]
    act_ref, grad_ref, score_ref, *tops_refs, sums, scores, sems = refs
    blocks, rows, _ = own_ref.shape
    score_kernel(*weight_refs, scores)
    copies = [pltpu.make_async_copy(scores, score_ref, sems.at[blocks // GROUP])]
    copies[0].start()
    load_tops(messages, rows, sent_refs, tops_refs)
    for step in range(blocks // GROUP):
        for block, total in add_group(messages, rows, own_ref, sent_refs, tops_refs, step):
            sums[block] = total
        first = step * GROUP
        ref, at = act_ref, first
        if first >= act_ref.shape[0]:
            ref, at = grad_ref, first - act_ref.shape[0]
        copies.append(
            pltpu.make_async_copy(
                sums.at[pl.ds(first, GROUP)], ref.at[pl.ds(at, GROUP)], sems.at[step]
            )
        )
        copies[-1].start()
    for copy in copies:
        copy.wait()


def pairs_of(part, side, halves, act_ref, grad_ref):
    half = lax.rem(side + part, halves)
    for ref in (act_ref, grad_ref):
        count = ref.shape[1] // PAIR // halves
        for pair in range(count):
            yield ref, pl.multiple_of((half * count + pair) * PAIR, PAIR)


def eigen_kernel(part, halves, masks, pieces, scale, me_ref, side_ref, act_ref, grad_ref, *refs):
    *shard_refs, power_ref, sums_ref, basis_ref = refs
    me, side = me_ref[0], side_ref[0]
    rows = BLK // pieces
    done = 0
    if part:
        *shard_refs, done_ref = shard_refs
        done = done_ref.shape[0]
        sums_ref[:done] = done_ref[...]
    half = lax.rem(side + part, halves)
    act_half = act_ref.shape[1] // BLK // halves
    grad_half = grad_ref.shape[1] // BLK // halves
    basis_ref[...] = jnp.zeros_like(basis_ref)
    for mask, ref in zip(masks, shard_refs):
        whole = halves > 1 and ref.shape[0] == halves * (act_half + grad_half)
        for block in range(act_half + grad_half):
            at = block
            if whole and block < act_half:
                at = half * act_half + block
            elif whole:
                at = (halves - 1) * act_half + half * grad_half + block
            corner = block % 2
            row = pl.multiple_of(corner * BLK + (me ^ mask) * rows, rows)
            columns = slice(corner * BLK, (corner + 1) * BLK)
            basis_ref[block // 2, pl.ds(row, rows), columns] = ref[at]

    for pair, (ref, column) in enumerate(pairs_of(part, side, halves, act_ref, grad_ref)):
        projected = lax.dot_general(
            ref[:, pl.ds(column, PAIR)],
            basis_ref[pair],
            contract_inner,
            preferred_element_type=jnp.float32,
        )
        power = projected * projected
        power_ref[pair] = power
        sums = scale * jnp.sum(power, axis=0, keepdims=True)
        row = done + 2 * pair
        sums_ref[row : row + 1, :] = sums[:, :BLK]
        sums_ref[row + 1 : row + 2, :] = sums[:, BLK:]


def combine_kernel(halves, act_half, *refs):
    *sums_refs, eigen_ref, total_ref = refs
    eigen = sums_refs[0][...]
    for sums_ref in sums_refs[1:]:
        eigen = eigen + sums_ref[...]
    eigen_ref[...] = eigen
    blocks_half = eigen.shape[0] // halves
    act_total = jnp.zeros((1, BLK), jnp.float32)
    grad_total = jnp.zeros((1, BLK), jnp.float32)
    for part in range(halves):
        first = part * blocks_half
        act_total += jnp.sum(eigen[first : first + act_half], axis=0, keepdims=True)
        grad_total += jnp.sum(eigen[first + act_half : first + blocks_half], axis=0, keepdims=True)
    total_ref[0:1, :] = act_total
    total_ref[1:2, :] = grad_total


def order_kernel(halves, side_ref, eigen_ref, act_eigen_ref, grad_eigen_ref):
    side = side_ref[0]
    act_half, grad_half = act_eigen_ref.shape[0] // halves, grad_eigen_ref.shape[0] // halves
    for part in range(halves):
        half = lax.rem(side + part, halves)
        first = part * (act_half + grad_half)
        middle = first + act_half
        act_eigen_ref[pl.ds(half * act_half, act_half), :] = eigen_ref[first:middle]
        grad_eigen_ref[pl.ds(half * grad_half, grad_half), :] = eigen_ref[
            middle : middle + grad_half
        ]


def weight_kernel(halves, act_half, eigen_ref, *refs):
    *refs, weight_ref, inverse, act_sum, grad_sum = refs
    power_refs, total_refs = refs[:halves], refs[halves:]
    totals = total_refs[0][...]
    for total_ref in total_refs[1:]:
        totals = totals + total_ref[...]
    totals = jnp.sum(totals, axis=1, keepdims=True)
    blocks_half = eigen_ref.shape[0] // halves
    for part in range(halves):
        first = part * blocks_half
        act = slice(first, first + act_half)
        grad = slice(first + act_half, first + blocks_half)
        inverse[act] = 1.0 / (eigen_ref[act] + totals[0:1] * (damp_root / D))
        inverse[grad] = 1.0 / (eigen_ref[grad] + totals[1:2] * (damp_root / FF))
    tokens = act_sum.shape[0]

    @pl.loop(0, tokens // TILE)
    def _(tile):
        here = pl.ds(pl.multiple_of(tile * TILE, TILE), TILE)
        sums = [jnp.zeros((TILE, BLK), jnp.float32), jnp.zeros((TILE, BLK), jnp.float32)]
        for part, power_ref in enumerate(power_refs):
            for pair in range(power_ref.shape[0]):
                which = 0 if 2 * pair < act_half else 1
                for side in range(2):
                    row = part * blocks_half + 2 * pair + side
                    power = power_ref[pair, here, side * BLK : (side + 1) * BLK]
                    sums[which] += power * inverse[row : row + 1, :]
        act_sum[here, :], grad_sum[here, :] = sums

    ones = jnp.ones((8, BLK), jnp.float32)
    for index, total in enumerate((act_sum, grad_sum)):
        sums = lax.dot_general(
            ones,
            total[...],
            contract_lanes,
            precision=lax.Precision.HIGHEST,
            preferred_element_type=jnp.float32,
        )
        weight_ref[index : index + 1, :] = sums[0:1]


def score_kernel(*refs):
    *weight_refs, score_ref = refs
    weights = weight_refs[0][...]
    for weight_ref in weight_refs[1:]:
        weights = weights + weight_ref[...]
    score_ref[...] = weights[0:1] * weights[1:2] * (1.0 / (D * FF))


def swap(value, axis, mask):
    count = lax.axis_size(axis)
    return lax.ppermute(value, axis, [(i, i ^ mask) for i in range(count)])


def share(value, axis, direct):
    if not direct:
        return [lax.psum(value, axis)]
    return [value] + [swap(value, axis, mask) for mask in reversed(range(1, lax.axis_size(axis)))]


def after(values, done):
    return list(lax.optimization_barrier((tuple(values), done))[0])


def local(activations, gradients, basis_act, basis_grad):
    tokens = activations.shape[0]
    act_blocks, grad_blocks = basis_act.shape[0], basis_grad.shape[0]
    blocks = act_blocks + grad_blocks
    dp, owners = lax.axis_size("dp"), lax.axis_size("owner")
    scale = 1.0 / (tokens * dp)
    direct = dp in (2, 4) and owners in (1, 2, 4)
    pieces = dp if direct else 1
    halves = 2 if pieces == 4 and lax.axis_size("groups") == 2 else 1
    rows = BLK // pieces
    me = jnp.full((1,), lax.axis_index("dp") if direct else 0, jnp.int32)
    side = jnp.full((1,), lax.axis_index("groups"), jnp.int32)
    macs = tokens * blocks * BLK * BLK
    input_bytes = 2 * tokens * blocks * BLK
    if direct:
        shards = call(
            pack_kernel,
            [bf16(blocks // part, rows, BLK) for part in range(1, halves + 1)],
            "pack_basis", 0, 2 * blocks * rows * BLK,
            [IN_SMEM, IN_HBM, IN_HBM], [pltpu.SemaphoreType.DMA((2 * halves,))],
        )(side, in_hbm(basis_act), in_hbm(basis_grad))
        near = [shards[0], swap(shards[0], "dp", 1)]
        far = {mask: swap(shards[-1], "dp", mask) for mask in range(pieces - 1, 1, -1)}
    else:
        near = [
            jnp.concatenate(
                [lax.all_gather(part, "dp", axis=1, tiled=True) for part in (basis_act, basis_grad)]
            )
        ]
        far = {}
    masks = [*range(len(near)), *far]

    message = bf16(blocks * rows + scale_rows(0, blocks), BLK)
    whole_range = (0, blocks)
    coded = {4: [(3, *whole_range), (1, *whole_range)], 2: [(1, *whole_range)], 1: []}[pieces]
    plain = 2 if pieces == 4 else 1
    act_here, grad_here, *grams = call(
        functools.partial(gram_kernel, pieces, coded, scale),
        [
            bf16(*activations.shape),
            bf16(*gradients.shape),
            *[f32(blocks, rows, BLK)] * plain,
            *[message] * len(coded),
        ],
        "partial_gram", 4 * macs, input_bytes,
        [IN_SMEM, IN_HBM, IN_HBM],
        [
            pltpu.VMEM((GROUP, BLK, BLK), jnp.float32),
            pltpu.VMEM((scale_rows(0, blocks), BLK), jnp.float32),
            pltpu.SemaphoreType.DMA((blocks // GROUP,)),
        ],
    )(me, in_hbm(activations), in_hbm(gradients))
    own = grams[0]
    sent = {message[0]: chunk for message, chunk in zip(coded, grams[plain:])}
    if not direct:
        own = lax.psum_scatter(own, "dp", scatter_dimension=1, tiled=True)
    if pieces == 4:
        middle = lax.ppermute(sent[3], "dp", [(1, 2), (2, 1)])
        relayed = lax.ppermute(sent[3], "dp", [(0, 1), (3, 2)])

    parts = [[*near, *far.values()]]
    if halves == 2:
        swapped = [swap(after([part], own)[0], "groups", 1) for part in far.values()]
        parts.append([*near, *swapped])
    powers, sums = [], []
    for part, shards in enumerate(parts):
        power, *sums = call(
            functools.partial(eigen_kernel, part, halves, masks, pieces, scale),
            [f32(blocks // halves // 2, tokens, PAIR), f32(blocks // halves * (part + 1), BLK)],
            "partial_eigen", 2 * macs // halves, input_bytes // halves,
            [IN_SMEM, IN_SMEM] + [IN_VMEM] * (2 + len(shards) + len(sums)),
            [pltpu.VMEM((blocks // halves // 2, PAIR, PAIR), jnp.bfloat16)],
        )(me, side, act_here, grad_here, *shards, *sums)
        powers.append(power)
    if pieces == 4:
        sent[2] = call(
            functools.partial(relay_kernel, coded[0]), message, "relay_chunk", 0, 12 * own.size,
            [IN_VMEM, IN_VMEM],
            [pltpu.VMEM((scale_rows(0, blocks), BLK), jnp.float32)] * 2,
        )(*after([grams[1], relayed], sums))
    sums = share(sums[0], "dp", direct)
    if pieces == 4:
        sums = after(sums, (middle, sent[2]))
    eigen, totals = call(
        functools.partial(combine_kernel, halves, act_blocks // halves),
        [f32(blocks, BLK), f32(2, BLK)],
        "combine_eigen", 0, 4 * blocks * BLK * pieces, [IN_VMEM] * len(sums),
    )(*sums)
    arrived = {}
    sent.pop(3, None)
    for mask in sent:
        arrived[mask] = swap(after([sent[mask]], totals)[0], "dp", mask)
    totals = share(totals, "owner", direct)
    weights = call(
        functools.partial(weight_kernel, halves, act_blocks // halves),
        f32(2, tokens), "partial_weights", 0, 4 * tokens * blocks * BLK,
        [IN_VMEM] * (1 + halves + len(totals)),
        [
            pltpu.VMEM((blocks, BLK), jnp.float32),
            pltpu.VMEM((tokens, BLK), jnp.float32),
            pltpu.VMEM((tokens, BLK), jnp.float32),
        ],
    )(eigen, *powers, *totals)
    weights = share(weights, "owner", direct)

    def tops_of(count):
        return [pltpu.VMEM((scale_rows(0, blocks), BLK), jnp.float32)] * count

    eigens = [f32(act_blocks, BLK), f32(grad_blocks, BLK)]
    if pieces == 4:
        own, *eigens = call(
            functools.partial(add_kernel, [(None, 0, blocks)], halves),
            [f32(*own.shape), *eigens], "add_chunk", 0, 12 * own.size,
            [IN_SMEM] + [IN_VMEM] * 3, tops_of(1),
        )(side, eigen, own, middle)
        weights[1:] = after(weights[1:], own)
    else:
        eigens = call(
            functools.partial(order_kernel, halves), eigens, "order_eigen", 0,
            8 * blocks * BLK, [IN_SMEM, IN_VMEM],
        )(side, eigen)
    if pieces == 4:
        own = call(
            functools.partial(near_kernel, [(None, 0, blocks)]), f32(*own.shape), "add_near", 0,
            12 * own.size, [IN_VMEM] * 2, tops_of(1),
        )(own, arrived.pop(1))
    chunks = list(arrived.values())
    if chunks:
        *covariance, token_scores = call(
            functools.partial(last_add_kernel, [(None, 0, blocks)] * len(chunks), len(weights)),
            [f32(act_blocks, rows, BLK), f32(grad_blocks, rows, BLK), f32(1, tokens)],
            "last_sums", 0, 16 * own.size, [IN_VMEM] * (1 + len(chunks) + len(weights)),
            [
                *tops_of(len(chunks)),
                pltpu.VMEM(own.shape, jnp.float32),
                pltpu.VMEM((1, tokens), jnp.float32),
                pltpu.SemaphoreType.DMA((blocks // GROUP + 1,)),
            ],
            out_spec=[pl.BlockSpec(memory_space=pl.ANY)] * 3,
        )(own, *chunks, *weights)
    else:
        covariance = own[:act_blocks], own[act_blocks:]
        token_scores = call(
            score_kernel, f32(1, tokens), "token_scores", 0, 8 * tokens, [IN_VMEM] * len(weights)
        )(*weights)
    return (
        *covariance,
        *[eigen.reshape(-1) for eigen in eigens],
        token_scores.reshape(-1),
    )


def solution(mesh):
    return jax.shard_map(
        local,
        mesh=mesh,
        in_specs=(
            P(("groups", "dp"), "owner"),
            P(("groups", "dp"), "owner"),
            P("owner", "dp", None),
            P("owner", "dp", None),
        ),
        out_specs=(
            P(("groups", "owner"), "dp", None),
            P(("groups", "owner"), "dp", None),
            P(("groups", "owner")),
            P(("groups", "owner")),
            P(("groups", "dp")),
        ),
        check_vma=False,
    )
```

```python
import functools
import math

import jax
import jax.numpy as jnp
from jax import lax
from jax.experimental import pallas as pl
from jax.experimental.pallas import tpu as pltpu
from jax.sharding import PartitionSpec as P

D = 4096
FF = 14336
BLK = 128
PAIR = 2 * BLK
GROUP = 4
TILE = 64
VMEM_LIMIT = 24 * 1024 * 1024
CODE_TOP = 2.0**7.875
SMALLEST = 1e-36
SIXTEENTH = 1.0 / (16.0 * math.log(2.0))

damp_root = 0.31622776601683794
contract_rows = (((0,), (0,)), ((), ()))
contract_inner = (((1,), (0,)), ((), ()))
contract_lanes = (((1,), (1,)), ((), ()))

IN_VMEM = pl.BlockSpec(memory_space=pltpu.VMEM)
IN_SMEM = pl.BlockSpec(memory_space=pltpu.SMEM)
IN_HBM = pl.BlockSpec(memory_space=pltpu.HBM)


def scale_rows(first, end):
    return 16 * pl.cdiv(end - first, 16)


def call(
    kernel, out_shape, name, flops, bytes_accessed, in_specs, scratch_shapes=(),
    out_spec=None,
):
    return pl.pallas_call(
        kernel,
        out_shape=out_shape,
        in_specs=in_specs,
        out_specs=out_spec or jax.tree.map(lambda _: IN_VMEM, out_shape),
        scratch_shapes=scratch_shapes,
        compiler_params=pltpu.CompilerParams(vmem_limit_bytes=VMEM_LIMIT),
        cost_estimate=pl.CostEstimate(
            flops=flops, bytes_accessed=bytes_accessed, transcendentals=0
        ),
        name=name,
    )


def in_hbm(value):
    return pltpu.with_memory_space_constraint(value, pltpu.HBM)


def f32(*shape):
    return jax.ShapeDtypeStruct(shape, jnp.float32)


def bf16(*shape):
    return jax.ShapeDtypeStruct(shape, jnp.bfloat16)


def encode(values):
    power = values * values
    power = power * power
    power = power * power
    power = power * power
    return jnp.where(values < 0.0, -power, power).astype(jnp.bfloat16)


def top_of(values):
    top = jnp.maximum(jnp.max(jnp.abs(values), axis=0, keepdims=True), SMALLEST)
    return (top * (1.0 + 2.0**-8)).astype(jnp.bfloat16).astype(jnp.float32)


def decode(coded):
    coded = coded.astype(jnp.float32)
    root = jnp.exp2(jnp.log(jnp.abs(coded)) * SIXTEENTH)
    return jnp.where(coded > 0.0, root, jnp.where(coded < 0.0, -root, 0.0))


def pack_kernel(side_ref, act_ref, grad_ref, *refs):
    *out_refs, sems = refs
    side = side_ref[0]
    blocks = out_refs[0].shape[0]
    copies = []
    for out_ref in reversed(out_refs):
        halves = blocks // out_ref.shape[0]
        at = 0
        for ref in (act_ref, grad_ref):
            count = ref.shape[0] // halves
            copies.append(
                pltpu.make_async_copy(
                    ref.at[pl.ds(side * count if halves > 1 else 0, count)],
                    out_ref.at[pl.ds(at, count)],
                    sems.at[len(copies)],
                )
            )
            at += count
    for copy in copies:
        copy.start()
    for copy in copies:
        copy.wait()


def gram_kernel(pieces, messages, scale, me_ref, act_hbm, grad_hbm, act_ref, grad_ref, *refs):
    refs, (whole, tops, sems) = refs[:-3], refs[-3:]
    plain_refs, sent_refs = refs[: len(refs) - len(messages)], refs[len(refs) - len(messages) :]
    rows = BLK // pieces
    me = me_ref[0]
    steps = []
    for source, target in ((act_hbm, act_ref), (grad_hbm, grad_ref)):
        for first in range(0, source.shape[1], GROUP * BLK):
            columns = slice(first, first + GROUP * BLK)
            copy = pltpu.make_async_copy(
                source.at[:, columns], target.at[:, columns], sems.at[len(steps)]
            )
            copy.start()
            steps.append((target, columns, copy))
    tops[...] = jnp.zeros_like(tops)
    for step, (ref, columns, copy) in enumerate(steps):
        copy.wait()
        for offset in range(GROUP):
            block = step * GROUP + offset
            at = columns.start + offset * BLK
            values = ref[:, at : at + BLK]
            gram = scale * lax.dot_general(
                values, values, contract_rows, preferred_element_type=jnp.float32
            )
            if pieces == 1:
                plain_refs[0][block] = gram
                continue
            whole[offset] = gram
            for ref_at, mask in zip(plain_refs, (0, 2)):
                row = pl.multiple_of((me ^ mask) * rows, rows)
                ref_at[block] = whole[offset, pl.ds(row, rows), :]
            top = top_of(gram)
            tops[block : block + 1, :] = top
            gain = CODE_TOP / top
            for sent_ref, (mask, first, end) in zip(sent_refs, messages):
                if first <= block < end:
                    row = pl.multiple_of((me ^ mask) * rows, rows)
                    place = slice((block - first) * rows, (block - first + 1) * rows)
                    sent_ref[place, :] = encode(whole[offset, pl.ds(row, rows), :] * gain)
    for sent_ref, (_, first, end) in zip(sent_refs, messages):
        sent_ref[(end - first) * rows :, :] = tops[
            first : first + scale_rows(first, end), :
        ].astype(jnp.bfloat16)


def add_group(messages, rows, own_ref, sent_refs, tops_refs, step):
    for block in range(step * GROUP, (step + 1) * GROUP):
        total = own_ref[block]
        for (_, first, end), sent_ref, tops in zip(messages, sent_refs, tops_refs):
            if first <= block < end:
                at = block - first
                values = decode(sent_ref[at * rows : (at + 1) * rows, :])
                total = total + values * tops[at : at + 1, :]
        yield block, total


def load_tops(messages, rows, sent_refs, tops_refs):
    for (_, first, end), sent_ref, tops in zip(messages, sent_refs, tops_refs):
        tops[...] = sent_ref[(end - first) * rows :, :].astype(jnp.float32) * (1.0 / CODE_TOP)


def add_kernel(messages, halves, side_ref, eigen_ref, own_ref, *refs):
    sent_refs, refs = refs[: len(messages)], refs[len(messages) :]
    sum_ref, act_eigen_ref, grad_eigen_ref, *tops_refs = refs
    order_kernel(halves, side_ref, eigen_ref, act_eigen_ref, grad_eigen_ref)
    blocks, rows, _ = own_ref.shape
    load_tops(messages, rows, sent_refs, tops_refs)
    for step in range(blocks // GROUP):
        for block, total in add_group(messages, rows, own_ref, sent_refs, tops_refs, step):
            sum_ref[block] = total


def near_kernel(messages, own_ref, sent_ref, *refs):
    *weight_refs, sum_ref, score_ref, tops, scores, sem = refs
    blocks, rows, _ = own_ref.shape
    score_kernel(*weight_refs, scores)
    copy = pltpu.make_async_copy(scores, score_ref, sem)
    copy.start()
    load_tops(messages, rows, (sent_ref,), (tops,))
    for step in range(blocks // GROUP):
        for block, total in add_group(messages, rows, own_ref, (sent_ref,), (tops,), step):
            sum_ref[block] = total
    copy.wait()


def relay_kernel(message, far_ref, relayed_ref, sent_ref, relayed_tops, tops):
    messages = (message,)
    blocks, rows, _ = far_ref.shape
    load_tops(messages, rows, (relayed_ref,), (relayed_tops,))
    tops[...] = jnp.zeros_like(tops)
    for step in range(blocks // GROUP):
        for block, total in add_group(
            messages, rows, far_ref, (relayed_ref,), (relayed_tops,), step
        ):
            top = top_of(total)
            tops[block : block + 1, :] = top
            sent_ref[block * rows : (block + 1) * rows, :] = encode(total * (CODE_TOP / top))
    sent_ref[blocks * rows :, :] = tops[...].astype(jnp.bfloat16)


def last_add_kernel(messages, owners, own_ref, *refs):
    sent_refs, refs = refs[: len(messages)], refs[len(messages) :]
    weight_refs, refs = refs[:owners], refs[owners:]
    act_ref, grad_ref, *score_ref = refs[: 3 if owners else 2]
    *tops_refs, sums, scores, sems = refs[3 if owners else 2 :]
    blocks, rows, _ = own_ref.shape
    copies = []
    if weight_refs:
        score_kernel(*weight_refs, scores)
        copies = [pltpu.make_async_copy(scores, score_ref[0], sems.at[blocks // GROUP])]
        copies[0].start()
    load_tops(messages, rows, sent_refs, tops_refs)
    for step in range(blocks // GROUP):
        for block, total in add_group(messages, rows, own_ref, sent_refs, tops_refs, step):
            sums[block] = total
        first = step * GROUP
        ref, at = act_ref, first
        if first >= act_ref.shape[0]:
            ref, at = grad_ref, first - act_ref.shape[0]
        copies.append(
            pltpu.make_async_copy(
                sums.at[pl.ds(first, GROUP)], ref.at[pl.ds(at, GROUP)], sems.at[step]
            )
        )
        copies[-1].start()
    for copy in copies:
        copy.wait()


def pairs_of(part, side, halves, act_ref, grad_ref):
    half = lax.rem(side + part, halves)
    for ref in (act_ref, grad_ref):
        count = ref.shape[1] // PAIR // halves
        for pair in range(count):
            yield ref, pl.multiple_of((half * count + pair) * PAIR, PAIR)


def eigen_kernel(part, halves, masks, pieces, scale, me_ref, side_ref, act_ref, grad_ref, *refs):
    *shard_refs, power_ref, sums_ref, basis_ref = refs
    me, side = me_ref[0], side_ref[0]
    rows = BLK // pieces
    done = 0
    if part:
        *shard_refs, done_ref = shard_refs
        done = done_ref.shape[0]
        sums_ref[:done] = done_ref[...]
    half = lax.rem(side + part, halves)
    act_half = act_ref.shape[1] // BLK // halves
    grad_half = grad_ref.shape[1] // BLK // halves
    basis_ref[...] = jnp.zeros_like(basis_ref)
    for mask, ref in zip(masks, shard_refs):
        whole = halves > 1 and ref.shape[0] == halves * (act_half + grad_half)
        for block in range(act_half + grad_half):
            at = block
            if whole and block < act_half:
                at = half * act_half + block
            elif whole:
                at = (halves - 1) * act_half + half * grad_half + block
            corner = block % 2
            row = pl.multiple_of(corner * BLK + (me ^ mask) * rows, rows)
            columns = slice(corner * BLK, (corner + 1) * BLK)
            basis_ref[block // 2, pl.ds(row, rows), columns] = ref[at]

    for pair, (ref, column) in enumerate(pairs_of(part, side, halves, act_ref, grad_ref)):
        projected = lax.dot_general(
            ref[:, pl.ds(column, PAIR)],
            basis_ref[pair],
            contract_inner,
            preferred_element_type=jnp.float32,
        )
        power = projected * projected
        power_ref[pair] = power
        sums = scale * jnp.sum(power, axis=0, keepdims=True)
        row = done + 2 * pair
        sums_ref[row : row + 1, :] = sums[:, :BLK]
        sums_ref[row + 1 : row + 2, :] = sums[:, BLK:]


def combine_kernel(halves, act_half, *refs):
    *sums_refs, eigen_ref, total_ref = refs
    eigen = sums_refs[0][...]
    for sums_ref in sums_refs[1:]:
        eigen = eigen + sums_ref[...]
    eigen_ref[...] = eigen
    blocks_half = eigen.shape[0] // halves
    act_total = jnp.zeros((1, BLK), jnp.float32)
    grad_total = jnp.zeros((1, BLK), jnp.float32)
    for part in range(halves):
        first = part * blocks_half
        act_total += jnp.sum(eigen[first : first + act_half], axis=0, keepdims=True)
        grad_total += jnp.sum(eigen[first + act_half : first + blocks_half], axis=0, keepdims=True)
    total_ref[0:1, :] = act_total
    total_ref[1:2, :] = grad_total


def order_kernel(halves, side_ref, eigen_ref, act_eigen_ref, grad_eigen_ref):
    side = side_ref[0]
    act_half, grad_half = act_eigen_ref.shape[0] // halves, grad_eigen_ref.shape[0] // halves
    for part in range(halves):
        half = lax.rem(side + part, halves)
        first = part * (act_half + grad_half)
        middle = first + act_half
        act_eigen_ref[pl.ds(half * act_half, act_half), :] = eigen_ref[first:middle]
        grad_eigen_ref[pl.ds(half * grad_half, grad_half), :] = eigen_ref[
            middle : middle + grad_half
        ]


def weight_kernel(halves, act_half, eigen_ref, *refs):
    *refs, weight_ref, inverse, act_sum, grad_sum = refs
    power_refs, total_refs = refs[:halves], refs[halves:]
    totals = total_refs[0][...]
    for total_ref in total_refs[1:]:
        totals = totals + total_ref[...]
    totals = jnp.sum(totals, axis=1, keepdims=True)
    blocks_half = eigen_ref.shape[0] // halves
    for part in range(halves):
        first = part * blocks_half
        act = slice(first, first + act_half)
        grad = slice(first + act_half, first + blocks_half)
        inverse[act] = 1.0 / (eigen_ref[act] + totals[0:1] * (damp_root / D))
        inverse[grad] = 1.0 / (eigen_ref[grad] + totals[1:2] * (damp_root / FF))
    tokens = act_sum.shape[0]

    @pl.loop(0, tokens // TILE)
    def _(tile):
        here = pl.ds(pl.multiple_of(tile * TILE, TILE), TILE)
        sums = [jnp.zeros((TILE, BLK), jnp.float32), jnp.zeros((TILE, BLK), jnp.float32)]
        for part, power_ref in enumerate(power_refs):
            for pair in range(power_ref.shape[0]):
                which = 0 if 2 * pair < act_half else 1
                for side in range(2):
                    row = part * blocks_half + 2 * pair + side
                    power = power_ref[pair, here, side * BLK : (side + 1) * BLK]
                    sums[which] += power * inverse[row : row + 1, :]
        act_sum[here, :], grad_sum[here, :] = sums

    ones = jnp.ones((8, BLK), jnp.float32)
    for index, total in enumerate((act_sum, grad_sum)):
        sums = lax.dot_general(
            ones,
            total[...],
            contract_lanes,
            precision=lax.Precision.HIGHEST,
            preferred_element_type=jnp.float32,
        )
        weight_ref[index : index + 1, :] = sums[0:1]


def score_kernel(*refs):
    *weight_refs, score_ref = refs
    weights = weight_refs[0][...]
    for weight_ref in weight_refs[1:]:
        weights = weights + weight_ref[...]
    score_ref[...] = weights[0:1] * weights[1:2] * (1.0 / (D * FF))


def swap(value, axis, mask):
    count = lax.axis_size(axis)
    return lax.ppermute(value, axis, [(i, i ^ mask) for i in range(count)])


def share(value, axis, direct):
    if not direct:
        return [lax.psum(value, axis)]
    return [value] + [swap(value, axis, mask) for mask in reversed(range(1, lax.axis_size(axis)))]


def after(values, done):
    return list(lax.optimization_barrier((tuple(values), done))[0])


def local(activations, gradients, basis_act, basis_grad):
    tokens = activations.shape[0]
    act_blocks, grad_blocks = basis_act.shape[0], basis_grad.shape[0]
    blocks = act_blocks + grad_blocks
    dp, owners = lax.axis_size("dp"), lax.axis_size("owner")
    scale = 1.0 / (tokens * dp)
    direct = dp in (2, 4) and owners in (1, 2, 4)
    pieces = dp if direct else 1
    halves = 2 if pieces == 4 and lax.axis_size("groups") == 2 else 1
    rows = BLK // pieces
    me = jnp.full((1,), lax.axis_index("dp") if direct else 0, jnp.int32)
    side = jnp.full((1,), lax.axis_index("groups"), jnp.int32)
    macs = tokens * blocks * BLK * BLK
    input_bytes = 2 * tokens * blocks * BLK
    if direct:
        shards = call(
            pack_kernel,
            [bf16(blocks // part, rows, BLK) for part in range(1, halves + 1)],
            "pack_basis", 0, 2 * blocks * rows * BLK,
            [IN_SMEM, IN_HBM, IN_HBM], [pltpu.SemaphoreType.DMA((2 * halves,))],
        )(side, in_hbm(basis_act), in_hbm(basis_grad))
        near = [shards[0], swap(shards[0], "dp", 1)]
        far = {mask: swap(shards[-1], "dp", mask) for mask in range(pieces - 1, 1, -1)}
    else:
        near = [
            jnp.concatenate(
                [lax.all_gather(part, "dp", axis=1, tiled=True) for part in (basis_act, basis_grad)]
            )
        ]
        far = {}
    masks = [*range(len(near)), *far]

    message = bf16(blocks * rows + scale_rows(0, blocks), BLK)
    whole_range = (0, blocks)
    coded = {4: [(3, *whole_range), (1, *whole_range)], 2: [(1, *whole_range)], 1: []}[pieces]
    plain = 2 if pieces == 4 else 1
    act_here, grad_here, *grams = call(
        functools.partial(gram_kernel, pieces, coded, scale),
        [
            bf16(*activations.shape),
            bf16(*gradients.shape),
            *[f32(blocks, rows, BLK)] * plain,
            *[message] * len(coded),
        ],
        "partial_gram", 4 * macs, input_bytes,
        [IN_SMEM, IN_HBM, IN_HBM],
        [
            pltpu.VMEM((GROUP, BLK, BLK), jnp.float32),
            pltpu.VMEM((scale_rows(0, blocks), BLK), jnp.float32),
            pltpu.SemaphoreType.DMA((blocks // GROUP,)),
        ],
    )(me, in_hbm(activations), in_hbm(gradients))
    own = grams[0]
    sent = {message[0]: chunk for message, chunk in zip(coded, grams[plain:])}
    if not direct:
        own = lax.psum_scatter(own, "dp", scatter_dimension=1, tiled=True)
    if pieces == 4:
        middle = lax.ppermute(sent[3], "dp", [(1, 2), (2, 1)])
        relayed = lax.ppermute(sent[3], "dp", [(0, 1), (3, 2)])

    parts = [[*near, *far.values()]]
    if halves == 2:
        swapped = [swap(after([part], own)[0], "groups", 1) for part in far.values()]
        parts.append([*near, *swapped])
    powers, sums = [], []
    for part, shards in enumerate(parts):
        power, *sums = call(
            functools.partial(eigen_kernel, part, halves, masks, pieces, scale),
            [f32(blocks // halves // 2, tokens, PAIR), f32(blocks // halves * (part + 1), BLK)],
            "partial_eigen", 2 * macs // halves, input_bytes // halves,
            [IN_SMEM, IN_SMEM] + [IN_VMEM] * (2 + len(shards) + len(sums)),
            [pltpu.VMEM((blocks // halves // 2, PAIR, PAIR), jnp.bfloat16)],
        )(me, side, act_here, grad_here, *shards, *sums)
        powers.append(power)
    if pieces == 4:
        sent[2] = call(
            functools.partial(relay_kernel, coded[0]), message, "relay_chunk", 0, 12 * own.size,
            [IN_VMEM, IN_VMEM],
            [pltpu.VMEM((scale_rows(0, blocks), BLK), jnp.float32)] * 2,
        )(*after([grams[1], relayed], sums))
    sums = share(sums[0], "dp", direct)
    if pieces == 4:
        sums = after(sums, (middle, sent[2]))
    eigen, totals = call(
        functools.partial(combine_kernel, halves, act_blocks // halves),
        [f32(blocks, BLK), f32(2, BLK)],
        "combine_eigen", 0, 4 * blocks * BLK * pieces, [IN_VMEM] * len(sums),
    )(*sums)
    arrived = {}
    sent.pop(3, None)
    for mask in sent:
        arrived[mask] = swap(after([sent[mask]], totals)[0], "dp", mask)
    totals = share(totals, "owner", direct)
    weights = call(
        functools.partial(weight_kernel, halves, act_blocks // halves),
        f32(2, tokens), "partial_weights", 0, 4 * tokens * blocks * BLK,
        [IN_VMEM] * (1 + halves + len(totals)),
        [
            pltpu.VMEM((blocks, BLK), jnp.float32),
            pltpu.VMEM((tokens, BLK), jnp.float32),
            pltpu.VMEM((tokens, BLK), jnp.float32),
        ],
    )(eigen, *powers, *totals)
    weights = share(weights, "owner", direct)

    def tops_of(count):
        return [pltpu.VMEM((scale_rows(0, blocks), BLK), jnp.float32)] * count

    eigens = [f32(act_blocks, BLK), f32(grad_blocks, BLK)]
    if pieces == 4:
        own, *eigens = call(
            functools.partial(add_kernel, [(None, 0, blocks)], halves),
            [f32(*own.shape), *eigens], "add_chunk", 0, 12 * own.size,
            [IN_SMEM] + [IN_VMEM] * 3, tops_of(1),
        )(side, eigen, own, middle)
        weights[1:] = after(weights[1:], own)
    else:
        eigens = call(
            functools.partial(order_kernel, halves), eigens, "order_eigen", 0,
            8 * blocks * BLK, [IN_SMEM, IN_VMEM],
        )(side, eigen)
    if pieces == 4:
        own, token_scores = call(
            functools.partial(near_kernel, [(None, 0, blocks)]),
            [f32(*own.shape), f32(1, tokens)], "add_near", 0, 12 * own.size,
            [IN_VMEM] * (2 + len(weights)),
            [*tops_of(1), pltpu.VMEM((1, tokens), jnp.float32), pltpu.SemaphoreType.DMA],
            out_spec=[IN_VMEM, pl.BlockSpec(memory_space=pl.ANY)],
        )(own, arrived.pop(1), *weights)
        weights = []
    chunks = list(arrived.values())
    if chunks:
        outputs = call(
            functools.partial(last_add_kernel, [(None, 0, blocks)] * len(chunks), len(weights)),
            [f32(act_blocks, rows, BLK), f32(grad_blocks, rows, BLK)]
            + [f32(1, tokens)] * bool(weights),
            "last_sums", 0, 16 * own.size, [IN_VMEM] * (1 + len(chunks) + len(weights)),
            [
                *tops_of(len(chunks)),
                pltpu.VMEM(own.shape, jnp.float32),
                pltpu.VMEM((1, tokens), jnp.float32),
                pltpu.SemaphoreType.DMA((blocks // GROUP + 1,)),
            ],
            out_spec=[pl.BlockSpec(memory_space=pl.ANY)] * (3 if weights else 2),
        )(own, *chunks, *weights)
        covariance = outputs[:2]
        if weights:
            token_scores = outputs[2]
    else:
        covariance = own[:act_blocks], own[act_blocks:]
        token_scores = call(
            score_kernel, f32(1, tokens), "token_scores", 0, 8 * tokens, [IN_VMEM] * len(weights)
        )(*weights)
    return (
        *covariance,
        *[eigen.reshape(-1) for eigen in eigens],
        token_scores.reshape(-1),
    )


def solution(mesh):
    return jax.shard_map(
        local,
        mesh=mesh,
        in_specs=(
            P(("groups", "dp"), "owner"),
            P(("groups", "dp"), "owner"),
            P("owner", "dp", None),
            P("owner", "dp", None),
        ),
        out_specs=(
            P(("groups", "owner"), "dp", None),
            P(("groups", "owner"), "dp", None),
            P(("groups", "owner")),
            P(("groups", "owner")),
            P(("groups", "dp")),
        ),
        check_vma=False,
    )
```
